32 devices in a mesh: ctx: 8 (over y, x, core), fsdp: 4 (over z).
Axes of the slice: x: 2, y: 2, z: 4, core: 2. Of those that a mesh axis runs over, the one named last changes fastest.
Arguments:
- activations: bfloat16 [4, 16, 128, 1536], P('fsdp', 'ctx'), may hold values from -6 to 6
- span_order: int32 [16], replicated, may hold values from 0 to 15, each once
- w_query: bfloat16 [1536, 1536], P('fsdp'), may hold values from -0.15625 to 0.15625
- w_key: bfloat16 [1536, 768], P('fsdp'), may hold values from -0.15625 to 0.15625
- w_value: bfloat16 [1536, 768], P('fsdp'), may hold values from -0.15625 to 0.15625
- w_out: bfloat16 [1536, 1536], P('fsdp'), may hold values from -4 to 4
- w_gate: bfloat16 [1536, 4096], P('fsdp'), may hold values from -0.15625 to 0.15625
- w_up: bfloat16 [1536, 4096], P('fsdp'), may hold values from -0.15625 to 0.15625
- w_down: bfloat16 [4096, 1536], P('fsdp'), may hold values from -0.09375 to 0.09375
- attn_gain: bfloat16 [1536], P('fsdp'), may hold values from 0.25 to 1.75
- ffn_gain: bfloat16 [1536], P('fsdp'), may hold values from 0.25 to 1.75
- cotangent: bfloat16 [4, 16, 128, 1536], P('fsdp', 'ctx'), may hold values from -6 to 6
Outputs:
- output: bfloat16 [4, 16, 128, 1536], P('fsdp', 'ctx')
- input_grad: float32 [4, 16, 128, 1536], P('fsdp', 'ctx')
- grad_query: float32 [1536, 1536], P('fsdp')
- grad_key: float32 [1536, 768], P('fsdp')
- grad_value: float32 [1536, 768], P('fsdp')
- grad_out: float32 [1536, 1536], P('fsdp')
- grad_gate: float32 [1536, 4096], P('fsdp')
- grad_up: float32 [1536, 4096], P('fsdp')
- grad_down: float32 [4096, 1536], P('fsdp')
- grad_attn_gain: float32 [1536], P('fsdp')
- grad_ffn_gain: float32 [1536], P('fsdp')
The draws below stay inside these ranges and needn't reach their ends.
Inputs may be any that keep to these rules, and one draw needn't show every extreme that they name: `span_order`: each span number of a sequence appears in exactly one slot.
All inputs are finite; a program needn't handle non-finite values.
Results may differ from the reference program's by a relative error of at most 0.025.
Values may be sent and summed in bfloat16 or wider, within the bound.
No kernel may reach another device: no remote copies, remote signals or barrier semaphores. Data moves between devices by JAX's collectives and lax.ppermute only.
A program may use at most 320 MiB of HBM per device.

```python
import math
import jax
import jax.numpy as jnp
from jax import lax

D = 1536
H = 16
KV = 8
DH = 96
FF = 4096
SPAN = 128
SLOTS = 16
LENGTH = 2048
SEQS = 4


def level_of(key, extent, shards, least, high):
    def one(dim, shards_of):
        draws = jax.random.uniform(jax.random.fold_in(jax.random.fold_in(key, 6), dim), (shards_of,), jnp.float32, least / len(shards), high / len(shards))
        return jnp.repeat(jnp.exp(draws), extent[dim] // shards_of).reshape((-1,) + (1,) * (len(extent) - dim - 1))

    level = one(*shards[0])
    for cut in shards[1:]:
        level = level * one(*cut)
    return level


def scatter_about(stream_key, dims, deviation, reach, pieces=(), kind=jnp.bfloat16):
    factor_of = level_of(stream_key, dims, pieces, -0.22, 0.18) if pieces else 1.0
    values = jax.random.normal(stream_key, dims, jnp.float32) * deviation * factor_of
    return jnp.minimum(jnp.maximum(values, -reach), reach).astype(kind)


def setup_inputs(seed: int = 0) -> dict:
    streams_of = jax.random.split(jax.random.key(seed), 13)
    activations = scatter_about(streams_of[0], (SEQS, SLOTS, SPAN, D), 1.0, 6.0, ((0, 4), (1, 8)))
    span_order = jax.random.permutation(streams_of[1], SLOTS).astype(jnp.int32)
    w_query = scatter_about(streams_of[2], (D, H * DH), D ** -0.5, 0.15625, ((0, 4),))
    w_key = scatter_about(streams_of[3], (D, KV * DH), D ** -0.5, 0.15625, ((0, 4),))
    w_value = scatter_about(streams_of[4], (D, KV * DH), D ** -0.5, 0.15625, ((0, 4),))
    w_out = scatter_about(streams_of[5], (H * DH, D), (0.5 * (LENGTH / (4 * H * DH)) ** 0.5), 4.0, ((0, 4),))
    w_gate = scatter_about(streams_of[6], (D, FF), D ** -0.5, 0.15625, ((0, 4),))
    w_up = scatter_about(streams_of[7], (D, FF), D ** -0.5, 0.15625, ((0, 4),))
    w_down = scatter_about(streams_of[8], (FF, D), FF ** -0.5, 0.09375, ((0, 4),))
    attn_gain = jnp.clip(1.0 + 0.15 * jax.random.normal(streams_of[9], (D,), jnp.float32), 0.25, 1.75).astype(jnp.bfloat16)
    ffn_gain = jnp.clip(1.0 + 0.15 * jax.random.normal(streams_of[10], (D,), jnp.float32), 0.25, 1.75).astype(jnp.bfloat16)
    cotangent = scatter_about(streams_of[11], (SEQS, SLOTS, SPAN, D), 1.0, 6.0, ((0, 4), (1, 8)))
    return {"activations": activations, "span_order": span_order, "w_query": w_query, "w_key": w_key, "w_value": w_value, "w_out": w_out, "w_gate": w_gate, "w_up": w_up, "w_down": w_down, "attn_gain": attn_gain, "ffn_gain": ffn_gain, "cotangent": cotangent}


@jax.custom_vjp
def low(v):
    return lax.optimization_barrier(v.astype(jnp.bfloat16)).astype(jnp.float32)

@jax.custom_vjp
def low_back(v):
    return v

def low_keep(v):
    return (low(v), None)

def low_pass(kept, grad):
    return (grad,)

def back_keep(v):
    return (v, None)

def back_low(kept, grad):
    return (low(grad),)
low.defvjp(low_keep, low_pass)
low_back.defvjp(back_keep, back_low)
epsilon = 1e-05
rope_base = 100000.0
masked_score = -1e+30

def exact_dot(left, right):
    return jnp.dot(left, right, precision=lax.Precision.HIGHEST)

def rms_norm(stream, gain):
    return stream * lax.rsqrt(lax.optimization_barrier(jnp.mean(stream * stream, axis=-1, keepdims=True)) + epsilon) * gain

def rope_turn(field, places):
    half = DH // 2
    freqs = jnp.exp(-math.log(rope_base) * 2.0 * jnp.arange(half, dtype=jnp.float32) / DH)
    angle = places.astype(jnp.float32)[:, None] * freqs[None, :]
    cosine = jnp.cos(angle)[:, None, :]
    sine = jnp.sin(angle)[:, None, :]
    first = field[..., :half]
    second = field[..., half:]
    return jnp.concatenate([first * cosine - second * sine, second * cosine + first * sine], axis=-1)

def attend(queries, keys, values, places):
    block = math.gcd(LENGTH, 512)
    group = H // KV
    scale = 1.0 / math.sqrt(DH)
    query_blocks = queries.reshape(LENGTH // block, block, KV, group, DH)
    place_blocks = places.reshape(LENGTH // block, block)

    def one_block(pair):
        query_part, place_part = pair
        scores = jnp.einsum('tjgd,sjd->jgts', query_part, keys, precision=lax.Precision.HIGHEST) * scale
        scores = low_back(scores)
        counted = places[None, :] <= place_part[:, None]
        scores = jnp.where(counted, scores, masked_score)
        top = lax.optimization_barrier(jnp.max(scores, axis=-1, keepdims=True))
        expo = jnp.exp(scores - top)
        probs = low(expo / lax.optimization_barrier(jnp.sum(expo, axis=-1, keepdims=True)))
        mixed = jnp.einsum('jgts,sjd->tjgd', probs, values, precision=lax.Precision.HIGHEST)
        return mixed.reshape(block, H * DH)
    return lax.map(jax.checkpoint(one_block), (query_blocks, place_blocks)).reshape(LENGTH, H * DH)

def apply_layer(stream, places, weights):
    w_query, w_key, w_value, w_out, w_gate, w_up, w_down, attn_gain, ffn_gain = weights
    normed1 = low(rms_norm(stream, attn_gain))
    queries = low(rope_turn(low_back(exact_dot(normed1, w_query)).reshape(LENGTH, H, DH), places))
    keys = low(rope_turn(low_back(exact_dot(normed1, w_key)).reshape(LENGTH, KV, DH), places))
    values = low(low_back(exact_dot(normed1, w_value))).reshape(LENGTH, KV, DH)
    queries = queries.reshape(LENGTH, KV, H // KV, DH)
    attended = low(low_back(attend(queries, keys, values, places)))
    stream1 = stream + low_back(exact_dot(attended, w_out))
    normed2 = low(rms_norm(stream1, ffn_gain))
    gate = low_back(exact_dot(normed2, w_gate))
    up_part = low_back(exact_dot(normed2, w_up))
    hidden = low(jax.nn.silu(gate) * up_part)
    return stream1 + low_back(exact_dot(hidden, w_down))

def reference(activations, span_order, w_query, w_key, w_value, w_out, w_gate, w_up, w_down, attn_gain, ffn_gain, cotangent):
    offsets = jnp.arange(SPAN, dtype=jnp.int32)
    places = (span_order.astype(jnp.int32)[:, None] * SPAN + offsets[None, :]).reshape(LENGTH).astype(jnp.int32)
    weights = (w_query.astype(jnp.float32), w_key.astype(jnp.float32), w_value.astype(jnp.float32), w_out.astype(jnp.float32), w_gate.astype(jnp.float32), w_up.astype(jnp.float32), w_down.astype(jnp.float32), attn_gain.astype(jnp.float32), ffn_gain.astype(jnp.float32))
    streams = activations.astype(jnp.float32).reshape(SEQS, LENGTH, D)

    def forward(stream_all, weight_all):

        def one_sequence(stream):
            return apply_layer(stream, places, weight_all)
        return lax.map(jax.checkpoint(one_sequence), stream_all)
    result, pull = jax.vjp(forward, streams, weights)
    d_input, d_weights = pull(cotangent.astype(jnp.float32).reshape(SEQS, LENGTH, D))
    return (result.astype(jnp.bfloat16).reshape(activations.shape), d_input.reshape(activations.shape), d_weights[0], d_weights[1], d_weights[2], d_weights[3], d_weights[4], d_weights[5], d_weights[6], d_weights[7], d_weights[8])
```

```python
import functools
import math

import jax
import jax.numpy as jnp
from jax import lax
from jax.experimental import pallas as pl
from jax.experimental.pallas import tpu as pltpu
from jax.sharding import PartitionSpec as P

DH = 96


epsilon = 1e-05
rope_base = 100000.0
masked_score = -1e30
LOG2E = math.log2(math.e)


def passed_along(block, axis, distance):
    devices = range(lax.axis_size(axis))
    route = [((i - distance) % len(devices), i) for i in devices]
    return lax.ppermute(block, axis, route)


def rope_tables(places):
    half = DH // 2
    freqs = jnp.exp(-math.log(rope_base) * 2.0 * jnp.arange(half, dtype=jnp.float32) / DH)
    angle = places.astype(jnp.float32)[:, None] * freqs[None, :]
    return (jnp.cos(angle)[:, None, :], jnp.sin(angle)[:, None, :])


def rope_turn(field, cosine, sine):
    half = DH // 2
    first = field[..., :half]
    second = field[..., half:]
    return jnp.concatenate(
        [first * cosine - second * sine, second * cosine + first * sine], axis=-1
    )


def rope_back(field, cosine, sine):
    half = DH // 2
    first = field[..., :half]
    second = field[..., half:]
    return jnp.concatenate(
        [first * cosine + second * sine, second * cosine - first * sine], axis=-1
    )


def norm_back(d_normed, stream, inv_rms, gain):
    scaled = d_normed * gain
    cubed = inv_rms * inv_rms * inv_rms
    return inv_rms * scaled - stream * cubed * jnp.mean(scaled * stream, axis=-1, keepdims=True)


def ring_layer(
    activations,
    span_order,
    w_query,
    w_key,
    w_value,
    w_out,
    w_gate,
    w_up,
    w_down,
    attn_gain,
    ffn_gain,
    cotangent,
):
    cycles = lax.axis_size("ctx")
    mine = lax.axis_index("ctx")
    span = activations.shape[2]
    width = activations.shape[3]
    tokens = 2 * span
    heads = w_query.shape[1] // DH
    kv_heads = w_key.shape[1] // DH
    group = heads // kv_heads
    scale = 1.0 / math.sqrt(DH)
    offsets = jnp.arange(span, dtype=jnp.int32)

    def places_of(owner):
        span_ids = lax.dynamic_slice_in_dim(span_order, 2 * owner, 2)
        return (span_ids[:, None] * span + offsets[None, :]).reshape(tokens)

    query_places = places_of(mine)
    cosine, sine = rope_tables(query_places)
    gathered = (
        lax.all_gather(w_query, "fsdp", axis=0, tiled=True),
        lax.all_gather(w_key, "fsdp", axis=0, tiled=True),
        lax.all_gather(w_value, "fsdp", axis=0, tiled=True),
        lax.all_gather(w_out, "fsdp", axis=0, tiled=True),
        lax.all_gather(w_gate, "fsdp", axis=0, tiled=True),
        lax.all_gather(w_up, "fsdp", axis=0, tiled=True),
        lax.all_gather(w_down, "fsdp", axis=0, tiled=True),
        lax.all_gather(attn_gain, "fsdp", axis=0, tiled=True),
        lax.all_gather(ffn_gain, "fsdp", axis=0, tiled=True),
    )
    (
        full_query,
        full_key,
        full_value,
        full_out,
        full_gate,
        full_up,
        full_down,
        gain_one,
        gain_two,
    ) = gathered
    stream = activations.reshape(tokens, width).astype(jnp.float32)
    inv_one = lax.rsqrt(jnp.mean(stream * stream, axis=-1, keepdims=True) + epsilon)
    normed1 = (stream * inv_one * gain_one).astype(jnp.bfloat16)
    query_raw = jnp.dot(normed1, full_query, preferred_element_type=jnp.float32).reshape(
        tokens, heads, DH
    )
    queries = (
        rope_turn(query_raw, cosine, sine).astype(jnp.bfloat16).reshape(tokens, kv_heads, group, DH)
    )
    key_raw = jnp.dot(normed1, full_key, preferred_element_type=jnp.float32).reshape(
        tokens, kv_heads, DH
    )
    keys = rope_turn(key_raw, cosine, sine).astype(jnp.bfloat16)
    values = (
        jnp.dot(normed1, full_value, preferred_element_type=jnp.float32)
        .astype(jnp.bfloat16)
        .reshape(tokens, kv_heads, DH)
    )

    def scores_with(key_piece, owner):
        scores = (
            jnp.einsum("tjgd,sjd->jgts", queries, key_piece, preferred_element_type=jnp.float32)
            * scale
        )
        counted = places_of(owner)[None, :] <= query_places[:, None]
        return jnp.where(counted, scores, masked_score)

    def absorb(state, key_piece, value_piece, owner):
        running_top, running_total, running_sum = state
        scores = scores_with(key_piece, owner)
        new_top = jnp.maximum(running_top, jnp.max(scores, axis=-1, keepdims=True))
        fading = jnp.exp(running_top - new_top)
        weights = jnp.exp(scores - new_top)
        running_total = fading * running_total + jnp.sum(weights, axis=-1, keepdims=True)
        running_sum = fading * running_sum + jnp.einsum(
            "jgts,sjd->jgtd",
            weights.astype(jnp.bfloat16),
            value_piece,
            preferred_element_type=jnp.float32,
        )
        return (new_top, running_total, running_sum)

    start_state = (
        jnp.full((kv_heads, group, tokens, 1), masked_score, jnp.float32),
        jnp.zeros((kv_heads, group, tokens, 1), jnp.float32),
        jnp.zeros((kv_heads, group, tokens, DH), jnp.float32),
    )
    state = absorb(start_state, keys, values, mine)

    def forward_turn(turn_index, carry):
        state_now, key_piece, value_piece = carry
        key_piece, value_piece = passed_along((key_piece, value_piece), "ctx", 1)
        owner = (mine - turn_index) % cycles
        return (absorb(state_now, key_piece, value_piece, owner), key_piece, value_piece)

    state, _, _ = lax.fori_loop(1, cycles, forward_turn, (state, keys, values))
    running_top, running_total, running_sum = state
    attended = running_sum / running_total
    log_total = running_top + jnp.log(running_total)
    attended_low = (
        jnp.transpose(attended, (2, 0, 1, 3)).reshape(tokens, heads * DH).astype(jnp.bfloat16)
    )
    stream_one = stream + jnp.dot(attended_low, full_out, preferred_element_type=jnp.float32)
    inv_two = lax.rsqrt(jnp.mean(stream_one * stream_one, axis=-1, keepdims=True) + epsilon)
    normed2 = (stream_one * inv_two * gain_two).astype(jnp.bfloat16)
    gate = jnp.dot(normed2, full_gate, preferred_element_type=jnp.float32)
    up_part = jnp.dot(normed2, full_up, preferred_element_type=jnp.float32)
    sigma = jax.nn.sigmoid(gate)
    hidden = (gate * sigma * up_part).astype(jnp.bfloat16)
    stream_two = stream_one + jnp.dot(hidden, full_down, preferred_element_type=jnp.float32)
    output = stream_two.astype(jnp.bfloat16).reshape(activations.shape)
    back_weights = (
        lax.all_gather(w_query, "fsdp", axis=0, tiled=True),
        lax.all_gather(w_key, "fsdp", axis=0, tiled=True),
        lax.all_gather(w_value, "fsdp", axis=0, tiled=True),
        lax.all_gather(w_out, "fsdp", axis=0, tiled=True),
        lax.all_gather(w_gate, "fsdp", axis=0, tiled=True),
        lax.all_gather(w_up, "fsdp", axis=0, tiled=True),
        lax.all_gather(w_down, "fsdp", axis=0, tiled=True),
        lax.all_gather(attn_gain, "fsdp", axis=0, tiled=True),
        lax.all_gather(ffn_gain, "fsdp", axis=0, tiled=True),
    )
    (
        back_query,
        back_key,
        back_value,
        back_out,
        back_gate,
        back_up,
        back_down,
        back_gain_one,
        back_gain_two,
    ) = back_weights
    grad_rows = cotangent.reshape(tokens, width)
    grad_stream = grad_rows.astype(jnp.float32)
    grad_down = jnp.einsum("tf,td->fd", hidden, grad_rows, preferred_element_type=jnp.float32)
    d_hidden = jnp.einsum("td,fd->tf", grad_rows, back_down, preferred_element_type=jnp.float32)
    d_gate = (d_hidden * up_part * sigma * (1.0 + gate * (1.0 - sigma))).astype(jnp.bfloat16)
    d_up = (d_hidden * gate * sigma).astype(jnp.bfloat16)
    grad_gate = jnp.einsum("td,tf->df", normed2, d_gate, preferred_element_type=jnp.float32)
    grad_up = jnp.einsum("td,tf->df", normed2, d_up, preferred_element_type=jnp.float32)
    d_normed2 = jnp.einsum(
        "tf,df->td", d_gate, back_gate, preferred_element_type=jnp.float32
    ) + jnp.einsum("tf,df->td", d_up, back_up, preferred_element_type=jnp.float32)
    grad_ffn_gain = jnp.sum(d_normed2 * stream_one * inv_two, axis=0)
    d_stream_one = grad_stream + norm_back(d_normed2, stream_one, inv_two, back_gain_two)
    d_branch = d_stream_one.astype(jnp.bfloat16)
    grad_out = jnp.einsum("tk,td->kd", attended_low, d_branch, preferred_element_type=jnp.float32)
    d_attended = jnp.einsum(
        "td,kd->tk", d_branch, back_out, preferred_element_type=jnp.float32
    ).astype(jnp.bfloat16)
    d_heads = jnp.transpose(d_attended.reshape(tokens, kv_heads, group, DH), (1, 2, 0, 3))
    delta = jnp.sum(d_heads.astype(jnp.float32) * attended, axis=-1, keepdims=True)

    def back_step(d_queries, d_keys, d_values, key_piece, value_piece, owner):
        scores = scores_with(key_piece, owner)
        probs = jnp.exp(scores - log_total)
        d_values = d_values + jnp.einsum(
            "jgts,jgtd->sjd",
            probs.astype(jnp.bfloat16),
            d_heads,
            preferred_element_type=jnp.float32,
        )
        d_probs = jnp.einsum(
            "jgtd,sjd->jgts", d_heads, value_piece, preferred_element_type=jnp.float32
        )
        d_scores = (probs * (d_probs - delta)).astype(jnp.bfloat16)
        d_queries = (
            d_queries
            + jnp.einsum("jgts,sjd->jgtd", d_scores, key_piece, preferred_element_type=jnp.float32)
            * scale
        )
        d_keys = (
            d_keys
            + jnp.einsum("jgts,tjgd->sjd", d_scores, queries, preferred_element_type=jnp.float32)
            * scale
        )
        return (d_queries, d_keys, d_values)

    def pass_grads(d_keys, d_values):
        return (
            passed_along(d_keys.astype(jnp.bfloat16), "ctx", 1).astype(d_keys.dtype),
            passed_along(d_values.astype(jnp.bfloat16), "ctx", 1).astype(d_values.dtype),
        )

    zero_queries = jnp.zeros((kv_heads, group, tokens, DH), jnp.float32)
    zero_keys = jnp.zeros((tokens, kv_heads, DH), jnp.float32)
    d_queries, d_keys, d_values = back_step(zero_queries, zero_keys, zero_keys, keys, values, mine)

    def backward_turn(turn_index, carry):
        d_queries_now, d_keys_now, d_values_now, key_piece, value_piece = carry
        key_piece, value_piece = passed_along((key_piece, value_piece), "ctx", 1)
        d_keys_now, d_values_now = pass_grads(d_keys_now, d_values_now)
        owner = (mine - turn_index) % cycles
        d_queries_now, d_keys_now, d_values_now = back_step(
            d_queries_now, d_keys_now, d_values_now, key_piece, value_piece, owner
        )
        return (d_queries_now, d_keys_now, d_values_now, key_piece, value_piece)

    d_queries, d_keys, d_values, _, _ = lax.fori_loop(
        1, cycles, backward_turn, (d_queries, d_keys, d_values, keys, values)
    )
    d_keys, d_values = pass_grads(d_keys, d_values)
    d_query_rows = jnp.transpose(d_queries, (2, 0, 1, 3)).reshape(tokens, heads, DH)
    d_query = rope_back(d_query_rows, cosine, sine).astype(jnp.bfloat16).reshape(tokens, heads * DH)
    d_key = rope_back(d_keys, cosine, sine).astype(jnp.bfloat16).reshape(tokens, kv_heads * DH)
    d_value = d_values.astype(jnp.bfloat16).reshape(tokens, kv_heads * DH)
    grad_query = jnp.einsum("td,tk->dk", normed1, d_query, preferred_element_type=jnp.float32)
    grad_key = jnp.einsum("td,tk->dk", normed1, d_key, preferred_element_type=jnp.float32)
    grad_value = jnp.einsum("td,tk->dk", normed1, d_value, preferred_element_type=jnp.float32)
    d_normed1 = (
        jnp.einsum("tk,dk->td", d_query, back_query, preferred_element_type=jnp.float32)
        + jnp.einsum("tk,dk->td", d_key, back_key, preferred_element_type=jnp.float32)
        + jnp.einsum("tk,dk->td", d_value, back_value, preferred_element_type=jnp.float32)
    )
    grad_attn_gain = jnp.sum(d_normed1 * stream * inv_one, axis=0)
    input_grad = (d_stream_one + norm_back(d_normed1, stream, inv_one, back_gain_one)).reshape(
        activations.shape
    )
    shares = (
        lax.psum_scatter(
            grad_query.astype(jnp.bfloat16), "fsdp", scatter_dimension=0, tiled=True
        ).astype(jnp.float32),
        lax.psum_scatter(
            grad_key.astype(jnp.bfloat16), "fsdp", scatter_dimension=0, tiled=True
        ).astype(jnp.float32),
        lax.psum_scatter(
            grad_value.astype(jnp.bfloat16), "fsdp", scatter_dimension=0, tiled=True
        ).astype(jnp.float32),
        lax.psum_scatter(
            grad_out.astype(jnp.bfloat16), "fsdp", scatter_dimension=0, tiled=True
        ).astype(jnp.float32),
        lax.psum_scatter(
            grad_gate.astype(jnp.bfloat16), "fsdp", scatter_dimension=0, tiled=True
        ).astype(jnp.float32),
        lax.psum_scatter(
            grad_up.astype(jnp.bfloat16), "fsdp", scatter_dimension=0, tiled=True
        ).astype(jnp.float32),
        lax.psum_scatter(
            grad_down.astype(jnp.bfloat16), "fsdp", scatter_dimension=0, tiled=True
        ).astype(jnp.float32),
        lax.psum_scatter(
            grad_attn_gain.astype(jnp.bfloat16), "fsdp", scatter_dimension=0, tiled=True
        ).astype(jnp.float32),
        lax.psum_scatter(
            grad_ffn_gain.astype(jnp.bfloat16), "fsdp", scatter_dimension=0, tiled=True
        ).astype(jnp.float32),
    )
    shares = (
        lax.psum(shares[0].astype(jnp.bfloat16), "ctx").astype(jnp.float32),
        lax.psum(shares[1].astype(jnp.bfloat16), "ctx").astype(jnp.float32),
        lax.psum(shares[2].astype(jnp.bfloat16), "ctx").astype(jnp.float32),
        lax.psum(shares[3].astype(jnp.bfloat16), "ctx").astype(jnp.float32),
        lax.psum(shares[4].astype(jnp.bfloat16), "ctx").astype(jnp.float32),
        lax.psum(shares[5].astype(jnp.bfloat16), "ctx").astype(jnp.float32),
        lax.psum(shares[6].astype(jnp.bfloat16), "ctx").astype(jnp.float32),
        lax.psum(shares[7].astype(jnp.bfloat16), "ctx").astype(jnp.float32),
        lax.psum(shares[8].astype(jnp.bfloat16), "ctx").astype(jnp.float32),
    )
    return (
        output,
        input_grad,
        shares[0],
        shares[1],
        shares[2],
        shares[3],
        shares[4],
        shares[5],
        shares[6],
        shares[7],
        shares[8],
    )


LANES = 128
CORE, ALONG_X, ALONG_Y = 1, 2, 4
RELATIVE = (0, 2, 4, 6, 1, 3, 5, 7)


def lane_dot(left, right):
    return lax.dot_general(left, right, (((1,), (1,)), ((), ())), preferred_element_type=jnp.float32)


def plain_dot(left, right):
    return lax.dot_general(left, right, (((1,), (0,)), ((), ())), preferred_element_type=jnp.float32)


def row_dot(left, right):
    return lax.dot_general(left, right, (((0,), (0,)), ((), ())), preferred_element_type=jnp.float32)


def rows_at(index, size):
    return pl.ds(pl.multiple_of(index * size, size), size)


def attend_kernel(
    span,
    near_ref,
    slot_ref,
    raw_ref,
    cos_ref,
    sin_ref,
    query_ref,
    key_ref,
    value_ref,
    low_ref,
    mixed_ref,
    total_ref,
    score_ref,
):
    spans = near_ref.shape[0]
    block = 2 * span
    pair = 2 * block
    turns = spans // 2
    factor = LOG2E / math.sqrt(DH)

    def place(index, _):
        raw = raw_ref[rows_at(near_ref[index], span), :]
        cosine = cos_ref[rows_at(index, span), :]
        sine = sin_ref[rows_at(index, span), :]

        def turned(head):
            field = raw[:, head * LANES : (head + 1) * LANES]
            return (field * cosine + pltpu.roll(field, LANES // 2, 1) * sine).astype(jnp.bfloat16)

        first = (index // 2) * 4 + index % 2
        query_ref[rows_at(first, span), :] = turned(0)
        query_ref[rows_at(first + 2, span), :] = turned(1)
        key_ref[rows_at(index, span), :] = turned(2)
        value_ref[rows_at(index, span), :] = raw[:, 3 * LANES :].astype(jnp.bfloat16)
        return 0

    lax.fori_loop(0, spans, place, 0)
    row = lax.broadcasted_iota(jnp.int32, (pair, block), 0) % block
    column = lax.broadcasted_iota(jnp.int32, (pair, block), 1)
    keep = column <= row

    def widest(top, scores):
        for start in range(0, block, LANES):
            top = jnp.maximum(top, scores[:, start : start + LANES])
        return top

    def one_block(turn, _):
        query = query_ref[rows_at(turn, pair), :]

        def score(step, top):
            scores = lane_dot(query, key_ref[rows_at(step, block), :])
            score_ref[:, rows_at(step, block)] = scores
            return widest(top, scores)

        top = lax.fori_loop(0, turn, score, jnp.full((pair, LANES), masked_score, jnp.float32))
        scores = lane_dot(query, key_ref[rows_at(turn, block), :])
        scores = jnp.where(keep, scores, masked_score)
        score_ref[:, rows_at(turn, block)] = scores
        top = jnp.max(widest(top, scores), axis=1, keepdims=True) * factor

        def weigh(step, carry):
            total, mixed = carry
            weights = jnp.exp2(score_ref[:, rows_at(step, block)] * factor - top)
            for start in range(0, block, LANES):
                total = total + weights[:, start : start + LANES]
            mixed = mixed + plain_dot(
                weights.astype(jnp.bfloat16), value_ref[rows_at(step, block), :]
            )
            return (total, mixed)

        zero = jnp.zeros((pair, LANES), jnp.float32)
        total, mixed = lax.fori_loop(0, turn + 1, weigh, (zero, zero))
        total = jnp.sum(total, axis=1, keepdims=True)
        mixed = mixed / total
        mixed_ref[rows_at(turn, pair), :] = mixed
        level = jnp.broadcast_to(top + jnp.log2(total), (pair, LANES))
        total_ref[rows_at(turn, 8), :] = jnp.transpose(level)[:8]
        gap = jnp.zeros((block, LANES), jnp.float32)
        both = jnp.concatenate([mixed[:block], gap], axis=1) + pltpu.roll(
            jnp.concatenate([mixed[block:], gap], axis=1), DH, 1
        )
        both = both[:, : 2 * DH].astype(jnp.bfloat16)
        low_ref[rows_at(slot_ref[2 * turn], span), :] = both[:span]
        low_ref[rows_at(slot_ref[2 * turn + 1], span), :] = both[span:]
        return 0

    lax.fori_loop(0, turns, one_block, 0)


def attend(near, slot, raw, cosine, sine, span):
    tokens = raw.shape[0]
    whole = pl.BlockSpec(memory_space=pltpu.VMEM)
    small = pl.BlockSpec(memory_space=pltpu.SMEM)
    shapes = (
        jax.ShapeDtypeStruct((2 * tokens, LANES), jnp.bfloat16),
        jax.ShapeDtypeStruct((tokens, LANES), jnp.bfloat16),
        jax.ShapeDtypeStruct((tokens, LANES), jnp.bfloat16),
        jax.ShapeDtypeStruct((tokens, 2 * DH), jnp.bfloat16),
        jax.ShapeDtypeStruct((2 * tokens, LANES), jnp.float32),
        jax.ShapeDtypeStruct((8 * (tokens // (2 * span)), 4 * span), jnp.float32),
    )
    return pl.pallas_call(
        functools.partial(attend_kernel, span),
        out_shape=shapes,
        in_specs=[small, small, whole, whole, whole],
        out_specs=[whole] * len(shapes),
        scratch_shapes=[pltpu.VMEM((4 * span, tokens), jnp.float32)],
        compiler_params=pltpu.CompilerParams(vmem_limit_bytes=40 * 2**20),
        cost_estimate=pl.CostEstimate(
            flops=4 * tokens * tokens * LANES, bytes_accessed=16 * tokens * LANES, transcendentals=tokens * tokens
        ),
    )(near, slot, raw, cosine, sine)


def attend_back_kernel(
    span,
    near_ref,
    slot_ref,
    query_ref,
    key_ref,
    value_ref,
    mixed_ref,
    total_ref,
    grad_ref,
    cos_ref,
    sin_ref,
    out_ref,
    head_ref,
    delta_ref,
    query_sum,
):
    spans = near_ref.shape[0]
    block = 2 * span
    pair = 2 * block
    turns = spans // 2
    factor = LOG2E / math.sqrt(DH)
    scale = 1.0 / math.sqrt(DH)
    lane = lax.broadcasted_iota(jnp.int32, (span, LANES), 1)

    def split(index, _):
        grad = grad_ref[rows_at(slot_ref[index], span), :].astype(jnp.float32)
        first = (index // 2) * 4 + index % 2
        one = jnp.where(lane < DH, grad[:, :LANES], 0.0)
        two = jnp.where(lane < DH, pltpu.roll(grad, 2 * LANES - DH, 1)[:, :LANES], 0.0)
        head_ref[rows_at(first, span), :] = one.astype(jnp.bfloat16)
        head_ref[rows_at(first + 2, span), :] = two.astype(jnp.bfloat16)
        return 0

    lax.fori_loop(0, spans, split, 0)

    def prepare(turn, _):
        here = rows_at(turn, pair)
        product = head_ref[here, :].astype(jnp.float32) * mixed_ref[here, :]
        delta = jnp.sum(jnp.transpose(product), axis=0, keepdims=True)
        delta_ref[rows_at(turn, 8), :] = jnp.broadcast_to(delta, (8, pair))
        query_sum[here, :] = jnp.zeros((pair, LANES), jnp.float32)
        return 0

    lax.fori_loop(0, turns, prepare, 0)
    row = lax.broadcasted_iota(jnp.int32, (block, pair), 0)
    column = lax.broadcasted_iota(jnp.int32, (block, pair), 1) % block
    keep = row <= column

    def turned_back(field, index):
        cosine = cos_ref[rows_at(index, span), :]
        sine = sin_ref[rows_at(index, span), :]
        field = field * scale
        return (field * cosine - pltpu.roll(field, LANES // 2, 1) * sine).astype(jnp.bfloat16)

    def one_block(turn, _):
        key = key_ref[rows_at(turn, block), :]
        value = value_ref[rows_at(turn, block), :]

        def step_with(step, carry, mask):
            key_sum, value_sum = carry
            here = rows_at(step, pair)
            query = query_ref[here, :]
            head = head_ref[here, :]
            level = total_ref[rows_at(step, 8), :][:1]
            delta = delta_ref[rows_at(step, 8), :][:1]
            probs = jnp.exp2(lane_dot(key, query) * factor - level)
            if mask is not None:
                probs = jnp.where(mask, probs, 0.0)
            d_scores = (probs * (lane_dot(value, head) - delta)).astype(jnp.bfloat16)
            value_sum = value_sum + plain_dot(probs.astype(jnp.bfloat16), head)
            key_sum = key_sum + plain_dot(d_scores, query)
            query_sum[here, :] += row_dot(d_scores, key)
            return (key_sum, value_sum)

        zero = jnp.zeros((block, LANES), jnp.float32)
        carry = step_with(turn, (zero, zero), keep)
        key_sum, value_sum = lax.fori_loop(
            turn + 1, turns, lambda step, now: step_with(step, now, None), carry
        )
        for part in range(2):
            index = 2 * turn + part
            here = rows_at(near_ref[index], span)
            rows = slice(part * span, (part + 1) * span)
            out_ref[here, 2 * LANES : 3 * LANES] = turned_back(key_sum[rows], index)
            out_ref[here, 3 * LANES :] = value_sum[rows].astype(jnp.bfloat16)
        return 0

    lax.fori_loop(0, turns, one_block, 0)

    def place(index, _):
        first = (index // 2) * 4 + index % 2
        here = rows_at(near_ref[index], span)
        out_ref[here, :LANES] = turned_back(query_sum[rows_at(first, span), :], index)
        out_ref[here, LANES : 2 * LANES] = turned_back(
            query_sum[rows_at(first + 2, span), :], index
        )
        return 0

    lax.fori_loop(0, spans, place, 0)


def attend_back(near, slot, query, key, value, mixed, total, grad, cosine, sine, span):
    tokens = key.shape[0]
    whole = pl.BlockSpec(memory_space=pltpu.VMEM)
    small = pl.BlockSpec(memory_space=pltpu.SMEM)
    return pl.pallas_call(
        functools.partial(attend_back_kernel, span),
        out_shape=jax.ShapeDtypeStruct((tokens, 4 * LANES), jnp.bfloat16),
        in_specs=[small, small] + [whole] * 8,
        out_specs=whole,
        scratch_shapes=[
            pltpu.VMEM((2 * tokens, LANES), jnp.bfloat16),
            pltpu.VMEM(total.shape, jnp.float32),
            pltpu.VMEM((2 * tokens, LANES), jnp.float32),
        ],
        compiler_params=pltpu.CompilerParams(vmem_limit_bytes=40 * 2**20),
        cost_estimate=pl.CostEstimate(
            flops=10 * tokens * tokens * LANES, bytes_accessed=24 * tokens * LANES, transcendentals=tokens * tokens
        ),
    )(near, slot, query, key, value, mixed, total, grad, cosine, sine)


def turn_tables(tokens):
    half = DH // 2
    freqs = jnp.exp(-math.log(rope_base) * 2.0 * jnp.arange(half, dtype=jnp.float32) / DH)
    angle = jnp.arange(tokens, dtype=jnp.int32).astype(jnp.float32)[:, None] * freqs[None, :]
    gap = jnp.zeros((tokens, LANES // 2 - half), jnp.float32)
    cosine, sine = jnp.cos(angle), jnp.sin(angle)
    return (
        jnp.concatenate([cosine, gap, cosine, gap], axis=1),
        jnp.concatenate([-sine, gap, sine, gap], axis=1),
    )


def swap(block, bits):
    routes = [(i, i ^ bits) for i in range(lax.axis_size("ctx"))]
    return lax.ppermute(block, "ctx", routes)


def gather_spans(block):
    rows = block.shape[0]
    half = rows // 2
    twin = swap(block, CORE)
    from_x = swap(block, ALONG_X)
    from_y = swap(block, ALONG_Y)
    low_half = swap(from_x[:half], ALONG_Y)
    high_half = swap(from_y[half:], ALONG_X)
    corner = jnp.concatenate([low_half, high_half], axis=0)
    twin_x = swap(from_x, CORE)
    twin_y = swap(from_y, CORE)
    twin_corner = swap(corner, CORE)
    return jnp.stack([block, from_x, from_y, corner, twin, twin_x, twin_y, twin_corner])


def add_low(*parts):
    total = parts[0].astype(jnp.float32)
    for part in parts[1:]:
        total = total + part.astype(jnp.float32)
    return total


def scatter_spans(blocks):
    half = blocks.shape[1] // 2
    pairs = add_low(blocks[:4], swap(blocks[4:], CORE))
    low = pairs.astype(jnp.bfloat16)
    got_x = swap(jnp.concatenate([low[3, :half], low[1, :half]], axis=0), ALONG_X)
    got_y = swap(jnp.concatenate([low[3, half:], low[2, half:]], axis=0), ALONG_Y)
    to_y = add_low(low[2, :half], got_x[:half]).astype(jnp.bfloat16)
    to_x = add_low(low[1, half:], got_y[:half]).astype(jnp.bfloat16)
    late_x = swap(to_x, ALONG_X)
    late_y = swap(to_y, ALONG_Y)
    top = add_low(pairs[0, :half], got_x[half:], late_y)
    bottom = add_low(pairs[0, half:], got_y[half:], late_x)
    return jnp.concatenate([top, bottom], axis=0)


def columns_of(weight, start, size):
    return lax.dynamic_slice_in_dim(weight, start, size, axis=1)


def spread_heads(fields):
    rows = fields.shape[0]
    half = DH // 2
    turned = fields[:, : 3 * DH].reshape(rows, 3, 2, half)
    turned = jnp.pad(turned, ((0, 0), (0, 0), (0, 0), (0, LANES // 2 - half)))
    value = jnp.pad(fields[:, 3 * DH :], ((0, 0), (0, LANES - DH)))
    return jnp.concatenate([turned.reshape(rows, 3 * LANES), value], axis=1)


def pack_heads(fields):
    rows = fields.shape[0]
    half = DH // 2
    turned = fields[:, : 3 * LANES].reshape(rows, 3, 2, LANES // 2)[..., :half]
    return jnp.concatenate(
        [turned.reshape(rows, 3 * DH), fields[:, 3 * LANES : 3 * LANES + DH]], axis=1
    )


def plane_layer(
    activations,
    span_order,
    w_query,
    w_key,
    w_value,
    w_out,
    w_gate,
    w_up,
    w_down,
    attn_gain,
    ffn_gain,
    cotangent,
):
    bf16, f32 = jnp.bfloat16, jnp.float32
    cycles = lax.axis_size("ctx")
    quarters = lax.axis_size("fsdp")
    mine = lax.axis_index("ctx")
    span = activations.shape[2]
    width = activations.shape[3]
    tokens = 2 * span
    length = cycles * tokens
    shard = w_query.shape[0]
    hidden_size = quarters * w_down.shape[0]
    strip = hidden_size // (quarters * cycles)
    part = hidden_size // cycles
    slab = w_out.shape[0] // cycles
    relative = jnp.array(RELATIVE, jnp.int32)
    owners = mine ^ relative
    away = mine ^ jnp.arange(cycles, dtype=jnp.int32)
    seat = (away & 1) * 4 + (away >> 2) * 2 + ((away >> 1) & 1)
    slot_of = jnp.argsort(span_order).astype(jnp.int32)
    near_slot = 2 * seat[slot_of // 2] + slot_of % 2

    fields = jnp.concatenate(
        [
            columns_of(w_query, mine * 2 * DH, 2 * DH),
            columns_of(w_key, mine * DH, DH),
            columns_of(w_value, mine * DH, DH),
        ],
        axis=1,
    )
    four = fields.shape[1]
    out_rows = lax.dynamic_slice_in_dim(w_out, mine * slab, slab, axis=0)
    out_rows = jnp.concatenate(
        [out_rows[:, start : start + four] for start in range(0, width, four)], axis=0
    )
    gains = jnp.pad(jnp.stack([attn_gain, ffn_gain]), ((0, 14), (0, four - shard)))
    first = jnp.concatenate([fields, out_rows, gains], axis=0)
    first = lax.all_gather(first, "fsdp", axis=0)
    gate_up = jnp.concatenate(
        [
            columns_of(weight, (quarter * cycles + mine) * strip, strip)
            for weight in (w_gate, w_up)
            for quarter in range(quarters)
        ],
        axis=1,
    )
    gate_up = lax.all_gather(gate_up, "fsdp", axis=0, tiled=True)
    down = lax.dynamic_slice_in_dim(w_down, mine * strip, strip, axis=0)
    down = lax.all_gather(down, "fsdp", axis=0, tiled=True)

    raw_stream = activations.reshape(tokens, width)
    all_streams = gather_spans(raw_stream).reshape(length, width).astype(f32)
    grad_rows = cotangent.reshape(tokens, width)

    w_fields = first[:, :shard].reshape(width, four)
    w_spread = spread_heads(w_fields)
    gain_one = first[:, shard + slab * (width // four), :shard].reshape(width).astype(f32)
    gain_two = first[:, shard + slab * (width // four) + 1, :shard].reshape(width).astype(f32)
    out_part = first[:, shard : shard + slab * (width // four)]
    out_part = out_part.reshape(quarters * slab * (width // four), four)
    out_all = gather_spans(out_part).reshape(cycles, quarters, width // four, slab, four)
    full_out = jnp.transpose(out_all[seat], (1, 0, 3, 2, 4)).reshape(width, width)

    inv_all = lax.rsqrt(jnp.mean(all_streams * all_streams, axis=-1, keepdims=True) + epsilon)
    normed1 = (all_streams * inv_all * gain_one).astype(bf16)
    raw_fields = jnp.dot(normed1, w_spread, preferred_element_type=f32)
    cosine, sine = turn_tables(length)
    query, key, value, attended_low, attended, level = attend(
        near_slot, slot_of, raw_fields, cosine, sine, span
    )
    heads_low = lax.all_to_all(attended_low.reshape(cycles, tokens, 2 * DH), "ctx", 0, 0)
    heads_low = jnp.transpose(heads_low, (1, 0, 2)).reshape(tokens, width)
    stream = raw_stream.astype(f32)
    stream_one = stream + jnp.dot(heads_low, full_out, preferred_element_type=f32)
    inv_two = lax.rsqrt(jnp.mean(stream_one * stream_one, axis=-1, keepdims=True) + epsilon)
    normed2 = gather_spans((stream_one * inv_two * gain_two).astype(bf16)).reshape(length, width)
    all_grads = gather_spans(grad_rows).reshape(length, width)

    both = jnp.dot(normed2, gate_up, preferred_element_type=f32)
    gate, up_part = both[:, :part], both[:, part:]
    sigma = jax.nn.sigmoid(gate)
    hidden = (gate * sigma * up_part).astype(bf16)
    ffn_sum = jnp.dot(hidden, down, preferred_element_type=f32).astype(bf16)
    d_hidden = lax.dot_general(
        all_grads, down, (((1,), (1,)), ((), ())), preferred_element_type=f32
    )
    d_gate = d_hidden * up_part * sigma * (1.0 + gate * (1.0 - sigma))
    d_up = d_hidden * gate * sigma
    d_both = jnp.concatenate([d_gate, d_up], axis=1).astype(bf16)
    d_normed2 = lax.dot_general(
        d_both, gate_up, (((1,), (1,)), ((), ())), preferred_element_type=f32
    ).astype(bf16)
    d_normed2 = scatter_spans(d_normed2.reshape(cycles, tokens, width))

    scaled = d_normed2 * gain_two
    d_stream_one = (
        grad_rows.astype(f32)
        + inv_two * scaled
        - stream_one
        * (inv_two * inv_two * inv_two)
        * jnp.mean(scaled * stream_one, axis=-1, keepdims=True)
    )
    d_branch = d_stream_one.astype(bf16)
    d_attended = lax.dot_general(
        d_branch, full_out, (((1,), (1,)), ((), ())), preferred_element_type=f32
    ).astype(bf16)
    d_attended = jnp.transpose(d_attended.reshape(tokens, cycles, 2 * DH), (1, 0, 2))
    d_attended = lax.all_to_all(d_attended, "ctx", 0, 0).reshape(length, 2 * DH)
    d_attended = jnp.pad(d_attended, ((0, 0), (0, 2 * LANES - 2 * DH)))
    d_fields = attend_back(
        near_slot, slot_of, query, key, value, attended, level, d_attended, cosine, sine, span
    )
    d_normed1 = lax.dot_general(
        d_fields, w_spread, (((1,), (1,)), ((), ())), preferred_element_type=f32
    ).astype(bf16)
    d_normed1 = scatter_spans(d_normed1.reshape(cycles, tokens, width))
    inv_one = lax.rsqrt(jnp.mean(stream * stream, axis=-1, keepdims=True) + epsilon)
    scaled = d_normed1 * gain_one
    input_grad = (
        d_stream_one
        + inv_one * scaled
        - stream
        * (inv_one * inv_one * inv_one)
        * jnp.mean(scaled * stream, axis=-1, keepdims=True)
    )

    grad_down = row_dot(hidden, all_grads).astype(bf16)
    grad_both = row_dot(normed2, d_both)
    grad_ffn = jnp.sum(grad_both * gate_up.astype(f32), axis=1) / gain_two
    grad_down = lax.psum_scatter(grad_down, "fsdp", scatter_dimension=0, tiled=True)
    grad_both = lax.psum_scatter(grad_both.astype(bf16), "fsdp", scatter_dimension=0, tiled=True)
    grad_down = lax.all_gather(grad_down, "ctx", axis=0, tiled=True).astype(f32)
    grad_both = lax.all_gather(grad_both, "ctx", axis=0).reshape(
        cycles, shard, 2, quarters, strip
    )
    grad_both = jnp.transpose(grad_both, (2, 1, 3, 0, 4)).reshape(2, shard, hidden_size)

    grad_out = row_dot(heads_low, d_branch).astype(bf16)
    grad_out = grad_out.reshape(quarters, cycles, slab, width)
    grad_out = jnp.transpose(grad_out, (1, 0, 2, 3))[owners]
    grad_out = scatter_spans(grad_out.reshape(cycles, quarters * slab, width)).astype(bf16)
    grad_out = grad_out.reshape(quarters, slab, width // four, four)
    grad_out = jnp.transpose(grad_out, (0, 2, 1, 3)).reshape(quarters, -1, four)

    grad_fields = row_dot(normed1, d_fields)
    grad_attn = jnp.sum(grad_fields * w_spread.astype(f32), axis=1) / gain_one
    grad_gains = jnp.stack([grad_attn, grad_ffn]).reshape(2, quarters, shard)
    grad_gains = jnp.pad(jnp.transpose(grad_gains, (1, 0, 2)), ((0, 0), (0, 14), (0, four - shard)))
    grad_fields = pack_heads(grad_fields).reshape(quarters, shard, four)
    last = jnp.concatenate([grad_fields.astype(bf16), grad_out, grad_gains.astype(bf16)], axis=1)
    last = lax.psum_scatter(last, "fsdp", scatter_dimension=0, tiled=False)
    last = lax.all_gather(last, "ctx", axis=0).astype(f32)
    split = shard + slab * (width // four)
    grad_query = jnp.transpose(last[:, :shard, : 2 * DH], (1, 0, 2)).reshape(shard, -1)
    grad_key = jnp.transpose(last[:, :shard, 2 * DH : 3 * DH], (1, 0, 2)).reshape(shard, -1)
    grad_value = jnp.transpose(last[:, :shard, 3 * DH :], (1, 0, 2)).reshape(shard, -1)
    grad_out = last[:, shard:split].reshape(cycles, width // four, slab, four)
    grad_out = jnp.transpose(grad_out, (0, 2, 1, 3)).reshape(shard, width)
    grad_gains = jnp.sum(last[:, split : split + 2, :shard], axis=0)

    output = stream_one + scatter_spans(ffn_sum.reshape(cycles, tokens, width))
    return (
        output.astype(bf16).reshape(activations.shape),
        input_grad.reshape(activations.shape),
        grad_query,
        grad_key,
        grad_value,
        grad_out,
        grad_both[0].astype(f32),
        grad_both[1].astype(f32),
        grad_down,
        grad_gains[0],
        grad_gains[1],
    )


def solution(mesh):
    in_specs = (
        P("fsdp", "ctx", None, None),
        P(),
        P("fsdp", None),
        P("fsdp", None),
        P("fsdp", None),
        P("fsdp", None),
        P("fsdp", None),
        P("fsdp", None),
        P("fsdp", None),
        P("fsdp"),
        P("fsdp"),
        P("fsdp", "ctx", None, None),
    )
    out_specs = (
        P("fsdp", "ctx", None, None),
        P("fsdp", "ctx", None, None),
        P("fsdp", None),
        P("fsdp", None),
        P("fsdp", None),
        P("fsdp", None),
        P("fsdp", None),
        P("fsdp", None),
        P("fsdp", None),
        P("fsdp"),
        P("fsdp"),
    )
    cycles = mesh.shape["ctx"]

    def per_device(*arrays):
        heads = arrays[3].shape[1] // DH
        if cycles == len(RELATIVE) == heads and arrays[2].shape[1] == 2 * heads * DH:
            return plane_layer(*arrays)
        return ring_layer(*arrays)

    return jax.shard_map(
        per_device, mesh=mesh, in_specs=in_specs, out_specs=out_specs, check_vma=False
    )
```

```python
import functools
import math

import jax
import jax.numpy as jnp
from jax import lax
from jax.experimental import pallas as pl
from jax.experimental.pallas import tpu as pltpu
from jax.sharding import PartitionSpec as P

DH = 96


epsilon = 1e-05
rope_base = 100000.0
masked_score = -1e30
LOG2E = math.log2(math.e)


def passed_along(block, axis, distance):
    devices = range(lax.axis_size(axis))
    route = [((i - distance) % len(devices), i) for i in devices]
    return lax.ppermute(block, axis, route)


def rope_tables(places):
    half = DH // 2
    freqs = jnp.exp(-math.log(rope_base) * 2.0 * jnp.arange(half, dtype=jnp.float32) / DH)
    angle = places.astype(jnp.float32)[:, None] * freqs[None, :]
    return (jnp.cos(angle)[:, None, :], jnp.sin(angle)[:, None, :])


def rope_turn(field, cosine, sine):
    half = DH // 2
    first = field[..., :half]
    second = field[..., half:]
    return jnp.concatenate(
        [first * cosine - second * sine, second * cosine + first * sine], axis=-1
    )


def rope_back(field, cosine, sine):
    half = DH // 2
    first = field[..., :half]
    second = field[..., half:]
    return jnp.concatenate(
        [first * cosine + second * sine, second * cosine - first * sine], axis=-1
    )


def norm_back(d_normed, stream, inv_rms, gain):
    scaled = d_normed * gain
    cubed = inv_rms * inv_rms * inv_rms
    return inv_rms * scaled - stream * cubed * jnp.mean(scaled * stream, axis=-1, keepdims=True)


def ring_layer(
    activations,
    span_order,
    w_query,
    w_key,
    w_value,
    w_out,
    w_gate,
    w_up,
    w_down,
    attn_gain,
    ffn_gain,
    cotangent,
):
    cycles = lax.axis_size("ctx")
    mine = lax.axis_index("ctx")
    span = activations.shape[2]
    width = activations.shape[3]
    tokens = 2 * span
    heads = w_query.shape[1] // DH
    kv_heads = w_key.shape[1] // DH
    group = heads // kv_heads
    scale = 1.0 / math.sqrt(DH)
    offsets = jnp.arange(span, dtype=jnp.int32)

    def places_of(owner):
        span_ids = lax.dynamic_slice_in_dim(span_order, 2 * owner, 2)
        return (span_ids[:, None] * span + offsets[None, :]).reshape(tokens)

    query_places = places_of(mine)
    cosine, sine = rope_tables(query_places)
    gathered = (
        lax.all_gather(w_query, "fsdp", axis=0, tiled=True),
        lax.all_gather(w_key, "fsdp", axis=0, tiled=True),
        lax.all_gather(w_value, "fsdp", axis=0, tiled=True),
        lax.all_gather(w_out, "fsdp", axis=0, tiled=True),
        lax.all_gather(w_gate, "fsdp", axis=0, tiled=True),
        lax.all_gather(w_up, "fsdp", axis=0, tiled=True),
        lax.all_gather(w_down, "fsdp", axis=0, tiled=True),
        lax.all_gather(attn_gain, "fsdp", axis=0, tiled=True),
        lax.all_gather(ffn_gain, "fsdp", axis=0, tiled=True),
    )
    (
        full_query,
        full_key,
        full_value,
        full_out,
        full_gate,
        full_up,
        full_down,
        gain_one,
        gain_two,
    ) = gathered
    stream = activations.reshape(tokens, width).astype(jnp.float32)
    inv_one = lax.rsqrt(jnp.mean(stream * stream, axis=-1, keepdims=True) + epsilon)
    normed1 = (stream * inv_one * gain_one).astype(jnp.bfloat16)
    query_raw = jnp.dot(normed1, full_query, preferred_element_type=jnp.float32).reshape(
        tokens, heads, DH
    )
    queries = (
        rope_turn(query_raw, cosine, sine).astype(jnp.bfloat16).reshape(tokens, kv_heads, group, DH)
    )
    key_raw = jnp.dot(normed1, full_key, preferred_element_type=jnp.float32).reshape(
        tokens, kv_heads, DH
    )
    keys = rope_turn(key_raw, cosine, sine).astype(jnp.bfloat16)
    values = (
        jnp.dot(normed1, full_value, preferred_element_type=jnp.float32)
        .astype(jnp.bfloat16)
        .reshape(tokens, kv_heads, DH)
    )

    def scores_with(key_piece, owner):
        scores = (
            jnp.einsum("tjgd,sjd->jgts", queries, key_piece, preferred_element_type=jnp.float32)
            * scale
        )
        counted = places_of(owner)[None, :] <= query_places[:, None]
        return jnp.where(counted, scores, masked_score)

    def absorb(state, key_piece, value_piece, owner):
        running_top, running_total, running_sum = state
        scores = scores_with(key_piece, owner)
        new_top = jnp.maximum(running_top, jnp.max(scores, axis=-1, keepdims=True))
        fading = jnp.exp(running_top - new_top)
        weights = jnp.exp(scores - new_top)
        running_total = fading * running_total + jnp.sum(weights, axis=-1, keepdims=True)
        running_sum = fading * running_sum + jnp.einsum(
            "jgts,sjd->jgtd",
            weights.astype(jnp.bfloat16),
            value_piece,
            preferred_element_type=jnp.float32,
        )
        return (new_top, running_total, running_sum)

    start_state = (
        jnp.full((kv_heads, group, tokens, 1), masked_score, jnp.float32),
        jnp.zeros((kv_heads, group, tokens, 1), jnp.float32),
        jnp.zeros((kv_heads, group, tokens, DH), jnp.float32),
    )
    state = absorb(start_state, keys, values, mine)

    def forward_turn(turn_index, carry):
        state_now, key_piece, value_piece = carry
        key_piece, value_piece = passed_along((key_piece, value_piece), "ctx", 1)
        owner = (mine - turn_index) % cycles
        return (absorb(state_now, key_piece, value_piece, owner), key_piece, value_piece)

    state, _, _ = lax.fori_loop(1, cycles, forward_turn, (state, keys, values))
    running_top, running_total, running_sum = state
    attended = running_sum / running_total
    log_total = running_top + jnp.log(running_total)
    attended_low = (
        jnp.transpose(attended, (2, 0, 1, 3)).reshape(tokens, heads * DH).astype(jnp.bfloat16)
    )
    stream_one = stream + jnp.dot(attended_low, full_out, preferred_element_type=jnp.float32)
    inv_two = lax.rsqrt(jnp.mean(stream_one * stream_one, axis=-1, keepdims=True) + epsilon)
    normed2 = (stream_one * inv_two * gain_two).astype(jnp.bfloat16)
    gate = jnp.dot(normed2, full_gate, preferred_element_type=jnp.float32)
    up_part = jnp.dot(normed2, full_up, preferred_element_type=jnp.float32)
    sigma = jax.nn.sigmoid(gate)
    hidden = (gate * sigma * up_part).astype(jnp.bfloat16)
    stream_two = stream_one + jnp.dot(hidden, full_down, preferred_element_type=jnp.float32)
    output = stream_two.astype(jnp.bfloat16).reshape(activations.shape)
    back_weights = (
        lax.all_gather(w_query, "fsdp", axis=0, tiled=True),
        lax.all_gather(w_key, "fsdp", axis=0, tiled=True),
        lax.all_gather(w_value, "fsdp", axis=0, tiled=True),
        lax.all_gather(w_out, "fsdp", axis=0, tiled=True),
        lax.all_gather(w_gate, "fsdp", axis=0, tiled=True),
        lax.all_gather(w_up, "fsdp", axis=0, tiled=True),
        lax.all_gather(w_down, "fsdp", axis=0, tiled=True),
        lax.all_gather(attn_gain, "fsdp", axis=0, tiled=True),
        lax.all_gather(ffn_gain, "fsdp", axis=0, tiled=True),
    )
    (
        back_query,
        back_key,
        back_value,
        back_out,
        back_gate,
        back_up,
        back_down,
        back_gain_one,
        back_gain_two,
    ) = back_weights
    grad_rows = cotangent.reshape(tokens, width)
    grad_stream = grad_rows.astype(jnp.float32)
    grad_down = jnp.einsum("tf,td->fd", hidden, grad_rows, preferred_element_type=jnp.float32)
    d_hidden = jnp.einsum("td,fd->tf", grad_rows, back_down, preferred_element_type=jnp.float32)
    d_gate = (d_hidden * up_part * sigma * (1.0 + gate * (1.0 - sigma))).astype(jnp.bfloat16)
    d_up = (d_hidden * gate * sigma).astype(jnp.bfloat16)
    grad_gate = jnp.einsum("td,tf->df", normed2, d_gate, preferred_element_type=jnp.float32)
    grad_up = jnp.einsum("td,tf->df", normed2, d_up, preferred_element_type=jnp.float32)
    d_normed2 = jnp.einsum(
        "tf,df->td", d_gate, back_gate, preferred_element_type=jnp.float32
    ) + jnp.einsum("tf,df->td", d_up, back_up, preferred_element_type=jnp.float32)
    grad_ffn_gain = jnp.sum(d_normed2 * stream_one * inv_two, axis=0)
    d_stream_one = grad_stream + norm_back(d_normed2, stream_one, inv_two, back_gain_two)
    d_branch = d_stream_one.astype(jnp.bfloat16)
    grad_out = jnp.einsum("tk,td->kd", attended_low, d_branch, preferred_element_type=jnp.float32)
    d_attended = jnp.einsum(
        "td,kd->tk", d_branch, back_out, preferred_element_type=jnp.float32
    ).astype(jnp.bfloat16)
    d_heads = jnp.transpose(d_attended.reshape(tokens, kv_heads, group, DH), (1, 2, 0, 3))
    delta = jnp.sum(d_heads.astype(jnp.float32) * attended, axis=-1, keepdims=True)

    def back_step(d_queries, d_keys, d_values, key_piece, value_piece, owner):
        scores = scores_with(key_piece, owner)
        probs = jnp.exp(scores - log_total)
        d_values = d_values + jnp.einsum(
            "jgts,jgtd->sjd",
            probs.astype(jnp.bfloat16),
            d_heads,
            preferred_element_type=jnp.float32,
        )
        d_probs = jnp.einsum(
            "jgtd,sjd->jgts", d_heads, value_piece, preferred_element_type=jnp.float32
        )
        d_scores = (probs * (d_probs - delta)).astype(jnp.bfloat16)
        d_queries = (
            d_queries
            + jnp.einsum("jgts,sjd->jgtd", d_scores, key_piece, preferred_element_type=jnp.float32)
            * scale
        )
        d_keys = (
            d_keys
            + jnp.einsum("jgts,tjgd->sjd", d_scores, queries, preferred_element_type=jnp.float32)
            * scale
        )
        return (d_queries, d_keys, d_values)

    def pass_grads(d_keys, d_values):
        return (
            passed_along(d_keys.astype(jnp.bfloat16), "ctx", 1).astype(d_keys.dtype),
            passed_along(d_values.astype(jnp.bfloat16), "ctx", 1).astype(d_values.dtype),
        )

    zero_queries = jnp.zeros((kv_heads, group, tokens, DH), jnp.float32)
    zero_keys = jnp.zeros((tokens, kv_heads, DH), jnp.float32)
    d_queries, d_keys, d_values = back_step(zero_queries, zero_keys, zero_keys, keys, values, mine)

    def backward_turn(turn_index, carry):
        d_queries_now, d_keys_now, d_values_now, key_piece, value_piece = carry
        key_piece, value_piece = passed_along((key_piece, value_piece), "ctx", 1)
        d_keys_now, d_values_now = pass_grads(d_keys_now, d_values_now)
        owner = (mine - turn_index) % cycles
        d_queries_now, d_keys_now, d_values_now = back_step(
            d_queries_now, d_keys_now, d_values_now, key_piece, value_piece, owner
        )
        return (d_queries_now, d_keys_now, d_values_now, key_piece, value_piece)

    d_queries, d_keys, d_values, _, _ = lax.fori_loop(
        1, cycles, backward_turn, (d_queries, d_keys, d_values, keys, values)
    )
    d_keys, d_values = pass_grads(d_keys, d_values)
    d_query_rows = jnp.transpose(d_queries, (2, 0, 1, 3)).reshape(tokens, heads, DH)
    d_query = rope_back(d_query_rows, cosine, sine).astype(jnp.bfloat16).reshape(tokens, heads * DH)
    d_key = rope_back(d_keys, cosine, sine).astype(jnp.bfloat16).reshape(tokens, kv_heads * DH)
    d_value = d_values.astype(jnp.bfloat16).reshape(tokens, kv_heads * DH)
    grad_query = jnp.einsum("td,tk->dk", normed1, d_query, preferred_element_type=jnp.float32)
    grad_key = jnp.einsum("td,tk->dk", normed1, d_key, preferred_element_type=jnp.float32)
    grad_value = jnp.einsum("td,tk->dk", normed1, d_value, preferred_element_type=jnp.float32)
    d_normed1 = (
        jnp.einsum("tk,dk->td", d_query, back_query, preferred_element_type=jnp.float32)
        + jnp.einsum("tk,dk->td", d_key, back_key, preferred_element_type=jnp.float32)
        + jnp.einsum("tk,dk->td", d_value, back_value, preferred_element_type=jnp.float32)
    )
    grad_attn_gain = jnp.sum(d_normed1 * stream * inv_one, axis=0)
    input_grad = (d_stream_one + norm_back(d_normed1, stream, inv_one, back_gain_one)).reshape(
        activations.shape
    )
    shares = (
        lax.psum_scatter(
            grad_query.astype(jnp.bfloat16), "fsdp", scatter_dimension=0, tiled=True
        ).astype(jnp.float32),
        lax.psum_scatter(
            grad_key.astype(jnp.bfloat16), "fsdp", scatter_dimension=0, tiled=True
        ).astype(jnp.float32),
        lax.psum_scatter(
            grad_value.astype(jnp.bfloat16), "fsdp", scatter_dimension=0, tiled=True
        ).astype(jnp.float32),
        lax.psum_scatter(
            grad_out.astype(jnp.bfloat16), "fsdp", scatter_dimension=0, tiled=True
        ).astype(jnp.float32),
        lax.psum_scatter(
            grad_gate.astype(jnp.bfloat16), "fsdp", scatter_dimension=0, tiled=True
        ).astype(jnp.float32),
        lax.psum_scatter(
            grad_up.astype(jnp.bfloat16), "fsdp", scatter_dimension=0, tiled=True
        ).astype(jnp.float32),
        lax.psum_scatter(
            grad_down.astype(jnp.bfloat16), "fsdp", scatter_dimension=0, tiled=True
        ).astype(jnp.float32),
        lax.psum_scatter(
            grad_attn_gain.astype(jnp.bfloat16), "fsdp", scatter_dimension=0, tiled=True
        ).astype(jnp.float32),
        lax.psum_scatter(
            grad_ffn_gain.astype(jnp.bfloat16), "fsdp", scatter_dimension=0, tiled=True
        ).astype(jnp.float32),
    )
    shares = (
        lax.psum(shares[0].astype(jnp.bfloat16), "ctx").astype(jnp.float32),
        lax.psum(shares[1].astype(jnp.bfloat16), "ctx").astype(jnp.float32),
        lax.psum(shares[2].astype(jnp.bfloat16), "ctx").astype(jnp.float32),
        lax.psum(shares[3].astype(jnp.bfloat16), "ctx").astype(jnp.float32),
        lax.psum(shares[4].astype(jnp.bfloat16), "ctx").astype(jnp.float32),
        lax.psum(shares[5].astype(jnp.bfloat16), "ctx").astype(jnp.float32),
        lax.psum(shares[6].astype(jnp.bfloat16), "ctx").astype(jnp.float32),
        lax.psum(shares[7].astype(jnp.bfloat16), "ctx").astype(jnp.float32),
        lax.psum(shares[8].astype(jnp.bfloat16), "ctx").astype(jnp.float32),
    )
    return (
        output,
        input_grad,
        shares[0],
        shares[1],
        shares[2],
        shares[3],
        shares[4],
        shares[5],
        shares[6],
        shares[7],
        shares[8],
    )


LANES = 128
CORE, ALONG_X, ALONG_Y = 1, 2, 4
RELATIVE = (0, 2, 4, 6, 1, 3, 5, 7)
MIB = 2**20


def lane_dot(left, right):
    return lax.dot_general(left, right, (((1,), (1,)), ((), ())), preferred_element_type=jnp.float32)


def plain_dot(left, right):
    return lax.dot_general(left, right, (((1,), (0,)), ((), ())), preferred_element_type=jnp.float32)


def row_dot(left, right):
    return lax.dot_general(left, right, (((0,), (0,)), ((), ())), preferred_element_type=jnp.float32)


def rows_at(index, size):
    return pl.ds(pl.multiple_of(index * size, size), size)


def wide(value):
    return value.astype(jnp.float32)


def narrow(value):
    return value.astype(jnp.bfloat16)


def lanes_of(rows):
    return lax.broadcasted_iota(jnp.int32, (rows, LANES), 1)


def shape(dims, kind=jnp.bfloat16):
    return jax.ShapeDtypeStruct(dims, kind)


def local_kernel(body, outs, small, arrays, far=(), far_outs=(), scratch=(), limit=28, micros=2):
    near = pl.BlockSpec(memory_space=pltpu.VMEM)
    scalars = pl.BlockSpec(memory_space=pltpu.SMEM)
    away = pl.BlockSpec(memory_space=pl.ANY)
    single = not isinstance(outs, tuple)
    out_shapes = ((outs,) if single else outs) + tuple(far_outs)
    out_specs = [near] * (len(out_shapes) - len(far_outs)) + [away] * len(far_outs)
    results = pl.pallas_call(
        body,
        out_shape=out_shapes,
        in_specs=[scalars] * len(small) + [near] * len(arrays) + [away] * len(far),
        out_specs=out_specs,
        scratch_shapes=list(scratch),
        compiler_params=pltpu.CompilerParams(vmem_limit_bytes=limit * MIB),
        cost_estimate=pl.CostEstimate(flops=micros * 10**9, bytes_accessed=0, transcendentals=0),
    )(*small, *arrays, *far)
    return results[0] if single and not far_outs else results


def pick(weight_ref, start, size):
    window = 2 * LANES
    base = jnp.minimum(start // LANES * LANES, weight_ref.shape[1] - window)
    block = wide(weight_ref[:, pl.ds(pl.multiple_of(base, LANES), window)])
    return pltpu.roll(block, (window - (start - base)) % window, 1)


def join_fields(one, two, three, four):
    lane = lanes_of(one.shape[0])
    two = pltpu.roll(two, 96, 1)
    three = pltpu.roll(three, 64, 1)
    four = pltpu.roll(four, 32, 1)
    return jnp.concatenate(
        [
            jnp.where(lane < 96, one, two),
            jnp.where(lane < 64, two, three),
            jnp.where(lane < 32, three, four),
        ],
        axis=1,
    )


def part_fields(block):
    lane = lanes_of(block.shape[0])
    one, two, three = (block[:, start : start + LANES] for start in (0, LANES, 2 * LANES))
    fields = (
        one,
        jnp.where(lane < 32, pltpu.roll(one, 32, 1), pltpu.roll(two, 32, 1)),
        jnp.where(lane < 64, pltpu.roll(two, 64, 1), pltpu.roll(three, 64, 1)),
        pltpu.roll(three, 96, 1),
    )
    return [jnp.where(lane < DH, field, 0.0) for field in fields]


def pack_kernel(mine_ref, query_ref, key_ref, value_ref, out_ref, gain_ref, first_ref):
    mine = mine_ref[0]
    shard = query_ref.shape[0]
    four = 4 * DH
    slab = out_ref.shape[0] // 8
    slabs = out_ref.shape[1] // four
    query = pick(query_ref, mine * 2 * DH, 2 * DH)
    key = pick(key_ref, mine * DH, DH)[:, :LANES]
    value = pick(value_ref, mine * DH, DH)[:, :LANES]
    lane = lanes_of(shard)
    key = pltpu.roll(key, 64, 1)
    value = pltpu.roll(value, 32, 1)
    first_ref[:shard, :LANES] = narrow(query[:, :LANES])
    first_ref[:shard, LANES : 2 * LANES] = narrow(jnp.where(lane < 64, query[:, LANES:], key))
    first_ref[:shard, 2 * LANES :] = narrow(jnp.where(lane < 32, key, value))
    for index in range(slabs):
        here = shard + index * slab
        first_ref[here : here + slab, :] = out_ref[
            rows_at(mine, slab), index * four : (index + 1) * four
        ]
    first_ref[shard + slabs * slab :, :] = gain_ref[...]


def strip_kernel(mine_ref, gate_ref, up_ref, both_ref):
    quarters = both_ref.shape[1] // (2 * LANES)
    for index in range(quarters):
        place = rows_at(index * 8 + mine_ref[0], LANES)
        both_ref[:, index * LANES : (index + 1) * LANES] = gate_ref[:, place]
        both_ref[:, (quarters + index) * LANES : (quarters + index + 1) * LANES] = up_ref[:, place]


def place_out_kernel(owner_ref, *refs):
    pieces, (full_ref, done) = refs[:-2], refs[-2:]
    width = full_ref.shape[1]
    slab = width // 32
    four = pieces[0].shape[1]
    copies = []
    for index, piece in enumerate(pieces):
        for quarter in range(4):
            row = pl.multiple_of(quarter * 8 * slab + owner_ref[index] * slab, 16)
            for part in range(width // four):
                start = (quarter * (width // four) + part) * slab
                copies.append(
                    fetch(
                        piece.at[pl.ds(start, slab), :],
                        full_ref.at[pl.ds(row, slab), pl.ds(part * four, four)],
                        done.at[index, quarter, part],
                    )
                )
    for copy in copies:
        copy.wait()


def fold(block):
    rows = block.shape[0]
    tail = block[:, LANES:]
    lower = jnp.where(lanes_of(rows // 2) < 64, tail[: rows // 2], pltpu.roll(tail[rows // 2 :], 64, 1))
    return jnp.concatenate([block[:, :LANES], lower], axis=0)


def unfold(block):
    rows = block.shape[0] // 3 * 2
    half = rows // 2
    tail = block[rows:]
    keep = lanes_of(half) < 64
    tail = jnp.concatenate(
        [jnp.where(keep, tail, 0.0), jnp.where(keep, pltpu.roll(tail, 64, 1), 0.0)], axis=0
    )
    return jnp.concatenate([block[:rows], tail], axis=1)


def branch_kernel(
    folded_ref, full_ref, stream_ref, gain_ref, one_ref, normed_ref, inverse_ref, heads_ref
):
    size = heads_ref.shape[2]
    total = wide(stream_ref[...])
    for index in range(heads_ref.shape[0]):
        heads = narrow(unfold(wide(folded_ref[index])))[:, :size]
        heads_ref[index] = heads
        total = total + plain_dot(heads, full_ref[index * size : (index + 1) * size, :])
    one_ref[...] = total
    inverse = lax.rsqrt(jnp.mean(total * total, axis=1, keepdims=True) + epsilon)
    normed_ref[...] = narrow(total * inverse * gain_ref[8:9])
    inverse_ref[...] = jnp.broadcast_to(inverse, inverse_ref.shape)


def strips_kernel(count, *refs):
    (gate_up_in, down_in), refs = refs[:2], refs[2:]
    normed_in, grad_in, refs = refs[:count], refs[count : 2 * count], refs[2 * count :]
    (down_grad, stream_ref, sum_ref, both_out), refs = refs[:4], refs[4:]
    gate_up_ref, down_ref, normed_ref, grad_ref, both_ref, done, out_done = refs
    weights = [
        fetch(gate_up_in, gate_up_ref, out_done.at[0]),
        fetch(down_in, down_ref, out_done.at[1]),
    ]
    part = down_ref.shape[0]
    rows = normed_in[0].shape[0]
    size = 2 * rows
    copies = [
        (
            fetch(normed_in[index], normed_ref.at[pl.ds(index * rows, rows), :], done.at[index]),
            fetch(grad_in[index], grad_ref.at[pl.ds(index * rows, rows), :], done.at[count + index]),
        )
        for index in range(count)
    ]
    outs = []
    for copy in weights:
        copy.wait()
    for step in range(count // 2):
        for index in (2 * step, 2 * step + 1):
            copies[index][0].wait()
            copies[index][1].wait()
        here = slice(step * size, (step + 1) * size)
        normed = normed_ref[here, :]
        grad = grad_ref[here, :]
        gate = plain_dot(normed, gate_up_ref[:, :part])
        up = plain_dot(normed, gate_up_ref[:, part:])
        sigma = jax.nn.sigmoid(gate)
        turned = gate * sigma
        hidden = narrow(turned * up)
        d_hidden = lane_dot(grad, down_ref[...])
        d_gate = narrow(d_hidden * up * sigma * (1.0 + gate * (1.0 - sigma)))
        d_up = narrow(d_hidden * turned)
        both_ref[here, :part] = d_gate
        both_ref[here, part:] = d_up
        there = pl.ds(step * size, size)
        outs.append(fetch(both_ref.at[there, :], both_out.at[there, :], out_done.at[step]))
        stream_ref[here, :] = narrow(
            lane_dot(d_gate, gate_up_ref[:, :part]) + lane_dot(d_up, gate_up_ref[:, part:])
        )
        sum_ref[here, :] = narrow(plain_dot(hidden, down_ref[...]))
        product = row_dot(hidden, grad)
        if step == 0:
            down_grad[...] = product
        else:
            down_grad[...] += product
    for copy in outs:
        copy.wait()


def strip_grad_kernel(count, *refs):
    weight_ref, gain_ref, refs = refs[0], refs[1], refs[2:]
    normed_in, (own_in, twin_in), refs = refs[:count], refs[count : count + 2], refs[count + 2 :]
    out_ref, row_ref, normed_ref, both_ref, done = refs
    size = 2 * LANES
    rows = normed_in[0].shape[0]
    half = own_in.shape[0]
    copies = [
        fetch(piece, normed_ref.at[pl.ds(index * rows, rows), :], done.at[index])
        for index, piece in enumerate(normed_in)
    ]
    copies.append(fetch(own_in, both_ref.at[pl.ds(0, half), :], done.at[count]))
    copies.append(fetch(twin_in, both_ref.at[pl.ds(half, half), :], done.at[count + 1]))
    for copy in copies:
        copy.wait()
    ones = jnp.ones((8, out_ref.shape[1]), jnp.bfloat16)

    def one(index, _):
        columns = rows_at(index, size)
        total = row_dot(normed_ref[:, columns], both_ref[...])
        out_ref[columns, :] = narrow(total)
        share = narrow(total * wide(weight_ref[columns, :]))
        row_ref[:, columns] = lane_dot(ones, share) / gain_ref[8:, columns]
        return 0

    lax.fori_loop(0, out_ref.shape[0] // size, one, 0)


def add_twin_kernel(core_ref, own_ref, twin_ref, send_ref, keep_ref, self_ref):
    rows = keep_ref.shape[0]

    def total(index):
        here = rows_at(index, rows)
        return wide(own_ref[here, :]) + wide(twin_ref[here, :])

    core = core_ref[0]
    send_ref[:rows, :] = narrow(total(3))
    send_ref[rows:, :] = narrow(total(2 - core))
    keep_ref[...] = total(1 + core)
    self_ref[...] = total(0)


def add_late_kernel(keep_ref, got_ref, late_ref):
    rows = keep_ref.shape[0]
    late_ref[...] = narrow(keep_ref[...] + wide(got_ref[:rows, :]))


def summed(self_ref, got_ref, late_ref):
    rows = self_ref.shape[0]
    return self_ref[...] + wide(got_ref[rows:, :]) + wide(late_ref[...])


def norm_down(d_normed, stream, inverse, gain):
    scaled = d_normed * gain
    cubed = inverse * inverse * inverse
    return inverse * scaled - stream * cubed * jnp.mean(scaled * stream, axis=1, keepdims=True)


def branch_back_kernel(
    self_ref,
    got_ref,
    late_ref,
    grad_ref,
    one_ref,
    inverse_ref,
    gain_ref,
    full_ref,
    stream_out,
    branch_out,
    heads_out,
):
    d_normed = summed(self_ref, got_ref, late_ref)
    d_stream = wide(grad_ref[...]) + norm_down(
        d_normed, one_ref[...], inverse_ref[:, :1], gain_ref[8:9]
    )
    stream_out[...] = d_stream
    d_branch = narrow(d_stream)
    branch_out[...] = d_branch
    size = 2 * DH
    gap = jnp.zeros((d_branch.shape[0], 2 * LANES - size), jnp.float32)
    for index in range(heads_out.shape[0]):
        heads = lane_dot(d_branch, full_ref[index * size : (index + 1) * size, :])
        heads_out[index] = narrow(fold(jnp.concatenate([heads, gap], axis=1)))


def input_back_kernel(
    self_ref, got_ref, late_ref, stream_ref, back_ref, gain_ref, out_ref
):
    d_normed = summed(self_ref, got_ref, late_ref)
    stream = wide(stream_ref[...])
    inverse = lax.rsqrt(jnp.mean(stream * stream, axis=1, keepdims=True) + epsilon)
    out_ref[...] = back_ref[...] + norm_down(d_normed, stream, inverse, gain_ref[:1])


def output_kernel(self_ref, got_ref, late_ref, one_ref, out_ref):
    out_ref[...] = narrow(one_ref[...] + summed(self_ref, got_ref, late_ref))


def out_grad_kernel(seat_ref, heads_ref, branch_ref, own_ref, twin_ref):
    blocks, _, size = heads_ref.shape
    slab = blocks * size // 32
    rows = 4 * slab
    for index in range(blocks):
        product = narrow(row_dot(heads_ref[index], branch_ref[...]))
        for part in range(size // slab):
            row = index * size + part * slab
            seat = seat_ref[row // slab % 8]
            here = pl.ds(pl.multiple_of(seat % 4 * rows + row // (8 * slab) * slab, 16), slab)
            values = product[part * slab : (part + 1) * slab]

            @pl.when(seat < 4)
            def _():
                own_ref[here, :] = values

            @pl.when(seat >= 4)
            def _():
                twin_ref[here, :] = values


def last_kernel(
    fields_ref, weight_ref, gain_ref, row_ref, self_ref, got_ref, late_ref, normed_in, last_ref, normed_ref, done
):
    quarters = last_ref.shape[0]
    four = weight_ref.shape[1]
    shard = weight_ref.shape[0] // quarters
    slab = self_ref.shape[0] // quarters
    slabs = self_ref.shape[1] // four
    copies = [
        fetch(
            normed_in.at[:, pl.ds(quarter * shard, shard)],
            normed_ref.at[:, pl.ds(quarter * shard, shard)],
            done.at[quarter],
        )
        for quarter in range(quarters)
    ]
    ones = jnp.ones((8, four), jnp.bfloat16)
    out_grad = narrow(summed(self_ref, got_ref, late_ref))
    for quarter in range(quarters):
        here = slice(quarter * shard, (quarter + 1) * shard)
        copies[quarter].wait()
        total = row_dot(normed_ref[:, here], fields_ref[...])
        last_ref[quarter, :shard, :] = narrow(total)
        share = narrow(total * wide(weight_ref[here, :]))
        attn = lane_dot(ones, share) / gain_ref[:8, here]
        rows = jnp.concatenate([attn, row_ref[:, here]], axis=0)
        for part in range(slabs):
            start = shard + part * slab
            last_ref[quarter, start : start + slab, :] = out_grad[
                quarter * slab : (quarter + 1) * slab, part * four : (part + 1) * four
            ]
        end = shard + slabs * slab
        last_ref[quarter, end : end + 16, :] = narrow(rows)
        last_ref[quarter, end + 16 :, :] = jnp.zeros_like(last_ref[quarter, end + 16 :, :])


def stream_grad_kernel(start, fields_ref, weight_ref, out_ref):
    rows = out_ref.shape[0]
    size = rows // 2
    for step in range(2):
        here = slice(step * size, (step + 1) * size)
        there = slice(start + step * size, start + (step + 1) * size)
        out_ref[here, :] = narrow(lane_dot(fields_ref[there, :], weight_ref[...]))


def place_strips_kernel(owner_ref, *refs):
    pieces, (gate_ref, up_ref) = refs[:-2], refs[-2:]
    for index, piece in enumerate(pieces):
        quarters = piece.shape[1] // (2 * LANES)
        for quarter in range(quarters):
            there = rows_at(quarter * 8 + owner_ref[index], LANES)
            start = quarter * LANES
            gate_ref[:, there] = wide(piece[:, start : start + LANES])
            start += quarters * LANES
            up_ref[:, there] = wide(piece[:, start : start + LANES])


def place_down_kernel(owner_ref, *refs):
    pieces, down_ref = refs[:-1], refs[-1]
    for index, piece in enumerate(pieces):
        down_ref[rows_at(owner_ref[index], piece.shape[0]), :] = wide(piece[...])


def put(target_ref, field, start):
    window = 2 * LANES
    base = jnp.minimum(start // LANES * LANES, target_ref.shape[1] - window)
    here = pl.ds(pl.multiple_of(base, LANES), window)
    target_ref[:, here] += pltpu.roll(field, start - base, 1)


def place_last_kernel(owner_ref, *refs):
    pieces, (query_ref, key_ref, value_ref, out_ref, gain_ref) = refs[:-5], refs[-5:]
    shard, width = out_ref.shape
    four = pieces[0].shape[1]
    slab = shard // 8
    slabs = width // four
    end = shard + slabs * slab
    gap = jnp.zeros((shard, LANES), jnp.float32)
    for ref in (query_ref, key_ref, value_ref):
        ref[...] = jnp.zeros_like(ref)
    gains = jnp.zeros((16, four), jnp.float32)
    for index, piece in enumerate(pieces):
        owner = owner_ref[index]
        one, two, key, value = part_fields(wide(piece[:shard, :]))
        query = jnp.concatenate([one, gap], axis=1) + pltpu.roll(
            jnp.concatenate([two, gap], axis=1), DH, 1
        )
        put(query_ref, query, owner * 2 * DH)
        put(key_ref, jnp.concatenate([key, gap], axis=1), owner * DH)
        put(value_ref, jnp.concatenate([value, gap], axis=1), owner * DH)
        for part in range(slabs):
            start = shard + part * slab
            out_ref[rows_at(owner, slab), part * four : (part + 1) * four] = wide(
                piece[start : start + slab, :]
            )
        gains = gains + wide(piece[end : end + 16, :])
    gain_ref[...] = gains


def swapped(field):
    half = DH // 2
    lane = lanes_of(field.shape[0])
    return jnp.where(lane < half, pltpu.roll(field, LANES - half, 1), pltpu.roll(field, half, 1))


def fetch(source, target, done):
    copy = pltpu.make_async_copy(source, target, done)
    copy.start()
    return copy


def attend_kernel(
    span,
    near_ref,
    slot_ref,
    cos_ref,
    sin_ref,
    *refs,
):
    (first_ref, *piece_refs), refs = refs[:9], refs[9:]
    (low_ref, gain_ref, level_ref), refs = refs[:3], refs[3:]
    (normed_out, weight_out, query_out, key_out, value_out, mixed_out), refs = refs[:6], refs[6:]
    stream_ref, weight_ref, gains_ref, raw_ref, query_ref, key_ref, value_ref, mixed_ref = refs[:8]
    score_ref, top_ref, total_ref, sum_ref, in_done, out_done = refs[8:]
    spans = near_ref.shape[0]
    block = 2 * span
    pair = 2 * block
    turns = spans // 2
    quarters, packed, four = first_ref.shape
    shard = weight_ref.shape[0] // quarters
    factor = LOG2E / math.sqrt(DH)

    copies = [
        fetch(piece, stream_ref.at[pl.ds(index * block, block), :], in_done.at[index])
        for index, piece in enumerate(piece_refs)
    ]
    gain_copies = [
        fetch(
            first_ref.at[quarter, pl.ds(packed - 32, 32), :],
            gains_ref.at[pl.ds(quarter * 32, 32), :],
            in_done.at[turns + quarter],
        )
        for quarter in range(quarters)
    ]
    weight_copies = [
        fetch(
            first_ref.at[quarter, pl.ds(0, shard), :],
            weight_ref.at[pl.ds(quarter * shard, shard), :],
            in_done.at[turns + quarters + quarter],
        )
        for quarter in range(quarters)
    ]
    for copy in gain_copies:
        copy.wait()
    for quarter in range(quarters):
        rows = wide(gains_ref[quarter * 32 : quarter * 32 + 16, :])
        here = slice(quarter * shard, (quarter + 1) * shard)
        gain_ref[:8, here] = jnp.broadcast_to(rows[:1, :shard], (8, shard))
        gain_ref[8:, here] = jnp.broadcast_to(rows[1:2, :shard], (8, shard))
    for copy in weight_copies:
        copy.wait()
    out_copies = [fetch(weight_ref, weight_out, out_done.at[0])]
    gain = gain_ref[:1, :]

    def norm(start):
        here = pl.ds(start, span)
        stream = wide(stream_ref[here, :])
        inverse = lax.rsqrt(jnp.mean(stream * stream, axis=1, keepdims=True) + epsilon)
        stream_ref[here, :] = narrow(stream * inverse * gain)

    for step in range(turns // 2):
        copies[2 * step].wait()
        copies[2 * step + 1].wait()
        here = pl.ds(step * pair, pair)
        for part in range(4):
            norm(step * pair + part * span)
        raw_ref[here, :] = plain_dot(stream_ref[here, :], weight_ref[...])
        out_copies.append(
            fetch(stream_ref.at[here, :], normed_out.at[here, :], out_done.at[1 + step])
        )

    def place(index, _):
        raw = raw_ref[rows_at(near_ref[index], span), :]
        cosine = cos_ref[rows_at(index, span), :]
        sine = sin_ref[rows_at(index, span), :]
        one, two, three, four = part_fields(raw)

        def turned(field):
            return narrow(field * cosine + swapped(field) * sine)

        first = (index // 2) * 4 + index % 2
        query_ref[rows_at(first, span), :] = turned(one)
        query_ref[rows_at(first + 2, span), :] = turned(two)
        key_ref[rows_at(index, span), :] = turned(three)
        value_ref[rows_at(index, span), :] = narrow(four)
        return 0

    lax.fori_loop(0, spans, place, 0)
    next_done = 1 + turns // 2
    for source, target in ((query_ref, query_out), (key_ref, key_out), (value_ref, value_out)):
        out_copies.append(fetch(source, target, out_done.at[next_done]))
        next_done += 1

    def store(index, both):
        slot = slot_ref[index]
        low_ref[slot // 2, rows_at(slot % 2, span), :] = narrow(both[:, :LANES])
        tail = narrow(both[:, LANES:])
        turned = narrow(pltpu.roll(both[:, LANES:], 64, 1))

        @pl.when(slot % 2 == 0)
        def _():
            low_ref[slot // 2, 2 * span :, :64] = tail[:, :64]

        @pl.when(slot % 2 == 1)
        def _():
            low_ref[slot // 2, 2 * span :, 64:] = turned[:, 64:]

    def widest(top, scores):
        for start in range(0, block, LANES):
            top = jnp.maximum(top, scores[:, start : start + LANES])
        return top

    def score(turn, step):
        scores = lane_dot(query_ref[rows_at(turn, pair), :], key_ref[rows_at(step, block), :])
        score_ref[turn % 2, :, rows_at(step, block)] = scores
        top_ref[...] = widest(top_ref[...], scores)

    def edge(turn):
        row = lax.broadcasted_iota(jnp.int32, (pair, block), 0) % block
        column = lax.broadcasted_iota(jnp.int32, (pair, block), 1)
        scores = lane_dot(query_ref[rows_at(turn, pair), :], key_ref[rows_at(turn, block), :])
        scores = jnp.where(column <= row, scores, masked_score)
        score_ref[turn % 2, :, rows_at(turn, block)] = scores
        top = jnp.max(widest(top_ref[...], scores), axis=1, keepdims=True) * factor
        return jnp.broadcast_to(top, (pair, LANES))

    def weigh(turn, step, top):
        scores = score_ref[turn % 2, :, rows_at(step, block)]
        weights = jnp.exp2(scores * factor - top[:, :1])
        total = total_ref[...]
        for start in range(0, block, LANES):
            total = total + weights[:, start : start + LANES]
        total_ref[...] = total
        sum_ref[...] += plain_dot(narrow(weights), value_ref[rows_at(step, block), :])

    def finish(turn, top):
        total = jnp.sum(total_ref[...], axis=1, keepdims=True)
        mixed = sum_ref[...] / total
        mixed_ref[rows_at(turn, pair), :] = mixed
        level = top + jnp.log2(total)
        level_ref[rows_at(turn, 8), :] = jnp.transpose(level)[:8]
        gap = jnp.zeros((block, LANES), jnp.float32)
        both = jnp.concatenate([mixed[:block], gap], axis=1) + pltpu.roll(
            jnp.concatenate([mixed[block:], gap], axis=1), DH, 1
        )
        store(2 * turn, both[:span])
        store(2 * turn + 1, both[span:])

    def clear():
        total_ref[...] = jnp.zeros_like(total_ref)
        sum_ref[...] = jnp.zeros_like(sum_ref)
        top_ref[...] = jnp.full(top_ref.shape, masked_score, jnp.float32)

    def one_turn(turn, top):
        clear()

        def both(step, _):
            weigh(turn, step, top)
            score(turn + 1, step)
            return 0

        lax.fori_loop(0, turn + 1, both, 0)
        finish(turn, top)
        return edge(turn + 1)

    clear()
    top = lax.fori_loop(0, turns - 1, one_turn, edge(0))
    clear()

    def only(step, _):
        weigh(turns - 1, step, top)
        return 0

    lax.fori_loop(0, turns, only, 0)
    finish(turns - 1, top)
    out_copies.append(fetch(mixed_ref, mixed_out, out_done.at[next_done]))
    for copy in out_copies:
        copy.wait()


def attend(near, slot, cosine, sine, first, pieces, span):
    tokens = cosine.shape[0]
    turns = tokens // (2 * span)
    quarters, _, four = first.shape
    block, width = pieces[0].shape
    f32 = jnp.float32
    near_out = (
        shape((turns, 3 * span, LANES)),
        shape((16, width), f32),
        shape((8 * turns, 4 * span), f32),
    )
    far_out = (
        shape((tokens, width)),
        shape((width, four)),
        shape((2 * tokens, LANES)),
        shape((tokens, LANES)),
        shape((tokens, LANES)),
        shape((2 * tokens, LANES), f32),
    )
    state = pltpu.VMEM((4 * span, LANES), f32)
    return local_kernel(
        functools.partial(attend_kernel, span),
        near_out,
        (near, slot),
        (cosine, sine),
        far=(first, *pieces),
        far_outs=far_out,
        scratch=(
            pltpu.VMEM((tokens, width), jnp.bfloat16),
            pltpu.VMEM((width, four), jnp.bfloat16),
            pltpu.VMEM((32 * quarters, four), jnp.bfloat16),
            pltpu.VMEM((tokens, four), f32),
            pltpu.VMEM((2 * tokens, LANES), jnp.bfloat16),
            pltpu.VMEM((tokens, LANES), jnp.bfloat16),
            pltpu.VMEM((tokens, LANES), jnp.bfloat16),
            pltpu.VMEM((2 * tokens, LANES), f32),
            pltpu.VMEM((2, 4 * span, tokens), f32),
            state,
            state,
            state,
            pltpu.SemaphoreType.DMA((turns + 2 * quarters,)),
            pltpu.SemaphoreType.DMA((5 + turns // 2,)),
        ),
        limit=44,
        micros=33,
    )


def attend_back_kernel(
    span,
    near_ref,
    slot_ref,
    grad_ref,
    total_ref,
    cos_ref,
    sin_ref,
    query_in,
    key_in,
    value_in,
    mixed_in,
    out_ref,
    query_ref,
    key_ref,
    value_ref,
    mixed_ref,
    head_ref,
    delta_ref,
    query_sum,
    key_sum,
    value_sum,
    done,
):
    spans = near_ref.shape[0]
    block = 2 * span
    pair = 2 * block
    turns = spans // 2
    factor = LOG2E / math.sqrt(DH)
    scale = 1.0 / math.sqrt(DH)
    lane = lax.broadcasted_iota(jnp.int32, (span, LANES), 1)
    copies = [
        fetch(source, target, done.at[index])
        for index, (source, target) in enumerate(
            ((mixed_in, mixed_ref), (key_in, key_ref), (query_in, query_ref), (value_in, value_ref))
        )
    ]

    def split(index, _):
        slot = slot_ref[index]
        grad = wide(grad_ref[slot // 2, rows_at(slot % 2, span), :])
        tail = wide(grad_ref[slot // 2, 2 * span :, :])
        first = (index // 2) * 4 + index % 2
        one = jnp.where(lane < DH, grad, 0.0)
        tail = pltpu.roll(tail, 32 + 64 * (slot % 2), 1)
        two = jnp.where(lane < 32, pltpu.roll(grad, 32, 1), tail)
        two = jnp.where(lane < DH, two, 0.0)
        head_ref[rows_at(first, span), :] = narrow(one)
        head_ref[rows_at(first + 2, span), :] = narrow(two)
        return 0

    lax.fori_loop(0, spans, split, 0)
    copies[0].wait()

    def prepare(turn, _):
        here = rows_at(turn, pair)
        product = wide(head_ref[here, :]) * mixed_ref[here, :]
        delta = jnp.sum(jnp.transpose(product), axis=0, keepdims=True)
        delta_ref[rows_at(turn, 8), :] = jnp.broadcast_to(delta, (8, pair))
        query_sum[here, :] = jnp.zeros((pair, LANES), jnp.float32)
        return 0

    lax.fori_loop(0, turns, prepare, 0)
    for copy in copies[1:]:
        copy.wait()

    def turned_back(field, index):
        cosine = cos_ref[rows_at(index, span), :]
        sine = sin_ref[rows_at(index, span), :]
        field = field * scale
        return wide(narrow(field * cosine - swapped(field) * sine))

    def one_block(turn, _):
        key = key_ref[rows_at(turn, block), :]
        value = value_ref[rows_at(turn, block), :]

        def one_step(step, diagonal):
            here = rows_at(step, pair)
            query = query_ref[here, :]
            head = head_ref[here, :]
            level = total_ref[rows_at(step, 8), :][:1]
            delta = delta_ref[rows_at(step, 8), :][:1]
            probs = jnp.exp2(lane_dot(key, query) * factor - level)
            if diagonal:
                row = lax.broadcasted_iota(jnp.int32, (block, pair), 0)
                column = lax.broadcasted_iota(jnp.int32, (block, pair), 1) % block
                probs = jnp.where(row <= column, probs, 0.0)
            d_scores = narrow(probs * (lane_dot(value, head) - delta))
            query_sum[here, :] += row_dot(d_scores, key)
            return plain_dot(d_scores, query), plain_dot(narrow(probs), head)

        key_part, value_part = one_step(turn, True)
        key_sum[...] = key_part
        value_sum[...] = value_part

        def two_steps(index, _):
            step = turn + 1 + 2 * index
            key_one, value_one = one_step(step, False)
            key_two, value_two = one_step(step + 1, False)
            key_sum[...] += key_one + key_two
            value_sum[...] += value_one + value_two
            return 0

        left = turns - 1 - turn
        lax.fori_loop(0, left // 2, two_steps, 0)

        @pl.when(left % 2 == 1)
        def _():
            key_one, value_one = one_step(turns - 1, False)
            key_sum[...] += key_one
            value_sum[...] += value_one

        for part in range(2):
            index = 2 * turn + part
            here = rows_at(near_ref[index], span)
            rows = slice(part * span, (part + 1) * span)
            first = rows_at((index // 2) * 4 + index % 2, span)
            second = rows_at((index // 2) * 4 + index % 2 + 2, span)
            one = turned_back(query_sum[first, :], index)
            two = turned_back(query_sum[second, :], index)
            three = turned_back(key_sum[rows, :], index)
            out_ref[here, :] = narrow(join_fields(one, two, three, value_sum[rows, :]))
        return 0

    lax.fori_loop(0, turns, one_block, 0)


def attend_back(near, slot, grad, total, cosine, sine, query, key, value, mixed, span):
    tokens = key.shape[0]
    f32 = jnp.float32
    rows = pltpu.VMEM((2 * span, LANES), f32)
    return local_kernel(
        functools.partial(attend_back_kernel, span),
        shape((tokens, 4 * DH)),
        (near, slot),
        (grad, total, cosine, sine),
        far=(query, key, value, mixed),
        scratch=(
            pltpu.VMEM(query.shape, jnp.bfloat16),
            pltpu.VMEM(key.shape, jnp.bfloat16),
            pltpu.VMEM(value.shape, jnp.bfloat16),
            pltpu.VMEM(mixed.shape, f32),
            pltpu.VMEM((2 * tokens, LANES), jnp.bfloat16),
            pltpu.VMEM(total.shape, f32),
            pltpu.VMEM((2 * tokens, LANES), f32),
            rows,
            rows,
            pltpu.SemaphoreType.DMA((4,)),
        ),
        limit=28,
        micros=29,
    )


def turn_tables(tokens):
    half = DH // 2
    freqs = jnp.exp(-math.log(rope_base) * 2.0 * jnp.arange(half, dtype=jnp.float32) / DH)
    angle = jnp.arange(tokens, dtype=jnp.int32).astype(jnp.float32)[:, None] * freqs[None, :]
    gap = jnp.zeros((tokens, LANES - DH), jnp.float32)
    cosine, sine = jnp.cos(angle), jnp.sin(angle)
    return (
        jnp.concatenate([cosine, cosine, gap], axis=1),
        jnp.concatenate([-sine, sine, gap], axis=1),
    )


def swap(block, bits):
    routes = [(i, i ^ bits) for i in range(lax.axis_size("ctx"))]
    return lax.ppermute(block, "ctx", routes)


def swap_split(block, even, odd):
    routes = [(i, i ^ (odd if i & CORE else even)) for i in range(lax.axis_size("ctx"))]
    return lax.ppermute(block, "ctx", routes)


def after(value, *others):
    return lax.optimization_barrier((value, *others))[0]


def gather_spans(block, core, *gate):
    from_x = swap(block, ALONG_X)
    from_y = swap(block, ALONG_Y)
    twin = swap(block, CORE)
    first = after(from_x, *gate) if gate else from_x
    corner = swap_split(jnp.where(core[0] == 0, first, from_y), ALONG_Y, ALONG_X)
    return [block, from_x, from_y, corner] + [
        twin,
        swap(first, CORE),
        swap(from_y, CORE),
        swap(corner, CORE),
    ]


def open_scatter(own, twin, core):
    rows, width = own.shape[0] // 4, own.shape[1]
    some = shape((rows, width), jnp.float32)
    return local_kernel(
        add_twin_kernel,
        (shape((2 * rows, width)), some, some),
        (core,),
        (own, swap(twin, CORE)),
        micros=2,
    )


def turn_scatter(keep, got):
    late = local_kernel(add_late_kernel, shape(keep.shape), (), (keep, got), micros=1)
    return late, swap_split(late, ALONG_X, ALONG_Y)


def plane_layer(
    activations,
    span_order,
    w_query,
    w_key,
    w_value,
    w_out,
    w_gate,
    w_up,
    w_down,
    attn_gain,
    ffn_gain,
    cotangent,
):
    f32 = jnp.float32
    cycles = lax.axis_size("ctx")
    quarters = lax.axis_size("fsdp")
    mine = lax.axis_index("ctx")
    span = activations.shape[2]
    width = activations.shape[3]
    tokens = 2 * span
    length = cycles * tokens
    half = length // 2
    shard = w_query.shape[0]
    four = 4 * DH
    hidden_size = quarters * w_down.shape[0]
    strip = hidden_size // (quarters * cycles)
    part = hidden_size // cycles
    slab = w_out.shape[0] // cycles
    slabs = width // four
    packed = shard + slabs * slab + 32
    owners = mine ^ jnp.array(RELATIVE, jnp.int32)
    away = mine ^ jnp.arange(cycles, dtype=jnp.int32)
    seat = (away & 1) * 4 + (away >> 2) * 2 + ((away >> 1) & 1)
    slot_of = jnp.argsort(span_order).astype(jnp.int32)
    near_slot = 2 * seat[slot_of // 2] + slot_of % 2
    here = mine.reshape(1).astype(jnp.int32)
    core = here & CORE
    stream = activations.reshape(tokens, width)
    grad_rows = cotangent.reshape(tokens, width)

    gains = jnp.pad(jnp.stack([attn_gain, ffn_gain]), ((0, 30), (0, four - shard)))
    first = local_kernel(
        pack_kernel, shape((packed, four)), (here,), (w_query, w_key, w_value, w_out, gains)
    )
    first = lax.all_gather(first, "fsdp", axis=0)
    cosine, sine = turn_tables(length)
    streams = gather_spans(stream, core, cosine, sine, near_slot, slot_of)
    gate_up = local_kernel(strip_kernel, shape((shard, 2 * part)), (here,), (w_gate, w_up))
    gate_up = lax.all_gather(gate_up, "fsdp", axis=0, tiled=True)
    down = lax.dynamic_slice_in_dim(w_down, mine * strip, strip, axis=0)
    down = lax.all_gather(down, "fsdp", axis=0, tiled=True)

    folded, gains, level, normed1, w_fields, query, key, value, attended = attend(
        near_slot, slot_of, cosine, sine, first, streams, span
    )
    grads = gather_spans(after(grad_rows, streams[3]), core, folded)
    out_part = first[:, shard : shard + slabs * slab].reshape(quarters * slabs * slab, four)
    full_out = local_kernel(
        place_out_kernel,
        (),
        (owners,),
        (),
        far=gather_spans(out_part, core, folded),
        far_outs=(shape((width, width)),),
        scratch=(pltpu.SemaphoreType.DMA((cycles, quarters, slabs)),),
        micros=4,
    )[0]
    folded = lax.all_to_all(folded, "ctx", 0, 0)
    one_tile = shape((tokens, LANES), f32)
    head_rows = shape((cycles, tokens, 2 * DH))
    stream_one, normed2, inverse, heads_low = local_kernel(
        branch_kernel,
        (shape((tokens, width), f32), shape((tokens, width)), one_tile, head_rows),
        (),
        (folded, full_out, stream, gains),
        micros=4,
    )
    normed2 = gather_spans(normed2, core)

    def strips(pieces, grad_pieces):
        low = jnp.bfloat16
        return local_kernel(
            functools.partial(strips_kernel, len(pieces)),
            (shape((part, width), f32), shape((half, width)), shape((half, width))),
            (),
            (),
            far=(gate_up, down, *pieces, *grad_pieces),
            far_outs=(shape((half, 2 * part)),),
            scratch=(
                pltpu.VMEM((width, 2 * part), low),
                pltpu.VMEM((part, width), low),
                pltpu.VMEM((half, width), low),
                pltpu.VMEM((half, width), low),
                pltpu.VMEM((half, 2 * part), low),
                pltpu.SemaphoreType.DMA((2 * len(pieces),)),
                pltpu.SemaphoreType.DMA((len(pieces) // 2,)),
            ),
            limit=32,
            micros=15,
        )

    down_twin, d_normed2_twin, sum_twin, both_twin = strips(normed2[4:], grads[4:])
    down_own, d_normed2_own, sum_own, both_own = strips(normed2[:4], grads[:4])
    down_sum = (down_own + down_twin).astype(jnp.bfloat16)
    grad_down = lax.psum_scatter(down_sum, "fsdp", scatter_dimension=0, tiled=True)
    send, keep, total = open_scatter(d_normed2_own, d_normed2_twin, core)
    grad_both, grad_ffn = local_kernel(
        functools.partial(strip_grad_kernel, cycles),
        (shape((width, 2 * part)), shape((8, width), f32)),
        (),
        (gate_up, gains),
        far=(*normed2, after(both_own, send, down_sum), both_twin),
        scratch=(
            pltpu.VMEM((length, width), jnp.bfloat16),
            pltpu.VMEM((length, 2 * part), jnp.bfloat16),
            pltpu.SemaphoreType.DMA((cycles + 2,)),
        ),
        limit=24,
        micros=12,
    )
    grad_both = lax.psum_scatter(grad_both, "fsdp", scatter_dimension=0, tiled=True)
    got = swap_split(send, ALONG_Y, ALONG_X)
    late, late_got = turn_scatter(after(keep, grad_ffn), got)
    ffn_send, ffn_keep, ffn_total = open_scatter(after(sum_own, late), sum_twin, core)
    d_stream_one, d_branch, d_heads = local_kernel(
        branch_back_kernel,
        (
            shape((tokens, width), f32),
            shape((tokens, width)),
            shape((cycles, 3 * span, LANES)),
        ),
        (),
        (after(total, ffn_send), got, late_got, grad_rows, stream_one, inverse, gains, full_out),
        micros=4,
    )
    d_heads = lax.all_to_all(d_heads, "ctx", 0, 0)
    block = shape((4 * quarters * slab, width))
    out_parts = local_kernel(
        out_grad_kernel, (block, block), (seat,), (heads_low, d_branch), micros=5
    )
    out_send, out_keep, out_total = open_scatter(*out_parts, core)
    ffn_got = swap_split(ffn_send, ALONG_Y, ALONG_X)
    out_got = swap_split(out_send, ALONG_Y, ALONG_X)
    d_heads = after(d_heads, out_send, grad_down)
    d_fields = attend_back(
        near_slot, slot_of, d_heads, level, cosine, sine, query, key, value, attended, span
    )
    out_late, out_late_got = turn_scatter(after(out_keep, d_fields), out_got)
    ffn_late, ffn_late_got = turn_scatter(after(ffn_keep, out_late), ffn_got)

    def stream_grad(start, fields):
        return local_kernel(
            functools.partial(stream_grad_kernel, start),
            shape((half, width)),
            (),
            (fields, w_fields),
            micros=3,
        )

    d_normed1_twin = stream_grad(half, after(d_fields, ffn_late))
    d_normed1_own = stream_grad(0, after(d_fields, d_normed1_twin))
    last = local_kernel(
        last_kernel,
        shape((quarters, packed, four)),
        (),
        (after(d_fields, d_normed1_own), w_fields, gains, grad_ffn, out_total, out_got, out_late_got),
        far=(normed1,),
        scratch=(
            pltpu.VMEM((length, width), jnp.bfloat16),
            pltpu.SemaphoreType.DMA((quarters,)),
        ),
        limit=24,
        micros=7,
    )
    send, keep, total = open_scatter(after(d_normed1_own, last), d_normed1_twin, core)
    last = lax.psum_scatter(last, "fsdp", scatter_dimension=0, tiled=False)
    got = swap_split(send, ALONG_Y, ALONG_X)
    late, late_got = turn_scatter(keep, got)
    input_grad = local_kernel(
        input_back_kernel,
        shape((tokens, width), f32),
        (),
        (total, got, late_got, stream, d_stream_one, gains),
    )
    output = local_kernel(output_kernel, shape((tokens, width)), (), (ffn_total, ffn_got, ffn_late_got, stream_one))
    grad_down = local_kernel(
        place_down_kernel,
        shape((hidden_size // quarters, width), f32),
        (owners,),
        gather_spans(grad_down, core, send),
        micros=4,
    )
    wide_strip = shape((shard, hidden_size), f32)
    grad_gate, grad_up = local_kernel(
        place_strips_kernel, (wide_strip, wide_strip), (owners,), gather_spans(after(grad_both, send), core, late), micros=8
    )
    narrow_grad = shape((shard, width // 2), f32)
    wide_grad = shape((shard, width), f32)
    grad_query, grad_key, grad_value, grad_out, grad_gains = local_kernel(
        place_last_kernel,
        (wide_grad, narrow_grad, narrow_grad, wide_grad, shape((16, four), f32)),
        (owners,),
        gather_spans(last, core, grad_gate, grad_down, output, input_grad),
        micros=7,
    )
    return (
        output.reshape(activations.shape),
        input_grad.reshape(activations.shape),
        grad_query,
        grad_key,
        grad_value,
        grad_out,
        grad_gate,
        grad_up,
        grad_down,
        grad_gains[0],
        grad_gains[8],
    )


def solution(mesh):
    in_specs = (
        P("fsdp", "ctx", None, None),
        P(),
        P("fsdp", None),
        P("fsdp", None),
        P("fsdp", None),
        P("fsdp", None),
        P("fsdp", None),
        P("fsdp", None),
        P("fsdp", None),
        P("fsdp"),
        P("fsdp"),
        P("fsdp", "ctx", None, None),
    )
    out_specs = (
        P("fsdp", "ctx", None, None),
        P("fsdp", "ctx", None, None),
        P("fsdp", None),
        P("fsdp", None),
        P("fsdp", None),
        P("fsdp", None),
        P("fsdp", None),
        P("fsdp", None),
        P("fsdp", None),
        P("fsdp"),
        P("fsdp"),
    )
    cycles = mesh.shape["ctx"]

    def per_device(*arrays):
        heads = arrays[3].shape[1] // DH
        if cycles == len(RELATIVE) == heads and arrays[2].shape == (4 * DH, 2 * heads * DH):
            return plane_layer(*arrays)
        return ring_layer(*arrays)

    return jax.shard_map(
        per_device, mesh=mesh, in_specs=in_specs, out_specs=out_specs, check_vma=False
    )
```

```python
import functools
import math

import jax
import jax.numpy as jnp
from jax import lax
from jax.experimental import pallas as pl
from jax.experimental.pallas import tpu as pltpu
from jax.sharding import PartitionSpec as P

DH = 96


epsilon = 1e-05
rope_base = 100000.0
masked_score = -1e30
LOG2E = math.log2(math.e)


def passed_along(block, axis, distance):
    devices = range(lax.axis_size(axis))
    route = [((i - distance) % len(devices), i) for i in devices]
    return lax.ppermute(block, axis, route)


def rope_tables(places):
    half = DH // 2
    freqs = jnp.exp(-math.log(rope_base) * 2.0 * jnp.arange(half, dtype=jnp.float32) / DH)
    angle = places.astype(jnp.float32)[:, None] * freqs[None, :]
    return (jnp.cos(angle)[:, None, :], jnp.sin(angle)[:, None, :])


def rope_turn(field, cosine, sine):
    half = DH // 2
    first = field[..., :half]
    second = field[..., half:]
    return jnp.concatenate(
        [first * cosine - second * sine, second * cosine + first * sine], axis=-1
    )


def rope_back(field, cosine, sine):
    half = DH // 2
    first = field[..., :half]
    second = field[..., half:]
    return jnp.concatenate(
        [first * cosine + second * sine, second * cosine - first * sine], axis=-1
    )


def norm_back(d_normed, stream, inv_rms, gain):
    scaled = d_normed * gain
    cubed = inv_rms * inv_rms * inv_rms
    return inv_rms * scaled - stream * cubed * jnp.mean(scaled * stream, axis=-1, keepdims=True)


def ring_layer(
    activations,
    span_order,
    w_query,
    w_key,
    w_value,
    w_out,
    w_gate,
    w_up,
    w_down,
    attn_gain,
    ffn_gain,
    cotangent,
):
    cycles = lax.axis_size("ctx")
    mine = lax.axis_index("ctx")
    span = activations.shape[2]
    width = activations.shape[3]
    tokens = 2 * span
    heads = w_query.shape[1] // DH
    kv_heads = w_key.shape[1] // DH
    group = heads // kv_heads
    scale = 1.0 / math.sqrt(DH)
    offsets = jnp.arange(span, dtype=jnp.int32)

    def places_of(owner):
        span_ids = lax.dynamic_slice_in_dim(span_order, 2 * owner, 2)
        return (span_ids[:, None] * span + offsets[None, :]).reshape(tokens)

    query_places = places_of(mine)
    cosine, sine = rope_tables(query_places)
    gathered = (
        lax.all_gather(w_query, "fsdp", axis=0, tiled=True),
        lax.all_gather(w_key, "fsdp", axis=0, tiled=True),
        lax.all_gather(w_value, "fsdp", axis=0, tiled=True),
        lax.all_gather(w_out, "fsdp", axis=0, tiled=True),
        lax.all_gather(w_gate, "fsdp", axis=0, tiled=True),
        lax.all_gather(w_up, "fsdp", axis=0, tiled=True),
        lax.all_gather(w_down, "fsdp", axis=0, tiled=True),
        lax.all_gather(attn_gain, "fsdp", axis=0, tiled=True),
        lax.all_gather(ffn_gain, "fsdp", axis=0, tiled=True),
    )
    (
        full_query,
        full_key,
        full_value,
        full_out,
        full_gate,
        full_up,
        full_down,
        gain_one,
        gain_two,
    ) = gathered
    stream = activations.reshape(tokens, width).astype(jnp.float32)
    inv_one = lax.rsqrt(jnp.mean(stream * stream, axis=-1, keepdims=True) + epsilon)
    normed1 = (stream * inv_one * gain_one).astype(jnp.bfloat16)
    query_raw = jnp.dot(normed1, full_query, preferred_element_type=jnp.float32).reshape(
        tokens, heads, DH
    )
    queries = (
        rope_turn(query_raw, cosine, sine).astype(jnp.bfloat16).reshape(tokens, kv_heads, group, DH)
    )
    key_raw = jnp.dot(normed1, full_key, preferred_element_type=jnp.float32).reshape(
        tokens, kv_heads, DH
    )
    keys = rope_turn(key_raw, cosine, sine).astype(jnp.bfloat16)
    values = (
        jnp.dot(normed1, full_value, preferred_element_type=jnp.float32)
        .astype(jnp.bfloat16)
        .reshape(tokens, kv_heads, DH)
    )

    def scores_with(key_piece, owner):
        scores = (
            jnp.einsum("tjgd,sjd->jgts", queries, key_piece, preferred_element_type=jnp.float32)
            * scale
        )
        counted = places_of(owner)[None, :] <= query_places[:, None]
        return jnp.where(counted, scores, masked_score)

    def absorb(state, key_piece, value_piece, owner):
        running_top, running_total, running_sum = state
        scores = scores_with(key_piece, owner)
        new_top = jnp.maximum(running_top, jnp.max(scores, axis=-1, keepdims=True))
        fading = jnp.exp(running_top - new_top)
        weights = jnp.exp(scores - new_top)
        running_total = fading * running_total + jnp.sum(weights, axis=-1, keepdims=True)
        running_sum = fading * running_sum + jnp.einsum(
            "jgts,sjd->jgtd",
            weights.astype(jnp.bfloat16),
            value_piece,
            preferred_element_type=jnp.float32,
        )
        return (new_top, running_total, running_sum)

    start_state = (
        jnp.full((kv_heads, group, tokens, 1), masked_score, jnp.float32),
        jnp.zeros((kv_heads, group, tokens, 1), jnp.float32),
        jnp.zeros((kv_heads, group, tokens, DH), jnp.float32),
    )
    state = absorb(start_state, keys, values, mine)

    def forward_turn(turn_index, carry):
        state_now, key_piece, value_piece = carry
        key_piece, value_piece = passed_along((key_piece, value_piece), "ctx", 1)
        owner = (mine - turn_index) % cycles
        return (absorb(state_now, key_piece, value_piece, owner), key_piece, value_piece)

    state, _, _ = lax.fori_loop(1, cycles, forward_turn, (state, keys, values))
    running_top, running_total, running_sum = state
    attended = running_sum / running_total
    log_total = running_top + jnp.log(running_total)
    attended_low = (
        jnp.transpose(attended, (2, 0, 1, 3)).reshape(tokens, heads * DH).astype(jnp.bfloat16)
    )
    stream_one = stream + jnp.dot(attended_low, full_out, preferred_element_type=jnp.float32)
    inv_two = lax.rsqrt(jnp.mean(stream_one * stream_one, axis=-1, keepdims=True) + epsilon)
    normed2 = (stream_one * inv_two * gain_two).astype(jnp.bfloat16)
    gate = jnp.dot(normed2, full_gate, preferred_element_type=jnp.float32)
    up_part = jnp.dot(normed2, full_up, preferred_element_type=jnp.float32)
    sigma = jax.nn.sigmoid(gate)
    hidden = (gate * sigma * up_part).astype(jnp.bfloat16)
    stream_two = stream_one + jnp.dot(hidden, full_down, preferred_element_type=jnp.float32)
    output = stream_two.astype(jnp.bfloat16).reshape(activations.shape)
    back_weights = (
        lax.all_gather(w_query, "fsdp", axis=0, tiled=True),
        lax.all_gather(w_key, "fsdp", axis=0, tiled=True),
        lax.all_gather(w_value, "fsdp", axis=0, tiled=True),
        lax.all_gather(w_out, "fsdp", axis=0, tiled=True),
        lax.all_gather(w_gate, "fsdp", axis=0, tiled=True),
        lax.all_gather(w_up, "fsdp", axis=0, tiled=True),
        lax.all_gather(w_down, "fsdp", axis=0, tiled=True),
        lax.all_gather(attn_gain, "fsdp", axis=0, tiled=True),
        lax.all_gather(ffn_gain, "fsdp", axis=0, tiled=True),
    )
    (
        back_query,
        back_key,
        back_value,
        back_out,
        back_gate,
        back_up,
        back_down,
        back_gain_one,
        back_gain_two,
    ) = back_weights
    grad_rows = cotangent.reshape(tokens, width)
    grad_stream = grad_rows.astype(jnp.float32)
    grad_down = jnp.einsum("tf,td->fd", hidden, grad_rows, preferred_element_type=jnp.float32)
    d_hidden = jnp.einsum("td,fd->tf", grad_rows, back_down, preferred_element_type=jnp.float32)
    d_gate = (d_hidden * up_part * sigma * (1.0 + gate * (1.0 - sigma))).astype(jnp.bfloat16)
    d_up = (d_hidden * gate * sigma).astype(jnp.bfloat16)
    grad_gate = jnp.einsum("td,tf->df", normed2, d_gate, preferred_element_type=jnp.float32)
    grad_up = jnp.einsum("td,tf->df", normed2, d_up, preferred_element_type=jnp.float32)
    d_normed2 = jnp.einsum(
        "tf,df->td", d_gate, back_gate, preferred_element_type=jnp.float32
    ) + jnp.einsum("tf,df->td", d_up, back_up, preferred_element_type=jnp.float32)
    grad_ffn_gain = jnp.sum(d_normed2 * stream_one * inv_two, axis=0)
    d_stream_one = grad_stream + norm_back(d_normed2, stream_one, inv_two, back_gain_two)
    d_branch = d_stream_one.astype(jnp.bfloat16)
    grad_out = jnp.einsum("tk,td->kd", attended_low, d_branch, preferred_element_type=jnp.float32)
    d_attended = jnp.einsum(
        "td,kd->tk", d_branch, back_out, preferred_element_type=jnp.float32
    ).astype(jnp.bfloat16)
    d_heads = jnp.transpose(d_attended.reshape(tokens, kv_heads, group, DH), (1, 2, 0, 3))
    delta = jnp.sum(d_heads.astype(jnp.float32) * attended, axis=-1, keepdims=True)

    def back_step(d_queries, d_keys, d_values, key_piece, value_piece, owner):
        scores = scores_with(key_piece, owner)
        probs = jnp.exp(scores - log_total)
        d_values = d_values + jnp.einsum(
            "jgts,jgtd->sjd",
            probs.astype(jnp.bfloat16),
            d_heads,
            preferred_element_type=jnp.float32,
        )
        d_probs = jnp.einsum(
            "jgtd,sjd->jgts", d_heads, value_piece, preferred_element_type=jnp.float32
        )
        d_scores = (probs * (d_probs - delta)).astype(jnp.bfloat16)
        d_queries = (
            d_queries
            + jnp.einsum("jgts,sjd->jgtd", d_scores, key_piece, preferred_element_type=jnp.float32)
            * scale
        )
        d_keys = (
            d_keys
            + jnp.einsum("jgts,tjgd->sjd", d_scores, queries, preferred_element_type=jnp.float32)
            * scale
        )
        return (d_queries, d_keys, d_values)

    def pass_grads(d_keys, d_values):
        return (
            passed_along(d_keys.astype(jnp.bfloat16), "ctx", 1).astype(d_keys.dtype),
            passed_along(d_values.astype(jnp.bfloat16), "ctx", 1).astype(d_values.dtype),
        )

    zero_queries = jnp.zeros((kv_heads, group, tokens, DH), jnp.float32)
    zero_keys = jnp.zeros((tokens, kv_heads, DH), jnp.float32)
    d_queries, d_keys, d_values = back_step(zero_queries, zero_keys, zero_keys, keys, values, mine)

    def backward_turn(turn_index, carry):
        d_queries_now, d_keys_now, d_values_now, key_piece, value_piece = carry
        key_piece, value_piece = passed_along((key_piece, value_piece), "ctx", 1)
        d_keys_now, d_values_now = pass_grads(d_keys_now, d_values_now)
        owner = (mine - turn_index) % cycles
        d_queries_now, d_keys_now, d_values_now = back_step(
            d_queries_now, d_keys_now, d_values_now, key_piece, value_piece, owner
        )
        return (d_queries_now, d_keys_now, d_values_now, key_piece, value_piece)

    d_queries, d_keys, d_values, _, _ = lax.fori_loop(
        1, cycles, backward_turn, (d_queries, d_keys, d_values, keys, values)
    )
    d_keys, d_values = pass_grads(d_keys, d_values)
    d_query_rows = jnp.transpose(d_queries, (2, 0, 1, 3)).reshape(tokens, heads, DH)
    d_query = rope_back(d_query_rows, cosine, sine).astype(jnp.bfloat16).reshape(tokens, heads * DH)
    d_key = rope_back(d_keys, cosine, sine).astype(jnp.bfloat16).reshape(tokens, kv_heads * DH)
    d_value = d_values.astype(jnp.bfloat16).reshape(tokens, kv_heads * DH)
    grad_query = jnp.einsum("td,tk->dk", normed1, d_query, preferred_element_type=jnp.float32)
    grad_key = jnp.einsum("td,tk->dk", normed1, d_key, preferred_element_type=jnp.float32)
    grad_value = jnp.einsum("td,tk->dk", normed1, d_value, preferred_element_type=jnp.float32)
    d_normed1 = (
        jnp.einsum("tk,dk->td", d_query, back_query, preferred_element_type=jnp.float32)
        + jnp.einsum("tk,dk->td", d_key, back_key, preferred_element_type=jnp.float32)
        + jnp.einsum("tk,dk->td", d_value, back_value, preferred_element_type=jnp.float32)
    )
    grad_attn_gain = jnp.sum(d_normed1 * stream * inv_one, axis=0)
    input_grad = (d_stream_one + norm_back(d_normed1, stream, inv_one, back_gain_one)).reshape(
        activations.shape
    )
    shares = (
        lax.psum_scatter(
            grad_query.astype(jnp.bfloat16), "fsdp", scatter_dimension=0, tiled=True
        ).astype(jnp.float32),
        lax.psum_scatter(
            grad_key.astype(jnp.bfloat16), "fsdp", scatter_dimension=0, tiled=True
        ).astype(jnp.float32),
        lax.psum_scatter(
            grad_value.astype(jnp.bfloat16), "fsdp", scatter_dimension=0, tiled=True
        ).astype(jnp.float32),
        lax.psum_scatter(
            grad_out.astype(jnp.bfloat16), "fsdp", scatter_dimension=0, tiled=True
        ).astype(jnp.float32),
        lax.psum_scatter(
            grad_gate.astype(jnp.bfloat16), "fsdp", scatter_dimension=0, tiled=True
        ).astype(jnp.float32),
        lax.psum_scatter(
            grad_up.astype(jnp.bfloat16), "fsdp", scatter_dimension=0, tiled=True
        ).astype(jnp.float32),
        lax.psum_scatter(
            grad_down.astype(jnp.bfloat16), "fsdp", scatter_dimension=0, tiled=True
        ).astype(jnp.float32),
        lax.psum_scatter(
            grad_attn_gain.astype(jnp.bfloat16), "fsdp", scatter_dimension=0, tiled=True
        ).astype(jnp.float32),
        lax.psum_scatter(
            grad_ffn_gain.astype(jnp.bfloat16), "fsdp", scatter_dimension=0, tiled=True
        ).astype(jnp.float32),
    )
    shares = (
        lax.psum(shares[0].astype(jnp.bfloat16), "ctx").astype(jnp.float32),
        lax.psum(shares[1].astype(jnp.bfloat16), "ctx").astype(jnp.float32),
        lax.psum(shares[2].astype(jnp.bfloat16), "ctx").astype(jnp.float32),
        lax.psum(shares[3].astype(jnp.bfloat16), "ctx").astype(jnp.float32),
        lax.psum(shares[4].astype(jnp.bfloat16), "ctx").astype(jnp.float32),
        lax.psum(shares[5].astype(jnp.bfloat16), "ctx").astype(jnp.float32),
        lax.psum(shares[6].astype(jnp.bfloat16), "ctx").astype(jnp.float32),
        lax.psum(shares[7].astype(jnp.bfloat16), "ctx").astype(jnp.float32),
        lax.psum(shares[8].astype(jnp.bfloat16), "ctx").astype(jnp.float32),
    )
    return (
        output,
        input_grad,
        shares[0],
        shares[1],
        shares[2],
        shares[3],
        shares[4],
        shares[5],
        shares[6],
        shares[7],
        shares[8],
    )


LANES = 128
CORE, ALONG_X, ALONG_Y = 1, 2, 4
RELATIVE = (0, 2, 4, 6, 1, 3, 5, 7)
MIB = 2**20
COST = 10**6


def lane_dot(left, right):
    return lax.dot_general(left, right, (((1,), (1,)), ((), ())), preferred_element_type=jnp.float32)


def plain_dot(left, right):
    return lax.dot_general(left, right, (((1,), (0,)), ((), ())), preferred_element_type=jnp.float32)


def row_dot(left, right):
    return lax.dot_general(left, right, (((0,), (0,)), ((), ())), preferred_element_type=jnp.float32)


def rows_at(index, size):
    return pl.ds(pl.multiple_of(index * size, size), size)


def wide(value):
    return value.astype(jnp.float32)


def narrow(value):
    return value.astype(jnp.bfloat16)


def lanes_of(rows):
    return lax.broadcasted_iota(jnp.int32, (rows, LANES), 1)


def shape(dims, kind=jnp.bfloat16):
    return jax.ShapeDtypeStruct(dims, kind)


def after(value, *others):
    return lax.optimization_barrier((value, *others))[0]


class Steps:

    def __init__(self, ticket):
        self.ticket = ticket
        self.pending = []

    def wait(self, *values):
        self.pending.extend(values)

    def run(
        self,
        body,
        outs,
        small,
        arrays,
        far=(),
        pinned=(),
        far_outs=(),
        scratch=(),
        limit=20,
        micros=2,
    ):
        near = pl.BlockSpec(memory_space=pltpu.VMEM)
        scalars = pl.BlockSpec(memory_space=pltpu.SMEM)
        away = pl.BlockSpec(memory_space=pl.ANY)
        stored = pl.BlockSpec(memory_space=pltpu.HBM)
        single = not isinstance(outs, tuple)
        out_shapes = ((outs,) if single else outs) + tuple(far_outs)
        out_specs = [near] * (len(out_shapes) - len(far_outs)) + [stored] * len(far_outs)
        ticket = after(self.ticket, *self.pending) if self.pending else self.ticket
        results = pl.pallas_call(
            lambda _, *refs: body(*refs),
            out_shape=out_shapes,
            in_specs=[scalars] * (1 + len(small))
            + [near] * len(arrays)
            + [away] * len(far)
            + [stored] * len(pinned),
            out_specs=out_specs,
            scratch_shapes=list(scratch),
            compiler_params=pltpu.CompilerParams(vmem_limit_bytes=limit * MIB),
            cost_estimate=pl.CostEstimate(
                flops=micros * COST, bytes_accessed=0, transcendentals=0
            ),
        )(ticket, *small, *arrays, *far, *pinned)
        self.pending = [results[-1]]
        return results[0] if single and not far_outs else results


def window_of(weight, start):
    base = jnp.minimum(start // LANES * LANES, weight.shape[1] - 2 * LANES)
    return weight.at[:, pl.ds(pl.multiple_of(base, LANES), 2 * LANES)], start - base


def drawn(window_ref, shift):
    size = 2 * LANES
    return pltpu.roll(wide(window_ref[...]), (size - shift) % size, 1)


def join_fields(one, two, three, four):
    lane = lanes_of(one.shape[0])
    two = pltpu.roll(two, 96, 1)
    three = pltpu.roll(three, 64, 1)
    four = pltpu.roll(four, 32, 1)
    return jnp.concatenate(
        [
            jnp.where(lane < 96, one, two),
            jnp.where(lane < 64, two, three),
            jnp.where(lane < 32, three, four),
        ],
        axis=1,
    )


def part_fields(block):
    lane = lanes_of(block.shape[0])
    one, two, three = (block[:, start : start + LANES] for start in (0, LANES, 2 * LANES))
    fields = (
        one,
        jnp.where(lane < 32, pltpu.roll(one, 32, 1), pltpu.roll(two, 32, 1)),
        jnp.where(lane < 64, pltpu.roll(two, 64, 1), pltpu.roll(three, 64, 1)),
        pltpu.roll(three, 96, 1),
    )
    return [jnp.where(lane < DH, field, 0.0) for field in fields]


def pack_kernel(
    mine_ref,
    gain_ref,
    query_in,
    key_in,
    value_in,
    out_in,
    first_ref,
    query_ref,
    key_ref,
    value_ref,
    out_ref,
    done,
):
    mine = mine_ref[0]
    shard = query_ref.shape[0]
    four = 4 * DH
    slab = out_ref.shape[0]
    slabs = out_ref.shape[1] // four
    query_window, query_shift = window_of(query_in, mine * 2 * DH)
    key_window, shift = window_of(key_in, mine * DH)
    value_window, _ = window_of(value_in, mine * DH)
    copies = [
        fetch(source, target, done.at[index])
        for index, (source, target) in enumerate(
            (
                (query_window, query_ref),
                (key_window, key_ref),
                (value_window, value_ref),
                (out_in.at[rows_at(mine, slab), :], out_ref),
            )
        )
    ]
    for copy in copies:
        copy.wait()
    query = drawn(query_ref, query_shift)
    key = pltpu.roll(drawn(key_ref, shift)[:, :LANES], 64, 1)
    value = pltpu.roll(drawn(value_ref, shift)[:, :LANES], 32, 1)
    lane = lanes_of(shard)
    first_ref[:shard, :LANES] = narrow(query[:, :LANES])
    first_ref[:shard, LANES : 2 * LANES] = narrow(jnp.where(lane < 64, query[:, LANES:], key))
    first_ref[:shard, 2 * LANES :] = narrow(jnp.where(lane < 32, key, value))
    for index in range(slabs):
        here = shard + index * slab
        first_ref[here : here + slab, :] = out_ref[:, index * four : (index + 1) * four]
    first_ref[shard + slabs * slab :, :] = gain_ref[...]


def strip_kernel(mine_ref, gate_ref, up_ref, both_ref):
    quarters = both_ref.shape[1] // (2 * LANES)
    for index in range(quarters):
        place = rows_at(index * 8 + mine_ref[0], LANES)
        both_ref[:, index * LANES : (index + 1) * LANES] = gate_ref[:, place]
        both_ref[:, (quarters + index) * LANES : (quarters + index + 1) * LANES] = up_ref[:, place]


def fold(block):
    rows = block.shape[0]
    tail = block[:, LANES:]
    lower = jnp.where(lanes_of(rows // 2) < 64, tail[: rows // 2], pltpu.roll(tail[rows // 2 :], 64, 1))
    return jnp.concatenate([block[:, :LANES], lower], axis=0)


def unfold(block):
    rows = block.shape[0] // 3 * 2
    half = rows // 2
    tail = block[rows:]
    keep = lanes_of(half) < 64
    tail = jnp.concatenate(
        [jnp.where(keep, tail, 0.0), jnp.where(keep, pltpu.roll(tail, 64, 1), 0.0)], axis=0
    )
    return jnp.concatenate([block[:rows], tail], axis=1)


def branch_kernel(owner_ref, folded_ref, stream_ref, gain_ref, *refs):
    pieces, refs = refs[:8], refs[8:]
    one_ref, normed_ref, inverse_ref, heads_ref, full_out, full_ref, piece_ref, done = refs
    copies = [fetch(piece, piece_ref.at[i], done.at[i]) for i, piece in enumerate(pieces)]
    width = full_ref.shape[1]
    slab = width // 32
    size = 2 * DH
    four = pieces[0].shape[1]
    gap = jnp.zeros((folded_ref.shape[1] // 3 * 2, LANES), jnp.float32)
    for index in range(0, folded_ref.shape[0], 2):
        one = unfold(wide(folded_ref[index]))
        two = unfold(wide(folded_ref[index + 1]))
        both = jnp.concatenate([one, gap], axis=1) + pltpu.roll(
            jnp.concatenate([two, gap], axis=1), size, 1
        )
        heads_ref[:, index * size : (index + 2) * size] = narrow(both)
    for index, copy in enumerate(copies):
        copy.wait()
        for quarter in range(4):
            row = pl.multiple_of(quarter * 8 * slab + owner_ref[index] * slab, 16)
            for part in range(width // four):
                start = (quarter * (width // four) + part) * slab
                full_ref[pl.ds(row, slab), part * four : (part + 1) * four] = piece_ref[
                    index, start : start + slab, :
                ]
    copy = fetch(full_ref, full_out, done.at[0])
    total = wide(stream_ref[...]) + plain_dot(heads_ref[...], full_ref[...])
    one_ref[...] = total
    inverse = lax.rsqrt(jnp.mean(total * total, axis=1, keepdims=True) + epsilon)
    normed_ref[...] = narrow(total * inverse * gain_ref[8:9])
    inverse_ref[...] = jnp.broadcast_to(inverse, inverse_ref.shape)
    copy.wait()


def strips_kernel(count, carry, *refs):
    before, refs = refs[: int(carry)], refs[int(carry) :]
    normed_in, grad_in, refs = refs[:count], refs[count : 2 * count], refs[2 * count :]
    (gate_up_in, down_in), refs = refs[:2], refs[2:]
    grad_out, stream_refs, sum_refs, refs = refs[0], refs[1 : 1 + count], refs[1 + count : 1 + 2 * count], refs[1 + 2 * count :]
    both_out, refs = refs[0], refs[1:]
    down_grad, gate_up_ref, down_ref, normed_ref, grad_ref, both_ref, done, out_done, weight_done = refs
    weights = [
        fetch(gate_up_in, gate_up_ref, weight_done.at[0]),
        fetch(down_in, down_ref, weight_done.at[1]),
    ]
    part = down_ref.shape[0]
    rows = normed_in[0].shape[0]
    size = 2 * rows
    copies = [
        (
            fetch(normed_in[index], normed_ref.at[pl.ds(index * rows, rows), :], done.at[index]),
            fetch(grad_in[index], grad_ref.at[pl.ds(index * rows, rows), :], done.at[count + index]),
        )
        for index in range(count)
    ]
    outs = []
    for copy in weights:
        copy.wait()
    for step in range(count // 2):
        for index in (2 * step, 2 * step + 1):
            copies[index][0].wait()
            copies[index][1].wait()
        here = slice(step * size, (step + 1) * size)
        normed = normed_ref[here, :]
        grad = grad_ref[here, :]
        gate = plain_dot(normed, gate_up_ref[:, :part])
        up = plain_dot(normed, gate_up_ref[:, part:])
        sigma = jax.nn.sigmoid(gate)
        turned = gate * sigma
        hidden = narrow(turned * up)
        d_hidden = lane_dot(grad, down_ref[...])
        d_gate = narrow(d_hidden * up * sigma * (1.0 + gate * (1.0 - sigma)))
        d_up = narrow(d_hidden * turned)
        both_ref[here, :part] = d_gate
        both_ref[here, part:] = d_up
        there = pl.ds(step * size, size)
        outs.append(fetch(both_ref.at[there, :], both_out.at[there, :], out_done.at[step]))
        d_normed = narrow(
            lane_dot(d_gate, gate_up_ref[:, :part]) + lane_dot(d_up, gate_up_ref[:, part:])
        )
        sums = narrow(plain_dot(hidden, down_ref[...]))
        for index in range(2):
            stream_refs[2 * step + index][...] = d_normed[index * rows : (index + 1) * rows]
            sum_refs[2 * step + index][...] = sums[index * rows : (index + 1) * rows]
        product = row_dot(hidden, grad)
        if step == 0:
            down_grad[...] = product + before[0][...] if carry else product
        elif step < count // 2 - 1:
            down_grad[...] += product
        else:
            grad_out[...] = (down_grad[...] + product).astype(grad_out.dtype)
    for copy in outs:
        copy.wait()


def strip_grad_kernel(count, *refs):
    weight_ref, gain_ref, refs = refs[0], refs[1], refs[2:]
    normed_in, (own_in, twin_in), refs = refs[:count], refs[count : count + 2], refs[count + 2 :]
    out_ref, row_ref, normed_ref, both_ref, done = refs
    size = 2 * LANES
    rows = normed_in[0].shape[0]
    half = own_in.shape[0]
    copies = [
        fetch(piece, normed_ref.at[pl.ds(index * rows, rows), :], done.at[index])
        for index, piece in enumerate(normed_in)
    ]
    copies.append(fetch(own_in, both_ref.at[pl.ds(0, half), :], done.at[count]))
    copies.append(fetch(twin_in, both_ref.at[pl.ds(half, half), :], done.at[count + 1]))
    for copy in copies:
        copy.wait()
    ones = jnp.ones((8, out_ref.shape[1]), jnp.bfloat16)

    def one(index, _):
        columns = rows_at(index, size)
        total = row_dot(normed_ref[:, columns], both_ref[...])
        out_ref[columns, :] = narrow(total)
        share = narrow(total * wide(weight_ref[columns, :]))
        row_ref[:, columns] = lane_dot(ones, share) / gain_ref[8:, columns]
        return 0

    lax.fori_loop(0, out_ref.shape[0] // size, one, 0)


def add_twin_kernel(core_ref, *refs):
    own_refs, twin_refs, (send_ref, keep_ref, self_ref) = refs[:4], refs[4:8], refs[8:]
    rows = keep_ref.shape[0]
    self_ref[...] = wide(own_refs[0][...]) + wide(twin_refs[0][...])
    send_ref[:rows, :] = narrow(wide(own_refs[3][...]) + wide(twin_refs[3][...]))
    along_x = wide(own_refs[1][...]) + wide(twin_refs[1][...])
    along_y = wide(own_refs[2][...]) + wide(twin_refs[2][...])

    @pl.when(core_ref[0] == 0)
    def _():
        send_ref[rows:, :] = narrow(along_y)
        keep_ref[...] = along_x

    @pl.when(core_ref[0] == 1)
    def _():
        send_ref[rows:, :] = narrow(along_x)
        keep_ref[...] = along_y


def add_late_kernel(keep_ref, got_ref, late_ref):
    rows = keep_ref.shape[0]
    late_ref[...] = narrow(keep_ref[...] + wide(got_ref[:rows, :]))


def summed(self_ref, got_ref, late_ref):
    rows = self_ref.shape[0]
    return self_ref[...] + wide(got_ref[rows:, :]) + wide(late_ref[...])


def norm_down(d_normed, stream, inverse, gain):
    scaled = d_normed * gain
    cubed = inverse * inverse * inverse
    return inverse * scaled - stream * cubed * jnp.mean(scaled * stream, axis=1, keepdims=True)


def branch_back_kernel(
    self_ref,
    got_ref,
    late_ref,
    grad_ref,
    one_ref,
    inverse_ref,
    gain_ref,
    full_ref,
    stream_out,
    heads_out,
):
    d_normed = summed(self_ref, got_ref, late_ref)
    d_stream = wide(grad_ref[...]) + norm_down(
        d_normed, one_ref[...], inverse_ref[:, :1], gain_ref[8:9]
    )
    stream_out[...] = d_stream
    d_branch = narrow(d_stream)
    rows = d_branch.shape[0]
    size = 2 * DH
    gap = jnp.zeros((rows, 2 * LANES - size), jnp.float32)
    keep = lanes_of(rows) < size - LANES
    tall = heads_out.shape[1] // 2
    for index in range(heads_out.shape[0]):
        heads = lane_dot(d_branch, full_ref[index * size : (index + 1) * size, :])
        heads_out[index, :tall, :] = narrow(fold(jnp.concatenate([heads, gap], axis=1)))
        start = index * size // LANES * LANES
        columns = wide(d_branch[:, start : start + 2 * LANES])
        if index % 2:
            columns = pltpu.roll(columns, 2 * LANES - 64, 1)
        columns = jnp.concatenate(
            [columns[:, :LANES], jnp.where(keep, columns[:, LANES:], 0.0)], axis=1
        )
        heads_out[index, tall:, :] = narrow(fold(columns))


def input_back_kernel(
    self_ref, got_ref, late_ref, stream_ref, back_ref, gain_ref, out_ref
):
    d_normed = summed(self_ref, got_ref, late_ref)
    stream = wide(stream_ref[...])
    inverse = lax.rsqrt(jnp.mean(stream * stream, axis=1, keepdims=True) + epsilon)
    out_ref[...] = back_ref[...] + norm_down(d_normed, stream, inverse, gain_ref[:1])


def output_kernel(self_ref, got_ref, late_ref, one_ref, out_ref):
    out_ref[...] = narrow(one_ref[...] + summed(self_ref, got_ref, late_ref))


def stream_grad_kernel(start, fields_ref, weight_ref, *out_refs):
    rows = out_refs[0].shape[0]
    for step in range(len(out_refs) // 2):
        first = start + 2 * step * rows
        product = narrow(lane_dot(fields_ref[first : first + 2 * rows, :], weight_ref[...]))
        out_refs[2 * step][...] = product[:rows]
        out_refs[2 * step + 1][...] = product[rows:]


def place_strips_kernel(owner_ref, *refs):
    pieces, (gate_out, up_out, low_ref, wide_ref, done, out_done) = refs[:-6], refs[-6:]
    copies = [fetch(piece, low_ref.at[i], done.at[i]) for i, piece in enumerate(pieces)]
    quarters = low_ref.shape[2] // (2 * LANES)
    outs = []
    for index, copy in enumerate(copies):
        copy.wait()
        wide_ref[index] = wide(low_ref[index])
        for part in range(2 * quarters):
            there = rows_at(part % quarters * 8 + owner_ref[index], LANES)
            target = gate_out if part < quarters else up_out
            outs.append(
                fetch(
                    wide_ref.at[index, :, pl.ds(part * LANES, LANES)],
                    target.at[:, there],
                    out_done.at[index, part],
                )
            )
    for copy in outs:
        copy.wait()


def place_down_kernel(owner_ref, *refs):
    pieces, (down_out, low_ref, wide_ref, done) = refs[:-4], refs[-4:]
    copies = [fetch(piece, low_ref.at[i], done.at[0, i]) for i, piece in enumerate(pieces)]
    outs = []
    for index, copy in enumerate(copies):
        copy.wait()
        wide_ref[index] = wide(low_ref[index])
        there = rows_at(owner_ref[index], wide_ref.shape[1])
        outs.append(fetch(wide_ref.at[index], down_out.at[there, :], done.at[1, index]))
    for copy in outs:
        copy.wait()


def place_last_kernel(owner_ref, *refs):
    pieces, gain_ref, outs, refs = refs[:8], refs[8], refs[9:13], refs[13:]
    low_ref, query_ref, key_ref, value_ref, out_ref, done, out_done = refs
    shard = query_ref.shape[0]
    half = shard // 2
    end = shard + half
    copies = [
        fetch(piece, low_ref.at[owner_ref[index]], done.at[index])
        for index, piece in enumerate(pieces)
    ]
    for copy in copies:
        copy.wait()
    full = lanes_of(shard) < 64
    keep = lanes_of(half) < 64
    gains = jnp.zeros(gain_ref.shape, jnp.float32)
    targets = []
    for quad in range(2):
        keys, values = [], []
        for pair in (2 * quad, 2 * quad + 1):
            columns = slice(pair * 4 * DH, (pair + 1) * 4 * DH)
            tiles = []
            for index in (2 * pair, 2 * pair + 1):
                block = wide(low_ref[index, :shard, :])
                one, two, key, value = part_fields(block)
                keys.append(key)
                values.append(value)
                tiles.append((block[:, :LANES], block[:, LANES : 2 * LANES]))
                gains = gains + wide(low_ref[index, end : end + 16, :])
            (one, two), (three, four) = tiles
            three, four = pltpu.roll(three, 64, 1), pltpu.roll(four, 64, 1)
            query_ref[:, columns] = jnp.concatenate(
                [one, jnp.where(full, two, three), jnp.where(full, three, four)], axis=1
            )
            for part in range(2):
                tiles = []
                for index in (2 * pair, 2 * pair + 1):
                    block = wide(low_ref[index, shard:end, :])
                    one, two, three = (
                        block[:, start : start + LANES] for start in (0, LANES, 2 * LANES)
                    )
                    if part:
                        two, three = pltpu.roll(two, 64, 1), pltpu.roll(three, 64, 1)
                        one, two = jnp.where(keep, two, three), three
                    tiles.append((one, two))
                (one, two), (three, four) = tiles
                three, four = pltpu.roll(three, 64, 1), pltpu.roll(four, 64, 1)
                out_ref[part * half : (part + 1) * half, columns] = jnp.concatenate(
                    [one, jnp.where(keep, two, three), jnp.where(keep, three, four)], axis=1
                )
        columns = slice(quad * 4 * DH, (quad + 1) * 4 * DH)
        key_ref[:, columns] = join_fields(*keys)
        value_ref[:, columns] = join_fields(*values)
        wide_columns = pl.ds(quad * 8 * DH, 8 * DH)
        some_columns = pl.ds(quad * 4 * DH, 4 * DH)
        for index, (ref, out, here) in enumerate(
            (
                (query_ref, outs[0], wide_columns),
                (key_ref, outs[1], some_columns),
                (value_ref, outs[2], some_columns),
                (out_ref, outs[3], wide_columns),
            )
        ):
            targets.append(fetch(ref.at[:, here], out.at[:, here], out_done.at[4 * quad + index]))
    gain_ref[...] = gains
    for copy in targets:
        copy.wait()


def swapped(field):
    half = DH // 2
    lane = lanes_of(field.shape[0])
    return jnp.where(lane < half, pltpu.roll(field, LANES - half, 1), pltpu.roll(field, half, 1))


def rows_of(weights, field):
    return lax.dot_general(
        weights,
        field,
        (((1,), (1,)), ((), ())),
        precision=lax.Precision.HIGHEST,
        preferred_element_type=jnp.float32,
    )


def fetch(source, target, done):
    copy = pltpu.make_async_copy(source, target, done)
    copy.start()
    return copy


def attend_kernel(
    span,
    near_ref,
    slot_ref,
    cos_ref,
    sin_ref,
    *refs,
):
    (*piece_refs, first_ref), refs = refs[:9], refs[9:]
    (low_ref, gain_ref, level_ref), refs = refs[:3], refs[3:]
    (normed_out, weight_out, query_out, key_out, value_out, mixed_out), refs = refs[:6], refs[6:]
    stream_ref, weight_ref, gains_ref, raw_ref, query_ref, key_ref, value_ref, mixed_ref = refs[:8]
    score_ref, top_ref, sum_ref, in_done, out_done = refs[8:]
    spans = near_ref.shape[0]
    block = 2 * span
    pair = 2 * block
    turns = spans // 2
    quarters, packed, four = first_ref.shape
    shard = weight_ref.shape[0] // quarters
    factor = LOG2E / math.sqrt(DH)

    gain_copies = [
        fetch(
            first_ref.at[quarter, pl.ds(packed - 32, 32), :],
            gains_ref.at[pl.ds(quarter * 32, 32), :],
            in_done.at[turns + quarter],
        )
        for quarter in range(quarters)
    ]
    weight_copies = [
        fetch(
            first_ref.at[quarter, pl.ds(0, shard), :],
            weight_ref.at[pl.ds(quarter * shard, shard), :],
            in_done.at[turns + quarters + quarter],
        )
        for quarter in range(quarters)
    ]
    copies = [
        fetch(piece, stream_ref.at[pl.ds(index * block, block), :], in_done.at[index])
        for index, piece in enumerate(piece_refs)
    ]
    for copy in gain_copies:
        copy.wait()
    for quarter in range(quarters):
        rows = wide(gains_ref[quarter * 32 : quarter * 32 + 16, :])
        here = slice(quarter * shard, (quarter + 1) * shard)
        gain_ref[:8, here] = jnp.broadcast_to(rows[:1, :shard], (8, shard))
        gain_ref[8:, here] = jnp.broadcast_to(rows[1:2, :shard], (8, shard))
    for copy in weight_copies:
        copy.wait()
    out_copies = [fetch(weight_ref, weight_out, out_done.at[0])]
    gain = gain_ref[:1, :]

    def norm(start):
        here = pl.ds(start, span)
        stream = wide(stream_ref[here, :])
        inverse = lax.rsqrt(jnp.mean(stream * stream, axis=1, keepdims=True) + epsilon)
        stream_ref[here, :] = narrow(stream * inverse * gain)

    for step in range(turns // 2):
        copies[2 * step].wait()
        copies[2 * step + 1].wait()
        here = pl.ds(step * pair, pair)
        for part in range(4):
            norm(step * pair + part * span)
        raw_ref[here, :] = plain_dot(stream_ref[here, :], weight_ref[...])
        out_copies.append(
            fetch(stream_ref.at[here, :], normed_out.at[here, :], out_done.at[1 + step])
        )

    lane = lanes_of(span)

    def place(index, _):
        raw = raw_ref[rows_at(near_ref[index], span), :]
        cosine = cos_ref[rows_at(index, span), :]
        sine = sin_ref[rows_at(index, span), :]
        one, two, three, four = part_fields(raw)

        def turned(field):
            return narrow(field * cosine + swapped(field) * sine)

        first = (index // 2) * 4 + index % 2
        query_ref[rows_at(first, span), :] = turned(one)
        query_ref[rows_at(first + 2, span), :] = turned(two)
        key_ref[rows_at(index, span), :] = turned(three)
        value_ref[rows_at(index, span), :] = narrow(jnp.where(lane == DH, 1.0, four))
        return 0

    lax.fori_loop(0, spans, place, 0, unroll=2)
    next_done = 1 + turns // 2
    for source, target in ((query_ref, query_out), (key_ref, key_out), (value_ref, value_out)):
        out_copies.append(fetch(source, target, out_done.at[next_done]))
        next_done += 1

    wide_lane = lanes_of(pair)
    picked = (lanes_of(8) == 0).astype(jnp.float32)

    def store(index, both, rest):
        slot = slot_ref[index]
        low_ref[slot // 2, rows_at(slot % 2, span), :] = narrow(both)
        tail = narrow(rest)
        turned = narrow(pltpu.roll(rest, 64, 1))

        @pl.when(slot % 2 == 0)
        def _():
            low_ref[slot // 2, 2 * span :, :64] = tail[:, :64]

        @pl.when(slot % 2 == 1)
        def _():
            low_ref[slot // 2, 2 * span :, 64:] = turned[:, 64:]

    def widest(top, scores):
        for start in range(0, block, LANES):
            top = jnp.maximum(top, scores[:, start : start + LANES])
        return top

    def score(turn, step):
        scores = lane_dot(query_ref[rows_at(turn, pair), :], key_ref[rows_at(step, block), :])
        score_ref[turn % 2, :, rows_at(step, block)] = scores
        top_ref[...] = widest(top_ref[...], scores)

    def edge(turn):
        row = lax.broadcasted_iota(jnp.int32, (pair, block), 0) % block
        column = lax.broadcasted_iota(jnp.int32, (pair, block), 1)
        scores = lane_dot(query_ref[rows_at(turn, pair), :], key_ref[rows_at(turn, block), :])
        scores = jnp.where(column <= row, scores, masked_score)
        score_ref[turn % 2, :, rows_at(turn, block)] = scores
        top = jnp.max(widest(top_ref[...], scores), axis=1, keepdims=True) * factor
        return jnp.broadcast_to(top, (pair, LANES))

    def weigh(turn, step, top):
        scores = score_ref[turn % 2, :, rows_at(step, block)]
        weights = jnp.exp2(scores * factor - top[:, :1])
        sum_ref[...] += plain_dot(narrow(weights), value_ref[rows_at(step, block), :])

    def finish(turn, top):
        total = sum_ref[:, DH : DH + 1]
        mixed = jnp.where(wide_lane < DH, sum_ref[...] / total, 0.0)
        mixed_ref[rows_at(turn, pair), :] = mixed
        level = top + jnp.log2(total)
        level_ref[rows_at(turn, 8), :] = rows_of(picked, level)
        fetch(
            mixed_ref.at[rows_at(turn, pair), :],
            mixed_out.at[rows_at(turn, pair), :],
            out_done.at[next_done + turn],
        )
        one, two = mixed[:block], pltpu.roll(mixed[block:], DH, 1)
        first = jnp.where(wide_lane[:block] < DH, one, two)
        store(2 * turn, first[:span], two[:span])
        store(2 * turn + 1, first[span:], two[span:])

    def clear():
        sum_ref[...] = jnp.zeros_like(sum_ref)
        top_ref[...] = jnp.full(top_ref.shape, masked_score, jnp.float32)

    def one_turn(turn, top):
        clear()

        def both(step, _):
            weigh(turn, step, top)
            score(turn + 1, step)
            return 0

        lax.fori_loop(0, turn + 1, both, 0)
        finish(turn, top)
        return edge(turn + 1)

    clear()
    top = lax.fori_loop(0, turns - 1, one_turn, edge(0))
    clear()

    def only(step, _):
        weigh(turns - 1, step, top)
        return 0

    lax.fori_loop(0, turns, only, 0)
    finish(turns - 1, top)
    for copy in out_copies:
        copy.wait()
    for turn in range(turns):
        here = pl.ds(turn * pair, pair)
        pltpu.make_async_copy(
            mixed_ref.at[here, :], mixed_out.at[here, :], out_done.at[next_done + turn]
        ).wait()


def attend(steps, near, slot, cosine, sine, first, pieces, span):
    tokens = cosine.shape[0]
    turns = tokens // (2 * span)
    quarters, _, four = first.shape
    block, width = pieces[0].shape
    f32 = jnp.float32
    near_out = (
        shape((turns, 3 * span, LANES)),
        shape((16, width), f32),
        shape((8 * turns, 4 * span), f32),
    )
    far_out = (
        shape((tokens, width)),
        shape((width, four)),
        shape((2 * tokens, LANES)),
        shape((tokens, LANES)),
        shape((tokens, LANES)),
        shape((2 * tokens, LANES), f32),
    )
    state = pltpu.VMEM((4 * span, LANES), f32)
    return steps.run(
        functools.partial(attend_kernel, span),
        near_out,
        (near, slot),
        (cosine, sine),
        far=(*pieces,),
        pinned=(first,),
        far_outs=far_out,
        scratch=(
            pltpu.VMEM((tokens, width), jnp.bfloat16),
            pltpu.VMEM((width, four), jnp.bfloat16),
            pltpu.VMEM((32 * quarters, four), jnp.bfloat16),
            pltpu.VMEM((tokens, four), f32),
            pltpu.VMEM((2 * tokens, LANES), jnp.bfloat16),
            pltpu.VMEM((tokens, LANES), jnp.bfloat16),
            pltpu.VMEM((tokens, LANES), jnp.bfloat16),
            pltpu.VMEM((2 * tokens, LANES), f32),
            pltpu.VMEM((2, 4 * span, tokens), f32),
            state,
            state,
            pltpu.SemaphoreType.DMA((turns + 2 * quarters,)),
            pltpu.SemaphoreType.DMA((4 + turns // 2 + turns,)),
        ),
        limit=60,
        micros=33,
    )


def weight_grads(
    owner_ref, fields_ref, weight_ref, gain_ref, row_ref, branch_ref, heads, copies, last_ref, normed_ref, heads_ref, sum_ref
):
    quarters = last_ref.shape[0]
    four = weight_ref.shape[1]
    shard = weight_ref.shape[0] // quarters
    half = shard // 2
    size = 2 * DH
    tall = branch_ref.shape[1] // 2
    for index, copy in enumerate(heads):
        columns = narrow(unfold(wide(branch_ref[owner_ref[index], tall:, :])))
        copy.wait()
        product = row_dot(heads_ref[index], columns)
        if index == 0:
            sum_ref[...] = product
        else:
            sum_ref[...] += product
    ones = jnp.ones((8, four), jnp.bfloat16)
    gap = jnp.zeros((half, LANES), jnp.float32)
    for quarter in range(quarters):
        here = slice(quarter * shard, (quarter + 1) * shard)
        copies[quarter].wait()
        total = row_dot(normed_ref[:, here], fields_ref[...])
        last_ref[quarter, :shard, :] = narrow(total)
        share = narrow(total * wide(weight_ref[here, :]))
        attn = lane_dot(ones, share) / gain_ref[:8, here]
        rows = jnp.concatenate([attn, row_ref[:, here]], axis=0)
        one = sum_ref[quarter * shard : quarter * shard + half, :]
        two = sum_ref[quarter * shard + half : (quarter + 1) * shard, :]
        both = jnp.concatenate([one, gap], axis=1) + pltpu.roll(
            jnp.concatenate([two, gap], axis=1), size, 1
        )
        last_ref[quarter, shard : shard + half, :] = narrow(both)
        end = shard + half
        last_ref[quarter, end : end + 16, :] = narrow(rows)
        last_ref[quarter, end + 16 :, :] = jnp.zeros_like(last_ref[quarter, end + 16 :, :])


def attend_back_kernel(
    span,
    near_ref,
    slot_ref,
    owner_ref,
    grad_ref,
    total_ref,
    weight_ref,
    gain_ref,
    row_ref,
    *refs,
):
    (*heads_in, normed_in, cos_in, sin_in, query_in, key_in, value_in, mixed_in), refs = refs[:15], refs[15:]
    out_ref, last_ref, cos_ref, sin_ref, query_ref, key_ref, value_ref, mixed_ref, *refs = refs
    head_ref, delta_ref, query_sum, key_sum, value_sum, normed_ref, heads_ref, sum_ref, done = refs
    spans = near_ref.shape[0]
    block = 2 * span
    pair = 2 * block
    turns = spans // 2
    factor = LOG2E / math.sqrt(DH)
    scale = 1.0 / math.sqrt(DH)
    lane = lax.broadcasted_iota(jnp.int32, (span, LANES), 1)
    copies = [
        fetch(source, target, done.at[index])
        for index, (source, target) in enumerate(
            (
                (mixed_in, mixed_ref),
                (key_in, key_ref),
                (query_in, query_ref),
                (value_in, value_ref),
                (cos_in, cos_ref),
                (sin_in, sin_ref),
            )
        )
    ]

    quarters = last_ref.shape[0]
    shard = normed_ref.shape[1] // quarters
    heads = [
        fetch(piece, heads_ref.at[index], done.at[6 + index]) for index, piece in enumerate(heads_in)
    ]
    normed = [
        fetch(
            normed_in.at[:, pl.ds(quarter * shard, shard)],
            normed_ref.at[:, pl.ds(quarter * shard, shard)],
            done.at[6 + len(heads) + quarter],
        )
        for quarter in range(quarters)
    ]

    def split(index, _):
        slot = slot_ref[index]
        grad = wide(grad_ref[slot // 2, rows_at(slot % 2, span), :])
        tail = wide(grad_ref[slot // 2, 2 * span : 3 * span, :])
        first = (index // 2) * 4 + index % 2
        one = jnp.where(lane < DH, grad, 0.0)
        tail = pltpu.roll(tail, 32 + 64 * (slot % 2), 1)
        two = jnp.where(lane < 32, pltpu.roll(grad, 32, 1), tail)
        two = jnp.where(lane < DH, two, 0.0)
        head_ref[rows_at(first, span), :] = narrow(one)
        head_ref[rows_at(first + 2, span), :] = narrow(two)
        return 0

    lax.fori_loop(0, spans, split, 0, unroll=4)
    copies[0].wait()

    def prepare(turn, _):
        here = rows_at(turn, pair)
        product = wide(head_ref[here, :]) * mixed_ref[here, :]
        delta_ref[rows_at(turn, 8), :] = rows_of(jnp.ones((8, LANES), jnp.float32), product)
        query_sum[here, :] = jnp.zeros((pair, LANES), jnp.float32)
        return 0

    lax.fori_loop(0, turns, prepare, 0, unroll=2)
    for copy in copies[1:]:
        copy.wait()

    def turned_back(field, index):
        cosine = cos_ref[rows_at(index, span), :]
        sine = sin_ref[rows_at(index, span), :]
        field = field * scale
        return wide(narrow(field * cosine - swapped(field) * sine))

    def one_block(turn, _):
        key = key_ref[rows_at(turn, block), :]
        value = value_ref[rows_at(turn, block), :]

        def one_step(step, diagonal):
            here = rows_at(step, pair)
            query = query_ref[here, :]
            head = head_ref[here, :]
            level = total_ref[rows_at(step, 8), :][:1]
            delta = delta_ref[rows_at(step, 8), :][:1]
            probs = jnp.exp2(lane_dot(key, query) * factor - level)
            if diagonal:
                row = lax.broadcasted_iota(jnp.int32, (block, pair), 0)
                column = lax.broadcasted_iota(jnp.int32, (block, pair), 1) % block
                probs = jnp.where(row <= column, probs, 0.0)
            d_scores = narrow(probs * (lane_dot(value, head) - delta))
            query_sum[here, :] += row_dot(d_scores, key)
            return plain_dot(d_scores, query), plain_dot(narrow(probs), head)

        key_part, value_part = one_step(turn, True)
        key_sum[...] = key_part
        value_sum[...] = value_part

        def two_steps(index, _):
            step = turn + 1 + 2 * index
            key_one, value_one = one_step(step, False)
            key_two, value_two = one_step(step + 1, False)
            key_sum[...] += key_one + key_two
            value_sum[...] += value_one + value_two
            return 0

        left = turns - 1 - turn
        lax.fori_loop(0, left // 2, two_steps, 0)

        @pl.when(left % 2 == 1)
        def _():
            key_one, value_one = one_step(turns - 1, False)
            key_sum[...] += key_one
            value_sum[...] += value_one

        for part in range(2):
            index = 2 * turn + part
            here = rows_at(near_ref[index], span)
            rows = slice(part * span, (part + 1) * span)
            first = rows_at((index // 2) * 4 + index % 2, span)
            second = rows_at((index // 2) * 4 + index % 2 + 2, span)
            one = turned_back(query_sum[first, :], index)
            two = turned_back(query_sum[second, :], index)
            three = turned_back(key_sum[rows, :], index)
            out_ref[here, :] = narrow(join_fields(one, two, three, value_sum[rows, :]))
        return 0

    lax.fori_loop(0, turns, one_block, 0)
    weight_grads(
        owner_ref, out_ref, weight_ref, gain_ref, row_ref, grad_ref, heads, normed, last_ref, normed_ref, heads_ref, sum_ref
    )


def attend_back(
    steps, near, slot, owners, grad, total, weights, cosine, sine, query, key, value, mixed, heads, normed, packed, span
):
    tokens, width = normed.shape
    f32 = jnp.float32
    rows = pltpu.VMEM((2 * span, LANES), f32)
    shard = 4 * DH
    return steps.run(
        functools.partial(attend_back_kernel, span),
        (shape((tokens, 4 * DH)), shape((width // shard, packed, 4 * DH))),
        (near, slot, owners),
        (grad, total, *weights),
        far=heads,
        pinned=(normed, cosine, sine, query, key, value, mixed),
        scratch=(
            pltpu.VMEM(cosine.shape, f32),
            pltpu.VMEM(cosine.shape, f32),
            pltpu.VMEM(query.shape, jnp.bfloat16),
            pltpu.VMEM(key.shape, jnp.bfloat16),
            pltpu.VMEM(value.shape, jnp.bfloat16),
            pltpu.VMEM(mixed.shape, f32),
            pltpu.VMEM((2 * tokens, LANES), jnp.bfloat16),
            pltpu.VMEM(total.shape, f32),
            pltpu.VMEM((2 * tokens, LANES), f32),
            rows,
            rows,
            pltpu.VMEM((tokens, width), jnp.bfloat16),
            pltpu.VMEM((len(heads), *heads[0].shape), jnp.bfloat16),
            pltpu.VMEM((width, 2 * LANES), f32),
            pltpu.SemaphoreType.DMA((6 + len(heads) + width // shard,)),
        ),
        limit=60,
        micros=38,
    )


def turn_tables(tokens):
    half = DH // 2
    freqs = jnp.exp(-math.log(rope_base) * 2.0 * jnp.arange(half, dtype=jnp.float32) / DH)
    angle = jnp.arange(tokens, dtype=jnp.int32).astype(jnp.float32)[:, None] * freqs[None, :]
    gap = jnp.zeros((tokens, LANES - DH), jnp.float32)
    cosine, sine = jnp.cos(angle), jnp.sin(angle)
    return (
        jnp.concatenate([cosine, cosine, gap], axis=1),
        jnp.concatenate([-sine, sine, gap], axis=1),
    )


def swap(block, bits):
    routes = [(i, i ^ bits) for i in range(lax.axis_size("ctx"))]
    return lax.ppermute(block, "ctx", routes)


def swap_split(block, even, odd):
    routes = [(i, i ^ (odd if i & CORE else even)) for i in range(lax.axis_size("ctx"))]
    return lax.ppermute(block, "ctx", routes)


def gather_spans(block, core, between=None):
    from_x = swap(block, ALONG_X)
    from_y = swap(block, ALONG_Y)
    twin = swap(block, CORE)
    first = between(from_x, from_y) if between else from_x
    corner = swap_split(jnp.where(core[0] == 0, first, from_y), ALONG_Y, ALONG_X)
    return [block, from_x, from_y, corner] + [
        twin,
        swap(first, CORE),
        swap(from_y, CORE),
        swap(corner, CORE),
    ]


def gather_direct(block):
    blocks = [block] + [swap(block, way) for way in (ALONG_X, ALONG_Y, ALONG_X | ALONG_Y)]
    return blocks + [swap(part, CORE) for part in blocks]


def open_scatter(steps, own, twin, core, limit=20):
    rows, width = own[0].shape
    some = shape((rows, width), jnp.float32)
    return steps.run(
        add_twin_kernel,
        (shape((2 * rows, width)), some, some),
        (core,),
        (*own, *twin),
        limit=limit,
    )


def turn_scatter(steps, keep, got, limit=20):
    late = steps.run(add_late_kernel, shape(keep.shape), (), (keep, got), limit=limit)
    return swap_split(late, ALONG_X, ALONG_Y)


def plane_layer(
    activations,
    span_order,
    w_query,
    w_key,
    w_value,
    w_out,
    w_gate,
    w_up,
    w_down,
    attn_gain,
    ffn_gain,
    cotangent,
):
    f32 = jnp.float32
    cycles = lax.axis_size("ctx")
    quarters = lax.axis_size("fsdp")
    mine = lax.axis_index("ctx")
    span = activations.shape[2]
    width = activations.shape[3]
    tokens = 2 * span
    length = cycles * tokens
    half = length // 2
    shard = w_query.shape[0]
    four = 4 * DH
    hidden_size = quarters * w_down.shape[0]
    strip = hidden_size // (quarters * cycles)
    part = hidden_size // cycles
    slab = w_out.shape[0] // cycles
    slabs = width // four
    packed = shard + slabs * slab + 32
    owners = mine ^ jnp.array(RELATIVE, jnp.int32)
    away = mine ^ jnp.arange(cycles, dtype=jnp.int32)
    seat = (away & 1) * 4 + (away >> 2) * 2 + ((away >> 1) & 1)
    slot_of = jnp.argsort(span_order).astype(jnp.int32)
    near_slot = 2 * seat[slot_of // 2] + slot_of % 2
    here = mine.reshape(1).astype(jnp.int32)
    core = here & CORE
    stream = activations.reshape(tokens, width)
    grad_rows = cotangent.reshape(tokens, width)

    steps = Steps(core)
    low = jnp.bfloat16

    gains = jnp.pad(jnp.stack([attn_gain, ffn_gain]), ((0, 30), (0, four - shard)))
    window = pltpu.VMEM((shard, 2 * LANES), low)
    first = steps.run(
        pack_kernel,
        shape((packed, four)),
        (here,),
        (gains,),
        pinned=(w_query, w_key, w_value, w_out),
        scratch=(
            window,
            window,
            window,
            pltpu.VMEM((slab, width), low),
            pltpu.SemaphoreType.DMA((4,)),
        ),
        limit=60,
    )
    first = lax.all_gather(first, "fsdp", axis=0)
    own_strips = steps.run(strip_kernel, shape((shard, 2 * part)), (here,), (w_gate, w_up), limit=28)
    gate_up = lax.all_gather(own_strips, "fsdp", axis=0, tiled=True)
    down = lax.dynamic_slice_in_dim(w_down, mine * strip, strip, axis=0)
    down = lax.all_gather(down, "fsdp", axis=0, tiled=True)
    cosine, sine = turn_tables(length)
    streams = gather_spans(
        stream, core, lambda one, two: after(one, two, own_strips, cosine, sine, near_slot, slot_of)
    )
    grads = gather_spans(after(grad_rows, streams[1], streams[2]), core)
    steps.wait(grads[1], grads[2])
    out_part = first[:, shard : shard + slabs * slab].reshape(quarters * slabs * slab, four)
    folded, gains, level, normed1, w_fields, query, key, value, attended = attend(
        steps, near_slot, slot_of, cosine, sine, first, streams, span
    )
    outs = gather_spans(out_part, core, lambda one, two: after(one, two, folded))
    steps.wait(*outs)
    folded = lax.all_to_all(folded, "ctx", 0, 0)
    one_tile = shape((tokens, LANES), f32)
    stream_one, normed2, inverse, heads_low, full_out = steps.run(
        branch_kernel,
        (shape((tokens, width), f32), shape((tokens, width)), one_tile, shape((tokens, width))),
        (owners,),
        (folded, stream, gains),
        far=outs,
        far_outs=(shape((width, width)),),
        scratch=(
            pltpu.VMEM((width, width), low),
            pltpu.VMEM((cycles, *outs[0].shape), low),
            pltpu.SemaphoreType.DMA((cycles,)),
        ),
        limit=60,
        micros=6,
    )
    normed2 = gather_spans(normed2, core)
    def strips(pieces, grad_pieces, *before):
        results = steps.run(
            functools.partial(strips_kernel, len(pieces), bool(before)),
            (shape((part, width), low if before else f32),) + (shape((tokens, width)),) * 8,
            (),
            before,
            far=(*pieces, *grad_pieces),
            pinned=(gate_up, down),
            far_outs=(shape((half, 2 * part)),),
            scratch=(
                pltpu.VMEM((part, width), f32),
                pltpu.VMEM((width, 2 * part), low),
                pltpu.VMEM((part, width), low),
                pltpu.VMEM((half, width), low),
                pltpu.VMEM((half, width), low),
                pltpu.VMEM((half, 2 * part), low),
                pltpu.SemaphoreType.DMA((2 * len(pieces),)),
                pltpu.SemaphoreType.DMA((len(pieces) // 2,)),
                pltpu.SemaphoreType.DMA((2,)),
            ),
                limit=42,
            micros=20,
        )
        return results[0], results[1:5], results[5:9], results[9]

    down_twin, d_normed2_twin, sum_twin, both_twin = strips(normed2[4:], grads[4:])
    heads = gather_spans(
        after(heads_low, normed2[3]), core, lambda one, two: after(one, two, down_twin)
    )
    steps.wait(heads[1], heads[2])
    d_normed2_twin = [swap(block, CORE) for block in d_normed2_twin]
    sum_twin = [swap(block, CORE) for block in sum_twin]
    down_sum, d_normed2_own, sum_own, both_own = strips(normed2[:4], grads[:4], down_twin)
    grad_down = lax.psum_scatter(after(down_sum, heads[3]), "fsdp", scatter_dimension=0, tiled=True)
    send, keep, total = open_scatter(steps, d_normed2_own, d_normed2_twin, core, 60)
    got = swap_split(send, ALONG_Y, ALONG_X)
    steps.wait(heads[3])
    grad_both, grad_ffn = steps.run(
        functools.partial(strip_grad_kernel, cycles),
        (shape((width, 2 * part)), shape((8, width), f32)),
        (),
        (gate_up, gains),
        far=(*normed2,),
        pinned=(both_own, both_twin),
        scratch=(
            pltpu.VMEM((length, width), low),
            pltpu.VMEM((length, 2 * part), low),
            pltpu.SemaphoreType.DMA((cycles + 2,)),
        ),
        limit=60,
        micros=12,
    )
    grad_both = lax.psum_scatter(after(grad_both, got), "fsdp", scatter_dimension=0, tiled=True)
    late_got = turn_scatter(steps, keep, got)
    ffn_send, ffn_keep, ffn_total = open_scatter(steps, sum_own, sum_twin, core)
    d_stream_one, d_heads = steps.run(
        branch_back_kernel,
        (
            shape((tokens, width), f32),
            shape((cycles, 6 * span, LANES)),
        ),
        (),
        (total, got, late_got, grad_rows, stream_one, inverse, gains, full_out),
        limit=28,
        micros=4,
    )
    d_heads = lax.all_to_all(d_heads, "ctx", 0, 0)
    ffn_got = swap_split(after(ffn_send, d_heads), ALONG_Y, ALONG_X)
    grad_downs = gather_direct(after(grad_down, d_heads))
    d_fields, last = attend_back(
        steps,
        near_slot,
        slot_of,
        owners,
        d_heads,
        level,
        (w_fields, gains, grad_ffn),
        cosine,
        sine,
        query,
        key,
        value,
        attended,
        heads,
        normed1,
        packed,
        span,
    )
    last = after(last, ffn_got, *grad_downs[1:4])
    last = lax.psum_scatter(last, "fsdp", scatter_dimension=0, tiled=False)
    steps.wait(ffn_got, *grad_downs[1:4])
    both_pieces = gather_spans(
        after(grad_both, d_fields), core, lambda one, two: after(one, two, last)
    )

    def stream_grad(start):
        return steps.run(
            functools.partial(stream_grad_kernel, start),
            (shape((tokens, width)),) * 4,
            (),
            (d_fields, w_fields),
            micros=2,
        )

    d_normed1_twin = [swap(block, CORE) for block in stream_grad(half)]
    d_normed1_own = stream_grad(0)
    send, keep, total = open_scatter(steps, d_normed1_own, d_normed1_twin, core)
    got = swap_split(send, ALONG_Y, ALONG_X)
    ffn_late_got = turn_scatter(steps, ffn_keep, ffn_got)
    steps.wait(both_pieces[1], both_pieces[2])
    grad_down = steps.run(
        place_down_kernel,
        (),
        (owners,),
        (),
        far=grad_downs,
        far_outs=(shape((hidden_size // quarters, width), f32),),
        scratch=(
            pltpu.VMEM((cycles, strip, width), low),
            pltpu.VMEM((cycles, strip, width), f32),
            pltpu.SemaphoreType.DMA((2, cycles)),
        ),
        limit=60,
        micros=1000,
    )[0]
    steps.wait(last)
    last = gather_direct(last)
    late_got = turn_scatter(steps, keep, got)
    output = steps.run(
        output_kernel,
        shape((tokens, width)),
        (),
        (ffn_total, ffn_got, ffn_late_got, stream_one),
        micros=700,
    )
    wide_strip = shape((shard, hidden_size), f32)
    grad_gate, grad_up = steps.run(
        place_strips_kernel,
        (),
        (owners,),
        (),
        far=both_pieces,
        far_outs=(wide_strip, wide_strip),
        scratch=(
            pltpu.VMEM((cycles, shard, 2 * part), low),
            pltpu.VMEM((cycles, shard, 2 * part), f32),
            pltpu.SemaphoreType.DMA((cycles,)),
            pltpu.SemaphoreType.DMA((cycles, 2 * quarters)),
        ),
        limit=60,
        micros=1000,
    )
    input_grad = steps.run(
        input_back_kernel,
        shape((tokens, width), f32),
        (),
        (total, got, late_got, stream, d_stream_one, gains),
        micros=700,
    )
    narrow_grad = shape((shard, width // 2), f32)
    wide_grad = shape((shard, width), f32)
    grad_gains, grad_query, grad_key, grad_value, grad_out = steps.run(
        place_last_kernel,
        (shape((16, four), f32),),
        (owners,),
        (),
        far=last,
        far_outs=(wide_grad, narrow_grad, narrow_grad, wide_grad),
        scratch=(
            pltpu.VMEM((cycles, packed, four), low),
            pltpu.VMEM((shard, width), f32),
            pltpu.VMEM((shard, width // 2), f32),
            pltpu.VMEM((shard, width // 2), f32),
            pltpu.VMEM((shard, width), f32),
            pltpu.SemaphoreType.DMA((cycles,)),
            pltpu.SemaphoreType.DMA((8,)),
        ),
        limit=60,
    )
    return (
        output.reshape(activations.shape),
        input_grad.reshape(activations.shape),
        grad_query,
        grad_key,
        grad_value,
        grad_out,
        grad_gate,
        grad_up,
        grad_down,
        grad_gains[0],
        grad_gains[8],
    )


def solution(mesh):
    in_specs = (
        P("fsdp", "ctx", None, None),
        P(),
        P("fsdp", None),
        P("fsdp", None),
        P("fsdp", None),
        P("fsdp", None),
        P("fsdp", None),
        P("fsdp", None),
        P("fsdp", None),
        P("fsdp"),
        P("fsdp"),
        P("fsdp", "ctx", None, None),
    )
    out_specs = (
        P("fsdp", "ctx", None, None),
        P("fsdp", "ctx", None, None),
        P("fsdp", None),
        P("fsdp", None),
        P("fsdp", None),
        P("fsdp", None),
        P("fsdp", None),
        P("fsdp", None),
        P("fsdp", None),
        P("fsdp"),
        P("fsdp"),
    )
    cycles = mesh.shape["ctx"]

    def per_device(*arrays):
        heads = arrays[3].shape[1] // DH
        if cycles == len(RELATIVE) == heads and arrays[2].shape == (4 * DH, 2 * heads * DH):
            return plane_layer(*arrays)
        return ring_layer(*arrays)

    return jax.shard_map(
        per_device, mesh=mesh, in_specs=in_specs, out_specs=out_specs, check_vma=False
    )
```

```python
import functools
import math

import jax
import jax.numpy as jnp
from jax import lax
from jax.experimental import pallas as pl
from jax.experimental.pallas import tpu as pltpu
from jax.sharding import PartitionSpec as P

DH = 96


epsilon = 1e-05
rope_base = 100000.0
masked_score = -1e30
LOG2E = math.log2(math.e)


def passed_along(block, axis, distance):
    devices = range(lax.axis_size(axis))
    route = [((i - distance) % len(devices), i) for i in devices]
    return lax.ppermute(block, axis, route)


def rope_tables(places):
    half = DH // 2
    freqs = jnp.exp(-math.log(rope_base) * 2.0 * jnp.arange(half, dtype=jnp.float32) / DH)
    angle = places.astype(jnp.float32)[:, None] * freqs[None, :]
    return (jnp.cos(angle)[:, None, :], jnp.sin(angle)[:, None, :])


def rope_turn(field, cosine, sine):
    half = DH // 2
    first = field[..., :half]
    second = field[..., half:]
    return jnp.concatenate(
        [first * cosine - second * sine, second * cosine + first * sine], axis=-1
    )


def rope_back(field, cosine, sine):
    half = DH // 2
    first = field[..., :half]
    second = field[..., half:]
    return jnp.concatenate(
        [first * cosine + second * sine, second * cosine - first * sine], axis=-1
    )


def norm_back(d_normed, stream, inv_rms, gain):
    scaled = d_normed * gain
    cubed = inv_rms * inv_rms * inv_rms
    return inv_rms * scaled - stream * cubed * jnp.mean(scaled * stream, axis=-1, keepdims=True)


def ring_layer(
    activations,
    span_order,
    w_query,
    w_key,
    w_value,
    w_out,
    w_gate,
    w_up,
    w_down,
    attn_gain,
    ffn_gain,
    cotangent,
):
    cycles = lax.axis_size("ctx")
    mine = lax.axis_index("ctx")
    span = activations.shape[2]
    width = activations.shape[3]
    tokens = 2 * span
    heads = w_query.shape[1] // DH
    kv_heads = w_key.shape[1] // DH
    group = heads // kv_heads
    scale = 1.0 / math.sqrt(DH)
    offsets = jnp.arange(span, dtype=jnp.int32)

    def places_of(owner):
        span_ids = lax.dynamic_slice_in_dim(span_order, 2 * owner, 2)
        return (span_ids[:, None] * span + offsets[None, :]).reshape(tokens)

    query_places = places_of(mine)
    cosine, sine = rope_tables(query_places)
    gathered = (
        lax.all_gather(w_query, "fsdp", axis=0, tiled=True),
        lax.all_gather(w_key, "fsdp", axis=0, tiled=True),
        lax.all_gather(w_value, "fsdp", axis=0, tiled=True),
        lax.all_gather(w_out, "fsdp", axis=0, tiled=True),
        lax.all_gather(w_gate, "fsdp", axis=0, tiled=True),
        lax.all_gather(w_up, "fsdp", axis=0, tiled=True),
        lax.all_gather(w_down, "fsdp", axis=0, tiled=True),
        lax.all_gather(attn_gain, "fsdp", axis=0, tiled=True),
        lax.all_gather(ffn_gain, "fsdp", axis=0, tiled=True),
    )
    (
        full_query,
        full_key,
        full_value,
        full_out,
        full_gate,
        full_up,
        full_down,
        gain_one,
        gain_two,
    ) = gathered
    stream = activations.reshape(tokens, width).astype(jnp.float32)
    inv_one = lax.rsqrt(jnp.mean(stream * stream, axis=-1, keepdims=True) + epsilon)
    normed1 = (stream * inv_one * gain_one).astype(jnp.bfloat16)
    query_raw = jnp.dot(normed1, full_query, preferred_element_type=jnp.float32).reshape(
        tokens, heads, DH
    )
    queries = (
        rope_turn(query_raw, cosine, sine).astype(jnp.bfloat16).reshape(tokens, kv_heads, group, DH)
    )
    key_raw = jnp.dot(normed1, full_key, preferred_element_type=jnp.float32).reshape(
        tokens, kv_heads, DH
    )
    keys = rope_turn(key_raw, cosine, sine).astype(jnp.bfloat16)
    values = (
        jnp.dot(normed1, full_value, preferred_element_type=jnp.float32)
        .astype(jnp.bfloat16)
        .reshape(tokens, kv_heads, DH)
    )

    def scores_with(key_piece, owner):
        scores = (
            jnp.einsum("tjgd,sjd->jgts", queries, key_piece, preferred_element_type=jnp.float32)
            * scale
        )
        counted = places_of(owner)[None, :] <= query_places[:, None]
        return jnp.where(counted, scores, masked_score)

    def absorb(state, key_piece, value_piece, owner):
        running_top, running_total, running_sum = state
        scores = scores_with(key_piece, owner)
        new_top = jnp.maximum(running_top, jnp.max(scores, axis=-1, keepdims=True))
        fading = jnp.exp(running_top - new_top)
        weights = jnp.exp(scores - new_top)
        running_total = fading * running_total + jnp.sum(weights, axis=-1, keepdims=True)
        running_sum = fading * running_sum + jnp.einsum(
            "jgts,sjd->jgtd",
            weights.astype(jnp.bfloat16),
            value_piece,
            preferred_element_type=jnp.float32,
        )
        return (new_top, running_total, running_sum)

    start_state = (
        jnp.full((kv_heads, group, tokens, 1), masked_score, jnp.float32),
        jnp.zeros((kv_heads, group, tokens, 1), jnp.float32),
        jnp.zeros((kv_heads, group, tokens, DH), jnp.float32),
    )
    state = absorb(start_state, keys, values, mine)

    def forward_turn(turn_index, carry):
        state_now, key_piece, value_piece = carry
        key_piece, value_piece = passed_along((key_piece, value_piece), "ctx", 1)
        owner = (mine - turn_index) % cycles
        return (absorb(state_now, key_piece, value_piece, owner), key_piece, value_piece)

    state, _, _ = lax.fori_loop(1, cycles, forward_turn, (state, keys, values))
    running_top, running_total, running_sum = state
    attended = running_sum / running_total
    log_total = running_top + jnp.log(running_total)
    attended_low = (
        jnp.transpose(attended, (2, 0, 1, 3)).reshape(tokens, heads * DH).astype(jnp.bfloat16)
    )
    stream_one = stream + jnp.dot(attended_low, full_out, preferred_element_type=jnp.float32)
    inv_two = lax.rsqrt(jnp.mean(stream_one * stream_one, axis=-1, keepdims=True) + epsilon)
    normed2 = (stream_one * inv_two * gain_two).astype(jnp.bfloat16)
    gate = jnp.dot(normed2, full_gate, preferred_element_type=jnp.float32)
    up_part = jnp.dot(normed2, full_up, preferred_element_type=jnp.float32)
    sigma = jax.nn.sigmoid(gate)
    hidden = (gate * sigma * up_part).astype(jnp.bfloat16)
    stream_two = stream_one + jnp.dot(hidden, full_down, preferred_element_type=jnp.float32)
    output = stream_two.astype(jnp.bfloat16).reshape(activations.shape)
    back_weights = (
        lax.all_gather(w_query, "fsdp", axis=0, tiled=True),
        lax.all_gather(w_key, "fsdp", axis=0, tiled=True),
        lax.all_gather(w_value, "fsdp", axis=0, tiled=True),
        lax.all_gather(w_out, "fsdp", axis=0, tiled=True),
        lax.all_gather(w_gate, "fsdp", axis=0, tiled=True),
        lax.all_gather(w_up, "fsdp", axis=0, tiled=True),
        lax.all_gather(w_down, "fsdp", axis=0, tiled=True),
        lax.all_gather(attn_gain, "fsdp", axis=0, tiled=True),
        lax.all_gather(ffn_gain, "fsdp", axis=0, tiled=True),
    )
    (
        back_query,
        back_key,
        back_value,
        back_out,
        back_gate,
        back_up,
        back_down,
        back_gain_one,
        back_gain_two,
    ) = back_weights
    grad_rows = cotangent.reshape(tokens, width)
    grad_stream = grad_rows.astype(jnp.float32)
    grad_down = jnp.einsum("tf,td->fd", hidden, grad_rows, preferred_element_type=jnp.float32)
    d_hidden = jnp.einsum("td,fd->tf", grad_rows, back_down, preferred_element_type=jnp.float32)
    d_gate = (d_hidden * up_part * sigma * (1.0 + gate * (1.0 - sigma))).astype(jnp.bfloat16)
    d_up = (d_hidden * gate * sigma).astype(jnp.bfloat16)
    grad_gate = jnp.einsum("td,tf->df", normed2, d_gate, preferred_element_type=jnp.float32)
    grad_up = jnp.einsum("td,tf->df", normed2, d_up, preferred_element_type=jnp.float32)
    d_normed2 = jnp.einsum(
        "tf,df->td", d_gate, back_gate, preferred_element_type=jnp.float32
    ) + jnp.einsum("tf,df->td", d_up, back_up, preferred_element_type=jnp.float32)
    grad_ffn_gain = jnp.sum(d_normed2 * stream_one * inv_two, axis=0)
    d_stream_one = grad_stream + norm_back(d_normed2, stream_one, inv_two, back_gain_two)
    d_branch = d_stream_one.astype(jnp.bfloat16)
    grad_out = jnp.einsum("tk,td->kd", attended_low, d_branch, preferred_element_type=jnp.float32)
    d_attended = jnp.einsum(
        "td,kd->tk", d_branch, back_out, preferred_element_type=jnp.float32
    ).astype(jnp.bfloat16)
    d_heads = jnp.transpose(d_attended.reshape(tokens, kv_heads, group, DH), (1, 2, 0, 3))
    delta = jnp.sum(d_heads.astype(jnp.float32) * attended, axis=-1, keepdims=True)

    def back_step(d_queries, d_keys, d_values, key_piece, value_piece, owner):
        scores = scores_with(key_piece, owner)
        probs = jnp.exp(scores - log_total)
        d_values = d_values + jnp.einsum(
            "jgts,jgtd->sjd",
            probs.astype(jnp.bfloat16),
            d_heads,
            preferred_element_type=jnp.float32,
        )
        d_probs = jnp.einsum(
            "jgtd,sjd->jgts", d_heads, value_piece, preferred_element_type=jnp.float32
        )
        d_scores = (probs * (d_probs - delta)).astype(jnp.bfloat16)
        d_queries = (
            d_queries
            + jnp.einsum("jgts,sjd->jgtd", d_scores, key_piece, preferred_element_type=jnp.float32)
            * scale
        )
        d_keys = (
            d_keys
            + jnp.einsum("jgts,tjgd->sjd", d_scores, queries, preferred_element_type=jnp.float32)
            * scale
        )
        return (d_queries, d_keys, d_values)

    def pass_grads(d_keys, d_values):
        return (
            passed_along(d_keys.astype(jnp.bfloat16), "ctx", 1).astype(d_keys.dtype),
            passed_along(d_values.astype(jnp.bfloat16), "ctx", 1).astype(d_values.dtype),
        )

    zero_queries = jnp.zeros((kv_heads, group, tokens, DH), jnp.float32)
    zero_keys = jnp.zeros((tokens, kv_heads, DH), jnp.float32)
    d_queries, d_keys, d_values = back_step(zero_queries, zero_keys, zero_keys, keys, values, mine)

    def backward_turn(turn_index, carry):
        d_queries_now, d_keys_now, d_values_now, key_piece, value_piece = carry
        key_piece, value_piece = passed_along((key_piece, value_piece), "ctx", 1)
        d_keys_now, d_values_now = pass_grads(d_keys_now, d_values_now)
        owner = (mine - turn_index) % cycles
        d_queries_now, d_keys_now, d_values_now = back_step(
            d_queries_now, d_keys_now, d_values_now, key_piece, value_piece, owner
        )
        return (d_queries_now, d_keys_now, d_values_now, key_piece, value_piece)

    d_queries, d_keys, d_values, _, _ = lax.fori_loop(
        1, cycles, backward_turn, (d_queries, d_keys, d_values, keys, values)
    )
    d_keys, d_values = pass_grads(d_keys, d_values)
    d_query_rows = jnp.transpose(d_queries, (2, 0, 1, 3)).reshape(tokens, heads, DH)
    d_query = rope_back(d_query_rows, cosine, sine).astype(jnp.bfloat16).reshape(tokens, heads * DH)
    d_key = rope_back(d_keys, cosine, sine).astype(jnp.bfloat16).reshape(tokens, kv_heads * DH)
    d_value = d_values.astype(jnp.bfloat16).reshape(tokens, kv_heads * DH)
    grad_query = jnp.einsum("td,tk->dk", normed1, d_query, preferred_element_type=jnp.float32)
    grad_key = jnp.einsum("td,tk->dk", normed1, d_key, preferred_element_type=jnp.float32)
    grad_value = jnp.einsum("td,tk->dk", normed1, d_value, preferred_element_type=jnp.float32)
    d_normed1 = (
        jnp.einsum("tk,dk->td", d_query, back_query, preferred_element_type=jnp.float32)
        + jnp.einsum("tk,dk->td", d_key, back_key, preferred_element_type=jnp.float32)
        + jnp.einsum("tk,dk->td", d_value, back_value, preferred_element_type=jnp.float32)
    )
    grad_attn_gain = jnp.sum(d_normed1 * stream * inv_one, axis=0)
    input_grad = (d_stream_one + norm_back(d_normed1, stream, inv_one, back_gain_one)).reshape(
        activations.shape
    )
    shares = (
        lax.psum_scatter(
            grad_query.astype(jnp.bfloat16), "fsdp", scatter_dimension=0, tiled=True
        ).astype(jnp.float32),
        lax.psum_scatter(
            grad_key.astype(jnp.bfloat16), "fsdp", scatter_dimension=0, tiled=True
        ).astype(jnp.float32),
        lax.psum_scatter(
            grad_value.astype(jnp.bfloat16), "fsdp", scatter_dimension=0, tiled=True
        ).astype(jnp.float32),
        lax.psum_scatter(
            grad_out.astype(jnp.bfloat16), "fsdp", scatter_dimension=0, tiled=True
        ).astype(jnp.float32),
        lax.psum_scatter(
            grad_gate.astype(jnp.bfloat16), "fsdp", scatter_dimension=0, tiled=True
        ).astype(jnp.float32),
        lax.psum_scatter(
            grad_up.astype(jnp.bfloat16), "fsdp", scatter_dimension=0, tiled=True
        ).astype(jnp.float32),
        lax.psum_scatter(
            grad_down.astype(jnp.bfloat16), "fsdp", scatter_dimension=0, tiled=True
        ).astype(jnp.float32),
        lax.psum_scatter(
            grad_attn_gain.astype(jnp.bfloat16), "fsdp", scatter_dimension=0, tiled=True
        ).astype(jnp.float32),
        lax.psum_scatter(
            grad_ffn_gain.astype(jnp.bfloat16), "fsdp", scatter_dimension=0, tiled=True
        ).astype(jnp.float32),
    )
    shares = (
        lax.psum(shares[0].astype(jnp.bfloat16), "ctx").astype(jnp.float32),
        lax.psum(shares[1].astype(jnp.bfloat16), "ctx").astype(jnp.float32),
        lax.psum(shares[2].astype(jnp.bfloat16), "ctx").astype(jnp.float32),
        lax.psum(shares[3].astype(jnp.bfloat16), "ctx").astype(jnp.float32),
        lax.psum(shares[4].astype(jnp.bfloat16), "ctx").astype(jnp.float32),
        lax.psum(shares[5].astype(jnp.bfloat16), "ctx").astype(jnp.float32),
        lax.psum(shares[6].astype(jnp.bfloat16), "ctx").astype(jnp.float32),
        lax.psum(shares[7].astype(jnp.bfloat16), "ctx").astype(jnp.float32),
        lax.psum(shares[8].astype(jnp.bfloat16), "ctx").astype(jnp.float32),
    )
    return (
        output,
        input_grad,
        shares[0],
        shares[1],
        shares[2],
        shares[3],
        shares[4],
        shares[5],
        shares[6],
        shares[7],
        shares[8],
    )


LANES = 128
CORE, ALONG_X, ALONG_Y = 1, 2, 4
RELATIVE = (0, 2, 4, 6, 1, 3, 5, 7)
MIB = 2**20
COST = 10**6


def lane_dot(left, right):
    return lax.dot_general(left, right, (((1,), (1,)), ((), ())), preferred_element_type=jnp.float32)


def plain_dot(left, right):
    return lax.dot_general(left, right, (((1,), (0,)), ((), ())), preferred_element_type=jnp.float32)


def row_dot(left, right):
    return lax.dot_general(left, right, (((0,), (0,)), ((), ())), preferred_element_type=jnp.float32)


def rows_at(index, size):
    return pl.ds(pl.multiple_of(index * size, size), size)


def wide(value):
    return value.astype(jnp.float32)


def narrow(value):
    return value.astype(jnp.bfloat16)


def lanes_of(rows):
    return lax.broadcasted_iota(jnp.int32, (rows, LANES), 1)


def shape(dims, kind=jnp.bfloat16):
    return jax.ShapeDtypeStruct(dims, kind)


def after(value, *others):
    return lax.optimization_barrier((value, *others))[0]


class Steps:

    def __init__(self, ticket):
        self.ticket = ticket
        self.pending = []

    def wait(self, *values):
        self.pending.extend(values)

    def run(
        self,
        body,
        outs,
        small,
        arrays,
        far=(),
        pinned=(),
        far_outs=(),
        scratch=(),
        limit=20,
        micros=2,
    ):
        near = pl.BlockSpec(memory_space=pltpu.VMEM)
        scalars = pl.BlockSpec(memory_space=pltpu.SMEM)
        away = pl.BlockSpec(memory_space=pl.ANY)
        stored = pl.BlockSpec(memory_space=pltpu.HBM)
        single = not isinstance(outs, tuple)
        out_shapes = ((outs,) if single else outs) + tuple(far_outs)
        out_specs = [near] * (len(out_shapes) - len(far_outs)) + [stored] * len(far_outs)
        ticket = after(self.ticket, *self.pending) if self.pending else self.ticket
        results = pl.pallas_call(
            lambda _, *refs: body(*refs),
            out_shape=out_shapes,
            in_specs=[scalars] * (1 + len(small))
            + [near] * len(arrays)
            + [away] * len(far)
            + [stored] * len(pinned),
            out_specs=out_specs,
            scratch_shapes=list(scratch),
            compiler_params=pltpu.CompilerParams(vmem_limit_bytes=limit * MIB),
            cost_estimate=pl.CostEstimate(
                flops=micros * COST, bytes_accessed=0, transcendentals=0
            ),
        )(ticket, *small, *arrays, *far, *pinned)
        self.pending = [results[-1]]
        return results[0] if single and not far_outs else results


def window_of(weight, start):
    base = jnp.minimum(start // LANES * LANES, weight.shape[1] - 2 * LANES)
    return weight.at[:, pl.ds(pl.multiple_of(base, LANES), 2 * LANES)], start - base


def drawn(window_ref, shift):
    size = 2 * LANES
    return pltpu.roll(wide(window_ref[...]), (size - shift) % size, 1)


def join_fields(one, two, three, four):
    lane = lanes_of(one.shape[0])
    two = pltpu.roll(two, 96, 1)
    three = pltpu.roll(three, 64, 1)
    four = pltpu.roll(four, 32, 1)
    return jnp.concatenate(
        [
            jnp.where(lane < 96, one, two),
            jnp.where(lane < 64, two, three),
            jnp.where(lane < 32, three, four),
        ],
        axis=1,
    )


def part_fields(block):
    lane = lanes_of(block.shape[0])
    one, two, three = (block[:, start : start + LANES] for start in (0, LANES, 2 * LANES))
    fields = (
        one,
        jnp.where(lane < 32, pltpu.roll(one, 32, 1), pltpu.roll(two, 32, 1)),
        jnp.where(lane < 64, pltpu.roll(two, 64, 1), pltpu.roll(three, 64, 1)),
        pltpu.roll(three, 96, 1),
    )
    return [jnp.where(lane < DH, field, 0.0) for field in fields]


def pack_kernel(
    mine_ref,
    gain_ref,
    query_in,
    key_in,
    value_in,
    out_in,
    first_ref,
    query_ref,
    key_ref,
    value_ref,
    out_ref,
    done,
):
    mine = mine_ref[0]
    shard = query_ref.shape[0]
    four = 4 * DH
    slab = out_ref.shape[0]
    slabs = out_ref.shape[1] // four
    query_window, query_shift = window_of(query_in, mine * 2 * DH)
    key_window, shift = window_of(key_in, mine * DH)
    value_window, _ = window_of(value_in, mine * DH)
    copies = [
        fetch(source, target, done.at[index])
        for index, (source, target) in enumerate(
            (
                (query_window, query_ref),
                (key_window, key_ref),
                (value_window, value_ref),
                (out_in.at[rows_at(mine, slab), :], out_ref),
            )
        )
    ]
    for copy in copies:
        copy.wait()
    query = drawn(query_ref, query_shift)
    key = pltpu.roll(drawn(key_ref, shift)[:, :LANES], 64, 1)
    value = pltpu.roll(drawn(value_ref, shift)[:, :LANES], 32, 1)
    lane = lanes_of(shard)
    first_ref[:shard, :LANES] = narrow(query[:, :LANES])
    first_ref[:shard, LANES : 2 * LANES] = narrow(jnp.where(lane < 64, query[:, LANES:], key))
    first_ref[:shard, 2 * LANES :] = narrow(jnp.where(lane < 32, key, value))
    for index in range(slabs):
        here = shard + index * slab
        first_ref[here : here + slab, :] = out_ref[:, index * four : (index + 1) * four]
    first_ref[shard + slabs * slab :, :] = gain_ref[...]


def strip_kernel(mine_ref, gate_ref, up_ref, both_ref):
    quarters = both_ref.shape[1] // (2 * LANES)
    for index in range(quarters):
        place = rows_at(index * 8 + mine_ref[0], LANES)
        both_ref[:, index * LANES : (index + 1) * LANES] = gate_ref[:, place]
        both_ref[:, (quarters + index) * LANES : (quarters + index + 1) * LANES] = up_ref[:, place]


def fold(block):
    rows = block.shape[0]
    tail = block[:, LANES:]
    lower = jnp.where(lanes_of(rows // 2) < 64, tail[: rows // 2], pltpu.roll(tail[rows // 2 :], 64, 1))
    return jnp.concatenate([block[:, :LANES], lower], axis=0)


def unfold(block):
    rows = block.shape[0] // 3 * 2
    half = rows // 2
    tail = block[rows:]
    keep = lanes_of(half) < 64
    tail = jnp.concatenate(
        [jnp.where(keep, tail, 0.0), jnp.where(keep, pltpu.roll(tail, 64, 1), 0.0)], axis=0
    )
    return jnp.concatenate([block[:rows], tail], axis=1)


def branch_kernel(owner_ref, folded_ref, stream_ref, gain_ref, *refs):
    pieces, refs = refs[:8], refs[8:]
    one_ref, normed_ref, inverse_ref, heads_ref, full_out, full_ref, piece_ref, done = refs
    copies = [fetch(piece, piece_ref.at[i], done.at[i]) for i, piece in enumerate(pieces)]
    width = full_ref.shape[1]
    slab = width // 32
    size = 2 * DH
    four = pieces[0].shape[1]
    gap = jnp.zeros((folded_ref.shape[1] // 3 * 2, LANES), jnp.float32)
    for index in range(0, folded_ref.shape[0], 2):
        one = unfold(wide(folded_ref[index]))
        two = unfold(wide(folded_ref[index + 1]))
        both = jnp.concatenate([one, gap], axis=1) + pltpu.roll(
            jnp.concatenate([two, gap], axis=1), size, 1
        )
        heads_ref[:, index * size : (index + 2) * size] = narrow(both)
    for index, copy in enumerate(copies):
        copy.wait()
        for quarter in range(4):
            row = pl.multiple_of(quarter * 8 * slab + owner_ref[index] * slab, 16)
            for part in range(width // four):
                start = (quarter * (width // four) + part) * slab
                full_ref[pl.ds(row, slab), part * four : (part + 1) * four] = piece_ref[
                    index, start : start + slab, :
                ]
    copy = fetch(full_ref, full_out, done.at[0])
    total = wide(stream_ref[...]) + plain_dot(heads_ref[...], full_ref[...])
    one_ref[...] = total
    inverse = lax.rsqrt(jnp.mean(total * total, axis=1, keepdims=True) + epsilon)
    normed_ref[...] = narrow(total * inverse * gain_ref[8:9])
    inverse_ref[...] = jnp.broadcast_to(inverse, inverse_ref.shape)
    copy.wait()


def strips_kernel(count, carry, *refs):
    before, refs = refs[: int(carry)], refs[int(carry) :]
    normed_in, grad_in, refs = refs[:count], refs[count : 2 * count], refs[2 * count :]
    (gate_up_in, down_in), refs = refs[:2], refs[2:]
    grad_out, stream_refs, refs = refs[0], refs[1 : 1 + count], refs[1 + count :]
    sum_ref, both_out, *refs = refs
    down_grad, gate_up_ref, down_ref, normed_ref, grad_ref, both_ref, done, out_done, weight_done = refs
    weights = [
        fetch(gate_up_in, gate_up_ref, weight_done.at[0]),
        fetch(down_in, down_ref, weight_done.at[1]),
    ]
    part = down_ref.shape[0]
    rows = normed_in[0].shape[0]
    size = 2 * rows
    copies = [
        (
            fetch(normed_in[index], normed_ref.at[pl.ds(index * rows, rows), :], done.at[index]),
            fetch(grad_in[index], grad_ref.at[pl.ds(index * rows, rows), :], done.at[count + index]),
        )
        for index in range(count)
    ]
    outs = []
    for copy in weights:
        copy.wait()
    for step in range(count // 2):
        for index in (2 * step, 2 * step + 1):
            copies[index][0].wait()
            copies[index][1].wait()
        here = slice(step * size, (step + 1) * size)
        normed = normed_ref[here, :]
        grad = grad_ref[here, :]
        gate = plain_dot(normed, gate_up_ref[:, :part])
        up = plain_dot(normed, gate_up_ref[:, part:])
        sigma = jax.nn.sigmoid(gate)
        turned = gate * sigma
        hidden = narrow(turned * up)
        d_hidden = lane_dot(grad, down_ref[...])
        d_gate = narrow(d_hidden * up * sigma * (1.0 + gate * (1.0 - sigma)))
        d_up = narrow(d_hidden * turned)
        both_ref[here, :part] = d_gate
        both_ref[here, part:] = d_up
        there = pl.ds(step * size, size)
        outs.append(fetch(both_ref.at[there, :], both_out.at[there, :], out_done.at[step]))
        d_normed = narrow(
            lane_dot(d_gate, gate_up_ref[:, :part]) + lane_dot(d_up, gate_up_ref[:, part:])
        )
        sum_ref[here, :] = narrow(plain_dot(hidden, down_ref[...]))
        for index in range(2):
            stream_refs[2 * step + index][...] = d_normed[index * rows : (index + 1) * rows]
        product = row_dot(hidden, grad)
        if step == 0:
            down_grad[...] = product + before[0][...] if carry else product
        elif step < count // 2 - 1:
            down_grad[...] += product
        else:
            grad_out[...] = (down_grad[...] + product).astype(grad_out.dtype)
    for copy in outs:
        copy.wait()


def strip_grad_kernel(count, *refs):
    weight_ref, gain_ref, refs = refs[0], refs[1], refs[2:]
    normed_in, (own_in, twin_in), refs = refs[:count], refs[count : count + 2], refs[count + 2 :]
    out_ref, row_ref, normed_ref, both_ref, done = refs
    size = 2 * LANES
    rows = normed_in[0].shape[0]
    half = own_in.shape[0]
    copies = [
        fetch(piece, normed_ref.at[pl.ds(index * rows, rows), :], done.at[index])
        for index, piece in enumerate(normed_in)
    ]
    copies.append(fetch(own_in, both_ref.at[pl.ds(0, half), :], done.at[count]))
    copies.append(fetch(twin_in, both_ref.at[pl.ds(half, half), :], done.at[count + 1]))
    for copy in copies:
        copy.wait()
    ones = jnp.ones((8, out_ref.shape[1]), jnp.bfloat16)

    def one(index, _):
        columns = rows_at(index, size)
        total = row_dot(normed_ref[:, columns], both_ref[...])
        out_ref[columns, :] = narrow(total)
        share = narrow(total * wide(weight_ref[columns, :]))
        row_ref[:, columns] = lane_dot(ones, share) / gain_ref[8:, columns]
        return 0

    lax.fori_loop(0, out_ref.shape[0] // size, one, 0)


def add_twin_kernel(core_ref, *refs):
    (*refs, send_ref, keep_ref, self_ref) = refs
    rows = keep_ref.shape[0]
    count = len(refs) // 2
    core = core_ref[0]

    def total(index):
        if count == 4:
            return wide(refs[index][...]) + wide(refs[4 + index][...])
        here = slice(index * rows, (index + 1) * rows)
        return wide(refs[0][here, :]) + wide(refs[1][here, :])

    self_ref[...] = total(0)
    send_ref[:rows, :] = narrow(total(3))
    along_x = total(1)
    along_y = total(2)

    @pl.when(core == 0)
    def _():
        send_ref[rows:, :] = narrow(along_y)
        keep_ref[...] = along_x

    @pl.when(core == 1)
    def _():
        send_ref[rows:, :] = narrow(along_x)
        keep_ref[...] = along_y


def add_late_kernel(keep_in, got_in, late_ref, keep_ref, got_ref, done):
    rows = keep_ref.shape[0]
    copies = (
        fetch(keep_in, keep_ref, done.at[0]),
        fetch(got_in.at[pl.ds(0, rows), :], got_ref, done.at[1]),
    )
    for copy in copies:
        copy.wait()
    late_ref[...] = narrow(keep_ref[...] + wide(got_ref[...]))


def summed(self_ref, got_ref, late_ref):
    rows = self_ref.shape[0]
    return self_ref[...] + wide(got_ref[rows:, :]) + wide(late_ref[...])


def norm_down(d_normed, stream, inverse, gain):
    scaled = d_normed * gain
    cubed = inverse * inverse * inverse
    return inverse * scaled - stream * cubed * jnp.mean(scaled * stream, axis=1, keepdims=True)


def branch_back_kernel(
    self_ref,
    got_ref,
    late_ref,
    grad_ref,
    one_ref,
    inverse_ref,
    gain_ref,
    full_ref,
    stream_out,
    heads_out,
):
    d_normed = summed(self_ref, got_ref, late_ref)
    d_stream = wide(grad_ref[...]) + norm_down(
        d_normed, one_ref[...], inverse_ref[:, :1], gain_ref[8:9]
    )
    stream_out[...] = d_stream
    d_branch = narrow(d_stream)
    rows = d_branch.shape[0]
    size = 2 * DH
    gap = jnp.zeros((rows, 2 * LANES - size), jnp.float32)
    keep = lanes_of(rows) < size - LANES
    tall = heads_out.shape[1] // 2
    for index in range(heads_out.shape[0]):
        heads = lane_dot(d_branch, full_ref[index * size : (index + 1) * size, :])
        heads_out[index, :tall, :] = narrow(fold(jnp.concatenate([heads, gap], axis=1)))
        start = index * size // LANES * LANES
        columns = wide(d_branch[:, start : start + 2 * LANES])
        if index % 2:
            columns = pltpu.roll(columns, 2 * LANES - 64, 1)
        columns = jnp.concatenate(
            [columns[:, :LANES], jnp.where(keep, columns[:, LANES:], 0.0)], axis=1
        )
        heads_out[index, tall:, :] = narrow(fold(columns))


def stream_grad_kernel(start, fields_ref, weight_ref, out_ref):
    rows = out_ref.shape[0]
    size = rows // 2
    for step in range(2):
        here = slice(step * size, (step + 1) * size)
        there = slice(start + step * size, start + (step + 1) * size)
        out_ref[here, :] = narrow(lane_dot(fields_ref[there, :], weight_ref[...]))


def place_strips(owner_ref, copies, low_ref, wide_ref, gate_out, up_out, done):
    quarters = low_ref.shape[2] // (2 * LANES)
    outs = []
    for index, copy in enumerate(copies):
        copy.wait()
        wide_ref[index] = wide(low_ref[index])
        for part in range(2 * quarters):
            there = rows_at(part % quarters * 8 + owner_ref[index], LANES)
            target = gate_out if part < quarters else up_out
            outs.append(
                fetch(
                    wide_ref.at[index, :, pl.ds(part * LANES, LANES)],
                    target.at[:, there],
                    done.at[index, part],
                )
            )
    return outs


def place_down_kernel(owner_ref, *refs):
    pieces, (down_out, low_ref, wide_ref, done) = refs[:-4], refs[-4:]
    copies = [fetch(piece, low_ref.at[i], done.at[0, i]) for i, piece in enumerate(pieces)]
    outs = []
    for index, copy in enumerate(copies):
        copy.wait()
        wide_ref[index] = wide(low_ref[index])
        there = rows_at(owner_ref[index], wide_ref.shape[1])
        outs.append(fetch(wide_ref.at[index], down_out.at[there, :], done.at[1, index]))
    for copy in outs:
        copy.wait()


def place_last(copies, low_ref, refs, outs, gain_ref, out_done):
    query_ref, key_ref, value_ref, out_ref = refs
    shard = query_ref.shape[0]
    half = shard // 2
    end = shard + half
    for copy in copies:
        copy.wait()
    full = lanes_of(shard) < 64
    keep = lanes_of(half) < 64
    gains = jnp.zeros(gain_ref.shape, jnp.float32)
    targets = []
    for quad in range(2):
        keys, values = [], []
        for pair in (2 * quad, 2 * quad + 1):
            columns = slice(pair * 4 * DH, (pair + 1) * 4 * DH)
            tiles = []
            for index in (2 * pair, 2 * pair + 1):
                block = wide(low_ref[index, :shard, :])
                one, two, key, value = part_fields(block)
                keys.append(key)
                values.append(value)
                tiles.append((block[:, :LANES], block[:, LANES : 2 * LANES]))
                gains = gains + wide(low_ref[index, end : end + 16, :])
            (one, two), (three, four) = tiles
            three, four = pltpu.roll(three, 64, 1), pltpu.roll(four, 64, 1)
            query_ref[:, columns] = jnp.concatenate(
                [one, jnp.where(full, two, three), jnp.where(full, three, four)], axis=1
            )
            for part in range(2):
                tiles = []
                for index in (2 * pair, 2 * pair + 1):
                    block = wide(low_ref[index, shard:end, :])
                    one, two, three = (
                        block[:, start : start + LANES] for start in (0, LANES, 2 * LANES)
                    )
                    if part:
                        two, three = pltpu.roll(two, 64, 1), pltpu.roll(three, 64, 1)
                        one, two = jnp.where(keep, two, three), three
                    tiles.append((one, two))
                (one, two), (three, four) = tiles
                three, four = pltpu.roll(three, 64, 1), pltpu.roll(four, 64, 1)
                out_ref[part * half : (part + 1) * half, columns] = jnp.concatenate(
                    [one, jnp.where(keep, two, three), jnp.where(keep, three, four)], axis=1
                )
        columns = slice(quad * 4 * DH, (quad + 1) * 4 * DH)
        key_ref[:, columns] = join_fields(*keys)
        value_ref[:, columns] = join_fields(*values)
        wide_columns = pl.ds(quad * 8 * DH, 8 * DH)
        some_columns = pl.ds(quad * 4 * DH, 4 * DH)
        for index, (ref, out, here) in enumerate(
            (
                (query_ref, outs[0], wide_columns),
                (key_ref, outs[1], some_columns),
                (value_ref, outs[2], some_columns),
                (out_ref, outs[3], wide_columns),
            )
        ):
            targets.append(fetch(ref.at[:, here], out.at[:, here], out_done.at[4 * quad + index]))
    gain_ref[...] = gains
    return targets


def finish_kernel(
    owner_ref,
    ffn_self,
    ffn_got,
    ffn_late,
    one_ref,
    self_ref,
    got_ref,
    late_ref,
    stream_ref,
    back_ref,
    norm_ref,
    *refs,
):
    strip_pieces, last_pieces, gain_ref, refs = refs[:8], refs[8:16], refs[16], refs[17:]
    (layer_out, input_out, gate_out, up_out, *last_outs), refs = refs[:8], refs[8:]
    layer_ref, input_ref, strip_low, strip_wide, last_low, *refs = refs
    last_refs, (done, out_done, strip_done, last_done) = refs[:4], refs[4:]
    strips = [
        fetch(piece, strip_low.at[index], done.at[index]) for index, piece in enumerate(strip_pieces)
    ]
    lasts = [
        fetch(piece, last_low.at[owner_ref[index]], done.at[8 + index])
        for index, piece in enumerate(last_pieces)
    ]
    layer_ref[...] = narrow(one_ref[...] + summed(ffn_self, ffn_got, ffn_late))
    outs = [fetch(layer_ref, layer_out, out_done.at[0])]
    d_normed = summed(self_ref, got_ref, late_ref)
    stream = wide(stream_ref[...])
    inverse = lax.rsqrt(jnp.mean(stream * stream, axis=1, keepdims=True) + epsilon)
    input_ref[...] = back_ref[...] + norm_down(d_normed, stream, inverse, norm_ref[:1])
    outs.append(fetch(input_ref, input_out, out_done.at[1]))
    outs += place_strips(owner_ref, strips, strip_low, strip_wide, gate_out, up_out, strip_done)
    outs += place_last(lasts, last_low, last_refs, last_outs, gain_ref, last_done)
    for copy in outs:
        copy.wait()


def swapped(field):
    half = DH // 2
    lane = lanes_of(field.shape[0])
    return jnp.where(lane < half, pltpu.roll(field, LANES - half, 1), pltpu.roll(field, half, 1))


def rows_of(weights, field):
    return lax.dot_general(
        weights,
        field,
        (((1,), (1,)), ((), ())),
        precision=lax.Precision.HIGHEST,
        preferred_element_type=jnp.float32,
    )


def fetch(source, target, done):
    copy = pltpu.make_async_copy(source, target, done)
    copy.start()
    return copy


def attend_kernel(
    span,
    near_ref,
    slot_ref,
    cos_ref,
    sin_ref,
    *refs,
):
    (*piece_refs, first_ref), refs = refs[:9], refs[9:]
    (low_ref, gain_ref, level_ref), refs = refs[:3], refs[3:]
    (normed_out, weight_out, query_out, key_out, value_out, mixed_out), refs = refs[:6], refs[6:]
    stream_ref, weight_ref, gains_ref, raw_ref, query_ref, key_ref, value_ref, mixed_ref = refs[:8]
    score_ref, top_ref, sum_ref, in_done, out_done = refs[8:]
    spans = near_ref.shape[0]
    block = 2 * span
    pair = 2 * block
    turns = spans // 2
    quarters, packed, four = first_ref.shape
    shard = weight_ref.shape[0] // quarters
    factor = LOG2E / math.sqrt(DH)

    gain_copies = [
        fetch(
            first_ref.at[quarter, pl.ds(packed - 32, 32), :],
            gains_ref.at[pl.ds(quarter * 32, 32), :],
            in_done.at[turns + quarter],
        )
        for quarter in range(quarters)
    ]
    weight_copies = [
        fetch(
            first_ref.at[quarter, pl.ds(0, shard), :],
            weight_ref.at[pl.ds(quarter * shard, shard), :],
            in_done.at[turns + quarters + quarter],
        )
        for quarter in range(quarters)
    ]
    copies = [
        fetch(piece, stream_ref.at[pl.ds(index * block, block), :], in_done.at[index])
        for index, piece in enumerate(piece_refs)
    ]
    for copy in gain_copies:
        copy.wait()
    for quarter in range(quarters):
        rows = wide(gains_ref[quarter * 32 : quarter * 32 + 16, :])
        here = slice(quarter * shard, (quarter + 1) * shard)
        gain_ref[:8, here] = jnp.broadcast_to(rows[:1, :shard], (8, shard))
        gain_ref[8:, here] = jnp.broadcast_to(rows[1:2, :shard], (8, shard))
    for copy in weight_copies:
        copy.wait()
    out_copies = [fetch(weight_ref, weight_out, out_done.at[0])]
    gain = gain_ref[:1, :]

    def norm(start):
        here = pl.ds(start, span)
        stream = wide(stream_ref[here, :])
        inverse = lax.rsqrt(jnp.mean(stream * stream, axis=1, keepdims=True) + epsilon)
        stream_ref[here, :] = narrow(stream * inverse * gain)

    for step in range(turns // 2):
        copies[2 * step].wait()
        copies[2 * step + 1].wait()
        here = pl.ds(step * pair, pair)
        for part in range(4):
            norm(step * pair + part * span)
        raw_ref[here, :] = plain_dot(stream_ref[here, :], weight_ref[...])
        out_copies.append(
            fetch(stream_ref.at[here, :], normed_out.at[here, :], out_done.at[1 + step])
        )

    lane = lanes_of(span)

    def place(index, _):
        raw = raw_ref[rows_at(near_ref[index], span), :]
        cosine = cos_ref[rows_at(index, span), :]
        sine = sin_ref[rows_at(index, span), :]
        one, two, three, four = part_fields(raw)

        def turned(field):
            return narrow(field * cosine + swapped(field) * sine)

        first = (index // 2) * 4 + index % 2
        query_ref[rows_at(first, span), :] = turned(one)
        query_ref[rows_at(first + 2, span), :] = turned(two)
        key_ref[rows_at(index, span), :] = turned(three)
        value_ref[rows_at(index, span), :] = narrow(jnp.where(lane == DH, 1.0, four))
        return 0

    lax.fori_loop(0, spans, place, 0, unroll=2)
    next_done = 1 + turns // 2
    for source, target in ((query_ref, query_out), (key_ref, key_out), (value_ref, value_out)):
        out_copies.append(fetch(source, target, out_done.at[next_done]))
        next_done += 1

    wide_lane = lanes_of(pair)
    picked = (lanes_of(8) == 0).astype(jnp.float32)

    def store(index, both, rest):
        slot = slot_ref[index]
        low_ref[slot // 2, rows_at(slot % 2, span), :] = narrow(both)
        tail = narrow(rest)
        turned = narrow(pltpu.roll(rest, 64, 1))

        @pl.when(slot % 2 == 0)
        def _():
            low_ref[slot // 2, 2 * span :, :64] = tail[:, :64]

        @pl.when(slot % 2 == 1)
        def _():
            low_ref[slot // 2, 2 * span :, 64:] = turned[:, 64:]

    def widest(top, scores):
        for start in range(0, block, LANES):
            top = jnp.maximum(top, scores[:, start : start + LANES])
        return top

    def score(turn, step):
        scores = lane_dot(query_ref[rows_at(turn, pair), :], key_ref[rows_at(step, block), :])
        score_ref[turn % 2, :, rows_at(step, block)] = scores
        top_ref[...] = widest(top_ref[...], scores)

    def edge(turn):
        row = lax.broadcasted_iota(jnp.int32, (pair, block), 0) % block
        column = lax.broadcasted_iota(jnp.int32, (pair, block), 1)
        scores = lane_dot(query_ref[rows_at(turn, pair), :], key_ref[rows_at(turn, block), :])
        scores = jnp.where(column <= row, scores, masked_score)
        score_ref[turn % 2, :, rows_at(turn, block)] = scores
        top = jnp.max(widest(top_ref[...], scores), axis=1, keepdims=True) * factor
        return jnp.broadcast_to(top, (pair, LANES))

    def weigh(turn, step, top):
        scores = score_ref[turn % 2, :, rows_at(step, block)]
        weights = jnp.exp2(scores * factor - top[:, :1])
        sum_ref[...] += plain_dot(narrow(weights), value_ref[rows_at(step, block), :])

    def finish(turn, top):
        total = sum_ref[:, DH : DH + 1]
        mixed = jnp.where(wide_lane < DH, sum_ref[...] / total, 0.0)
        mixed_ref[rows_at(turn, pair), :] = mixed
        level = top + jnp.log2(total)
        level_ref[rows_at(turn, 8), :] = rows_of(picked, level)
        fetch(
            mixed_ref.at[rows_at(turn, pair), :],
            mixed_out.at[rows_at(turn, pair), :],
            out_done.at[next_done + turn],
        )
        one, two = mixed[:block], pltpu.roll(mixed[block:], DH, 1)
        first = jnp.where(wide_lane[:block] < DH, one, two)
        store(2 * turn, first[:span], two[:span])
        store(2 * turn + 1, first[span:], two[span:])

    def clear():
        sum_ref[...] = jnp.zeros_like(sum_ref)
        top_ref[...] = jnp.full(top_ref.shape, masked_score, jnp.float32)

    def one_turn(turn, top):
        clear()

        def both(step, _):
            weigh(turn, step, top)
            score(turn + 1, step)
            return 0

        lax.fori_loop(0, turn + 1, both, 0)
        finish(turn, top)
        return edge(turn + 1)

    clear()
    top = lax.fori_loop(0, turns - 1, one_turn, edge(0))
    clear()

    def only(step, _):
        weigh(turns - 1, step, top)
        return 0

    lax.fori_loop(0, turns, only, 0)
    finish(turns - 1, top)
    for copy in out_copies:
        copy.wait()
    for turn in range(turns):
        here = pl.ds(turn * pair, pair)
        pltpu.make_async_copy(
            mixed_ref.at[here, :], mixed_out.at[here, :], out_done.at[next_done + turn]
        ).wait()


def attend(steps, near, slot, cosine, sine, first, pieces, span):
    tokens = cosine.shape[0]
    turns = tokens // (2 * span)
    quarters, _, four = first.shape
    block, width = pieces[0].shape
    f32 = jnp.float32
    near_out = (
        shape((turns, 3 * span, LANES)),
        shape((16, width), f32),
        shape((8 * turns, 4 * span), f32),
    )
    far_out = (
        shape((tokens, width)),
        shape((width, four)),
        shape((2 * tokens, LANES)),
        shape((tokens, LANES)),
        shape((tokens, LANES)),
        shape((2 * tokens, LANES), f32),
    )
    state = pltpu.VMEM((4 * span, LANES), f32)
    return steps.run(
        functools.partial(attend_kernel, span),
        near_out,
        (near, slot),
        (cosine, sine),
        far=(*pieces,),
        pinned=(first,),
        far_outs=far_out,
        scratch=(
            pltpu.VMEM((tokens, width), jnp.bfloat16),
            pltpu.VMEM((width, four), jnp.bfloat16),
            pltpu.VMEM((32 * quarters, four), jnp.bfloat16),
            pltpu.VMEM((tokens, four), f32),
            pltpu.VMEM((2 * tokens, LANES), jnp.bfloat16),
            pltpu.VMEM((tokens, LANES), jnp.bfloat16),
            pltpu.VMEM((tokens, LANES), jnp.bfloat16),
            pltpu.VMEM((2 * tokens, LANES), f32),
            pltpu.VMEM((2, 4 * span, tokens), f32),
            state,
            state,
            pltpu.SemaphoreType.DMA((turns + 2 * quarters,)),
            pltpu.SemaphoreType.DMA((4 + turns // 2 + turns,)),
        ),
        limit=60,
        micros=33,
    )


def weight_grads(
    owner_ref, fields_ref, weight_ref, gain_ref, row_ref, branch_ref, heads, copies, last_ref, normed_ref, heads_ref, sum_ref
):
    quarters = last_ref.shape[0]
    four = weight_ref.shape[1]
    shard = weight_ref.shape[0] // quarters
    half = shard // 2
    size = 2 * DH
    tall = branch_ref.shape[1] // 2
    for index, copy in enumerate(heads):
        columns = narrow(unfold(wide(branch_ref[owner_ref[index], tall:, :])))
        copy.wait()
        rows = columns.shape[0]
        sum_ref[index * rows : (index + 1) * rows, :] = columns
    ones = jnp.ones((8, four), jnp.bfloat16)
    gap = jnp.zeros((half, LANES), jnp.float32)
    for quarter in range(quarters):
        here = slice(quarter * shard, (quarter + 1) * shard)
        copies[quarter].wait()
        total = row_dot(normed_ref[:, here], fields_ref[...])
        last_ref[quarter, :shard, :] = narrow(total)
        share = narrow(total * wide(weight_ref[here, :]))
        attn = lane_dot(ones, share) / gain_ref[:8, here]
        rows = jnp.concatenate([attn, row_ref[:, here]], axis=0)
        out_grad = row_dot(heads_ref[:, here], sum_ref[...])
        one, two = out_grad[:half], out_grad[half:]
        both = jnp.concatenate([one, gap], axis=1) + pltpu.roll(
            jnp.concatenate([two, gap], axis=1), size, 1
        )
        last_ref[quarter, shard : shard + half, :] = narrow(both)
        end = shard + half
        last_ref[quarter, end : end + 16, :] = narrow(rows)
        last_ref[quarter, end + 16 :, :] = jnp.zeros_like(last_ref[quarter, end + 16 :, :])


def attend_back_kernel(
    span,
    near_ref,
    slot_ref,
    owner_ref,
    grad_ref,
    total_ref,
    weight_ref,
    gain_ref,
    row_ref,
    *refs,
):
    (*heads_in, normed_in, cos_in, sin_in, query_in, key_in, value_in, mixed_in), refs = refs[:15], refs[15:]
    out_ref, last_ref, cos_ref, sin_ref, query_ref, key_ref, value_ref, mixed_ref, *refs = refs
    head_ref, delta_ref, query_sum, key_sum, value_sum, normed_ref, heads_ref, sum_ref, done = refs
    spans = near_ref.shape[0]
    block = 2 * span
    pair = 2 * block
    turns = spans // 2
    factor = LOG2E / math.sqrt(DH)
    scale = 1.0 / math.sqrt(DH)
    lane = lax.broadcasted_iota(jnp.int32, (span, LANES), 1)
    copies = [
        fetch(source, target, done.at[index])
        for index, (source, target) in enumerate(
            (
                (mixed_in, mixed_ref),
                (key_in, key_ref),
                (query_in, query_ref),
                (value_in, value_ref),
                (cos_in, cos_ref),
                (sin_in, sin_ref),
            )
        )
    ]

    quarters = last_ref.shape[0]
    shard = normed_ref.shape[1] // quarters
    heads = [
        fetch(piece, heads_ref.at[pl.ds(index * block, block), :], done.at[6 + index])
        for index, piece in enumerate(heads_in)
    ]
    normed = [
        fetch(
            normed_in.at[:, pl.ds(quarter * shard, shard)],
            normed_ref.at[:, pl.ds(quarter * shard, shard)],
            done.at[6 + len(heads) + quarter],
        )
        for quarter in range(quarters)
    ]

    def split(index, _):
        slot = slot_ref[index]
        grad = wide(grad_ref[slot // 2, rows_at(slot % 2, span), :])
        tail = wide(grad_ref[slot // 2, 2 * span : 3 * span, :])
        first = (index // 2) * 4 + index % 2
        one = jnp.where(lane < DH, grad, 0.0)
        tail = pltpu.roll(tail, 32 + 64 * (slot % 2), 1)
        two = jnp.where(lane < 32, pltpu.roll(grad, 32, 1), tail)
        two = jnp.where(lane < DH, two, 0.0)
        head_ref[rows_at(first, span), :] = narrow(one)
        head_ref[rows_at(first + 2, span), :] = narrow(two)
        return 0

    lax.fori_loop(0, spans, split, 0, unroll=4)
    copies[0].wait()

    def prepare(turn, _):
        here = rows_at(turn, pair)
        product = wide(head_ref[here, :]) * mixed_ref[here, :]
        delta_ref[rows_at(turn, 8), :] = rows_of(jnp.ones((8, LANES), jnp.float32), product)
        query_sum[here, :] = jnp.zeros((pair, LANES), jnp.float32)
        return 0

    lax.fori_loop(0, turns, prepare, 0, unroll=2)
    for copy in copies[1:]:
        copy.wait()

    def turned_back(field, index):
        cosine = cos_ref[rows_at(index, span), :]
        sine = sin_ref[rows_at(index, span), :]
        field = field * scale
        return wide(narrow(field * cosine - swapped(field) * sine))

    def one_block(turn, _):
        key = key_ref[rows_at(turn, block), :]
        value = value_ref[rows_at(turn, block), :]

        def one_step(step, diagonal):
            here = rows_at(step, pair)
            query = query_ref[here, :]
            head = head_ref[here, :]
            level = total_ref[rows_at(step, 8), :][:1]
            delta = delta_ref[rows_at(step, 8), :][:1]
            probs = jnp.exp2(lane_dot(key, query) * factor - level)
            if diagonal:
                row = lax.broadcasted_iota(jnp.int32, (block, pair), 0)
                column = lax.broadcasted_iota(jnp.int32, (block, pair), 1) % block
                probs = jnp.where(row <= column, probs, 0.0)
            d_scores = narrow(probs * (lane_dot(value, head) - delta))
            query_sum[here, :] += row_dot(d_scores, key)
            return plain_dot(d_scores, query), plain_dot(narrow(probs), head)

        key_part, value_part = one_step(turn, True)
        key_sum[...] = key_part
        value_sum[...] = value_part

        def two_steps(index, _):
            step = turn + 1 + 2 * index
            key_one, value_one = one_step(step, False)
            key_two, value_two = one_step(step + 1, False)
            key_sum[...] += key_one + key_two
            value_sum[...] += value_one + value_two
            return 0

        left = turns - 1 - turn
        lax.fori_loop(0, left // 2, two_steps, 0)

        @pl.when(left % 2 == 1)
        def _():
            key_one, value_one = one_step(turns - 1, False)
            key_sum[...] += key_one
            value_sum[...] += value_one

        for part in range(2):
            index = 2 * turn + part
            here = rows_at(near_ref[index], span)
            rows = slice(part * span, (part + 1) * span)
            first = rows_at((index // 2) * 4 + index % 2, span)
            second = rows_at((index // 2) * 4 + index % 2 + 2, span)
            one = turned_back(query_sum[first, :], index)
            two = turned_back(query_sum[second, :], index)
            three = turned_back(key_sum[rows, :], index)
            out_ref[here, :] = narrow(join_fields(one, two, three, value_sum[rows, :]))
        return 0

    lax.fori_loop(0, turns, one_block, 0)
    weight_grads(
        owner_ref, out_ref, weight_ref, gain_ref, row_ref, grad_ref, heads, normed, last_ref, normed_ref, heads_ref, sum_ref
    )


def attend_back(
    steps, near, slot, owners, grad, total, weights, cosine, sine, query, key, value, mixed, heads, normed, packed, span
):
    tokens, width = normed.shape
    f32 = jnp.float32
    rows = pltpu.VMEM((2 * span, LANES), f32)
    shard = 4 * DH
    return steps.run(
        functools.partial(attend_back_kernel, span),
        (shape((tokens, 4 * DH)), shape((width // shard, packed, 4 * DH))),
        (near, slot, owners),
        (grad, total, *weights),
        far=heads,
        pinned=(normed, cosine, sine, query, key, value, mixed),
        scratch=(
            pltpu.VMEM(cosine.shape, f32),
            pltpu.VMEM(cosine.shape, f32),
            pltpu.VMEM(query.shape, jnp.bfloat16),
            pltpu.VMEM(key.shape, jnp.bfloat16),
            pltpu.VMEM(value.shape, jnp.bfloat16),
            pltpu.VMEM(mixed.shape, f32),
            pltpu.VMEM((2 * tokens, LANES), jnp.bfloat16),
            pltpu.VMEM(total.shape, f32),
            pltpu.VMEM((2 * tokens, LANES), f32),
            rows,
            rows,
            pltpu.VMEM((tokens, width), jnp.bfloat16),
            pltpu.VMEM((tokens, width), jnp.bfloat16),
            pltpu.VMEM((tokens, 2 * LANES), jnp.bfloat16),
            pltpu.SemaphoreType.DMA((6 + len(heads) + width // shard,)),
        ),
        limit=60,
        micros=38,
    )


def turn_tables(tokens):
    half = DH // 2
    freqs = jnp.exp(-math.log(rope_base) * 2.0 * jnp.arange(half, dtype=jnp.float32) / DH)
    angle = jnp.arange(tokens, dtype=jnp.int32).astype(jnp.float32)[:, None] * freqs[None, :]
    gap = jnp.zeros((tokens, LANES - DH), jnp.float32)
    cosine, sine = jnp.cos(angle), jnp.sin(angle)
    return (
        jnp.concatenate([cosine, cosine, gap], axis=1),
        jnp.concatenate([-sine, sine, gap], axis=1),
    )


def swap(block, bits):
    routes = [(i, i ^ bits) for i in range(lax.axis_size("ctx"))]
    return lax.ppermute(block, "ctx", routes)


def swap_split(block, even, odd):
    routes = [(i, i ^ (odd if i & CORE else even)) for i in range(lax.axis_size("ctx"))]
    return lax.ppermute(block, "ctx", routes)


def gather_spans(block, core, between=None):
    from_x = swap(block, ALONG_X)
    from_y = swap(block, ALONG_Y)
    twin = swap(block, CORE)
    first = between(from_x, from_y) if between else from_x
    corner = swap_split(jnp.where(core[0] == 0, first, from_y), ALONG_Y, ALONG_X)
    return [block, from_x, from_y, corner] + [
        twin,
        swap(first, CORE),
        swap(from_y, CORE),
        swap(corner, CORE),
    ]


def gather_direct(block):
    blocks = [block] + [swap(block, way) for way in (ALONG_X, ALONG_Y, ALONG_X | ALONG_Y)]
    return blocks + [swap(part, CORE) for part in blocks]


def open_scatter(steps, own, twin, core, limit=20):
    rows, width = own[0].shape[0] * len(own) // 4, own[0].shape[1]
    some = shape((rows, width), jnp.float32)
    return steps.run(
        add_twin_kernel,
        (shape((2 * rows, width)), some, some),
        (core,),
        (*own, *twin),
        limit=limit,
    )


def turn_scatter(steps, keep, got):
    late = steps.run(
        add_late_kernel,
        shape(keep.shape),
        (),
        (),
        far=(keep, got),
        scratch=(
            pltpu.VMEM(keep.shape, jnp.float32),
            pltpu.VMEM(keep.shape, jnp.bfloat16),
            pltpu.SemaphoreType.DMA((2,)),
        ),
        limit=60,
    )
    return swap_split(late, ALONG_X, ALONG_Y)


def plane_layer(
    activations,
    span_order,
    w_query,
    w_key,
    w_value,
    w_out,
    w_gate,
    w_up,
    w_down,
    attn_gain,
    ffn_gain,
    cotangent,
):
    f32 = jnp.float32
    cycles = lax.axis_size("ctx")
    quarters = lax.axis_size("fsdp")
    mine = lax.axis_index("ctx")
    span = activations.shape[2]
    width = activations.shape[3]
    tokens = 2 * span
    length = cycles * tokens
    half = length // 2
    shard = w_query.shape[0]
    four = 4 * DH
    hidden_size = quarters * w_down.shape[0]
    strip = hidden_size // (quarters * cycles)
    part = hidden_size // cycles
    slab = w_out.shape[0] // cycles
    slabs = width // four
    packed = shard + slabs * slab + 32
    owners = mine ^ jnp.array(RELATIVE, jnp.int32)
    away = mine ^ jnp.arange(cycles, dtype=jnp.int32)
    seat = (away & 1) * 4 + (away >> 2) * 2 + ((away >> 1) & 1)
    slot_of = jnp.argsort(span_order).astype(jnp.int32)
    near_slot = 2 * seat[slot_of // 2] + slot_of % 2
    here = mine.reshape(1).astype(jnp.int32)
    core = here & CORE
    stream = activations.reshape(tokens, width)
    grad_rows = cotangent.reshape(tokens, width)

    steps = Steps(core)
    low = jnp.bfloat16

    gains = jnp.pad(jnp.stack([attn_gain, ffn_gain]), ((0, 30), (0, four - shard)))
    window = pltpu.VMEM((shard, 2 * LANES), low)
    first = steps.run(
        pack_kernel,
        shape((packed, four)),
        (here,),
        (gains,),
        pinned=(w_query, w_key, w_value, w_out),
        scratch=(
            window,
            window,
            window,
            pltpu.VMEM((slab, width), low),
            pltpu.SemaphoreType.DMA((4,)),
        ),
        limit=60,
    )
    first = lax.all_gather(first, "fsdp", axis=0)
    own_strips = steps.run(strip_kernel, shape((shard, 2 * part)), (here,), (w_gate, w_up), limit=28)
    gate_up = lax.all_gather(own_strips, "fsdp", axis=0, tiled=True)
    down = lax.dynamic_slice_in_dim(w_down, mine * strip, strip, axis=0)
    down = lax.all_gather(down, "fsdp", axis=0, tiled=True)
    cosine, sine = turn_tables(length)
    streams = gather_spans(
        stream, core, lambda one, two: after(one, two, own_strips, cosine, sine, near_slot, slot_of)
    )
    grads = gather_spans(after(grad_rows, streams[3]), core)
    out_part = first[:, shard : shard + slabs * slab].reshape(quarters * slabs * slab, four)
    folded, gains, level, normed1, w_fields, query, key, value, attended = attend(
        steps, near_slot, slot_of, cosine, sine, first, streams, span
    )
    outs = gather_direct(out_part)
    steps.wait(*outs)
    folded = lax.all_to_all(after(folded, *grads[1:3], *outs[1:4]), "ctx", 0, 0)
    one_tile = shape((tokens, LANES), f32)
    stream_one, normed2, inverse, heads_low, full_out = steps.run(
        branch_kernel,
        (shape((tokens, width), f32), shape((tokens, width)), one_tile, shape((tokens, width))),
        (owners,),
        (folded, stream, gains),
        far=outs,
        far_outs=(shape((width, width)),),
        scratch=(
            pltpu.VMEM((width, width), low),
            pltpu.VMEM((cycles, *outs[0].shape), low),
            pltpu.SemaphoreType.DMA((cycles,)),
        ),
        limit=60,
        micros=6,
    )
    normed2 = gather_spans(normed2, core)
    def strips(pieces, grad_pieces, *before):
        results = steps.run(
            functools.partial(strips_kernel, len(pieces), bool(before)),
            (
                shape((part, width), low if before else f32),
                *(shape((tokens, width)),) * 4,
                shape((half, width)),
            ),
            (),
            before,
            far=(*pieces, *grad_pieces),
            pinned=(gate_up, down),
            far_outs=(shape((half, 2 * part)),),
            scratch=(
                pltpu.VMEM((part, width), f32),
                pltpu.VMEM((width, 2 * part), low),
                pltpu.VMEM((part, width), low),
                pltpu.VMEM((half, width), low),
                pltpu.VMEM((half, width), low),
                pltpu.VMEM((half, 2 * part), low),
                pltpu.SemaphoreType.DMA((2 * len(pieces),)),
                pltpu.SemaphoreType.DMA((len(pieces) // 2,)),
                pltpu.SemaphoreType.DMA((2,)),
            ),
                limit=60,
            micros=20,
        )
        return results[0], results[1:5], results[5], results[6]

    down_twin, d_normed2_twin, sum_twin, both_twin = strips(normed2[4:], grads[4:])
    heads = gather_spans(
        after(heads_low, normed2[3]), core, lambda one, two: after(one, two, down_twin)
    )
    steps.wait(heads[1], heads[2])
    d_normed2_twin = [swap(block, CORE) for block in d_normed2_twin]
    down_sum, d_normed2_own, sum_own, both_own = strips(normed2[:4], grads[:4], down_twin)
    grad_down = lax.psum_scatter(after(down_sum, heads[3]), "fsdp", scatter_dimension=0, tiled=True)
    sum_twin = swap(after(sum_twin, down_sum), CORE)
    send, keep, total = open_scatter(steps, d_normed2_own, d_normed2_twin, core, 60)
    got = swap_split(send, ALONG_Y, ALONG_X)
    steps.wait(heads[3])
    grad_both, grad_ffn = steps.run(
        functools.partial(strip_grad_kernel, cycles),
        (shape((width, 2 * part)), shape((8, width), f32)),
        (),
        (gate_up, gains),
        far=(*normed2,),
        pinned=(both_own, both_twin),
        scratch=(
            pltpu.VMEM((length, width), low),
            pltpu.VMEM((length, 2 * part), low),
            pltpu.SemaphoreType.DMA((cycles + 2,)),
        ),
        limit=60,
        micros=12,
    )
    grad_both = lax.psum_scatter(after(grad_both, got), "fsdp", scatter_dimension=0, tiled=True)
    late_got = turn_scatter(steps, keep, got)
    ffn_send, ffn_keep, ffn_total = open_scatter(steps, (sum_own,), (sum_twin,), core)
    d_stream_one, d_heads = steps.run(
        branch_back_kernel,
        (
            shape((tokens, width), f32),
            shape((cycles, 6 * span, LANES)),
        ),
        (),
        (total, got, late_got, grad_rows, stream_one, inverse, gains, full_out),
        limit=28,
        micros=4,
    )
    d_heads = lax.all_to_all(d_heads, "ctx", 0, 0)
    ffn_got = swap_split(after(ffn_send, d_heads), ALONG_Y, ALONG_X)
    grad_downs = gather_direct(after(grad_down, d_heads))
    d_fields, last = attend_back(
        steps,
        near_slot,
        slot_of,
        owners,
        d_heads,
        level,
        (w_fields, gains, grad_ffn),
        cosine,
        sine,
        query,
        key,
        value,
        attended,
        heads,
        normed1,
        packed,
        span,
    )
    last = after(last, ffn_got, *grad_downs[1:4])
    last = lax.psum_scatter(last, "fsdp", scatter_dimension=0, tiled=False)
    steps.wait(ffn_got, *grad_downs[1:4])
    both_pieces = gather_spans(
        after(grad_both, d_fields), core, lambda one, two: after(one, two, d_fields)
    )

    def stream_grad(start):
        return steps.run(
            functools.partial(stream_grad_kernel, start),
            shape((half, width)),
            (),
            (d_fields, w_fields),
            micros=2,
        )

    d_normed1_twin = swap(stream_grad(half), CORE)
    d_normed1_own = stream_grad(0)
    send, keep, total = open_scatter(steps, (d_normed1_own,), (d_normed1_twin,), core)
    got = swap_split(send, ALONG_Y, ALONG_X)
    ffn_late_got = turn_scatter(steps, ffn_keep, ffn_got)
    steps.wait(both_pieces[1], both_pieces[2])
    grad_down = steps.run(
        place_down_kernel,
        (),
        (owners,),
        (),
        far=grad_downs,
        far_outs=(shape((hidden_size // quarters, width), f32),),
        scratch=(
            pltpu.VMEM((cycles, strip, width), low),
            pltpu.VMEM((cycles, strip, width), f32),
            pltpu.SemaphoreType.DMA((2, cycles)),
        ),
        limit=60,
        micros=1000,
    )[0]
    late_got = turn_scatter(steps, keep, got)
    last = gather_direct(after(last, grad_down))
    wide_strip = shape((shard, hidden_size), f32)
    narrow_grad = shape((shard, width // 2), f32)
    wide_grad = shape((shard, width), f32)
    grad_gains, output, input_grad, *weight_grads = steps.run(
        finish_kernel,
        (shape((16, four), f32),),
        (owners,),
        (
            ffn_total,
            ffn_got,
            ffn_late_got,
            stream_one,
            total,
            got,
            late_got,
            stream,
            d_stream_one,
            gains,
        ),
        far=(*both_pieces, *last),
        far_outs=(
            shape((tokens, width)),
            shape((tokens, width), f32),
            wide_strip,
            wide_strip,
            wide_grad,
            narrow_grad,
            narrow_grad,
            wide_grad,
        ),
        scratch=(
            pltpu.VMEM((tokens, width), low),
            pltpu.VMEM((tokens, width), f32),
            pltpu.VMEM((cycles, shard, 2 * part), low),
            pltpu.VMEM((cycles, shard, 2 * part), f32),
            pltpu.VMEM((cycles, packed, four), low),
            pltpu.VMEM((shard, width), f32),
            pltpu.VMEM((shard, width // 2), f32),
            pltpu.VMEM((shard, width // 2), f32),
            pltpu.VMEM((shard, width), f32),
            pltpu.SemaphoreType.DMA((2 * cycles,)),
            pltpu.SemaphoreType.DMA((2,)),
            pltpu.SemaphoreType.DMA((cycles, 2 * quarters)),
            pltpu.SemaphoreType.DMA((8,)),
        ),
        limit=60,
    )
    grad_gate, grad_up, grad_query, grad_key, grad_value, grad_out = weight_grads
    return (
        output.reshape(activations.shape),
        input_grad.reshape(activations.shape),
        grad_query,
        grad_key,
        grad_value,
        grad_out,
        grad_gate,
        grad_up,
        grad_down,
        grad_gains[0],
        grad_gains[8],
    )


def solution(mesh):
    in_specs = (
        P("fsdp", "ctx", None, None),
        P(),
        P("fsdp", None),
        P("fsdp", None),
        P("fsdp", None),
        P("fsdp", None),
        P("fsdp", None),
        P("fsdp", None),
        P("fsdp", None),
        P("fsdp"),
        P("fsdp"),
        P("fsdp", "ctx", None, None),
    )
    out_specs = (
        P("fsdp", "ctx", None, None),
        P("fsdp", "ctx", None, None),
        P("fsdp", None),
        P("fsdp", None),
        P("fsdp", None),
        P("fsdp", None),
        P("fsdp", None),
        P("fsdp", None),
        P("fsdp", None),
        P("fsdp"),
        P("fsdp"),
    )
    cycles = mesh.shape["ctx"]

    def per_device(*arrays):
        heads = arrays[3].shape[1] // DH
        if cycles == len(RELATIVE) == heads and arrays[2].shape == (4 * DH, 2 * heads * DH):
            return plane_layer(*arrays)
        return ring_layer(*arrays)

    return jax.shard_map(
        per_device, mesh=mesh, in_specs=in_specs, out_specs=out_specs, check_vma=False
    )
```

```python
import functools
import math

import jax
import jax.numpy as jnp
from jax import lax
from jax.experimental import pallas as pl
from jax.experimental.pallas import tpu as pltpu
from jax.sharding import PartitionSpec as P

DH = 96


epsilon = 1e-05
rope_base = 100000.0
masked_score = -1e30
LOG2E = math.log2(math.e)


def passed_along(block, axis, distance):
    devices = range(lax.axis_size(axis))
    route = [((i - distance) % len(devices), i) for i in devices]
    return lax.ppermute(block, axis, route)


def rope_tables(places):
    half = DH // 2
    freqs = jnp.exp(-math.log(rope_base) * 2.0 * jnp.arange(half, dtype=jnp.float32) / DH)
    angle = places.astype(jnp.float32)[:, None] * freqs[None, :]
    return (jnp.cos(angle)[:, None, :], jnp.sin(angle)[:, None, :])


def rope_turn(field, cosine, sine):
    half = DH // 2
    first = field[..., :half]
    second = field[..., half:]
    return jnp.concatenate(
        [first * cosine - second * sine, second * cosine + first * sine], axis=-1
    )


def rope_back(field, cosine, sine):
    half = DH // 2
    first = field[..., :half]
    second = field[..., half:]
    return jnp.concatenate(
        [first * cosine + second * sine, second * cosine - first * sine], axis=-1
    )


def norm_back(d_normed, stream, inv_rms, gain):
    scaled = d_normed * gain
    cubed = inv_rms * inv_rms * inv_rms
    return inv_rms * scaled - stream * cubed * jnp.mean(scaled * stream, axis=-1, keepdims=True)


def ring_layer(
    activations,
    span_order,
    w_query,
    w_key,
    w_value,
    w_out,
    w_gate,
    w_up,
    w_down,
    attn_gain,
    ffn_gain,
    cotangent,
):
    cycles = lax.axis_size("ctx")
    mine = lax.axis_index("ctx")
    span = activations.shape[2]
    width = activations.shape[3]
    tokens = 2 * span
    heads = w_query.shape[1] // DH
    kv_heads = w_key.shape[1] // DH
    group = heads // kv_heads
    scale = 1.0 / math.sqrt(DH)
    offsets = jnp.arange(span, dtype=jnp.int32)

    def places_of(owner):
        span_ids = lax.dynamic_slice_in_dim(span_order, 2 * owner, 2)
        return (span_ids[:, None] * span + offsets[None, :]).reshape(tokens)

    query_places = places_of(mine)
    cosine, sine = rope_tables(query_places)
    gathered = (
        lax.all_gather(w_query, "fsdp", axis=0, tiled=True),
        lax.all_gather(w_key, "fsdp", axis=0, tiled=True),
        lax.all_gather(w_value, "fsdp", axis=0, tiled=True),
        lax.all_gather(w_out, "fsdp", axis=0, tiled=True),
        lax.all_gather(w_gate, "fsdp", axis=0, tiled=True),
        lax.all_gather(w_up, "fsdp", axis=0, tiled=True),
        lax.all_gather(w_down, "fsdp", axis=0, tiled=True),
        lax.all_gather(attn_gain, "fsdp", axis=0, tiled=True),
        lax.all_gather(ffn_gain, "fsdp", axis=0, tiled=True),
    )
    (
        full_query,
        full_key,
        full_value,
        full_out,
        full_gate,
        full_up,
        full_down,
        gain_one,
        gain_two,
    ) = gathered
    stream = activations.reshape(tokens, width).astype(jnp.float32)
    inv_one = lax.rsqrt(jnp.mean(stream * stream, axis=-1, keepdims=True) + epsilon)
    normed1 = (stream * inv_one * gain_one).astype(jnp.bfloat16)
    query_raw = jnp.dot(normed1, full_query, preferred_element_type=jnp.float32).reshape(
        tokens, heads, DH
    )
    queries = (
        rope_turn(query_raw, cosine, sine).astype(jnp.bfloat16).reshape(tokens, kv_heads, group, DH)
    )
    key_raw = jnp.dot(normed1, full_key, preferred_element_type=jnp.float32).reshape(
        tokens, kv_heads, DH
    )
    keys = rope_turn(key_raw, cosine, sine).astype(jnp.bfloat16)
    values = (
        jnp.dot(normed1, full_value, preferred_element_type=jnp.float32)
        .astype(jnp.bfloat16)
        .reshape(tokens, kv_heads, DH)
    )

    def scores_with(key_piece, owner):
        scores = (
            jnp.einsum("tjgd,sjd->jgts", queries, key_piece, preferred_element_type=jnp.float32)
            * scale
        )
        counted = places_of(owner)[None, :] <= query_places[:, None]
        return jnp.where(counted, scores, masked_score)

    def absorb(state, key_piece, value_piece, owner):
        running_top, running_total, running_sum = state
        scores = scores_with(key_piece, owner)
        new_top = jnp.maximum(running_top, jnp.max(scores, axis=-1, keepdims=True))
        fading = jnp.exp(running_top - new_top)
        weights = jnp.exp(scores - new_top)
        running_total = fading * running_total + jnp.sum(weights, axis=-1, keepdims=True)
        running_sum = fading * running_sum + jnp.einsum(
            "jgts,sjd->jgtd",
            weights.astype(jnp.bfloat16),
            value_piece,
            preferred_element_type=jnp.float32,
        )
        return (new_top, running_total, running_sum)

    start_state = (
        jnp.full((kv_heads, group, tokens, 1), masked_score, jnp.float32),
        jnp.zeros((kv_heads, group, tokens, 1), jnp.float32),
        jnp.zeros((kv_heads, group, tokens, DH), jnp.float32),
    )
    state = absorb(start_state, keys, values, mine)

    def forward_turn(turn_index, carry):
        state_now, key_piece, value_piece = carry
        key_piece, value_piece = passed_along((key_piece, value_piece), "ctx", 1)
        owner = (mine - turn_index) % cycles
        return (absorb(state_now, key_piece, value_piece, owner), key_piece, value_piece)

    state, _, _ = lax.fori_loop(1, cycles, forward_turn, (state, keys, values))
    running_top, running_total, running_sum = state
    attended = running_sum / running_total
    log_total = running_top + jnp.log(running_total)
    attended_low = (
        jnp.transpose(attended, (2, 0, 1, 3)).reshape(tokens, heads * DH).astype(jnp.bfloat16)
    )
    stream_one = stream + jnp.dot(attended_low, full_out, preferred_element_type=jnp.float32)
    inv_two = lax.rsqrt(jnp.mean(stream_one * stream_one, axis=-1, keepdims=True) + epsilon)
    normed2 = (stream_one * inv_two * gain_two).astype(jnp.bfloat16)
    gate = jnp.dot(normed2, full_gate, preferred_element_type=jnp.float32)
    up_part = jnp.dot(normed2, full_up, preferred_element_type=jnp.float32)
    sigma = jax.nn.sigmoid(gate)
    hidden = (gate * sigma * up_part).astype(jnp.bfloat16)
    stream_two = stream_one + jnp.dot(hidden, full_down, preferred_element_type=jnp.float32)
    output = stream_two.astype(jnp.bfloat16).reshape(activations.shape)
    back_weights = (
        lax.all_gather(w_query, "fsdp", axis=0, tiled=True),
        lax.all_gather(w_key, "fsdp", axis=0, tiled=True),
        lax.all_gather(w_value, "fsdp", axis=0, tiled=True),
        lax.all_gather(w_out, "fsdp", axis=0, tiled=True),
        lax.all_gather(w_gate, "fsdp", axis=0, tiled=True),
        lax.all_gather(w_up, "fsdp", axis=0, tiled=True),
        lax.all_gather(w_down, "fsdp", axis=0, tiled=True),
        lax.all_gather(attn_gain, "fsdp", axis=0, tiled=True),
        lax.all_gather(ffn_gain, "fsdp", axis=0, tiled=True),
    )
    (
        back_query,
        back_key,
        back_value,
        back_out,
        back_gate,
        back_up,
        back_down,
        back_gain_one,
        back_gain_two,
    ) = back_weights
    grad_rows = cotangent.reshape(tokens, width)
    grad_stream = grad_rows.astype(jnp.float32)
    grad_down = jnp.einsum("tf,td->fd", hidden, grad_rows, preferred_element_type=jnp.float32)
    d_hidden = jnp.einsum("td,fd->tf", grad_rows, back_down, preferred_element_type=jnp.float32)
    d_gate = (d_hidden * up_part * sigma * (1.0 + gate * (1.0 - sigma))).astype(jnp.bfloat16)
    d_up = (d_hidden * gate * sigma).astype(jnp.bfloat16)
    grad_gate = jnp.einsum("td,tf->df", normed2, d_gate, preferred_element_type=jnp.float32)
    grad_up = jnp.einsum("td,tf->df", normed2, d_up, preferred_element_type=jnp.float32)
    d_normed2 = jnp.einsum(
        "tf,df->td", d_gate, back_gate, preferred_element_type=jnp.float32
    ) + jnp.einsum("tf,df->td", d_up, back_up, preferred_element_type=jnp.float32)
    grad_ffn_gain = jnp.sum(d_normed2 * stream_one * inv_two, axis=0)
    d_stream_one = grad_stream + norm_back(d_normed2, stream_one, inv_two, back_gain_two)
    d_branch = d_stream_one.astype(jnp.bfloat16)
    grad_out = jnp.einsum("tk,td->kd", attended_low, d_branch, preferred_element_type=jnp.float32)
    d_attended = jnp.einsum(
        "td,kd->tk", d_branch, back_out, preferred_element_type=jnp.float32
    ).astype(jnp.bfloat16)
    d_heads = jnp.transpose(d_attended.reshape(tokens, kv_heads, group, DH), (1, 2, 0, 3))
    delta = jnp.sum(d_heads.astype(jnp.float32) * attended, axis=-1, keepdims=True)

    def back_step(d_queries, d_keys, d_values, key_piece, value_piece, owner):
        scores = scores_with(key_piece, owner)
        probs = jnp.exp(scores - log_total)
        d_values = d_values + jnp.einsum(
            "jgts,jgtd->sjd",
            probs.astype(jnp.bfloat16),
            d_heads,
            preferred_element_type=jnp.float32,
        )
        d_probs = jnp.einsum(
            "jgtd,sjd->jgts", d_heads, value_piece, preferred_element_type=jnp.float32
        )
        d_scores = (probs * (d_probs - delta)).astype(jnp.bfloat16)
        d_queries = (
            d_queries
            + jnp.einsum("jgts,sjd->jgtd", d_scores, key_piece, preferred_element_type=jnp.float32)
            * scale
        )
        d_keys = (
            d_keys
            + jnp.einsum("jgts,tjgd->sjd", d_scores, queries, preferred_element_type=jnp.float32)
            * scale
        )
        return (d_queries, d_keys, d_values)

    def pass_grads(d_keys, d_values):
        return (
            passed_along(d_keys.astype(jnp.bfloat16), "ctx", 1).astype(d_keys.dtype),
            passed_along(d_values.astype(jnp.bfloat16), "ctx", 1).astype(d_values.dtype),
        )

    zero_queries = jnp.zeros((kv_heads, group, tokens, DH), jnp.float32)
    zero_keys = jnp.zeros((tokens, kv_heads, DH), jnp.float32)
    d_queries, d_keys, d_values = back_step(zero_queries, zero_keys, zero_keys, keys, values, mine)

    def backward_turn(turn_index, carry):
        d_queries_now, d_keys_now, d_values_now, key_piece, value_piece = carry
        key_piece, value_piece = passed_along((key_piece, value_piece), "ctx", 1)
        d_keys_now, d_values_now = pass_grads(d_keys_now, d_values_now)
        owner = (mine - turn_index) % cycles
        d_queries_now, d_keys_now, d_values_now = back_step(
            d_queries_now, d_keys_now, d_values_now, key_piece, value_piece, owner
        )
        return (d_queries_now, d_keys_now, d_values_now, key_piece, value_piece)

    d_queries, d_keys, d_values, _, _ = lax.fori_loop(
        1, cycles, backward_turn, (d_queries, d_keys, d_values, keys, values)
    )
    d_keys, d_values = pass_grads(d_keys, d_values)
    d_query_rows = jnp.transpose(d_queries, (2, 0, 1, 3)).reshape(tokens, heads, DH)
    d_query = rope_back(d_query_rows, cosine, sine).astype(jnp.bfloat16).reshape(tokens, heads * DH)
    d_key = rope_back(d_keys, cosine, sine).astype(jnp.bfloat16).reshape(tokens, kv_heads * DH)
    d_value = d_values.astype(jnp.bfloat16).reshape(tokens, kv_heads * DH)
    grad_query = jnp.einsum("td,tk->dk", normed1, d_query, preferred_element_type=jnp.float32)
    grad_key = jnp.einsum("td,tk->dk", normed1, d_key, preferred_element_type=jnp.float32)
    grad_value = jnp.einsum("td,tk->dk", normed1, d_value, preferred_element_type=jnp.float32)
    d_normed1 = (
        jnp.einsum("tk,dk->td", d_query, back_query, preferred_element_type=jnp.float32)
        + jnp.einsum("tk,dk->td", d_key, back_key, preferred_element_type=jnp.float32)
        + jnp.einsum("tk,dk->td", d_value, back_value, preferred_element_type=jnp.float32)
    )
    grad_attn_gain = jnp.sum(d_normed1 * stream * inv_one, axis=0)
    input_grad = (d_stream_one + norm_back(d_normed1, stream, inv_one, back_gain_one)).reshape(
        activations.shape
    )
    shares = (
        lax.psum_scatter(
            grad_query.astype(jnp.bfloat16), "fsdp", scatter_dimension=0, tiled=True
        ).astype(jnp.float32),
        lax.psum_scatter(
            grad_key.astype(jnp.bfloat16), "fsdp", scatter_dimension=0, tiled=True
        ).astype(jnp.float32),
        lax.psum_scatter(
            grad_value.astype(jnp.bfloat16), "fsdp", scatter_dimension=0, tiled=True
        ).astype(jnp.float32),
        lax.psum_scatter(
            grad_out.astype(jnp.bfloat16), "fsdp", scatter_dimension=0, tiled=True
        ).astype(jnp.float32),
        lax.psum_scatter(
            grad_gate.astype(jnp.bfloat16), "fsdp", scatter_dimension=0, tiled=True
        ).astype(jnp.float32),
        lax.psum_scatter(
            grad_up.astype(jnp.bfloat16), "fsdp", scatter_dimension=0, tiled=True
        ).astype(jnp.float32),
        lax.psum_scatter(
            grad_down.astype(jnp.bfloat16), "fsdp", scatter_dimension=0, tiled=True
        ).astype(jnp.float32),
        lax.psum_scatter(
            grad_attn_gain.astype(jnp.bfloat16), "fsdp", scatter_dimension=0, tiled=True
        ).astype(jnp.float32),
        lax.psum_scatter(
            grad_ffn_gain.astype(jnp.bfloat16), "fsdp", scatter_dimension=0, tiled=True
        ).astype(jnp.float32),
    )
    shares = (
        lax.psum(shares[0].astype(jnp.bfloat16), "ctx").astype(jnp.float32),
        lax.psum(shares[1].astype(jnp.bfloat16), "ctx").astype(jnp.float32),
        lax.psum(shares[2].astype(jnp.bfloat16), "ctx").astype(jnp.float32),
        lax.psum(shares[3].astype(jnp.bfloat16), "ctx").astype(jnp.float32),
        lax.psum(shares[4].astype(jnp.bfloat16), "ctx").astype(jnp.float32),
        lax.psum(shares[5].astype(jnp.bfloat16), "ctx").astype(jnp.float32),
        lax.psum(shares[6].astype(jnp.bfloat16), "ctx").astype(jnp.float32),
        lax.psum(shares[7].astype(jnp.bfloat16), "ctx").astype(jnp.float32),
        lax.psum(shares[8].astype(jnp.bfloat16), "ctx").astype(jnp.float32),
    )
    return (
        output,
        input_grad,
        shares[0],
        shares[1],
        shares[2],
        shares[3],
        shares[4],
        shares[5],
        shares[6],
        shares[7],
        shares[8],
    )


LANES = 128
CORE, ALONG_X, ALONG_Y = 1, 2, 4
RELATIVE = (0, 2, 4, 6, 1, 3, 5, 7)
MIB = 2**20
COST = 10**6


def lane_dot(left, right):
    return lax.dot_general(left, right, (((1,), (1,)), ((), ())), preferred_element_type=jnp.float32)


def plain_dot(left, right):
    return lax.dot_general(left, right, (((1,), (0,)), ((), ())), preferred_element_type=jnp.float32)


def row_dot(left, right):
    return lax.dot_general(left, right, (((0,), (0,)), ((), ())), preferred_element_type=jnp.float32)


def rows_at(index, size):
    return pl.ds(pl.multiple_of(index * size, size), size)


def wide(value):
    return value.astype(jnp.float32)


def narrow(value):
    return value.astype(jnp.bfloat16)


def lanes_of(rows):
    return lax.broadcasted_iota(jnp.int32, (rows, LANES), 1)


def shape(dims, kind=jnp.bfloat16):
    return jax.ShapeDtypeStruct(dims, kind)


def after(value, *others):
    return lax.optimization_barrier((value, *others))[0]


class Steps:

    def __init__(self, ticket):
        self.ticket = ticket
        self.pending = []

    def wait(self, *values):
        self.pending.extend(values)

    def run(
        self,
        body,
        outs,
        small,
        arrays,
        far=(),
        pinned=(),
        far_outs=(),
        scratch=(),
        limit=20,
        micros=2,
    ):
        near = pl.BlockSpec(memory_space=pltpu.VMEM)
        scalars = pl.BlockSpec(memory_space=pltpu.SMEM)
        away = pl.BlockSpec(memory_space=pl.ANY)
        stored = pl.BlockSpec(memory_space=pltpu.HBM)
        single = not isinstance(outs, tuple)
        out_shapes = ((outs,) if single else outs) + tuple(far_outs)
        out_specs = [near] * (len(out_shapes) - len(far_outs)) + [stored] * len(far_outs)
        ticket = after(self.ticket, *self.pending) if self.pending else self.ticket
        results = pl.pallas_call(
            lambda _, *refs: body(*refs),
            out_shape=out_shapes,
            in_specs=[scalars] * (1 + len(small))
            + [near] * len(arrays)
            + [away] * len(far)
            + [stored] * len(pinned),
            out_specs=out_specs,
            scratch_shapes=list(scratch),
            compiler_params=pltpu.CompilerParams(vmem_limit_bytes=limit * MIB),
            cost_estimate=pl.CostEstimate(
                flops=micros * COST, bytes_accessed=0, transcendentals=0
            ),
        )(ticket, *small, *arrays, *far, *pinned)
        self.pending = [results[-1]]
        return results[0] if single and not far_outs else results


def window_of(weight, start):
    base = jnp.minimum(start // LANES * LANES, weight.shape[1] - 2 * LANES)
    return weight.at[:, pl.ds(pl.multiple_of(base, LANES), 2 * LANES)], start - base


def drawn(window_ref, shift):
    size = 2 * LANES
    return pltpu.roll(wide(window_ref[...]), (size - shift) % size, 1)


def join_fields(one, two, three, four):
    lane = lanes_of(one.shape[0])
    two = pltpu.roll(two, 96, 1)
    three = pltpu.roll(three, 64, 1)
    four = pltpu.roll(four, 32, 1)
    return jnp.concatenate(
        [
            jnp.where(lane < 96, one, two),
            jnp.where(lane < 64, two, three),
            jnp.where(lane < 32, three, four),
        ],
        axis=1,
    )


def part_fields(block):
    lane = lanes_of(block.shape[0])
    one, two, three = (block[:, start : start + LANES] for start in (0, LANES, 2 * LANES))
    fields = (
        one,
        jnp.where(lane < 32, pltpu.roll(one, 32, 1), pltpu.roll(two, 32, 1)),
        jnp.where(lane < 64, pltpu.roll(two, 64, 1), pltpu.roll(three, 64, 1)),
        pltpu.roll(three, 96, 1),
    )
    return [jnp.where(lane < DH, field, 0.0) for field in fields]


def pack_kernel(
    mine_ref,
    gain_ref,
    query_in,
    key_in,
    value_in,
    out_in,
    first_ref,
    query_ref,
    key_ref,
    value_ref,
    out_ref,
    done,
):
    mine = mine_ref[0]
    shard = query_ref.shape[0]
    four = 4 * DH
    slab = out_ref.shape[0]
    slabs = out_ref.shape[1] // four
    query_window, query_shift = window_of(query_in, mine * 2 * DH)
    key_window, shift = window_of(key_in, mine * DH)
    value_window, _ = window_of(value_in, mine * DH)
    copies = [
        fetch(source, target, done.at[index])
        for index, (source, target) in enumerate(
            (
                (query_window, query_ref),
                (key_window, key_ref),
                (value_window, value_ref),
                (out_in.at[rows_at(mine, slab), :], out_ref),
            )
        )
    ]
    for copy in copies:
        copy.wait()
    query = drawn(query_ref, query_shift)
    key = pltpu.roll(drawn(key_ref, shift)[:, :LANES], 64, 1)
    value = pltpu.roll(drawn(value_ref, shift)[:, :LANES], 32, 1)
    lane = lanes_of(shard)
    first_ref[:shard, :LANES] = narrow(query[:, :LANES])
    first_ref[:shard, LANES : 2 * LANES] = narrow(jnp.where(lane < 64, query[:, LANES:], key))
    first_ref[:shard, 2 * LANES :] = narrow(jnp.where(lane < 32, key, value))
    for index in range(slabs):
        here = shard + index * slab
        first_ref[here : here + slab, :] = out_ref[:, index * four : (index + 1) * four]
    first_ref[shard + slabs * slab :, :] = gain_ref[...]


def strip_kernel(mine_ref, gate_ref, up_ref, down_ref, all_ref):
    quarters = gate_ref.shape[1] // (8 * LANES)
    start = 2 * quarters * LANES
    for index in range(quarters):
        place = rows_at(index * 8 + mine_ref[0], LANES)
        here = index * LANES
        all_ref[:, here : here + LANES] = gate_ref[:, place]
        here += quarters * LANES
        all_ref[:, here : here + LANES] = up_ref[:, place]
    rows = down_ref.shape[0] // 8
    cut = all_ref.shape[1] - start
    for index in range(all_ref.shape[0] // rows):
        all_ref[index * rows : (index + 1) * rows, start:] = down_ref[
            rows_at(mine_ref[0], rows), index * cut : (index + 1) * cut
        ]


def fold(block):
    rows = block.shape[0]
    tail = block[:, LANES:]
    lower = jnp.where(lanes_of(rows // 2) < 64, tail[: rows // 2], pltpu.roll(tail[rows // 2 :], 64, 1))
    return jnp.concatenate([block[:, :LANES], lower], axis=0)


def unfold(block):
    rows = block.shape[0] // 3 * 2
    half = rows // 2
    tail = block[rows:]
    keep = lanes_of(half) < 64
    tail = jnp.concatenate(
        [jnp.where(keep, tail, 0.0), jnp.where(keep, pltpu.roll(tail, 64, 1), 0.0)], axis=0
    )
    return jnp.concatenate([block[:rows], tail], axis=1)


def branch_kernel(owner_ref, folded_ref, stream_ref, gain_ref, *refs):
    pieces, refs = refs[:8], refs[8:]
    one_ref, normed_ref, inverse_ref, heads_ref, full_out, full_ref, piece_ref, done = refs
    copies = [fetch(piece, piece_ref.at[i], done.at[i]) for i, piece in enumerate(pieces)]
    width = full_ref.shape[1]
    slab = width // 32
    size = 2 * DH
    four = pieces[0].shape[1]
    gap = jnp.zeros((folded_ref.shape[1] // 3 * 2, LANES), jnp.float32)
    for index in range(0, folded_ref.shape[0], 2):
        one = unfold(wide(folded_ref[index]))
        two = unfold(wide(folded_ref[index + 1]))
        both = jnp.concatenate([one, gap], axis=1) + pltpu.roll(
            jnp.concatenate([two, gap], axis=1), size, 1
        )
        heads_ref[:, index * size : (index + 2) * size] = narrow(both)
    for index, copy in enumerate(copies):
        copy.wait()
        for quarter in range(4):
            row = pl.multiple_of(quarter * 8 * slab + owner_ref[index] * slab, 16)
            for part in range(width // four):
                start = (quarter * (width // four) + part) * slab
                full_ref[pl.ds(row, slab), part * four : (part + 1) * four] = piece_ref[
                    index, start : start + slab, :
                ]
    copy = fetch(full_ref, full_out, done.at[0])
    total = wide(stream_ref[...]) + plain_dot(heads_ref[...], full_ref[...])
    one_ref[...] = total
    inverse = lax.rsqrt(jnp.mean(total * total, axis=1, keepdims=True) + epsilon)
    normed_ref[...] = narrow(total * inverse * gain_ref[8:9])
    inverse_ref[...] = jnp.broadcast_to(inverse, inverse_ref.shape)
    copy.wait()


def strips_kernel(count, carry, *refs):
    before, refs = refs[: int(carry)], refs[int(carry) :]
    normed_in, grad_in, refs = refs[:count], refs[count : 2 * count], refs[2 * count :]
    strips_in, refs = refs[0], refs[1:]
    grad_out, stream_refs, refs = refs[0], refs[1 : 1 + count], refs[1 + count :]
    sum_ref, tail_ref, both_out, *refs = refs
    down_grad, gate_up_ref, down_ref, normed_ref, grad_ref, both_ref, done, out_done, weight_done = refs
    part = down_ref.shape[0]
    rows = normed_in[0].shape[0]
    size = 2 * rows
    columns = gate_up_ref.shape[1]
    strip = down_ref.shape[0] // 4
    shard = strips_in.shape[0] // 4
    cut = strips_in.shape[1] - columns
    copies = []

    def fetch_rows(index):
        here = pl.ds(index * rows, rows)
        copies.append(
            (
                fetch(normed_in[index], normed_ref.at[here, :], done.at[index]),
                fetch(grad_in[index], grad_ref.at[here, :], done.at[count + index]),
            )
        )

    fetch_rows(0)
    fetch_rows(1)
    gate_up_copy = fetch(strips_in.at[:, pl.ds(0, columns)], gate_up_ref, weight_done.at[0])
    downs = []
    for quarter in range(4):
        for index in range(shard // strip):
            downs.append(
                fetch(
                    strips_in.at[
                        pl.ds(quarter * shard + index * strip, strip), pl.ds(columns, cut)
                    ],
                    down_ref.at[pl.ds(quarter * strip, strip), pl.ds(index * cut, cut)],
                    weight_done.at[1 + quarter * (shard // strip) + index],
                )
            )
    for index in range(2, count):
        fetch_rows(index)
    outs = []
    gate_up_copy.wait()
    for step in range(count // 2):
        for index in (2 * step, 2 * step + 1):
            copies[index][0].wait()
        here = slice(step * size, (step + 1) * size)
        normed = normed_ref[here, :]
        gate = plain_dot(normed, gate_up_ref[:, :part])
        up = plain_dot(normed, gate_up_ref[:, part:])
        sigma = jax.nn.sigmoid(gate)
        turned = gate * sigma
        hidden = narrow(turned * up)
        if step == 0:
            for copy in downs:
                copy.wait()
        for index in (2 * step, 2 * step + 1):
            copies[index][1].wait()
        grad = grad_ref[here, :]
        d_hidden = lane_dot(grad, down_ref[...])
        d_gate = narrow(d_hidden * up * sigma * (1.0 + gate * (1.0 - sigma)))
        d_up = narrow(d_hidden * turned)
        both_ref[here, :part] = d_gate
        both_ref[here, part:] = d_up
        there = pl.ds(step * size, size)
        outs.append(fetch(both_ref.at[there, :], both_out.at[there, :], out_done.at[step]))
        d_normed = narrow(
            lane_dot(d_gate, gate_up_ref[:, :part]) + lane_dot(d_up, gate_up_ref[:, part:])
        )
        sums = narrow(plain_dot(hidden, down_ref[...]))
        for index in range(2):
            block = 2 * step + index
            stream_refs[block][...] = d_normed[index * rows : (index + 1) * rows]
            if block < count - 1:
                sum_ref[block * rows : (block + 1) * rows, :] = sums[
                    index * rows : (index + 1) * rows
                ]
            else:
                tail_ref[...] = sums[index * rows : (index + 1) * rows]
        product = row_dot(hidden, grad)
        if step == 0:
            down_grad[...] = product + before[0][...] if carry else product
        elif step < count // 2 - 1:
            down_grad[...] += product
        else:
            grad_out[...] = (down_grad[...] + product).astype(grad_out.dtype)
    for copy in outs:
        copy.wait()


def strip_grad_kernel(count, *refs):
    gain_ref, refs = refs[0], refs[1:]
    normed_in, (own_in, twin_in, strips_in), refs = refs[:count], refs[count : count + 3], refs[count + 3 :]
    out_ref, row_ref, normed_ref, both_ref, weight_ref, done = refs
    size = 2 * LANES
    rows = normed_in[0].shape[0]
    half = own_in.shape[0]
    copies = [
        fetch(piece, normed_ref.at[pl.ds(index * rows, rows), :], done.at[index])
        for index, piece in enumerate(normed_in)
    ]
    copies.append(fetch(own_in, both_ref.at[pl.ds(0, half), :], done.at[count]))
    copies.append(fetch(twin_in, both_ref.at[pl.ds(half, half), :], done.at[count + 1]))
    columns = weight_ref.shape[1]
    copies.append(fetch(strips_in.at[:, pl.ds(0, columns)], weight_ref, done.at[count + 2]))
    for copy in copies:
        copy.wait()
    ones = jnp.ones((8, out_ref.shape[1]), jnp.bfloat16)

    def one(index, _):
        columns = rows_at(index, size)
        total = row_dot(normed_ref[:, columns], both_ref[...])
        out_ref[columns, :] = narrow(total)
        share = narrow(total * wide(weight_ref[columns, :]))
        row_ref[:, columns] = lane_dot(ones, share) / gain_ref[8:, columns]
        return 0

    lax.fori_loop(0, out_ref.shape[0] // size, one, 0)


def add_twin_kernel(core_ref, *refs):
    (*refs, send_ref, keep_ref, self_ref) = refs
    rows = keep_ref.shape[0]
    count = len(refs) // 2
    core = core_ref[0]

    def total(index):
        if count == 4:
            return wide(refs[index][...]) + wide(refs[4 + index][...])
        here = slice(index * rows, (index + 1) * rows)
        if count == 1:
            return wide(refs[0][here, :]) + wide(refs[1][here, :])
        before = slice((index - 1) * rows, index * rows)
        own = refs[1][before, :] if index else refs[0][...]
        twin = refs[2][here, :] if index < 3 else refs[3][...]
        return wide(own) + wide(twin)

    self_ref[...] = total(0)
    send_ref[:rows, :] = narrow(total(3))
    along_x = total(1)
    along_y = total(2)

    @pl.when(core == 0)
    def _():
        send_ref[rows:, :] = narrow(along_y)
        keep_ref[...] = along_x

    @pl.when(core == 1)
    def _():
        send_ref[rows:, :] = narrow(along_x)
        keep_ref[...] = along_y


def add_late_kernel(keep_in, got_in, late_ref, keep_ref, got_ref, done):
    rows = keep_ref.shape[0]
    copies = (
        fetch(keep_in, keep_ref, done.at[0]),
        fetch(got_in.at[pl.ds(0, rows), :], got_ref, done.at[1]),
    )
    for copy in copies:
        copy.wait()
    late_ref[...] = narrow(keep_ref[...] + wide(got_ref[...]))


def summed(self_ref, got_ref, late_ref):
    rows = self_ref.shape[0]
    return self_ref[...] + wide(got_ref[rows:, :]) + wide(late_ref[...])


def norm_down(d_normed, stream, inverse, gain):
    scaled = d_normed * gain
    cubed = inverse * inverse * inverse
    return inverse * scaled - stream * cubed * jnp.mean(scaled * stream, axis=1, keepdims=True)


def branch_back_kernel(
    self_ref,
    got_ref,
    late_ref,
    grad_ref,
    one_ref,
    inverse_ref,
    gain_ref,
    full_ref,
    stream_out,
    heads_out,
):
    d_normed = summed(self_ref, got_ref, late_ref)
    d_stream = wide(grad_ref[...]) + norm_down(
        d_normed, one_ref[...], inverse_ref[:, :1], gain_ref[8:9]
    )
    stream_out[...] = d_stream
    d_branch = narrow(d_stream)
    rows = d_branch.shape[0]
    size = 2 * DH
    gap = jnp.zeros((rows, 2 * LANES - size), jnp.float32)
    keep = lanes_of(rows) < size - LANES
    tall = heads_out.shape[1] // 2
    for index in range(heads_out.shape[0]):
        heads = lane_dot(d_branch, full_ref[index * size : (index + 1) * size, :])
        heads_out[index, :tall, :] = narrow(fold(jnp.concatenate([heads, gap], axis=1)))
        start = index * size // LANES * LANES
        columns = wide(d_branch[:, start : start + 2 * LANES])
        if index % 2:
            columns = pltpu.roll(columns, 2 * LANES - 64, 1)
        columns = jnp.concatenate(
            [columns[:, :LANES], jnp.where(keep, columns[:, LANES:], 0.0)], axis=1
        )
        heads_out[index, tall:, :] = narrow(fold(columns))


def stream_grad_kernel(start, fields_ref, weight_ref, out_ref):
    rows = out_ref.shape[0]
    size = rows // 2
    for step in range(2):
        here = slice(step * size, (step + 1) * size)
        there = slice(start + step * size, start + (step + 1) * size)
        out_ref[here, :] = narrow(lane_dot(fields_ref[there, :], weight_ref[...]))


def place_strips_kernel(owner_ref, *refs):
    pieces, (gate_out, up_out, low_ref, wide_ref, done, out_done) = refs[:-6], refs[-6:]
    copies = [fetch(piece, low_ref.at[i], done.at[i]) for i, piece in enumerate(pieces)]
    quarters = low_ref.shape[2] // (2 * LANES)
    outs = []
    for index, copy in enumerate(copies):
        copy.wait()
        wide_ref[index] = wide(low_ref[index])
        for part in range(2 * quarters):
            there = rows_at(part % quarters * 8 + owner_ref[index], LANES)
            target = gate_out if part < quarters else up_out
            outs.append(
                fetch(
                    wide_ref.at[index, :, pl.ds(part * LANES, LANES)],
                    target.at[:, there],
                    out_done.at[index, part],
                )
            )
    for copy in outs:
        copy.wait()


def place_down_kernel(owner_ref, *refs):
    pieces, (down_out, low_ref, wide_ref, done) = refs[:-4], refs[-4:]
    copies = [fetch(piece, low_ref.at[i], done.at[0, i]) for i, piece in enumerate(pieces)]
    outs = []
    for index, copy in enumerate(copies):
        copy.wait()
        wide_ref[index] = wide(low_ref[index])
        there = rows_at(owner_ref[index], wide_ref.shape[1])
        outs.append(fetch(wide_ref.at[index], down_out.at[there, :], done.at[1, index]))
    for copy in outs:
        copy.wait()


def place_last(copies, low_ref, refs, outs, gain_ref, out_done):
    query_ref, key_ref, value_ref, out_ref = refs
    shard = query_ref.shape[0]
    half = shard // 2
    end = shard + half
    for copy in copies:
        copy.wait()
    full = lanes_of(shard) < 64
    keep = lanes_of(half) < 64
    gains = jnp.zeros(gain_ref.shape, jnp.float32)
    targets = []
    for quad in range(2):
        keys, values = [], []
        for pair in (2 * quad, 2 * quad + 1):
            columns = slice(pair * 4 * DH, (pair + 1) * 4 * DH)
            tiles = []
            for index in (2 * pair, 2 * pair + 1):
                block = wide(low_ref[index, :shard, :])
                one, two, key, value = part_fields(block)
                keys.append(key)
                values.append(value)
                tiles.append((block[:, :LANES], block[:, LANES : 2 * LANES]))
                gains = gains + wide(low_ref[index, end : end + 16, :])
            (one, two), (three, four) = tiles
            three, four = pltpu.roll(three, 64, 1), pltpu.roll(four, 64, 1)
            query_ref[:, columns] = jnp.concatenate(
                [one, jnp.where(full, two, three), jnp.where(full, three, four)], axis=1
            )
            for part in range(2):
                tiles = []
                for index in (2 * pair, 2 * pair + 1):
                    block = wide(low_ref[index, shard:end, :])
                    one, two, three = (
                        block[:, start : start + LANES] for start in (0, LANES, 2 * LANES)
                    )
                    if part:
                        two, three = pltpu.roll(two, 64, 1), pltpu.roll(three, 64, 1)
                        one, two = jnp.where(keep, two, three), three
                    tiles.append((one, two))
                (one, two), (three, four) = tiles
                three, four = pltpu.roll(three, 64, 1), pltpu.roll(four, 64, 1)
                out_ref[part * half : (part + 1) * half, columns] = jnp.concatenate(
                    [one, jnp.where(keep, two, three), jnp.where(keep, three, four)], axis=1
                )
        columns = slice(quad * 4 * DH, (quad + 1) * 4 * DH)
        key_ref[:, columns] = join_fields(*keys)
        value_ref[:, columns] = join_fields(*values)
        wide_columns = pl.ds(quad * 8 * DH, 8 * DH)
        some_columns = pl.ds(quad * 4 * DH, 4 * DH)
        for index, (ref, out, here) in enumerate(
            (
                (query_ref, outs[0], wide_columns),
                (key_ref, outs[1], some_columns),
                (value_ref, outs[2], some_columns),
                (out_ref, outs[3], wide_columns),
            )
        ):
            targets.append(fetch(ref.at[:, here], out.at[:, here], out_done.at[4 * quad + index]))
    gain_ref[...] = gains
    return targets


def finish_kernel(
    owner_ref,
    ffn_self,
    ffn_got,
    ffn_late,
    one_ref,
    self_ref,
    got_ref,
    late_ref,
    stream_ref,
    back_ref,
    norm_ref,
    *refs,
):
    last_pieces, gain_ref, refs = refs[:8], refs[8], refs[9:]
    (layer_out, input_out, *last_outs), refs = refs[:6], refs[6:]
    layer_ref, input_ref, last_low, *refs = refs
    last_refs, (done, out_done, last_done) = refs[:4], refs[4:]
    lasts = [
        fetch(piece, last_low.at[owner_ref[index]], done.at[index])
        for index, piece in enumerate(last_pieces)
    ]
    layer_ref[...] = narrow(one_ref[...] + summed(ffn_self, ffn_got, ffn_late))
    outs = [fetch(layer_ref, layer_out, out_done.at[0])]
    d_normed = summed(self_ref, got_ref, late_ref)
    stream = wide(stream_ref[...])
    inverse = lax.rsqrt(jnp.mean(stream * stream, axis=1, keepdims=True) + epsilon)
    input_ref[...] = back_ref[...] + norm_down(d_normed, stream, inverse, norm_ref[:1])
    outs.append(fetch(input_ref, input_out, out_done.at[1]))
    outs += place_last(lasts, last_low, last_refs, last_outs, gain_ref, last_done)
    for copy in outs:
        copy.wait()


def swapped(field):
    half = DH // 2
    lane = lanes_of(field.shape[0])
    return jnp.where(lane < half, pltpu.roll(field, LANES - half, 1), pltpu.roll(field, half, 1))


def rows_of(weights, field):
    return lax.dot_general(
        weights,
        field,
        (((1,), (1,)), ((), ())),
        precision=lax.Precision.HIGHEST,
        preferred_element_type=jnp.float32,
    )


def fetch(source, target, done):
    copy = pltpu.make_async_copy(source, target, done)
    copy.start()
    return copy


def attend_kernel(
    span,
    near_ref,
    slot_ref,
    cos_ref,
    sin_ref,
    *refs,
):
    (*piece_refs, first_ref), refs = refs[:9], refs[9:]
    (low_ref, gain_ref, level_ref), refs = refs[:3], refs[3:]
    (normed_out, weight_out, query_out, key_out, value_out, mixed_out), refs = refs[:6], refs[6:]
    stream_ref, weight_ref, gains_ref, raw_ref, query_ref, key_ref, value_ref, mixed_ref = refs[:8]
    score_ref, top_ref, sum_ref, in_done, out_done = refs[8:]
    spans = near_ref.shape[0]
    block = 2 * span
    pair = 2 * block
    turns = spans // 2
    quarters, packed, four = first_ref.shape
    shard = weight_ref.shape[0] // quarters
    factor = LOG2E / math.sqrt(DH)

    gain_copies = [
        fetch(
            first_ref.at[quarter, pl.ds(packed - 32, 32), :],
            gains_ref.at[pl.ds(quarter * 32, 32), :],
            in_done.at[turns + quarter],
        )
        for quarter in range(quarters)
    ]
    weight_copies = [
        fetch(
            first_ref.at[quarter, pl.ds(0, shard), :],
            weight_ref.at[pl.ds(quarter * shard, shard), :],
            in_done.at[turns + quarters + quarter],
        )
        for quarter in range(quarters)
    ]
    copies = [
        fetch(piece, stream_ref.at[pl.ds(index * block, block), :], in_done.at[index])
        for index, piece in enumerate(piece_refs)
    ]
    for copy in gain_copies:
        copy.wait()
    for quarter in range(quarters):
        rows = wide(gains_ref[quarter * 32 : quarter * 32 + 16, :])
        here = slice(quarter * shard, (quarter + 1) * shard)
        gain_ref[:8, here] = jnp.broadcast_to(rows[:1, :shard], (8, shard))
        gain_ref[8:, here] = jnp.broadcast_to(rows[1:2, :shard], (8, shard))
    for copy in weight_copies:
        copy.wait()
    out_copies = [fetch(weight_ref, weight_out, out_done.at[0])]
    gain = gain_ref[:1, :]

    def norm(start):
        here = pl.ds(start, span)
        stream = wide(stream_ref[here, :])
        inverse = lax.rsqrt(jnp.mean(stream * stream, axis=1, keepdims=True) + epsilon)
        stream_ref[here, :] = narrow(stream * inverse * gain)

    for step in range(turns // 2):
        copies[2 * step].wait()
        copies[2 * step + 1].wait()
        here = pl.ds(step * pair, pair)
        for part in range(4):
            norm(step * pair + part * span)
        raw_ref[here, :] = plain_dot(stream_ref[here, :], weight_ref[...])
        out_copies.append(
            fetch(stream_ref.at[here, :], normed_out.at[here, :], out_done.at[1 + step])
        )

    lane = lanes_of(span)

    def place(index, _):
        raw = raw_ref[rows_at(near_ref[index], span), :]
        cosine = cos_ref[rows_at(index, span), :]
        sine = sin_ref[rows_at(index, span), :]
        one, two, three, four = part_fields(raw)

        def turned(field):
            return narrow(field * cosine + swapped(field) * sine)

        first = (index // 2) * 4 + index % 2
        query_ref[rows_at(first, span), :] = turned(one)
        query_ref[rows_at(first + 2, span), :] = turned(two)
        key_ref[rows_at(index, span), :] = turned(three)
        value_ref[rows_at(index, span), :] = narrow(jnp.where(lane == DH, 1.0, four))
        return 0

    lax.fori_loop(0, spans, place, 0, unroll=2)
    next_done = 1 + turns // 2
    for source, target in ((query_ref, query_out), (key_ref, key_out), (value_ref, value_out)):
        out_copies.append(fetch(source, target, out_done.at[next_done]))
        next_done += 1

    wide_lane = lanes_of(pair)
    picked = (lanes_of(8) == 0).astype(jnp.float32)

    def store(index, both, rest):
        slot = slot_ref[index]
        low_ref[slot // 2, rows_at(slot % 2, span), :] = narrow(both)
        tail = narrow(rest)
        turned = narrow(pltpu.roll(rest, 64, 1))

        @pl.when(slot % 2 == 0)
        def _():
            low_ref[slot // 2, 2 * span :, :64] = tail[:, :64]

        @pl.when(slot % 2 == 1)
        def _():
            low_ref[slot // 2, 2 * span :, 64:] = turned[:, 64:]

    def widest(top, scores):
        for start in range(0, block, LANES):
            top = jnp.maximum(top, scores[:, start : start + LANES])
        return top

    def score(turn, step):
        scores = lane_dot(query_ref[rows_at(turn, pair), :], key_ref[rows_at(step, block), :])
        score_ref[turn % 2, :, rows_at(step, block)] = scores
        top_ref[...] = widest(top_ref[...], scores)

    def edge(turn):
        row = lax.broadcasted_iota(jnp.int32, (pair, block), 0) % block
        column = lax.broadcasted_iota(jnp.int32, (pair, block), 1)
        scores = lane_dot(query_ref[rows_at(turn, pair), :], key_ref[rows_at(turn, block), :])
        scores = jnp.where(column <= row, scores, masked_score)
        score_ref[turn % 2, :, rows_at(turn, block)] = scores
        top = jnp.max(widest(top_ref[...], scores), axis=1, keepdims=True) * factor
        return jnp.broadcast_to(top, (pair, LANES))

    def weigh(turn, step, top):
        scores = score_ref[turn % 2, :, rows_at(step, block)]
        weights = jnp.exp2(scores * factor - top[:, :1])
        sum_ref[...] += plain_dot(narrow(weights), value_ref[rows_at(step, block), :])

    def finish(turn, top):
        total = sum_ref[:, DH : DH + 1]
        mixed = jnp.where(wide_lane < DH, sum_ref[...] / total, 0.0)
        mixed_ref[rows_at(turn, pair), :] = mixed
        level = top + jnp.log2(total)
        level_ref[rows_at(turn, 8), :] = rows_of(picked, level)
        fetch(
            mixed_ref.at[rows_at(turn, pair), :],
            mixed_out.at[rows_at(turn, pair), :],
            out_done.at[next_done + turn],
        )
        one, two = mixed[:block], pltpu.roll(mixed[block:], DH, 1)
        first = jnp.where(wide_lane[:block] < DH, one, two)
        store(2 * turn, first[:span], two[:span])
        store(2 * turn + 1, first[span:], two[span:])

    def clear():
        sum_ref[...] = jnp.zeros_like(sum_ref)
        top_ref[...] = jnp.full(top_ref.shape, masked_score, jnp.float32)

    def one_turn(turn, top):
        clear()

        def both(step, _):
            weigh(turn, step, top)
            score(turn + 1, step)
            return 0

        lax.fori_loop(0, turn + 1, both, 0)
        finish(turn, top)
        return edge(turn + 1)

    clear()
    top = lax.fori_loop(0, turns - 1, one_turn, edge(0))
    clear()

    def only(step, _):
        weigh(turns - 1, step, top)
        return 0

    lax.fori_loop(0, turns, only, 0)
    finish(turns - 1, top)
    for copy in out_copies:
        copy.wait()
    for turn in range(turns):
        here = pl.ds(turn * pair, pair)
        pltpu.make_async_copy(
            mixed_ref.at[here, :], mixed_out.at[here, :], out_done.at[next_done + turn]
        ).wait()


def attend(steps, near, slot, cosine, sine, first, pieces, span):
    tokens = cosine.shape[0]
    turns = tokens // (2 * span)
    quarters, _, four = first.shape
    block, width = pieces[0].shape
    f32 = jnp.float32
    near_out = (
        shape((turns, 3 * span, LANES)),
        shape((16, width), f32),
        shape((8 * turns, 4 * span), f32),
    )
    far_out = (
        shape((tokens, width)),
        shape((width, four)),
        shape((2 * tokens, LANES)),
        shape((tokens, LANES)),
        shape((tokens, LANES)),
        shape((2 * tokens, LANES), f32),
    )
    state = pltpu.VMEM((4 * span, LANES), f32)
    return steps.run(
        functools.partial(attend_kernel, span),
        near_out,
        (near, slot),
        (cosine, sine),
        far=(*pieces,),
        pinned=(first,),
        far_outs=far_out,
        scratch=(
            pltpu.VMEM((tokens, width), jnp.bfloat16),
            pltpu.VMEM((width, four), jnp.bfloat16),
            pltpu.VMEM((32 * quarters, four), jnp.bfloat16),
            pltpu.VMEM((tokens, four), f32),
            pltpu.VMEM((2 * tokens, LANES), jnp.bfloat16),
            pltpu.VMEM((tokens, LANES), jnp.bfloat16),
            pltpu.VMEM((tokens, LANES), jnp.bfloat16),
            pltpu.VMEM((2 * tokens, LANES), f32),
            pltpu.VMEM((2, 4 * span, tokens), f32),
            state,
            state,
            pltpu.SemaphoreType.DMA((turns + 2 * quarters,)),
            pltpu.SemaphoreType.DMA((4 + turns // 2 + turns,)),
        ),
        limit=60,
        micros=33,
    )


def weight_grads(
    owner_ref, fields_ref, weight_ref, gain_ref, row_ref, branch_ref, heads, copies, last_ref, normed_ref, heads_ref, sum_ref
):
    quarters = last_ref.shape[0]
    four = weight_ref.shape[1]
    shard = weight_ref.shape[0] // quarters
    half = shard // 2
    size = 2 * DH
    tall = branch_ref.shape[1] // 2
    for index, copy in enumerate(heads):
        columns = narrow(unfold(wide(branch_ref[owner_ref[index], tall:, :])))
        copy.wait()
        rows = columns.shape[0]
        sum_ref[index * rows : (index + 1) * rows, :] = columns
    ones = jnp.ones((8, four), jnp.bfloat16)
    gap = jnp.zeros((half, LANES), jnp.float32)
    for quarter in range(quarters):
        here = slice(quarter * shard, (quarter + 1) * shard)
        copies[quarter].wait()
        total = row_dot(normed_ref[:, here], fields_ref[...])
        last_ref[quarter, :shard, :] = narrow(total)
        share = narrow(total * wide(weight_ref[here, :]))
        attn = lane_dot(ones, share) / gain_ref[:8, here]
        rows = jnp.concatenate([attn, row_ref[:, here]], axis=0)
        out_grad = row_dot(heads_ref[:, here], sum_ref[...])
        one, two = out_grad[:half], out_grad[half:]
        both = jnp.concatenate([one, gap], axis=1) + pltpu.roll(
            jnp.concatenate([two, gap], axis=1), size, 1
        )
        last_ref[quarter, shard : shard + half, :] = narrow(both)
        end = shard + half
        last_ref[quarter, end : end + 16, :] = narrow(rows)
        last_ref[quarter, end + 16 :, :] = jnp.zeros_like(last_ref[quarter, end + 16 :, :])


def attend_back_kernel(
    span,
    near_ref,
    slot_ref,
    owner_ref,
    grad_ref,
    total_ref,
    weight_ref,
    gain_ref,
    row_ref,
    *refs,
):
    (*heads_in, normed_in, cos_in, sin_in, query_in, key_in, value_in, mixed_in), refs = refs[:15], refs[15:]
    out_ref, last_ref, cos_ref, sin_ref, query_ref, key_ref, value_ref, mixed_ref, *refs = refs
    head_ref, delta_ref, query_sum, key_sum, value_sum, normed_ref, heads_ref, sum_ref, done = refs
    spans = near_ref.shape[0]
    block = 2 * span
    pair = 2 * block
    turns = spans // 2
    factor = LOG2E / math.sqrt(DH)
    scale = 1.0 / math.sqrt(DH)
    lane = lax.broadcasted_iota(jnp.int32, (span, LANES), 1)
    copies = [
        fetch(source, target, done.at[index])
        for index, (source, target) in enumerate(
            (
                (mixed_in, mixed_ref),
                (key_in, key_ref),
                (query_in, query_ref),
                (value_in, value_ref),
                (cos_in, cos_ref),
                (sin_in, sin_ref),
            )
        )
    ]

    quarters = last_ref.shape[0]
    shard = normed_ref.shape[1] // quarters
    heads = [
        fetch(piece, heads_ref.at[pl.ds(index * block, block), :], done.at[6 + index])
        for index, piece in enumerate(heads_in)
    ]
    normed = [
        fetch(
            normed_in.at[:, pl.ds(quarter * shard, shard)],
            normed_ref.at[:, pl.ds(quarter * shard, shard)],
            done.at[6 + len(heads) + quarter],
        )
        for quarter in range(quarters)
    ]

    def split(index, _):
        slot = slot_ref[index]
        grad = wide(grad_ref[slot // 2, rows_at(slot % 2, span), :])
        tail = wide(grad_ref[slot // 2, 2 * span : 3 * span, :])
        first = (index // 2) * 4 + index % 2
        one = jnp.where(lane < DH, grad, 0.0)
        tail = pltpu.roll(tail, 32 + 64 * (slot % 2), 1)
        two = jnp.where(lane < 32, pltpu.roll(grad, 32, 1), tail)
        two = jnp.where(lane < DH, two, 0.0)
        head_ref[rows_at(first, span), :] = narrow(one)
        head_ref[rows_at(first + 2, span), :] = narrow(two)
        return 0

    lax.fori_loop(0, spans, split, 0, unroll=4)
    copies[0].wait()

    def prepare(turn, _):
        here = rows_at(turn, pair)
        product = wide(head_ref[here, :]) * mixed_ref[here, :]
        delta_ref[rows_at(turn, 8), :] = rows_of(jnp.ones((8, LANES), jnp.float32), product)
        query_sum[here, :] = jnp.zeros((pair, LANES), jnp.float32)
        return 0

    lax.fori_loop(0, turns, prepare, 0, unroll=2)
    for copy in copies[1:]:
        copy.wait()

    def turned_back(field, index):
        cosine = cos_ref[rows_at(index, span), :]
        sine = sin_ref[rows_at(index, span), :]
        field = field * scale
        return wide(narrow(field * cosine - swapped(field) * sine))

    def one_block(turn, _):
        key = key_ref[rows_at(turn, block), :]
        value = value_ref[rows_at(turn, block), :]

        def one_step(step, diagonal):
            here = rows_at(step, pair)
            query = query_ref[here, :]
            head = head_ref[here, :]
            level = total_ref[rows_at(step, 8), :][:1]
            delta = delta_ref[rows_at(step, 8), :][:1]
            probs = jnp.exp2(lane_dot(key, query) * factor - level)
            if diagonal:
                row = lax.broadcasted_iota(jnp.int32, (block, pair), 0)
                column = lax.broadcasted_iota(jnp.int32, (block, pair), 1) % block
                probs = jnp.where(row <= column, probs, 0.0)
            d_scores = narrow(probs * (lane_dot(value, head) - delta))
            query_sum[here, :] += row_dot(d_scores, key)
            return plain_dot(d_scores, query), plain_dot(narrow(probs), head)

        key_part, value_part = one_step(turn, True)
        key_sum[...] = key_part
        value_sum[...] = value_part

        def two_steps(index, _):
            step = turn + 1 + 2 * index
            key_one, value_one = one_step(step, False)
            key_two, value_two = one_step(step + 1, False)
            key_sum[...] += key_one + key_two
            value_sum[...] += value_one + value_two
            return 0

        left = turns - 1 - turn
        lax.fori_loop(0, left // 2, two_steps, 0)

        @pl.when(left % 2 == 1)
        def _():
            key_one, value_one = one_step(turns - 1, False)
            key_sum[...] += key_one
            value_sum[...] += value_one

        for part in range(2):
            index = 2 * turn + part
            here = rows_at(near_ref[index], span)
            rows = slice(part * span, (part + 1) * span)
            first = rows_at((index // 2) * 4 + index % 2, span)
            second = rows_at((index // 2) * 4 + index % 2 + 2, span)
            one = turned_back(query_sum[first, :], index)
            two = turned_back(query_sum[second, :], index)
            three = turned_back(key_sum[rows, :], index)
            out_ref[here, :] = narrow(join_fields(one, two, three, value_sum[rows, :]))
        return 0

    lax.fori_loop(0, turns, one_block, 0)
    weight_grads(
        owner_ref, out_ref, weight_ref, gain_ref, row_ref, grad_ref, heads, normed, last_ref, normed_ref, heads_ref, sum_ref
    )


def attend_back(
    steps, near, slot, owners, grad, total, weights, cosine, sine, query, key, value, mixed, heads, normed, packed, span
):
    tokens, width = normed.shape
    f32 = jnp.float32
    rows = pltpu.VMEM((2 * span, LANES), f32)
    shard = 4 * DH
    return steps.run(
        functools.partial(attend_back_kernel, span),
        (shape((tokens, 4 * DH)), shape((width // shard, packed, 4 * DH))),
        (near, slot, owners),
        (grad, total, *weights),
        far=heads,
        pinned=(normed, cosine, sine, query, key, value, mixed),
        scratch=(
            pltpu.VMEM(cosine.shape, f32),
            pltpu.VMEM(cosine.shape, f32),
            pltpu.VMEM(query.shape, jnp.bfloat16),
            pltpu.VMEM(key.shape, jnp.bfloat16),
            pltpu.VMEM(value.shape, jnp.bfloat16),
            pltpu.VMEM(mixed.shape, f32),
            pltpu.VMEM((2 * tokens, LANES), jnp.bfloat16),
            pltpu.VMEM(total.shape, f32),
            pltpu.VMEM((2 * tokens, LANES), f32),
            rows,
            rows,
            pltpu.VMEM((tokens, width), jnp.bfloat16),
            pltpu.VMEM((tokens, width), jnp.bfloat16),
            pltpu.VMEM((tokens, 2 * LANES), jnp.bfloat16),
            pltpu.SemaphoreType.DMA((6 + len(heads) + width // shard,)),
        ),
        limit=60,
        micros=38,
    )


def turn_tables(tokens):
    half = DH // 2
    freqs = jnp.exp(-math.log(rope_base) * 2.0 * jnp.arange(half, dtype=jnp.float32) / DH)
    angle = jnp.arange(tokens, dtype=jnp.int32).astype(jnp.float32)[:, None] * freqs[None, :]
    gap = jnp.zeros((tokens, LANES - DH), jnp.float32)
    cosine, sine = jnp.cos(angle), jnp.sin(angle)
    return (
        jnp.concatenate([cosine, cosine, gap], axis=1),
        jnp.concatenate([-sine, sine, gap], axis=1),
    )


def swap(block, bits):
    routes = [(i, i ^ bits) for i in range(lax.axis_size("ctx"))]
    return lax.ppermute(block, "ctx", routes)


def swap_split(block, even, odd):
    routes = [(i, i ^ (odd if i & CORE else even)) for i in range(lax.axis_size("ctx"))]
    return lax.ppermute(block, "ctx", routes)


def gather_spans(block, core, between=None):
    from_x = swap(block, ALONG_X)
    from_y = swap(block, ALONG_Y)
    twin = swap(block, CORE)
    first = between(from_x, from_y) if between else from_x
    corner = swap_split(jnp.where(core[0] == 0, first, from_y), ALONG_Y, ALONG_X)
    return [block, from_x, from_y, corner] + [
        twin,
        swap(first, CORE),
        swap(from_y, CORE),
        swap(corner, CORE),
    ]


def gather_direct(block):
    blocks = [block] + [swap(block, way) for way in (ALONG_X, ALONG_Y, ALONG_X | ALONG_Y)]
    return blocks + [swap(part, CORE) for part in blocks]


def open_scatter(steps, own, twin, core, limit=20):
    rows, width = sum(part.shape[0] for part in own) // 4, own[0].shape[1]
    some = shape((rows, width), jnp.float32)
    return steps.run(
        add_twin_kernel,
        (shape((2 * rows, width)), some, some),
        (core,),
        (*own, *twin),
        limit=limit,
    )


def turn_scatter(steps, keep, got):
    late = steps.run(
        add_late_kernel,
        shape(keep.shape),
        (),
        (),
        far=(keep, got),
        scratch=(
            pltpu.VMEM(keep.shape, jnp.float32),
            pltpu.VMEM(keep.shape, jnp.bfloat16),
            pltpu.SemaphoreType.DMA((2,)),
        ),
        limit=60,
    )
    return swap_split(late, ALONG_X, ALONG_Y)


def plane_layer(
    activations,
    span_order,
    w_query,
    w_key,
    w_value,
    w_out,
    w_gate,
    w_up,
    w_down,
    attn_gain,
    ffn_gain,
    cotangent,
):
    f32 = jnp.float32
    cycles = lax.axis_size("ctx")
    quarters = lax.axis_size("fsdp")
    mine = lax.axis_index("ctx")
    span = activations.shape[2]
    width = activations.shape[3]
    tokens = 2 * span
    length = cycles * tokens
    half = length // 2
    shard = w_query.shape[0]
    four = 4 * DH
    hidden_size = quarters * w_down.shape[0]
    strip = hidden_size // (quarters * cycles)
    part = hidden_size // cycles
    slab = w_out.shape[0] // cycles
    slabs = width // four
    packed = shard + slabs * slab + 32
    owners = mine ^ jnp.array(RELATIVE, jnp.int32)
    away = mine ^ jnp.arange(cycles, dtype=jnp.int32)
    seat = (away & 1) * 4 + (away >> 2) * 2 + ((away >> 1) & 1)
    slot_of = jnp.argsort(span_order).astype(jnp.int32)
    near_slot = 2 * seat[slot_of // 2] + slot_of % 2
    here = mine.reshape(1).astype(jnp.int32)
    core = here & CORE
    stream = activations.reshape(tokens, width)
    grad_rows = cotangent.reshape(tokens, width)

    steps = Steps(core)
    low = jnp.bfloat16

    gains = jnp.pad(jnp.stack([attn_gain, ffn_gain]), ((0, 30), (0, four - shard)))
    window = pltpu.VMEM((shard, 2 * LANES), low)
    first = steps.run(
        pack_kernel,
        shape((packed, four)),
        (here,),
        (gains,),
        pinned=(w_query, w_key, w_value, w_out),
        scratch=(
            window,
            window,
            window,
            pltpu.VMEM((slab, width), low),
            pltpu.SemaphoreType.DMA((4,)),
        ),
        limit=60,
    )
    first = lax.all_gather(first, "fsdp", axis=0)
    own_strips = steps.run(
        strip_kernel,
        shape((shard, 2 * part + width * strip // shard)),
        (here,),
        (w_gate, w_up, w_down),
        limit=28,
    )
    all_strips = lax.all_gather(own_strips, "fsdp", axis=0, tiled=True)
    cosine, sine = turn_tables(length)
    streams = gather_spans(
        stream, core, lambda one, two: after(one, two, own_strips, cosine, sine, near_slot, slot_of)
    )
    out_part = first[:, shard : shard + slabs * slab].reshape(quarters * slabs * slab, four)
    folded, gains, level, normed1, w_fields, query, key, value, attended = attend(
        steps, near_slot, slot_of, cosine, sine, first, streams, span
    )
    grads = gather_spans(
        after(grad_rows, streams[3]), core, lambda one, two: after(one, two, folded)
    )
    outs = gather_direct(out_part)
    steps.wait(*outs, grads[3])
    folded = lax.all_to_all(after(folded, *grads[1:3], *outs[1:4]), "ctx", 0, 0)
    one_tile = shape((tokens, LANES), f32)
    stream_one, normed2, inverse, heads_low, full_out = steps.run(
        branch_kernel,
        (shape((tokens, width), f32), shape((tokens, width)), one_tile, shape((tokens, width))),
        (owners,),
        (folded, stream, gains),
        far=outs,
        far_outs=(shape((width, width)),),
        scratch=(
            pltpu.VMEM((width, width), low),
            pltpu.VMEM((cycles, *outs[0].shape), low),
            pltpu.SemaphoreType.DMA((cycles,)),
        ),
        limit=60,
        micros=6,
    )
    normed2 = gather_spans(normed2, core)
    def strips(pieces, grad_pieces, *before):
        results = steps.run(
            functools.partial(strips_kernel, len(pieces), bool(before)),
            (
                shape((part, width), low if before else f32),
                *(shape((tokens, width)),) * 4,
                shape((3 * tokens, width)),
                shape((tokens, width)),
            ),
            (),
            before,
            far=(*pieces, *grad_pieces),
            pinned=(all_strips,),
            far_outs=(shape((half, 2 * part)),),
            scratch=(
                pltpu.VMEM((part, width), f32),
                pltpu.VMEM((width, 2 * part), low),
                pltpu.VMEM((part, width), low),
                pltpu.VMEM((half, width), low),
                pltpu.VMEM((half, width), low),
                pltpu.VMEM((half, 2 * part), low),
                pltpu.SemaphoreType.DMA((2 * len(pieces),)),
                pltpu.SemaphoreType.DMA((len(pieces) // 2,)),
                pltpu.SemaphoreType.DMA((1 + quarters * (shard // strip),)),
            ),
                limit=60,
            micros=20,
        )
        return results[0], results[1:5], results[5], results[6], results[7]

    early, later = (4, 5, 6, 0), (1, 2, 3, 7)
    down_early, streams_early, sums_twin, sum_self, both_early = strips(
        [normed2[i] for i in early], [grads[i] for i in early]
    )
    heads = gather_spans(
        after(heads_low, normed2[1], normed2[2]), core, lambda one, two: after(one, two, down_early)
    )
    steps.wait(heads[1], heads[2])
    twins = [swap(block, CORE) for block in streams_early[:3]]
    normed2[7] = swap(after(normed2[3], down_early), CORE)
    down_sum, streams_later, sums_own, sum_corner, both_later = strips(
        [normed2[i] for i in later], [grads[i] for i in later], down_early
    )
    twins.append(swap(streams_later[3], CORE))
    grad_down = lax.psum_scatter(
        after(down_sum, heads[3]), "fsdp", scatter_dimension=0, tiled=True
    )
    sums_twin = swap(after(sums_twin, down_sum), CORE)
    sum_corner = swap(sum_corner, CORE)
    send, keep, total = open_scatter(
        steps, (streams_early[3], *streams_later[:3]), twins, core, 60
    )
    got = swap_split(send, ALONG_Y, ALONG_X)
    steps.wait(heads[3])
    grad_both, grad_ffn = steps.run(
        functools.partial(strip_grad_kernel, cycles),
        (shape((width, 2 * part)), shape((8, width), f32)),
        (),
        (gains,),
        far=[normed2[i] for i in early + later],
        pinned=(both_early, both_later, all_strips),
        scratch=(
            pltpu.VMEM((length, width), low),
            pltpu.VMEM((length, 2 * part), low),
            pltpu.VMEM((width, 2 * part), low),
            pltpu.SemaphoreType.DMA((cycles + 3,)),
        ),
        limit=60,
        micros=12,
    )
    grad_both = lax.psum_scatter(after(grad_both, got), "fsdp", scatter_dimension=0, tiled=True)
    late_got = turn_scatter(steps, keep, got)
    ffn_send, ffn_keep, ffn_total = open_scatter(
        steps, (sum_self, sums_own), (sums_twin, sum_corner), core
    )
    d_stream_one, d_heads = steps.run(
        branch_back_kernel,
        (
            shape((tokens, width), f32),
            shape((cycles, 6 * span, LANES)),
        ),
        (),
        (total, got, late_got, grad_rows, stream_one, inverse, gains, full_out),
        limit=28,
        micros=4,
    )
    d_heads = lax.all_to_all(d_heads, "ctx", 0, 0)
    ffn_got = swap_split(after(ffn_send, d_heads), ALONG_Y, ALONG_X)
    grad_downs = gather_direct(after(grad_down, d_heads))
    d_fields, last = attend_back(
        steps,
        near_slot,
        slot_of,
        owners,
        d_heads,
        level,
        (w_fields, gains, grad_ffn),
        cosine,
        sine,
        query,
        key,
        value,
        attended,
        heads,
        normed1,
        packed,
        span,
    )
    last = after(last, ffn_got, *grad_downs[1:4])
    last = lax.psum_scatter(last, "fsdp", scatter_dimension=0, tiled=False)
    steps.wait(ffn_got, *grad_downs[1:4])

    def stream_grad(start):
        return steps.run(
            functools.partial(stream_grad_kernel, start),
            shape((half, width)),
            (),
            (d_fields, w_fields),
            micros=2,
        )

    d_normed1_twin = swap(stream_grad(half), CORE)
    d_normed1_own = stream_grad(0)
    send, keep, total = open_scatter(steps, (d_normed1_own,), (d_normed1_twin,), core)
    both_pieces = gather_spans(
        after(grad_both, d_fields), core, lambda one, two: after(one, two, send)
    )
    got = swap_split(send, ALONG_Y, ALONG_X)
    ffn_late_got = turn_scatter(steps, ffn_keep, ffn_got)
    steps.wait(both_pieces[1], both_pieces[2])
    grad_down = steps.run(
        place_down_kernel,
        (),
        (owners,),
        (),
        far=grad_downs,
        far_outs=(shape((hidden_size // quarters, width), f32),),
        scratch=(
            pltpu.VMEM((cycles, strip, width), low),
            pltpu.VMEM((cycles, strip, width), f32),
            pltpu.SemaphoreType.DMA((2, cycles)),
        ),
        limit=60,
        micros=1000,
    )[0]
    wide_strip = shape((shard, hidden_size), f32)
    grad_gate, grad_up = steps.run(
        place_strips_kernel,
        (),
        (owners,),
        (),
        far=both_pieces,
        far_outs=(wide_strip, wide_strip),
        scratch=(
            pltpu.VMEM((cycles, shard, 2 * part), low),
            pltpu.VMEM((cycles, shard, 2 * part), f32),
            pltpu.SemaphoreType.DMA((cycles,)),
            pltpu.SemaphoreType.DMA((cycles, 2 * quarters)),
        ),
        limit=60,
    )
    late_got = turn_scatter(steps, keep, got)
    last = gather_direct(after(last, grad_down))
    narrow_grad = shape((shard, width // 2), f32)
    wide_grad = shape((shard, width), f32)
    grad_gains, output, input_grad, *weight_grads = steps.run(
        finish_kernel,
        (shape((16, four), f32),),
        (owners,),
        (
            ffn_total,
            ffn_got,
            ffn_late_got,
            stream_one,
            total,
            got,
            late_got,
            stream,
            d_stream_one,
            gains,
        ),
        far=last,
        far_outs=(
            shape((tokens, width)),
            shape((tokens, width), f32),
            wide_grad,
            narrow_grad,
            narrow_grad,
            wide_grad,
        ),
        scratch=(
            pltpu.VMEM((tokens, width), low),
            pltpu.VMEM((tokens, width), f32),
            pltpu.VMEM((cycles, packed, four), low),
            pltpu.VMEM((shard, width), f32),
            pltpu.VMEM((shard, width // 2), f32),
            pltpu.VMEM((shard, width // 2), f32),
            pltpu.VMEM((shard, width), f32),
            pltpu.SemaphoreType.DMA((cycles,)),
            pltpu.SemaphoreType.DMA((2,)),
            pltpu.SemaphoreType.DMA((8,)),
        ),
        limit=60,
    )
    grad_query, grad_key, grad_value, grad_out = weight_grads
    return (
        output.reshape(activations.shape),
        input_grad.reshape(activations.shape),
        grad_query,
        grad_key,
        grad_value,
        grad_out,
        grad_gate,
        grad_up,
        grad_down,
        grad_gains[0],
        grad_gains[8],
    )


def solution(mesh):
    in_specs = (
        P("fsdp", "ctx", None, None),
        P(),
        P("fsdp", None),
        P("fsdp", None),
        P("fsdp", None),
        P("fsdp", None),
        P("fsdp", None),
        P("fsdp", None),
        P("fsdp", None),
        P("fsdp"),
        P("fsdp"),
        P("fsdp", "ctx", None, None),
    )
    out_specs = (
        P("fsdp", "ctx", None, None),
        P("fsdp", "ctx", None, None),
        P("fsdp", None),
        P("fsdp", None),
        P("fsdp", None),
        P("fsdp", None),
        P("fsdp", None),
        P("fsdp", None),
        P("fsdp", None),
        P("fsdp"),
        P("fsdp"),
    )
    cycles = mesh.shape["ctx"]

    def per_device(*arrays):
        heads = arrays[3].shape[1] // DH
        if cycles == len(RELATIVE) == heads and arrays[2].shape == (4 * DH, 2 * heads * DH):
            return plane_layer(*arrays)
        return ring_layer(*arrays)

    return jax.shard_map(
        per_device, mesh=mesh, in_specs=in_specs, out_specs=out_specs, check_vma=False
    )
```

```python
import functools
import math

import jax
import jax.numpy as jnp
from jax import lax
from jax.experimental import pallas as pl
from jax.experimental.pallas import tpu as pltpu
from jax.sharding import PartitionSpec as P

DH = 96


epsilon = 1e-05
rope_base = 100000.0
masked_score = -1e30
LOG2E = math.log2(math.e)


def passed_along(block, axis, distance):
    devices = range(lax.axis_size(axis))
    route = [((i - distance) % len(devices), i) for i in devices]
    return lax.ppermute(block, axis, route)


def rope_tables(places):
    half = DH // 2
    freqs = jnp.exp(-math.log(rope_base) * 2.0 * jnp.arange(half, dtype=jnp.float32) / DH)
    angle = places.astype(jnp.float32)[:, None] * freqs[None, :]
    return (jnp.cos(angle)[:, None, :], jnp.sin(angle)[:, None, :])


def rope_turn(field, cosine, sine):
    half = DH // 2
    first = field[..., :half]
    second = field[..., half:]
    return jnp.concatenate(
        [first * cosine - second * sine, second * cosine + first * sine], axis=-1
    )


def rope_back(field, cosine, sine):
    half = DH // 2
    first = field[..., :half]
    second = field[..., half:]
    return jnp.concatenate(
        [first * cosine + second * sine, second * cosine - first * sine], axis=-1
    )


def norm_back(d_normed, stream, inv_rms, gain):
    scaled = d_normed * gain
    cubed = inv_rms * inv_rms * inv_rms
    return inv_rms * scaled - stream * cubed * jnp.mean(scaled * stream, axis=-1, keepdims=True)


def ring_layer(
    activations,
    span_order,
    w_query,
    w_key,
    w_value,
    w_out,
    w_gate,
    w_up,
    w_down,
    attn_gain,
    ffn_gain,
    cotangent,
):
    cycles = lax.axis_size("ctx")
    mine = lax.axis_index("ctx")
    span = activations.shape[2]
    width = activations.shape[3]
    tokens = 2 * span
    heads = w_query.shape[1] // DH
    kv_heads = w_key.shape[1] // DH
    group = heads // kv_heads
    scale = 1.0 / math.sqrt(DH)
    offsets = jnp.arange(span, dtype=jnp.int32)

    def places_of(owner):
        span_ids = lax.dynamic_slice_in_dim(span_order, 2 * owner, 2)
        return (span_ids[:, None] * span + offsets[None, :]).reshape(tokens)

    query_places = places_of(mine)
    cosine, sine = rope_tables(query_places)
    gathered = (
        lax.all_gather(w_query, "fsdp", axis=0, tiled=True),
        lax.all_gather(w_key, "fsdp", axis=0, tiled=True),
        lax.all_gather(w_value, "fsdp", axis=0, tiled=True),
        lax.all_gather(w_out, "fsdp", axis=0, tiled=True),
        lax.all_gather(w_gate, "fsdp", axis=0, tiled=True),
        lax.all_gather(w_up, "fsdp", axis=0, tiled=True),
        lax.all_gather(w_down, "fsdp", axis=0, tiled=True),
        lax.all_gather(attn_gain, "fsdp", axis=0, tiled=True),
        lax.all_gather(ffn_gain, "fsdp", axis=0, tiled=True),
    )
    (
        full_query,
        full_key,
        full_value,
        full_out,
        full_gate,
        full_up,
        full_down,
        gain_one,
        gain_two,
    ) = gathered
    stream = activations.reshape(tokens, width).astype(jnp.float32)
    inv_one = lax.rsqrt(jnp.mean(stream * stream, axis=-1, keepdims=True) + epsilon)
    normed1 = (stream * inv_one * gain_one).astype(jnp.bfloat16)
    query_raw = jnp.dot(normed1, full_query, preferred_element_type=jnp.float32).reshape(
        tokens, heads, DH
    )
    queries = (
        rope_turn(query_raw, cosine, sine).astype(jnp.bfloat16).reshape(tokens, kv_heads, group, DH)
    )
    key_raw = jnp.dot(normed1, full_key, preferred_element_type=jnp.float32).reshape(
        tokens, kv_heads, DH
    )
    keys = rope_turn(key_raw, cosine, sine).astype(jnp.bfloat16)
    values = (
        jnp.dot(normed1, full_value, preferred_element_type=jnp.float32)
        .astype(jnp.bfloat16)
        .reshape(tokens, kv_heads, DH)
    )

    def scores_with(key_piece, owner):
        scores = (
            jnp.einsum("tjgd,sjd->jgts", queries, key_piece, preferred_element_type=jnp.float32)
            * scale
        )
        counted = places_of(owner)[None, :] <= query_places[:, None]
        return jnp.where(counted, scores, masked_score)

    def absorb(state, key_piece, value_piece, owner):
        running_top, running_total, running_sum = state
        scores = scores_with(key_piece, owner)
        new_top = jnp.maximum(running_top, jnp.max(scores, axis=-1, keepdims=True))
        fading = jnp.exp(running_top - new_top)
        weights = jnp.exp(scores - new_top)
        running_total = fading * running_total + jnp.sum(weights, axis=-1, keepdims=True)
        running_sum = fading * running_sum + jnp.einsum(
            "jgts,sjd->jgtd",
            weights.astype(jnp.bfloat16),
            value_piece,
            preferred_element_type=jnp.float32,
        )
        return (new_top, running_total, running_sum)

    start_state = (
        jnp.full((kv_heads, group, tokens, 1), masked_score, jnp.float32),
        jnp.zeros((kv_heads, group, tokens, 1), jnp.float32),
        jnp.zeros((kv_heads, group, tokens, DH), jnp.float32),
    )
    state = absorb(start_state, keys, values, mine)

    def forward_turn(turn_index, carry):
        state_now, key_piece, value_piece = carry
        key_piece, value_piece = passed_along((key_piece, value_piece), "ctx", 1)
        owner = (mine - turn_index) % cycles
        return (absorb(state_now, key_piece, value_piece, owner), key_piece, value_piece)

    state, _, _ = lax.fori_loop(1, cycles, forward_turn, (state, keys, values))
    running_top, running_total, running_sum = state
    attended = running_sum / running_total
    log_total = running_top + jnp.log(running_total)
    attended_low = (
        jnp.transpose(attended, (2, 0, 1, 3)).reshape(tokens, heads * DH).astype(jnp.bfloat16)
    )
    stream_one = stream + jnp.dot(attended_low, full_out, preferred_element_type=jnp.float32)
    inv_two = lax.rsqrt(jnp.mean(stream_one * stream_one, axis=-1, keepdims=True) + epsilon)
    normed2 = (stream_one * inv_two * gain_two).astype(jnp.bfloat16)
    gate = jnp.dot(normed2, full_gate, preferred_element_type=jnp.float32)
    up_part = jnp.dot(normed2, full_up, preferred_element_type=jnp.float32)
    sigma = jax.nn.sigmoid(gate)
    hidden = (gate * sigma * up_part).astype(jnp.bfloat16)
    stream_two = stream_one + jnp.dot(hidden, full_down, preferred_element_type=jnp.float32)
    output = stream_two.astype(jnp.bfloat16).reshape(activations.shape)
    back_weights = (
        lax.all_gather(w_query, "fsdp", axis=0, tiled=True),
        lax.all_gather(w_key, "fsdp", axis=0, tiled=True),
        lax.all_gather(w_value, "fsdp", axis=0, tiled=True),
        lax.all_gather(w_out, "fsdp", axis=0, tiled=True),
        lax.all_gather(w_gate, "fsdp", axis=0, tiled=True),
        lax.all_gather(w_up, "fsdp", axis=0, tiled=True),
        lax.all_gather(w_down, "fsdp", axis=0, tiled=True),
        lax.all_gather(attn_gain, "fsdp", axis=0, tiled=True),
        lax.all_gather(ffn_gain, "fsdp", axis=0, tiled=True),
    )
    (
        back_query,
        back_key,
        back_value,
        back_out,
        back_gate,
        back_up,
        back_down,
        back_gain_one,
        back_gain_two,
    ) = back_weights
    grad_rows = cotangent.reshape(tokens, width)
    grad_stream = grad_rows.astype(jnp.float32)
    grad_down = jnp.einsum("tf,td->fd", hidden, grad_rows, preferred_element_type=jnp.float32)
    d_hidden = jnp.einsum("td,fd->tf", grad_rows, back_down, preferred_element_type=jnp.float32)
    d_gate = (d_hidden * up_part * sigma * (1.0 + gate * (1.0 - sigma))).astype(jnp.bfloat16)
    d_up = (d_hidden * gate * sigma).astype(jnp.bfloat16)
    grad_gate = jnp.einsum("td,tf->df", normed2, d_gate, preferred_element_type=jnp.float32)
    grad_up = jnp.einsum("td,tf->df", normed2, d_up, preferred_element_type=jnp.float32)
    d_normed2 = jnp.einsum(
        "tf,df->td", d_gate, back_gate, preferred_element_type=jnp.float32
    ) + jnp.einsum("tf,df->td", d_up, back_up, preferred_element_type=jnp.float32)
    grad_ffn_gain = jnp.sum(d_normed2 * stream_one * inv_two, axis=0)
    d_stream_one = grad_stream + norm_back(d_normed2, stream_one, inv_two, back_gain_two)
    d_branch = d_stream_one.astype(jnp.bfloat16)
    grad_out = jnp.einsum("tk,td->kd", attended_low, d_branch, preferred_element_type=jnp.float32)
    d_attended = jnp.einsum(
        "td,kd->tk", d_branch, back_out, preferred_element_type=jnp.float32
    ).astype(jnp.bfloat16)
    d_heads = jnp.transpose(d_attended.reshape(tokens, kv_heads, group, DH), (1, 2, 0, 3))
    delta = jnp.sum(d_heads.astype(jnp.float32) * attended, axis=-1, keepdims=True)

    def back_step(d_queries, d_keys, d_values, key_piece, value_piece, owner):
        scores = scores_with(key_piece, owner)
        probs = jnp.exp(scores - log_total)
        d_values = d_values + jnp.einsum(
            "jgts,jgtd->sjd",
            probs.astype(jnp.bfloat16),
            d_heads,
            preferred_element_type=jnp.float32,
        )
        d_probs = jnp.einsum(
            "jgtd,sjd->jgts", d_heads, value_piece, preferred_element_type=jnp.float32
        )
        d_scores = (probs * (d_probs - delta)).astype(jnp.bfloat16)
        d_queries = (
            d_queries
            + jnp.einsum("jgts,sjd->jgtd", d_scores, key_piece, preferred_element_type=jnp.float32)
            * scale
        )
        d_keys = (
            d_keys
            + jnp.einsum("jgts,tjgd->sjd", d_scores, queries, preferred_element_type=jnp.float32)
            * scale
        )
        return (d_queries, d_keys, d_values)

    def pass_grads(d_keys, d_values):
        return (
            passed_along(d_keys.astype(jnp.bfloat16), "ctx", 1).astype(d_keys.dtype),
            passed_along(d_values.astype(jnp.bfloat16), "ctx", 1).astype(d_values.dtype),
        )

    zero_queries = jnp.zeros((kv_heads, group, tokens, DH), jnp.float32)
    zero_keys = jnp.zeros((tokens, kv_heads, DH), jnp.float32)
    d_queries, d_keys, d_values = back_step(zero_queries, zero_keys, zero_keys, keys, values, mine)

    def backward_turn(turn_index, carry):
        d_queries_now, d_keys_now, d_values_now, key_piece, value_piece = carry
        key_piece, value_piece = passed_along((key_piece, value_piece), "ctx", 1)
        d_keys_now, d_values_now = pass_grads(d_keys_now, d_values_now)
        owner = (mine - turn_index) % cycles
        d_queries_now, d_keys_now, d_values_now = back_step(
            d_queries_now, d_keys_now, d_values_now, key_piece, value_piece, owner
        )
        return (d_queries_now, d_keys_now, d_values_now, key_piece, value_piece)

    d_queries, d_keys, d_values, _, _ = lax.fori_loop(
        1, cycles, backward_turn, (d_queries, d_keys, d_values, keys, values)
    )
    d_keys, d_values = pass_grads(d_keys, d_values)
    d_query_rows = jnp.transpose(d_queries, (2, 0, 1, 3)).reshape(tokens, heads, DH)
    d_query = rope_back(d_query_rows, cosine, sine).astype(jnp.bfloat16).reshape(tokens, heads * DH)
    d_key = rope_back(d_keys, cosine, sine).astype(jnp.bfloat16).reshape(tokens, kv_heads * DH)
    d_value = d_values.astype(jnp.bfloat16).reshape(tokens, kv_heads * DH)
    grad_query = jnp.einsum("td,tk->dk", normed1, d_query, preferred_element_type=jnp.float32)
    grad_key = jnp.einsum("td,tk->dk", normed1, d_key, preferred_element_type=jnp.float32)
    grad_value = jnp.einsum("td,tk->dk", normed1, d_value, preferred_element_type=jnp.float32)
    d_normed1 = (
        jnp.einsum("tk,dk->td", d_query, back_query, preferred_element_type=jnp.float32)
        + jnp.einsum("tk,dk->td", d_key, back_key, preferred_element_type=jnp.float32)
        + jnp.einsum("tk,dk->td", d_value, back_value, preferred_element_type=jnp.float32)
    )
    grad_attn_gain = jnp.sum(d_normed1 * stream * inv_one, axis=0)
    input_grad = (d_stream_one + norm_back(d_normed1, stream, inv_one, back_gain_one)).reshape(
        activations.shape
    )
    shares = (
        lax.psum_scatter(
            grad_query.astype(jnp.bfloat16), "fsdp", scatter_dimension=0, tiled=True
        ).astype(jnp.float32),
        lax.psum_scatter(
            grad_key.astype(jnp.bfloat16), "fsdp", scatter_dimension=0, tiled=True
        ).astype(jnp.float32),
        lax.psum_scatter(
            grad_value.astype(jnp.bfloat16), "fsdp", scatter_dimension=0, tiled=True
        ).astype(jnp.float32),
        lax.psum_scatter(
            grad_out.astype(jnp.bfloat16), "fsdp", scatter_dimension=0, tiled=True
        ).astype(jnp.float32),
        lax.psum_scatter(
            grad_gate.astype(jnp.bfloat16), "fsdp", scatter_dimension=0, tiled=True
        ).astype(jnp.float32),
        lax.psum_scatter(
            grad_up.astype(jnp.bfloat16), "fsdp", scatter_dimension=0, tiled=True
        ).astype(jnp.float32),
        lax.psum_scatter(
            grad_down.astype(jnp.bfloat16), "fsdp", scatter_dimension=0, tiled=True
        ).astype(jnp.float32),
        lax.psum_scatter(
            grad_attn_gain.astype(jnp.bfloat16), "fsdp", scatter_dimension=0, tiled=True
        ).astype(jnp.float32),
        lax.psum_scatter(
            grad_ffn_gain.astype(jnp.bfloat16), "fsdp", scatter_dimension=0, tiled=True
        ).astype(jnp.float32),
    )
    shares = (
        lax.psum(shares[0].astype(jnp.bfloat16), "ctx").astype(jnp.float32),
        lax.psum(shares[1].astype(jnp.bfloat16), "ctx").astype(jnp.float32),
        lax.psum(shares[2].astype(jnp.bfloat16), "ctx").astype(jnp.float32),
        lax.psum(shares[3].astype(jnp.bfloat16), "ctx").astype(jnp.float32),
        lax.psum(shares[4].astype(jnp.bfloat16), "ctx").astype(jnp.float32),
        lax.psum(shares[5].astype(jnp.bfloat16), "ctx").astype(jnp.float32),
        lax.psum(shares[6].astype(jnp.bfloat16), "ctx").astype(jnp.float32),
        lax.psum(shares[7].astype(jnp.bfloat16), "ctx").astype(jnp.float32),
        lax.psum(shares[8].astype(jnp.bfloat16), "ctx").astype(jnp.float32),
    )
    return (
        output,
        input_grad,
        shares[0],
        shares[1],
        shares[2],
        shares[3],
        shares[4],
        shares[5],
        shares[6],
        shares[7],
        shares[8],
    )


LANES = 128
CORE, ALONG_X, ALONG_Y = 1, 2, 4
RELATIVE = (0, 2, 4, 6, 1, 3, 5, 7)
MIB = 2**20
COST = 10**6


def lane_dot(left, right):
    return lax.dot_general(left, right, (((1,), (1,)), ((), ())), preferred_element_type=jnp.float32)


def plain_dot(left, right):
    return lax.dot_general(left, right, (((1,), (0,)), ((), ())), preferred_element_type=jnp.float32)


def row_dot(left, right):
    return lax.dot_general(left, right, (((0,), (0,)), ((), ())), preferred_element_type=jnp.float32)


def rows_at(index, size):
    return pl.ds(pl.multiple_of(index * size, size), size)


def wide(value):
    return value.astype(jnp.float32)


def narrow(value):
    return value.astype(jnp.bfloat16)


def lanes_of(rows):
    return lax.broadcasted_iota(jnp.int32, (rows, LANES), 1)


def shape(dims, kind=jnp.bfloat16):
    return jax.ShapeDtypeStruct(dims, kind)


def after(value, *others):
    return lax.optimization_barrier((value, *others))[0]


class Steps:

    def __init__(self, ticket):
        self.ticket = ticket
        self.pending = []

    def wait(self, *values):
        self.pending.extend(values)

    def run(
        self,
        body,
        outs,
        small,
        arrays,
        far=(),
        pinned=(),
        far_outs=(),
        scratch=(),
        limit=20,
        micros=2,
    ):
        near = pl.BlockSpec(memory_space=pltpu.VMEM)
        scalars = pl.BlockSpec(memory_space=pltpu.SMEM)
        away = pl.BlockSpec(memory_space=pl.ANY)
        stored = pl.BlockSpec(memory_space=pltpu.HBM)
        single = not isinstance(outs, tuple)
        out_shapes = ((outs,) if single else outs) + tuple(far_outs)
        out_specs = [near] * (len(out_shapes) - len(far_outs)) + [stored] * len(far_outs)
        ticket = after(self.ticket, *self.pending) if self.pending else self.ticket
        results = pl.pallas_call(
            lambda _, *refs: body(*refs),
            out_shape=out_shapes,
            in_specs=[scalars] * (1 + len(small))
            + [near] * len(arrays)
            + [away] * len(far)
            + [stored] * len(pinned),
            out_specs=out_specs,
            scratch_shapes=list(scratch),
            compiler_params=pltpu.CompilerParams(vmem_limit_bytes=limit * MIB),
            cost_estimate=pl.CostEstimate(
                flops=micros * COST, bytes_accessed=0, transcendentals=0
            ),
        )(ticket, *small, *arrays, *far, *pinned)
        self.pending = [results[-1]]
        return results[0] if single and not far_outs else results


def window_of(weight, start):
    base = jnp.minimum(start // LANES * LANES, weight.shape[1] - 2 * LANES)
    return weight.at[:, pl.ds(pl.multiple_of(base, LANES), 2 * LANES)], start - base


def drawn(window_ref, shift):
    size = 2 * LANES
    return pltpu.roll(wide(window_ref[...]), (size - shift) % size, 1)


def join_fields(one, two, three, four):
    lane = lanes_of(one.shape[0])
    two = pltpu.roll(two, 96, 1)
    three = pltpu.roll(three, 64, 1)
    four = pltpu.roll(four, 32, 1)
    return jnp.concatenate(
        [
            jnp.where(lane < 96, one, two),
            jnp.where(lane < 64, two, three),
            jnp.where(lane < 32, three, four),
        ],
        axis=1,
    )


def part_fields(block):
    lane = lanes_of(block.shape[0])
    one, two, three = (block[:, start : start + LANES] for start in (0, LANES, 2 * LANES))
    fields = (
        one,
        jnp.where(lane < 32, pltpu.roll(one, 32, 1), pltpu.roll(two, 32, 1)),
        jnp.where(lane < 64, pltpu.roll(two, 64, 1), pltpu.roll(three, 64, 1)),
        pltpu.roll(three, 96, 1),
    )
    return [jnp.where(lane < DH, field, 0.0) for field in fields]


def pack_kernel(
    mine_ref,
    gain_ref,
    query_in,
    key_in,
    value_in,
    out_in,
    first_ref,
    query_ref,
    key_ref,
    value_ref,
    out_ref,
    done,
):
    mine = mine_ref[0]
    shard = query_ref.shape[0]
    four = 4 * DH
    slab = out_ref.shape[0]
    slabs = out_ref.shape[1] // four
    query_window, query_shift = window_of(query_in, mine * 2 * DH)
    key_window, shift = window_of(key_in, mine * DH)
    value_window, _ = window_of(value_in, mine * DH)
    copies = [
        fetch(source, target, done.at[index])
        for index, (source, target) in enumerate(
            (
                (query_window, query_ref),
                (key_window, key_ref),
                (value_window, value_ref),
                (out_in.at[rows_at(mine, slab), :], out_ref),
            )
        )
    ]
    for copy in copies:
        copy.wait()
    query = drawn(query_ref, query_shift)
    key = pltpu.roll(drawn(key_ref, shift)[:, :LANES], 64, 1)
    value = pltpu.roll(drawn(value_ref, shift)[:, :LANES], 32, 1)
    lane = lanes_of(shard)
    first_ref[:shard, :LANES] = narrow(query[:, :LANES])
    first_ref[:shard, LANES : 2 * LANES] = narrow(jnp.where(lane < 64, query[:, LANES:], key))
    first_ref[:shard, 2 * LANES :] = narrow(jnp.where(lane < 32, key, value))
    for index in range(slabs):
        here = shard + index * slab
        first_ref[here : here + slab, :] = out_ref[:, index * four : (index + 1) * four]
    first_ref[shard + slabs * slab :, :] = gain_ref[...]


def strip_kernel(mine_ref, gate_ref, up_ref, down_ref, all_ref):
    quarters = gate_ref.shape[1] // (8 * LANES)
    start = 2 * quarters * LANES
    for index in range(quarters):
        place = rows_at(index * 8 + mine_ref[0], LANES)
        here = index * LANES
        all_ref[:, here : here + LANES] = gate_ref[:, place]
        here += quarters * LANES
        all_ref[:, here : here + LANES] = up_ref[:, place]
    rows = down_ref.shape[0] // 8
    cut = all_ref.shape[1] - start
    for index in range(all_ref.shape[0] // rows):
        all_ref[index * rows : (index + 1) * rows, start:] = down_ref[
            rows_at(mine_ref[0], rows), index * cut : (index + 1) * cut
        ]


def fold(block):
    rows = block.shape[0]
    tail = block[:, LANES:]
    lower = jnp.where(lanes_of(rows // 2) < 64, tail[: rows // 2], pltpu.roll(tail[rows // 2 :], 64, 1))
    return jnp.concatenate([block[:, :LANES], lower], axis=0)


def unfold(block):
    rows = block.shape[0] // 3 * 2
    half = rows // 2
    tail = block[rows:]
    keep = lanes_of(half) < 64
    tail = jnp.concatenate(
        [jnp.where(keep, tail, 0.0), jnp.where(keep, pltpu.roll(tail, 64, 1), 0.0)], axis=0
    )
    return jnp.concatenate([block[:rows], tail], axis=1)


def branch_kernel(owner_ref, folded_ref, stream_ref, gain_ref, *refs):
    pieces, refs = refs[:8], refs[8:]
    one_ref, normed_ref, inverse_ref, heads_ref, full_out, full_ref, piece_ref, done = refs
    copies = [fetch(piece, piece_ref.at[i], done.at[i]) for i, piece in enumerate(pieces)]
    width = full_ref.shape[1]
    slab = width // 32
    size = 2 * DH
    four = pieces[0].shape[1]
    gap = jnp.zeros((folded_ref.shape[1] // 3 * 2, LANES), jnp.float32)
    for index in range(0, folded_ref.shape[0], 2):
        one = unfold(wide(folded_ref[index]))
        two = unfold(wide(folded_ref[index + 1]))
        both = jnp.concatenate([one, gap], axis=1) + pltpu.roll(
            jnp.concatenate([two, gap], axis=1), size, 1
        )
        heads_ref[:, index * size : (index + 2) * size] = narrow(both)
    for index, copy in enumerate(copies):
        copy.wait()
        for quarter in range(4):
            row = pl.multiple_of(quarter * 8 * slab + owner_ref[index] * slab, 16)
            for part in range(width // four):
                start = (quarter * (width // four) + part) * slab
                full_ref[pl.ds(row, slab), part * four : (part + 1) * four] = piece_ref[
                    index, start : start + slab, :
                ]
    copy = fetch(full_ref, full_out, done.at[0])
    total = wide(stream_ref[...]) + plain_dot(heads_ref[...], full_ref[...])
    one_ref[...] = total
    inverse = lax.rsqrt(jnp.mean(total * total, axis=1, keepdims=True) + epsilon)
    normed_ref[...] = narrow(total * inverse * gain_ref[8:9])
    inverse_ref[...] = jnp.broadcast_to(inverse, inverse_ref.shape)
    copy.wait()


def strips_kernel(count, carry, *refs):
    before, refs = refs[: int(carry)], refs[int(carry) :]
    normed_in, grad_in, refs = refs[:count], refs[count : 2 * count], refs[2 * count :]
    strips_in, refs = refs[0], refs[1:]
    grad_out, stream_refs, refs = refs[0], refs[1 : 1 + count], refs[1 + count :]
    sum_ref, tail_ref, both_out, *refs = refs
    down_grad, gate_up_ref, down_ref, normed_ref, grad_ref, both_ref, done, out_done, weight_done = refs
    part = down_ref.shape[0]
    rows = normed_in[0].shape[0]
    size = 2 * rows
    columns = gate_up_ref.shape[1]
    strip = down_ref.shape[0] // 4
    shard = strips_in.shape[0] // 4
    cut = strips_in.shape[1] - columns
    copies = []

    def fetch_rows(index):
        here = pl.ds(index * rows, rows)
        copies.append(
            (
                fetch(normed_in[index], normed_ref.at[here, :], done.at[index]),
                fetch(grad_in[index], grad_ref.at[here, :], done.at[count + index]),
            )
        )

    fetch_rows(0)
    fetch_rows(1)
    gate_up_copy = fetch(strips_in.at[:, pl.ds(0, columns)], gate_up_ref, weight_done.at[0])
    downs = []
    for quarter in range(4):
        for index in range(shard // strip):
            downs.append(
                fetch(
                    strips_in.at[
                        pl.ds(quarter * shard + index * strip, strip), pl.ds(columns, cut)
                    ],
                    down_ref.at[pl.ds(quarter * strip, strip), pl.ds(index * cut, cut)],
                    weight_done.at[1 + quarter * (shard // strip) + index],
                )
            )
    for index in range(2, count):
        fetch_rows(index)
    outs = []
    gate_up_copy.wait()
    for step in range(count // 2):
        for index in (2 * step, 2 * step + 1):
            copies[index][0].wait()
        here = slice(step * size, (step + 1) * size)
        normed = normed_ref[here, :]
        gate = plain_dot(normed, gate_up_ref[:, :part])
        up = plain_dot(normed, gate_up_ref[:, part:])
        sigma = jax.nn.sigmoid(gate)
        turned = gate * sigma
        hidden = narrow(turned * up)
        if step == 0:
            for copy in downs:
                copy.wait()
        for index in (2 * step, 2 * step + 1):
            copies[index][1].wait()
        grad = grad_ref[here, :]
        d_hidden = lane_dot(grad, down_ref[...])
        d_gate = narrow(d_hidden * up * sigma * (1.0 + gate * (1.0 - sigma)))
        d_up = narrow(d_hidden * turned)
        both_ref[here, :part] = d_gate
        both_ref[here, part:] = d_up
        there = pl.ds(step * size, size)
        outs.append(fetch(both_ref.at[there, :], both_out.at[there, :], out_done.at[step]))
        d_normed = narrow(
            lane_dot(d_gate, gate_up_ref[:, :part]) + lane_dot(d_up, gate_up_ref[:, part:])
        )
        sums = narrow(plain_dot(hidden, down_ref[...]))
        for index in range(2):
            block = 2 * step + index
            stream_refs[block][...] = d_normed[index * rows : (index + 1) * rows]
            if block < count - 1:
                sum_ref[block * rows : (block + 1) * rows, :] = sums[
                    index * rows : (index + 1) * rows
                ]
            else:
                tail_ref[...] = sums[index * rows : (index + 1) * rows]
        product = row_dot(hidden, grad)
        if step == 0:
            down_grad[...] = product + before[0][...] if carry else product
        elif step < count // 2 - 1:
            down_grad[...] += product
        else:
            grad_out[...] = (down_grad[...] + product).astype(grad_out.dtype)
    for copy in outs:
        copy.wait()


def strip_grad_kernel(count, *refs):
    gain_ref, refs = refs[0], refs[1:]
    normed_in, (own_in, twin_in, strips_in), refs = refs[:count], refs[count : count + 3], refs[count + 3 :]
    out_ref, row_ref, normed_ref, both_ref, weight_ref, done = refs
    size = 2 * LANES
    rows = normed_in[0].shape[0]
    half = own_in.shape[0]
    copies = [
        fetch(piece, normed_ref.at[pl.ds(index * rows, rows), :], done.at[index])
        for index, piece in enumerate(normed_in)
    ]
    copies.append(fetch(own_in, both_ref.at[pl.ds(0, half), :], done.at[count]))
    copies.append(fetch(twin_in, both_ref.at[pl.ds(half, half), :], done.at[count + 1]))
    columns = weight_ref.shape[1]
    copies.append(fetch(strips_in.at[:, pl.ds(0, columns)], weight_ref, done.at[count + 2]))
    for copy in copies:
        copy.wait()
    ones = jnp.ones((8, out_ref.shape[1]), jnp.bfloat16)

    def one(index, _):
        columns = rows_at(index, size)
        total = row_dot(normed_ref[:, columns], both_ref[...])
        out_ref[columns, :] = narrow(total)
        share = narrow(total * wide(weight_ref[columns, :]))
        row_ref[:, columns] = lane_dot(ones, share) / gain_ref[8:, columns]
        return 0

    lax.fori_loop(0, out_ref.shape[0] // size, one, 0)


def add_twin_kernel(core_ref, *refs):
    (*refs, send_ref, keep_ref, self_ref) = refs
    rows = keep_ref.shape[0]
    count = len(refs) // 2
    core = core_ref[0]

    def total(index):
        if count == 4:
            return wide(refs[index][...]) + wide(refs[4 + index][...])
        here = slice(index * rows, (index + 1) * rows)
        if count == 1:
            return wide(refs[0][here, :]) + wide(refs[1][here, :])
        before = slice((index - 1) * rows, index * rows)
        own = refs[1][before, :] if index else refs[0][...]
        twin = refs[2][here, :] if index < 3 else refs[3][...]
        return wide(own) + wide(twin)

    self_ref[...] = total(0)
    send_ref[:rows, :] = narrow(total(3))
    along_x = total(1)
    along_y = total(2)

    @pl.when(core == 0)
    def _():
        send_ref[rows:, :] = narrow(along_y)
        keep_ref[...] = along_x

    @pl.when(core == 1)
    def _():
        send_ref[rows:, :] = narrow(along_x)
        keep_ref[...] = along_y


def add_late_kernel(keep_in, got_in, late_ref, keep_ref, got_ref, done):
    rows = keep_ref.shape[0]
    copies = (
        fetch(keep_in, keep_ref, done.at[0]),
        fetch(got_in.at[pl.ds(0, rows), :], got_ref, done.at[1]),
    )
    for copy in copies:
        copy.wait()
    late_ref[...] = narrow(keep_ref[...] + wide(got_ref[...]))


def summed(self_ref, got_ref, late_ref):
    rows = self_ref.shape[0]
    return self_ref[...] + wide(got_ref[rows:, :]) + wide(late_ref[...])


def norm_down(d_normed, stream, inverse, gain):
    scaled = d_normed * gain
    cubed = inverse * inverse * inverse
    return inverse * scaled - stream * cubed * jnp.mean(scaled * stream, axis=1, keepdims=True)


def branch_back_kernel(
    self_ref,
    got_ref,
    late_ref,
    grad_ref,
    one_ref,
    inverse_ref,
    gain_ref,
    full_ref,
    stream_out,
    heads_out,
):
    d_normed = summed(self_ref, got_ref, late_ref)
    d_stream = wide(grad_ref[...]) + norm_down(
        d_normed, one_ref[...], inverse_ref[:, :1], gain_ref[8:9]
    )
    stream_out[...] = d_stream
    d_branch = narrow(d_stream)
    rows = d_branch.shape[0]
    size = 2 * DH
    gap = jnp.zeros((rows, 2 * LANES - size), jnp.float32)
    keep = lanes_of(rows) < size - LANES
    tall = heads_out.shape[1] // 2
    for index in range(heads_out.shape[0]):
        heads = lane_dot(d_branch, full_ref[index * size : (index + 1) * size, :])
        heads_out[index, :tall, :] = narrow(fold(jnp.concatenate([heads, gap], axis=1)))
        start = index * size // LANES * LANES
        columns = wide(d_branch[:, start : start + 2 * LANES])
        if index % 2:
            columns = pltpu.roll(columns, 2 * LANES - 64, 1)
        columns = jnp.concatenate(
            [columns[:, :LANES], jnp.where(keep, columns[:, LANES:], 0.0)], axis=1
        )
        heads_out[index, tall:, :] = narrow(fold(columns))


def stream_grad_kernel(start, fields_ref, weight_ref, out_ref):
    rows = out_ref.shape[0]
    size = rows // 2
    for step in range(2):
        here = slice(step * size, (step + 1) * size)
        there = slice(start + step * size, start + (step + 1) * size)
        out_ref[here, :] = narrow(lane_dot(fields_ref[there, :], weight_ref[...]))


def place_strips_kernel(owner_ref, *refs):
    pieces, (gate_out, up_out, low_ref, wide_ref, done, out_done) = refs[:-6], refs[-6:]
    copies = [fetch(piece, low_ref.at[i], done.at[i]) for i, piece in enumerate(pieces)]
    quarters = low_ref.shape[2] // (2 * LANES)
    outs = []
    for index, copy in enumerate(copies):
        copy.wait()
        wide_ref[index] = wide(low_ref[index])
        for part in range(2 * quarters):
            there = rows_at(part % quarters * 8 + owner_ref[index], LANES)
            target = gate_out if part < quarters else up_out
            outs.append(
                fetch(
                    wide_ref.at[index, :, pl.ds(part * LANES, LANES)],
                    target.at[:, there],
                    out_done.at[index, part],
                )
            )
    for copy in outs:
        copy.wait()


def place_down_kernel(owner_ref, *refs):
    pieces, (down_out, low_ref, wide_ref, done) = refs[:-4], refs[-4:]
    copies = [fetch(piece, low_ref.at[i], done.at[0, i]) for i, piece in enumerate(pieces)]
    outs = []
    for index, copy in enumerate(copies):
        copy.wait()
        wide_ref[index] = wide(low_ref[index])
        there = rows_at(owner_ref[index], wide_ref.shape[1])
        outs.append(fetch(wide_ref.at[index], down_out.at[there, :], done.at[1, index]))
    for copy in outs:
        copy.wait()


def place_last(copies, low_ref, refs, outs, gain_ref, out_done):
    query_ref, key_ref, value_ref, out_ref = refs
    shard = query_ref.shape[0]
    half = shard // 2
    end = shard + half
    for copy in copies:
        copy.wait()
    full = lanes_of(shard) < 64
    keep = lanes_of(half) < 64
    gains = jnp.zeros(gain_ref.shape, jnp.float32)
    targets = []
    for quad in range(2):
        keys, values = [], []
        for pair in (2 * quad, 2 * quad + 1):
            columns = slice(pair * 4 * DH, (pair + 1) * 4 * DH)
            tiles = []
            for index in (2 * pair, 2 * pair + 1):
                block = wide(low_ref[index, :shard, :])
                one, two, key, value = part_fields(block)
                keys.append(key)
                values.append(value)
                tiles.append((block[:, :LANES], block[:, LANES : 2 * LANES]))
                gains = gains + wide(low_ref[index, end : end + 16, :])
            (one, two), (three, four) = tiles
            three, four = pltpu.roll(three, 64, 1), pltpu.roll(four, 64, 1)
            query_ref[:, columns] = jnp.concatenate(
                [one, jnp.where(full, two, three), jnp.where(full, three, four)], axis=1
            )
            for part in range(2):
                tiles = []
                for index in (2 * pair, 2 * pair + 1):
                    block = wide(low_ref[index, shard:end, :])
                    one, two, three = (
                        block[:, start : start + LANES] for start in (0, LANES, 2 * LANES)
                    )
                    if part:
                        two, three = pltpu.roll(two, 64, 1), pltpu.roll(three, 64, 1)
                        one, two = jnp.where(keep, two, three), three
                    tiles.append((one, two))
                (one, two), (three, four) = tiles
                three, four = pltpu.roll(three, 64, 1), pltpu.roll(four, 64, 1)
                out_ref[part * half : (part + 1) * half, columns] = jnp.concatenate(
                    [one, jnp.where(keep, two, three), jnp.where(keep, three, four)], axis=1
                )
        columns = slice(quad * 4 * DH, (quad + 1) * 4 * DH)
        key_ref[:, columns] = join_fields(*keys)
        value_ref[:, columns] = join_fields(*values)
        wide_columns = pl.ds(quad * 8 * DH, 8 * DH)
        some_columns = pl.ds(quad * 4 * DH, 4 * DH)
        for index, (ref, out, here) in enumerate(
            (
                (query_ref, outs[0], wide_columns),
                (key_ref, outs[1], some_columns),
                (value_ref, outs[2], some_columns),
                (out_ref, outs[3], wide_columns),
            )
        ):
            targets.append(fetch(ref.at[:, here], out.at[:, here], out_done.at[4 * quad + index]))
    gain_ref[...] = gains
    return targets


def output_kernel(self_ref, got_ref, late_ref, one_ref, out_ref):
    out_ref[...] = narrow(one_ref[...] + summed(self_ref, got_ref, late_ref))


def finish_kernel(
    owner_ref,
    self_ref,
    got_ref,
    late_ref,
    stream_ref,
    back_ref,
    norm_ref,
    *refs,
):
    last_pieces, gain_ref, refs = refs[:8], refs[8], refs[9:]
    (input_out, *last_outs), refs = refs[:5], refs[5:]
    input_ref, last_low, *refs = refs
    last_refs, (done, out_done, last_done) = refs[:4], refs[4:]
    lasts = [
        fetch(piece, last_low.at[owner_ref[index]], done.at[index])
        for index, piece in enumerate(last_pieces)
    ]
    d_normed = summed(self_ref, got_ref, late_ref)
    stream = wide(stream_ref[...])
    inverse = lax.rsqrt(jnp.mean(stream * stream, axis=1, keepdims=True) + epsilon)
    input_ref[...] = back_ref[...] + norm_down(d_normed, stream, inverse, norm_ref[:1])
    outs = [fetch(input_ref, input_out, out_done.at[0])]
    outs += place_last(lasts, last_low, last_refs, last_outs, gain_ref, last_done)
    for copy in outs:
        copy.wait()


def swapped(field):
    half = DH // 2
    lane = lanes_of(field.shape[0])
    return jnp.where(lane < half, pltpu.roll(field, LANES - half, 1), pltpu.roll(field, half, 1))


def rows_of(weights, field):
    return lax.dot_general(
        weights,
        field,
        (((1,), (1,)), ((), ())),
        precision=lax.Precision.HIGHEST,
        preferred_element_type=jnp.float32,
    )


def fetch(source, target, done):
    copy = pltpu.make_async_copy(source, target, done)
    copy.start()
    return copy


def attend_kernel(
    span,
    near_ref,
    slot_ref,
    cos_ref,
    sin_ref,
    *refs,
):
    (*piece_refs, first_ref), refs = refs[:9], refs[9:]
    (low_ref, gain_ref, level_ref), refs = refs[:3], refs[3:]
    (normed_out, weight_out, query_out, key_out, value_out, mixed_out), refs = refs[:6], refs[6:]
    stream_ref, weight_ref, gains_ref, raw_ref, query_ref, key_ref, value_ref, mixed_ref = refs[:8]
    score_ref, top_ref, sum_ref, in_done, out_done = refs[8:]
    spans = near_ref.shape[0]
    block = 2 * span
    pair = 2 * block
    turns = spans // 2
    quarters, packed, four = first_ref.shape
    shard = weight_ref.shape[0] // quarters
    factor = LOG2E / math.sqrt(DH)

    gain_copies = [
        fetch(
            first_ref.at[quarter, pl.ds(packed - 32, 32), :],
            gains_ref.at[pl.ds(quarter * 32, 32), :],
            in_done.at[turns + quarter],
        )
        for quarter in range(quarters)
    ]
    weight_copies = [
        fetch(
            first_ref.at[quarter, pl.ds(0, shard), :],
            weight_ref.at[pl.ds(quarter * shard, shard), :],
            in_done.at[turns + quarters + quarter],
        )
        for quarter in range(quarters)
    ]
    copies = [
        fetch(piece, stream_ref.at[pl.ds(index * block, block), :], in_done.at[index])
        for index, piece in enumerate(piece_refs)
    ]
    for copy in gain_copies:
        copy.wait()
    for quarter in range(quarters):
        rows = wide(gains_ref[quarter * 32 : quarter * 32 + 16, :])
        here = slice(quarter * shard, (quarter + 1) * shard)
        gain_ref[:8, here] = jnp.broadcast_to(rows[:1, :shard], (8, shard))
        gain_ref[8:, here] = jnp.broadcast_to(rows[1:2, :shard], (8, shard))
    for copy in weight_copies:
        copy.wait()
    out_copies = [fetch(weight_ref, weight_out, out_done.at[0])]
    gain = gain_ref[:1, :]

    def norm(start):
        here = pl.ds(start, span)
        stream = wide(stream_ref[here, :])
        inverse = lax.rsqrt(jnp.mean(stream * stream, axis=1, keepdims=True) + epsilon)
        stream_ref[here, :] = narrow(stream * inverse * gain)

    for step in range(turns // 2):
        copies[2 * step].wait()
        copies[2 * step + 1].wait()
        here = pl.ds(step * pair, pair)
        for part in range(4):
            norm(step * pair + part * span)
        raw_ref[here, :] = plain_dot(stream_ref[here, :], weight_ref[...])
        out_copies.append(
            fetch(stream_ref.at[here, :], normed_out.at[here, :], out_done.at[1 + step])
        )

    lane = lanes_of(span)

    def place(index, _):
        raw = raw_ref[rows_at(near_ref[index], span), :]
        cosine = cos_ref[rows_at(index, span), :]
        sine = sin_ref[rows_at(index, span), :]
        one, two, three, four = part_fields(raw)

        def turned(field):
            return narrow(field * cosine + swapped(field) * sine)

        first = (index // 2) * 4 + index % 2
        query_ref[rows_at(first, span), :] = turned(one)
        query_ref[rows_at(first + 2, span), :] = turned(two)
        key_ref[rows_at(index, span), :] = turned(three)
        value_ref[rows_at(index, span), :] = narrow(jnp.where(lane == DH, 1.0, four))
        return 0

    lax.fori_loop(0, spans, place, 0, unroll=2)
    next_done = 1 + turns // 2
    for source, target in ((query_ref, query_out), (key_ref, key_out), (value_ref, value_out)):
        out_copies.append(fetch(source, target, out_done.at[next_done]))
        next_done += 1

    wide_lane = lanes_of(pair)
    picked = (lanes_of(8) == 0).astype(jnp.float32)

    def store(index, both, rest):
        slot = slot_ref[index]
        low_ref[slot // 2, rows_at(slot % 2, span), :] = narrow(both)
        tail = narrow(rest)
        turned = narrow(pltpu.roll(rest, 64, 1))

        @pl.when(slot % 2 == 0)
        def _():
            low_ref[slot // 2, 2 * span :, :64] = tail[:, :64]

        @pl.when(slot % 2 == 1)
        def _():
            low_ref[slot // 2, 2 * span :, 64:] = turned[:, 64:]

    def widest(top, scores):
        for start in range(0, block, LANES):
            top = jnp.maximum(top, scores[:, start : start + LANES])
        return top

    def score(turn, step):
        scores = lane_dot(query_ref[rows_at(turn, pair), :], key_ref[rows_at(step, block), :])
        score_ref[turn % 2, :, rows_at(step, block)] = scores
        top_ref[...] = widest(top_ref[...], scores)

    def edge(turn):
        row = lax.broadcasted_iota(jnp.int32, (pair, block), 0) % block
        column = lax.broadcasted_iota(jnp.int32, (pair, block), 1)
        scores = lane_dot(query_ref[rows_at(turn, pair), :], key_ref[rows_at(turn, block), :])
        scores = jnp.where(column <= row, scores, masked_score)
        score_ref[turn % 2, :, rows_at(turn, block)] = scores
        top = jnp.max(widest(top_ref[...], scores), axis=1, keepdims=True) * factor
        return jnp.broadcast_to(top, (pair, LANES))

    def weigh(turn, step, top):
        scores = score_ref[turn % 2, :, rows_at(step, block)]
        weights = jnp.exp2(scores * factor - top[:, :1])
        sum_ref[...] += plain_dot(narrow(weights), value_ref[rows_at(step, block), :])

    def finish(turn, top):
        total = sum_ref[:, DH : DH + 1]
        mixed = jnp.where(wide_lane < DH, sum_ref[...] / total, 0.0)
        mixed_ref[rows_at(turn, pair), :] = mixed
        level = top + jnp.log2(total)
        level_ref[rows_at(turn, 8), :] = rows_of(picked, level)
        fetch(
            mixed_ref.at[rows_at(turn, pair), :],
            mixed_out.at[rows_at(turn, pair), :],
            out_done.at[next_done + turn],
        )
        one, two = mixed[:block], pltpu.roll(mixed[block:], DH, 1)
        first = jnp.where(wide_lane[:block] < DH, one, two)
        store(2 * turn, first[:span], two[:span])
        store(2 * turn + 1, first[span:], two[span:])

    def clear():
        sum_ref[...] = jnp.zeros_like(sum_ref)
        top_ref[...] = jnp.full(top_ref.shape, masked_score, jnp.float32)

    def one_turn(turn, top):
        clear()

        def both(step, _):
            weigh(turn, step, top)
            score(turn + 1, step)
            return 0

        lax.fori_loop(0, turn + 1, both, 0)
        finish(turn, top)
        return edge(turn + 1)

    clear()
    top = lax.fori_loop(0, turns - 1, one_turn, edge(0))
    clear()

    def only(step, _):
        weigh(turns - 1, step, top)
        return 0

    lax.fori_loop(0, turns, only, 0)
    finish(turns - 1, top)
    for copy in out_copies:
        copy.wait()
    for turn in range(turns):
        here = pl.ds(turn * pair, pair)
        pltpu.make_async_copy(
            mixed_ref.at[here, :], mixed_out.at[here, :], out_done.at[next_done + turn]
        ).wait()


def attend(steps, near, slot, cosine, sine, first, pieces, span):
    tokens = cosine.shape[0]
    turns = tokens // (2 * span)
    quarters, _, four = first.shape
    block, width = pieces[0].shape
    f32 = jnp.float32
    near_out = (
        shape((turns, 3 * span, LANES)),
        shape((16, width), f32),
        shape((8 * turns, 4 * span), f32),
    )
    far_out = (
        shape((tokens, width)),
        shape((width, four)),
        shape((2 * tokens, LANES)),
        shape((tokens, LANES)),
        shape((tokens, LANES)),
        shape((2 * tokens, LANES), f32),
    )
    state = pltpu.VMEM((4 * span, LANES), f32)
    return steps.run(
        functools.partial(attend_kernel, span),
        near_out,
        (near, slot),
        (cosine, sine),
        far=(*pieces,),
        pinned=(first,),
        far_outs=far_out,
        scratch=(
            pltpu.VMEM((tokens, width), jnp.bfloat16),
            pltpu.VMEM((width, four), jnp.bfloat16),
            pltpu.VMEM((32 * quarters, four), jnp.bfloat16),
            pltpu.VMEM((tokens, four), f32),
            pltpu.VMEM((2 * tokens, LANES), jnp.bfloat16),
            pltpu.VMEM((tokens, LANES), jnp.bfloat16),
            pltpu.VMEM((tokens, LANES), jnp.bfloat16),
            pltpu.VMEM((2 * tokens, LANES), f32),
            pltpu.VMEM((2, 4 * span, tokens), f32),
            state,
            state,
            pltpu.SemaphoreType.DMA((turns + 2 * quarters,)),
            pltpu.SemaphoreType.DMA((4 + turns // 2 + turns,)),
        ),
        limit=60,
        micros=33,
    )


def weight_grads(
    owner_ref, fields_ref, weight_ref, gain_ref, row_ref, branch_ref, heads, copies, last_ref, normed_ref, heads_ref, sum_ref
):
    quarters = last_ref.shape[0]
    four = weight_ref.shape[1]
    shard = weight_ref.shape[0] // quarters
    half = shard // 2
    size = 2 * DH
    tall = branch_ref.shape[1] // 2
    for index, copy in enumerate(heads):
        columns = narrow(unfold(wide(branch_ref[owner_ref[index], tall:, :])))
        copy.wait()
        rows = columns.shape[0]
        sum_ref[index * rows : (index + 1) * rows, :] = columns
    ones = jnp.ones((8, four), jnp.bfloat16)
    gap = jnp.zeros((half, LANES), jnp.float32)
    for quarter in range(quarters):
        here = slice(quarter * shard, (quarter + 1) * shard)
        copies[quarter].wait()
        total = row_dot(normed_ref[:, here], fields_ref[...])
        last_ref[quarter, :shard, :] = narrow(total)
        share = narrow(total * wide(weight_ref[here, :]))
        attn = lane_dot(ones, share) / gain_ref[:8, here]
        rows = jnp.concatenate([attn, row_ref[:, here]], axis=0)
        out_grad = row_dot(heads_ref[:, here], sum_ref[...])
        one, two = out_grad[:half], out_grad[half:]
        both = jnp.concatenate([one, gap], axis=1) + pltpu.roll(
            jnp.concatenate([two, gap], axis=1), size, 1
        )
        last_ref[quarter, shard : shard + half, :] = narrow(both)
        end = shard + half
        last_ref[quarter, end : end + 16, :] = narrow(rows)
        last_ref[quarter, end + 16 :, :] = jnp.zeros_like(last_ref[quarter, end + 16 :, :])


def attend_back_kernel(
    span,
    near_ref,
    slot_ref,
    owner_ref,
    grad_ref,
    total_ref,
    weight_ref,
    gain_ref,
    row_ref,
    *refs,
):
    (*heads_in, normed_in, cos_in, sin_in, query_in, key_in, value_in, mixed_in), refs = refs[:15], refs[15:]
    out_ref, last_ref, cos_ref, sin_ref, query_ref, key_ref, value_ref, mixed_ref, *refs = refs
    head_ref, delta_ref, query_sum, key_sum, value_sum, normed_ref, heads_ref, sum_ref, done = refs
    spans = near_ref.shape[0]
    block = 2 * span
    pair = 2 * block
    turns = spans // 2
    factor = LOG2E / math.sqrt(DH)
    scale = 1.0 / math.sqrt(DH)
    lane = lax.broadcasted_iota(jnp.int32, (span, LANES), 1)
    copies = [
        fetch(source, target, done.at[index])
        for index, (source, target) in enumerate(
            (
                (mixed_in, mixed_ref),
                (key_in, key_ref),
                (query_in, query_ref),
                (value_in, value_ref),
                (cos_in, cos_ref),
                (sin_in, sin_ref),
            )
        )
    ]

    quarters = last_ref.shape[0]
    shard = normed_ref.shape[1] // quarters
    heads = [
        fetch(piece, heads_ref.at[pl.ds(index * block, block), :], done.at[6 + index])
        for index, piece in enumerate(heads_in)
    ]
    normed = [
        fetch(
            normed_in.at[:, pl.ds(quarter * shard, shard)],
            normed_ref.at[:, pl.ds(quarter * shard, shard)],
            done.at[6 + len(heads) + quarter],
        )
        for quarter in range(quarters)
    ]

    def split(index, _):
        slot = slot_ref[index]
        grad = wide(grad_ref[slot // 2, rows_at(slot % 2, span), :])
        tail = wide(grad_ref[slot // 2, 2 * span : 3 * span, :])
        first = (index // 2) * 4 + index % 2
        one = jnp.where(lane < DH, grad, 0.0)
        tail = pltpu.roll(tail, 32 + 64 * (slot % 2), 1)
        two = jnp.where(lane < 32, pltpu.roll(grad, 32, 1), tail)
        two = jnp.where(lane < DH, two, 0.0)
        head_ref[rows_at(first, span), :] = narrow(one)
        head_ref[rows_at(first + 2, span), :] = narrow(two)
        return 0

    lax.fori_loop(0, spans, split, 0, unroll=4)
    copies[0].wait()

    def prepare(turn, _):
        here = rows_at(turn, pair)
        product = wide(head_ref[here, :]) * mixed_ref[here, :]
        delta_ref[rows_at(turn, 8), :] = rows_of(jnp.ones((8, LANES), jnp.float32), product)
        query_sum[here, :] = jnp.zeros((pair, LANES), jnp.float32)
        return 0

    lax.fori_loop(0, turns, prepare, 0, unroll=2)
    for copy in copies[1:]:
        copy.wait()

    def turned_back(field, index):
        cosine = cos_ref[rows_at(index, span), :]
        sine = sin_ref[rows_at(index, span), :]
        field = field * scale
        return wide(narrow(field * cosine - swapped(field) * sine))

    def one_block(turn, _):
        key = key_ref[rows_at(turn, block), :]
        value = value_ref[rows_at(turn, block), :]

        def one_step(step, diagonal):
            here = rows_at(step, pair)
            query = query_ref[here, :]
            head = head_ref[here, :]
            level = total_ref[rows_at(step, 8), :][:1]
            delta = delta_ref[rows_at(step, 8), :][:1]
            probs = jnp.exp2(lane_dot(key, query) * factor - level)
            if diagonal:
                row = lax.broadcasted_iota(jnp.int32, (block, pair), 0)
                column = lax.broadcasted_iota(jnp.int32, (block, pair), 1) % block
                probs = jnp.where(row <= column, probs, 0.0)
            d_scores = narrow(probs * (lane_dot(value, head) - delta))
            query_sum[here, :] += row_dot(d_scores, key)
            return plain_dot(d_scores, query), plain_dot(narrow(probs), head)

        key_part, value_part = one_step(turn, True)
        key_sum[...] = key_part
        value_sum[...] = value_part

        def two_steps(index, _):
            step = turn + 1 + 2 * index
            key_one, value_one = one_step(step, False)
            key_two, value_two = one_step(step + 1, False)
            key_sum[...] += key_one + key_two
            value_sum[...] += value_one + value_two
            return 0

        left = turns - 1 - turn
        lax.fori_loop(0, left // 2, two_steps, 0)

        @pl.when(left % 2 == 1)
        def _():
            key_one, value_one = one_step(turns - 1, False)
            key_sum[...] += key_one
            value_sum[...] += value_one

        for part in range(2):
            index = 2 * turn + part
            here = rows_at(near_ref[index], span)
            rows = slice(part * span, (part + 1) * span)
            first = rows_at((index // 2) * 4 + index % 2, span)
            second = rows_at((index // 2) * 4 + index % 2 + 2, span)
            one = turned_back(query_sum[first, :], index)
            two = turned_back(query_sum[second, :], index)
            three = turned_back(key_sum[rows, :], index)
            out_ref[here, :] = narrow(join_fields(one, two, three, value_sum[rows, :]))
        return 0

    lax.fori_loop(0, turns, one_block, 0)
    weight_grads(
        owner_ref, out_ref, weight_ref, gain_ref, row_ref, grad_ref, heads, normed, last_ref, normed_ref, heads_ref, sum_ref
    )


def attend_back(
    steps, near, slot, owners, grad, total, weights, cosine, sine, query, key, value, mixed, heads, normed, packed, span
):
    tokens, width = normed.shape
    f32 = jnp.float32
    rows = pltpu.VMEM((2 * span, LANES), f32)
    shard = 4 * DH
    return steps.run(
        functools.partial(attend_back_kernel, span),
        (shape((tokens, 4 * DH)), shape((width // shard, packed, 4 * DH))),
        (near, slot, owners),
        (grad, total, *weights),
        far=heads,
        pinned=(normed, cosine, sine, query, key, value, mixed),
        scratch=(
            pltpu.VMEM(cosine.shape, f32),
            pltpu.VMEM(cosine.shape, f32),
            pltpu.VMEM(query.shape, jnp.bfloat16),
            pltpu.VMEM(key.shape, jnp.bfloat16),
            pltpu.VMEM(value.shape, jnp.bfloat16),
            pltpu.VMEM(mixed.shape, f32),
            pltpu.VMEM((2 * tokens, LANES), jnp.bfloat16),
            pltpu.VMEM(total.shape, f32),
            pltpu.VMEM((2 * tokens, LANES), f32),
            rows,
            rows,
            pltpu.VMEM((tokens, width), jnp.bfloat16),
            pltpu.VMEM((tokens, width), jnp.bfloat16),
            pltpu.VMEM((tokens, 2 * LANES), jnp.bfloat16),
            pltpu.SemaphoreType.DMA((6 + len(heads) + width // shard,)),
        ),
        limit=60,
        micros=38,
    )


def turn_tables(tokens):
    half = DH // 2
    freqs = jnp.exp(-math.log(rope_base) * 2.0 * jnp.arange(half, dtype=jnp.float32) / DH)
    angle = jnp.arange(tokens, dtype=jnp.int32).astype(jnp.float32)[:, None] * freqs[None, :]
    gap = jnp.zeros((tokens, LANES - DH), jnp.float32)
    cosine, sine = jnp.cos(angle), jnp.sin(angle)
    return (
        jnp.concatenate([cosine, cosine, gap], axis=1),
        jnp.concatenate([-sine, sine, gap], axis=1),
    )


def swap(block, bits):
    routes = [(i, i ^ bits) for i in range(lax.axis_size("ctx"))]
    return lax.ppermute(block, "ctx", routes)


def swap_split(block, even, odd):
    routes = [(i, i ^ (odd if i & CORE else even)) for i in range(lax.axis_size("ctx"))]
    return lax.ppermute(block, "ctx", routes)


def gather_spans(block, core, between=None):
    from_x = swap(block, ALONG_X)
    from_y = swap(block, ALONG_Y)
    twin = swap(block, CORE)
    first = between(from_x, from_y) if between else from_x
    corner = swap_split(jnp.where(core[0] == 0, first, from_y), ALONG_Y, ALONG_X)
    return [block, from_x, from_y, corner] + [
        twin,
        swap(first, CORE),
        swap(from_y, CORE),
        swap(corner, CORE),
    ]


def gather_direct(block):
    blocks = [block] + [swap(block, way) for way in (ALONG_X, ALONG_Y, ALONG_X | ALONG_Y)]
    return blocks + [swap(part, CORE) for part in blocks]


def open_scatter(steps, own, twin, core, limit=20):
    rows, width = sum(part.shape[0] for part in own) // 4, own[0].shape[1]
    some = shape((rows, width), jnp.float32)
    return steps.run(
        add_twin_kernel,
        (shape((2 * rows, width)), some, some),
        (core,),
        (*own, *twin),
        limit=limit,
    )


def turn_scatter(steps, keep, got):
    late = steps.run(
        add_late_kernel,
        shape(keep.shape),
        (),
        (),
        far=(keep, got),
        scratch=(
            pltpu.VMEM(keep.shape, jnp.float32),
            pltpu.VMEM(keep.shape, jnp.bfloat16),
            pltpu.SemaphoreType.DMA((2,)),
        ),
        limit=60,
    )
    return swap_split(late, ALONG_X, ALONG_Y)


def plane_layer(
    activations,
    span_order,
    w_query,
    w_key,
    w_value,
    w_out,
    w_gate,
    w_up,
    w_down,
    attn_gain,
    ffn_gain,
    cotangent,
):
    f32 = jnp.float32
    cycles = lax.axis_size("ctx")
    quarters = lax.axis_size("fsdp")
    mine = lax.axis_index("ctx")
    span = activations.shape[2]
    width = activations.shape[3]
    tokens = 2 * span
    length = cycles * tokens
    half = length // 2
    shard = w_query.shape[0]
    four = 4 * DH
    hidden_size = quarters * w_down.shape[0]
    strip = hidden_size // (quarters * cycles)
    part = hidden_size // cycles
    slab = w_out.shape[0] // cycles
    slabs = width // four
    packed = shard + slabs * slab + 32
    owners = mine ^ jnp.array(RELATIVE, jnp.int32)
    away = mine ^ jnp.arange(cycles, dtype=jnp.int32)
    seat = (away & 1) * 4 + (away >> 2) * 2 + ((away >> 1) & 1)
    slot_of = jnp.argsort(span_order).astype(jnp.int32)
    near_slot = 2 * seat[slot_of // 2] + slot_of % 2
    here = mine.reshape(1).astype(jnp.int32)
    core = here & CORE
    stream = activations.reshape(tokens, width)
    grad_rows = cotangent.reshape(tokens, width)

    steps = Steps(core)
    low = jnp.bfloat16

    gains = jnp.pad(jnp.stack([attn_gain, ffn_gain]), ((0, 30), (0, four - shard)))
    window = pltpu.VMEM((shard, 2 * LANES), low)
    first = steps.run(
        pack_kernel,
        shape((packed, four)),
        (here,),
        (gains,),
        pinned=(w_query, w_key, w_value, w_out),
        scratch=(
            window,
            window,
            window,
            pltpu.VMEM((slab, width), low),
            pltpu.SemaphoreType.DMA((4,)),
        ),
        limit=60,
    )
    first = lax.all_gather(first, "fsdp", axis=0)
    own_strips = steps.run(
        strip_kernel,
        shape((shard, 2 * part + width * strip // shard)),
        (here,),
        (w_gate, w_up, w_down),
        limit=28,
    )
    all_strips = lax.all_gather(own_strips, "fsdp", axis=0, tiled=True)
    cosine, sine = turn_tables(length)
    streams = gather_spans(
        stream, core, lambda one, two: after(one, two, own_strips, cosine, sine, near_slot, slot_of)
    )
    out_part = first[:, shard : shard + slabs * slab].reshape(quarters * slabs * slab, four)
    folded, gains, level, normed1, w_fields, query, key, value, attended = attend(
        steps, near_slot, slot_of, cosine, sine, first, streams, span
    )
    grads = gather_spans(
        after(grad_rows, streams[3]), core, lambda one, two: after(one, two, folded)
    )
    outs = gather_direct(out_part)
    steps.wait(*outs, grads[3])
    folded = lax.all_to_all(after(folded, *grads[1:3], *outs[1:4]), "ctx", 0, 0)
    one_tile = shape((tokens, LANES), f32)
    stream_one, normed2, inverse, heads_low, full_out = steps.run(
        branch_kernel,
        (shape((tokens, width), f32), shape((tokens, width)), one_tile, shape((tokens, width))),
        (owners,),
        (folded, stream, gains),
        far=outs,
        far_outs=(shape((width, width)),),
        scratch=(
            pltpu.VMEM((width, width), low),
            pltpu.VMEM((cycles, *outs[0].shape), low),
            pltpu.SemaphoreType.DMA((cycles,)),
        ),
        limit=60,
        micros=6,
    )
    normed2 = gather_spans(normed2, core)
    def strips(pieces, grad_pieces, *before):
        results = steps.run(
            functools.partial(strips_kernel, len(pieces), bool(before)),
            (
                shape((part, width), low if before else f32),
                *(shape((tokens, width)),) * 4,
                shape((3 * tokens, width)),
                shape((tokens, width)),
            ),
            (),
            before,
            far=(*pieces, *grad_pieces),
            pinned=(all_strips,),
            far_outs=(shape((half, 2 * part)),),
            scratch=(
                pltpu.VMEM((part, width), f32),
                pltpu.VMEM((width, 2 * part), low),
                pltpu.VMEM((part, width), low),
                pltpu.VMEM((half, width), low),
                pltpu.VMEM((half, width), low),
                pltpu.VMEM((half, 2 * part), low),
                pltpu.SemaphoreType.DMA((2 * len(pieces),)),
                pltpu.SemaphoreType.DMA((len(pieces) // 2,)),
                pltpu.SemaphoreType.DMA((1 + quarters * (shard // strip),)),
            ),
                limit=60,
            micros=20,
        )
        return results[0], results[1:5], results[5], results[6], results[7]

    early, later = (4, 5, 6, 0), (1, 2, 3, 7)
    down_early, streams_early, sums_twin, sum_self, both_early = strips(
        [normed2[i] for i in early], [grads[i] for i in early]
    )
    heads = gather_spans(
        after(heads_low, normed2[1], normed2[2]), core, lambda one, two: after(one, two, down_early)
    )
    steps.wait(heads[1], heads[2])
    twins = [swap(block, CORE) for block in streams_early[:3]]
    normed2[7] = swap(after(normed2[3], down_early), CORE)
    down_sum, streams_later, sums_own, sum_corner, both_later = strips(
        [normed2[i] for i in later], [grads[i] for i in later], down_early
    )
    twins.append(swap(streams_later[3], CORE))
    grad_down = lax.psum_scatter(
        after(down_sum, heads[3]), "fsdp", scatter_dimension=0, tiled=True
    )
    sums_twin = swap(after(sums_twin, down_sum), CORE)
    sum_corner = swap(sum_corner, CORE)
    send, keep, total = open_scatter(
        steps, (streams_early[3], *streams_later[:3]), twins, core, 60
    )
    got = swap_split(send, ALONG_Y, ALONG_X)
    steps.wait(heads[3])
    grad_both, grad_ffn = steps.run(
        functools.partial(strip_grad_kernel, cycles),
        (shape((width, 2 * part)), shape((8, width), f32)),
        (),
        (gains,),
        far=[normed2[i] for i in early + later],
        pinned=(both_early, both_later, all_strips),
        scratch=(
            pltpu.VMEM((length, width), low),
            pltpu.VMEM((length, 2 * part), low),
            pltpu.VMEM((width, 2 * part), low),
            pltpu.SemaphoreType.DMA((cycles + 3,)),
        ),
        limit=60,
        micros=12,
    )
    grad_both = lax.psum_scatter(after(grad_both, got), "fsdp", scatter_dimension=0, tiled=True)
    late_got = turn_scatter(steps, keep, got)
    ffn_send, ffn_keep, ffn_total = open_scatter(
        steps, (sum_self, sums_own), (sums_twin, sum_corner), core
    )
    d_stream_one, d_heads = steps.run(
        branch_back_kernel,
        (
            shape((tokens, width), f32),
            shape((cycles, 6 * span, LANES)),
        ),
        (),
        (total, got, late_got, grad_rows, stream_one, inverse, gains, full_out),
        limit=28,
        micros=4,
    )
    d_heads = lax.all_to_all(d_heads, "ctx", 0, 0)
    ffn_got = swap_split(after(ffn_send, d_heads), ALONG_Y, ALONG_X)
    grad_downs = gather_direct(after(grad_down, d_heads))
    d_fields, last = attend_back(
        steps,
        near_slot,
        slot_of,
        owners,
        d_heads,
        level,
        (w_fields, gains, grad_ffn),
        cosine,
        sine,
        query,
        key,
        value,
        attended,
        heads,
        normed1,
        packed,
        span,
    )
    last = after(last, ffn_got, *grad_downs[1:4])
    last = lax.psum_scatter(last, "fsdp", scatter_dimension=0, tiled=False)
    steps.wait(ffn_got, *grad_downs[1:4])

    def stream_grad(start):
        return steps.run(
            functools.partial(stream_grad_kernel, start),
            shape((half, width)),
            (),
            (d_fields, w_fields),
            micros=2,
        )

    d_normed1_twin = swap(stream_grad(half), CORE)
    d_normed1_own = stream_grad(0)
    send, keep, total = open_scatter(steps, (d_normed1_own,), (d_normed1_twin,), core)
    both_pieces = gather_spans(
        after(grad_both, d_fields), core, lambda one, two: after(one, two, send)
    )
    got = swap_split(send, ALONG_Y, ALONG_X)
    ffn_late_got = turn_scatter(steps, ffn_keep, ffn_got)
    steps.wait(both_pieces[1], both_pieces[2])
    grad_down = steps.run(
        place_down_kernel,
        (),
        (owners,),
        (),
        far=grad_downs,
        far_outs=(shape((hidden_size // quarters, width), f32),),
        scratch=(
            pltpu.VMEM((cycles, strip, width), low),
            pltpu.VMEM((cycles, strip, width), f32),
            pltpu.SemaphoreType.DMA((2, cycles)),
        ),
        limit=60,
        micros=1000,
    )[0]
    wide_strip = shape((shard, hidden_size), f32)
    grad_gate, grad_up = steps.run(
        place_strips_kernel,
        (),
        (owners,),
        (),
        far=both_pieces,
        far_outs=(wide_strip, wide_strip),
        scratch=(
            pltpu.VMEM((cycles, shard, 2 * part), low),
            pltpu.VMEM((cycles, shard, 2 * part), f32),
            pltpu.SemaphoreType.DMA((cycles,)),
            pltpu.SemaphoreType.DMA((cycles, 2 * quarters)),
        ),
        limit=60,
    )
    output = steps.run(
        output_kernel,
        shape((tokens, width)),
        (),
        (ffn_total, ffn_got, ffn_late_got, stream_one),
    )
    late_got = turn_scatter(steps, keep, got)
    last = gather_direct(after(last, grad_down))
    narrow_grad = shape((shard, width // 2), f32)
    wide_grad = shape((shard, width), f32)
    grad_gains, input_grad, *weight_grads = steps.run(
        finish_kernel,
        (shape((16, four), f32),),
        (owners,),
        (
            total,
            got,
            late_got,
            stream,
            d_stream_one,
            gains,
        ),
        far=last,
        far_outs=(
            shape((tokens, width), f32),
            wide_grad,
            narrow_grad,
            narrow_grad,
            wide_grad,
        ),
        scratch=(
            pltpu.VMEM((tokens, width), f32),
            pltpu.VMEM((cycles, packed, four), low),
            pltpu.VMEM((shard, width), f32),
            pltpu.VMEM((shard, width // 2), f32),
            pltpu.VMEM((shard, width // 2), f32),
            pltpu.VMEM((shard, width), f32),
            pltpu.SemaphoreType.DMA((cycles,)),
            pltpu.SemaphoreType.DMA((1,)),
            pltpu.SemaphoreType.DMA((8,)),
        ),
        limit=60,
    )
    grad_query, grad_key, grad_value, grad_out = weight_grads
    return (
        output.reshape(activations.shape),
        input_grad.reshape(activations.shape),
        grad_query,
        grad_key,
        grad_value,
        grad_out,
        grad_gate,
        grad_up,
        grad_down,
        grad_gains[0],
        grad_gains[8],
    )


def solution(mesh):
    in_specs = (
        P("fsdp", "ctx", None, None),
        P(),
        P("fsdp", None),
        P("fsdp", None),
        P("fsdp", None),
        P("fsdp", None),
        P("fsdp", None),
        P("fsdp", None),
        P("fsdp", None),
        P("fsdp"),
        P("fsdp"),
        P("fsdp", "ctx", None, None),
    )
    out_specs = (
        P("fsdp", "ctx", None, None),
        P("fsdp", "ctx", None, None),
        P("fsdp", None),
        P("fsdp", None),
        P("fsdp", None),
        P("fsdp", None),
        P("fsdp", None),
        P("fsdp", None),
        P("fsdp", None),
        P("fsdp"),
        P("fsdp"),
    )
    cycles = mesh.shape["ctx"]

    def per_device(*arrays):
        heads = arrays[3].shape[1] // DH
        if cycles == len(RELATIVE) == heads and arrays[2].shape == (4 * DH, 2 * heads * DH):
            return plane_layer(*arrays)
        return ring_layer(*arrays)

    return jax.shard_map(
        per_device, mesh=mesh, in_specs=in_specs, out_specs=out_specs, check_vma=False
    )
```

```python
import functools
import math

import jax
import jax.numpy as jnp
from jax import lax
from jax.experimental import pallas as pl
from jax.experimental.pallas import tpu as pltpu
from jax.sharding import PartitionSpec as P

DH = 96


epsilon = 1e-05
rope_base = 100000.0
masked_score = -1e30
LOG2E = math.log2(math.e)


def passed_along(block, axis, distance):
    devices = range(lax.axis_size(axis))
    route = [((i - distance) % len(devices), i) for i in devices]
    return lax.ppermute(block, axis, route)


def rope_tables(places):
    half = DH // 2
    freqs = jnp.exp(-math.log(rope_base) * 2.0 * jnp.arange(half, dtype=jnp.float32) / DH)
    angle = places.astype(jnp.float32)[:, None] * freqs[None, :]
    return (jnp.cos(angle)[:, None, :], jnp.sin(angle)[:, None, :])


def rope_turn(field, cosine, sine):
    half = DH // 2
    first = field[..., :half]
    second = field[..., half:]
    return jnp.concatenate(
        [first * cosine - second * sine, second * cosine + first * sine], axis=-1
    )


def rope_back(field, cosine, sine):
    half = DH // 2
    first = field[..., :half]
    second = field[..., half:]
    return jnp.concatenate(
        [first * cosine + second * sine, second * cosine - first * sine], axis=-1
    )


def norm_back(d_normed, stream, inv_rms, gain):
    scaled = d_normed * gain
    cubed = inv_rms * inv_rms * inv_rms
    return inv_rms * scaled - stream * cubed * jnp.mean(scaled * stream, axis=-1, keepdims=True)


def ring_layer(
    activations,
    span_order,
    w_query,
    w_key,
    w_value,
    w_out,
    w_gate,
    w_up,
    w_down,
    attn_gain,
    ffn_gain,
    cotangent,
):
    cycles = lax.axis_size("ctx")
    mine = lax.axis_index("ctx")
    span = activations.shape[2]
    width = activations.shape[3]
    tokens = 2 * span
    heads = w_query.shape[1] // DH
    kv_heads = w_key.shape[1] // DH
    group = heads // kv_heads
    scale = 1.0 / math.sqrt(DH)
    offsets = jnp.arange(span, dtype=jnp.int32)

    def places_of(owner):
        span_ids = lax.dynamic_slice_in_dim(span_order, 2 * owner, 2)
        return (span_ids[:, None] * span + offsets[None, :]).reshape(tokens)

    query_places = places_of(mine)
    cosine, sine = rope_tables(query_places)
    gathered = (
        lax.all_gather(w_query, "fsdp", axis=0, tiled=True),
        lax.all_gather(w_key, "fsdp", axis=0, tiled=True),
        lax.all_gather(w_value, "fsdp", axis=0, tiled=True),
        lax.all_gather(w_out, "fsdp", axis=0, tiled=True),
        lax.all_gather(w_gate, "fsdp", axis=0, tiled=True),
        lax.all_gather(w_up, "fsdp", axis=0, tiled=True),
        lax.all_gather(w_down, "fsdp", axis=0, tiled=True),
        lax.all_gather(attn_gain, "fsdp", axis=0, tiled=True),
        lax.all_gather(ffn_gain, "fsdp", axis=0, tiled=True),
    )
    (
        full_query,
        full_key,
        full_value,
        full_out,
        full_gate,
        full_up,
        full_down,
        gain_one,
        gain_two,
    ) = gathered
    stream = activations.reshape(tokens, width).astype(jnp.float32)
    inv_one = lax.rsqrt(jnp.mean(stream * stream, axis=-1, keepdims=True) + epsilon)
    normed1 = (stream * inv_one * gain_one).astype(jnp.bfloat16)
    query_raw = jnp.dot(normed1, full_query, preferred_element_type=jnp.float32).reshape(
        tokens, heads, DH
    )
    queries = (
        rope_turn(query_raw, cosine, sine).astype(jnp.bfloat16).reshape(tokens, kv_heads, group, DH)
    )
    key_raw = jnp.dot(normed1, full_key, preferred_element_type=jnp.float32).reshape(
        tokens, kv_heads, DH
    )
    keys = rope_turn(key_raw, cosine, sine).astype(jnp.bfloat16)
    values = (
        jnp.dot(normed1, full_value, preferred_element_type=jnp.float32)
        .astype(jnp.bfloat16)
        .reshape(tokens, kv_heads, DH)
    )

    def scores_with(key_piece, owner):
        scores = (
            jnp.einsum("tjgd,sjd->jgts", queries, key_piece, preferred_element_type=jnp.float32)
            * scale
        )
        counted = places_of(owner)[None, :] <= query_places[:, None]
        return jnp.where(counted, scores, masked_score)

    def absorb(state, key_piece, value_piece, owner):
        running_top, running_total, running_sum = state
        scores = scores_with(key_piece, owner)
        new_top = jnp.maximum(running_top, jnp.max(scores, axis=-1, keepdims=True))
        fading = jnp.exp(running_top - new_top)
        weights = jnp.exp(scores - new_top)
        running_total = fading * running_total + jnp.sum(weights, axis=-1, keepdims=True)
        running_sum = fading * running_sum + jnp.einsum(
            "jgts,sjd->jgtd",
            weights.astype(jnp.bfloat16),
            value_piece,
            preferred_element_type=jnp.float32,
        )
        return (new_top, running_total, running_sum)

    start_state = (
        jnp.full((kv_heads, group, tokens, 1), masked_score, jnp.float32),
        jnp.zeros((kv_heads, group, tokens, 1), jnp.float32),
        jnp.zeros((kv_heads, group, tokens, DH), jnp.float32),
    )
    state = absorb(start_state, keys, values, mine)

    def forward_turn(turn_index, carry):
        state_now, key_piece, value_piece = carry
        key_piece, value_piece = passed_along((key_piece, value_piece), "ctx", 1)
        owner = (mine - turn_index) % cycles
        return (absorb(state_now, key_piece, value_piece, owner), key_piece, value_piece)

    state, _, _ = lax.fori_loop(1, cycles, forward_turn, (state, keys, values))
    running_top, running_total, running_sum = state
    attended = running_sum / running_total
    log_total = running_top + jnp.log(running_total)
    attended_low = (
        jnp.transpose(attended, (2, 0, 1, 3)).reshape(tokens, heads * DH).astype(jnp.bfloat16)
    )
    stream_one = stream + jnp.dot(attended_low, full_out, preferred_element_type=jnp.float32)
    inv_two = lax.rsqrt(jnp.mean(stream_one * stream_one, axis=-1, keepdims=True) + epsilon)
    normed2 = (stream_one * inv_two * gain_two).astype(jnp.bfloat16)
    gate = jnp.dot(normed2, full_gate, preferred_element_type=jnp.float32)
    up_part = jnp.dot(normed2, full_up, preferred_element_type=jnp.float32)
    sigma = jax.nn.sigmoid(gate)
    hidden = (gate * sigma * up_part).astype(jnp.bfloat16)
    stream_two = stream_one + jnp.dot(hidden, full_down, preferred_element_type=jnp.float32)
    output = stream_two.astype(jnp.bfloat16).reshape(activations.shape)
    back_weights = (
        lax.all_gather(w_query, "fsdp", axis=0, tiled=True),
        lax.all_gather(w_key, "fsdp", axis=0, tiled=True),
        lax.all_gather(w_value, "fsdp", axis=0, tiled=True),
        lax.all_gather(w_out, "fsdp", axis=0, tiled=True),
        lax.all_gather(w_gate, "fsdp", axis=0, tiled=True),
        lax.all_gather(w_up, "fsdp", axis=0, tiled=True),
        lax.all_gather(w_down, "fsdp", axis=0, tiled=True),
        lax.all_gather(attn_gain, "fsdp", axis=0, tiled=True),
        lax.all_gather(ffn_gain, "fsdp", axis=0, tiled=True),
    )
    (
        back_query,
        back_key,
        back_value,
        back_out,
        back_gate,
        back_up,
        back_down,
        back_gain_one,
        back_gain_two,
    ) = back_weights
    grad_rows = cotangent.reshape(tokens, width)
    grad_stream = grad_rows.astype(jnp.float32)
    grad_down = jnp.einsum("tf,td->fd", hidden, grad_rows, preferred_element_type=jnp.float32)
    d_hidden = jnp.einsum("td,fd->tf", grad_rows, back_down, preferred_element_type=jnp.float32)
    d_gate = (d_hidden * up_part * sigma * (1.0 + gate * (1.0 - sigma))).astype(jnp.bfloat16)
    d_up = (d_hidden * gate * sigma).astype(jnp.bfloat16)
    grad_gate = jnp.einsum("td,tf->df", normed2, d_gate, preferred_element_type=jnp.float32)
    grad_up = jnp.einsum("td,tf->df", normed2, d_up, preferred_element_type=jnp.float32)
    d_normed2 = jnp.einsum(
        "tf,df->td", d_gate, back_gate, preferred_element_type=jnp.float32
    ) + jnp.einsum("tf,df->td", d_up, back_up, preferred_element_type=jnp.float32)
    grad_ffn_gain = jnp.sum(d_normed2 * stream_one * inv_two, axis=0)
    d_stream_one = grad_stream + norm_back(d_normed2, stream_one, inv_two, back_gain_two)
    d_branch = d_stream_one.astype(jnp.bfloat16)
    grad_out = jnp.einsum("tk,td->kd", attended_low, d_branch, preferred_element_type=jnp.float32)
    d_attended = jnp.einsum(
        "td,kd->tk", d_branch, back_out, preferred_element_type=jnp.float32
    ).astype(jnp.bfloat16)
    d_heads = jnp.transpose(d_attended.reshape(tokens, kv_heads, group, DH), (1, 2, 0, 3))
    delta = jnp.sum(d_heads.astype(jnp.float32) * attended, axis=-1, keepdims=True)

    def back_step(d_queries, d_keys, d_values, key_piece, value_piece, owner):
        scores = scores_with(key_piece, owner)
        probs = jnp.exp(scores - log_total)
        d_values = d_values + jnp.einsum(
            "jgts,jgtd->sjd",
            probs.astype(jnp.bfloat16),
            d_heads,
            preferred_element_type=jnp.float32,
        )
        d_probs = jnp.einsum(
            "jgtd,sjd->jgts", d_heads, value_piece, preferred_element_type=jnp.float32
        )
        d_scores = (probs * (d_probs - delta)).astype(jnp.bfloat16)
        d_queries = (
            d_queries
            + jnp.einsum("jgts,sjd->jgtd", d_scores, key_piece, preferred_element_type=jnp.float32)
            * scale
        )
        d_keys = (
            d_keys
            + jnp.einsum("jgts,tjgd->sjd", d_scores, queries, preferred_element_type=jnp.float32)
            * scale
        )
        return (d_queries, d_keys, d_values)

    def pass_grads(d_keys, d_values):
        return (
            passed_along(d_keys.astype(jnp.bfloat16), "ctx", 1).astype(d_keys.dtype),
            passed_along(d_values.astype(jnp.bfloat16), "ctx", 1).astype(d_values.dtype),
        )

    zero_queries = jnp.zeros((kv_heads, group, tokens, DH), jnp.float32)
    zero_keys = jnp.zeros((tokens, kv_heads, DH), jnp.float32)
    d_queries, d_keys, d_values = back_step(zero_queries, zero_keys, zero_keys, keys, values, mine)

    def backward_turn(turn_index, carry):
        d_queries_now, d_keys_now, d_values_now, key_piece, value_piece = carry
        key_piece, value_piece = passed_along((key_piece, value_piece), "ctx", 1)
        d_keys_now, d_values_now = pass_grads(d_keys_now, d_values_now)
        owner = (mine - turn_index) % cycles
        d_queries_now, d_keys_now, d_values_now = back_step(
            d_queries_now, d_keys_now, d_values_now, key_piece, value_piece, owner
        )
        return (d_queries_now, d_keys_now, d_values_now, key_piece, value_piece)

    d_queries, d_keys, d_values, _, _ = lax.fori_loop(
        1, cycles, backward_turn, (d_queries, d_keys, d_values, keys, values)
    )
    d_keys, d_values = pass_grads(d_keys, d_values)
    d_query_rows = jnp.transpose(d_queries, (2, 0, 1, 3)).reshape(tokens, heads, DH)
    d_query = rope_back(d_query_rows, cosine, sine).astype(jnp.bfloat16).reshape(tokens, heads * DH)
    d_key = rope_back(d_keys, cosine, sine).astype(jnp.bfloat16).reshape(tokens, kv_heads * DH)
    d_value = d_values.astype(jnp.bfloat16).reshape(tokens, kv_heads * DH)
    grad_query = jnp.einsum("td,tk->dk", normed1, d_query, preferred_element_type=jnp.float32)
    grad_key = jnp.einsum("td,tk->dk", normed1, d_key, preferred_element_type=jnp.float32)
    grad_value = jnp.einsum("td,tk->dk", normed1, d_value, preferred_element_type=jnp.float32)
    d_normed1 = (
        jnp.einsum("tk,dk->td", d_query, back_query, preferred_element_type=jnp.float32)
        + jnp.einsum("tk,dk->td", d_key, back_key, preferred_element_type=jnp.float32)
        + jnp.einsum("tk,dk->td", d_value, back_value, preferred_element_type=jnp.float32)
    )
    grad_attn_gain = jnp.sum(d_normed1 * stream * inv_one, axis=0)
    input_grad = (d_stream_one + norm_back(d_normed1, stream, inv_one, back_gain_one)).reshape(
        activations.shape
    )
    shares = (
        lax.psum_scatter(
            grad_query.astype(jnp.bfloat16), "fsdp", scatter_dimension=0, tiled=True
        ).astype(jnp.float32),
        lax.psum_scatter(
            grad_key.astype(jnp.bfloat16), "fsdp", scatter_dimension=0, tiled=True
        ).astype(jnp.float32),
        lax.psum_scatter(
            grad_value.astype(jnp.bfloat16), "fsdp", scatter_dimension=0, tiled=True
        ).astype(jnp.float32),
        lax.psum_scatter(
            grad_out.astype(jnp.bfloat16), "fsdp", scatter_dimension=0, tiled=True
        ).astype(jnp.float32),
        lax.psum_scatter(
            grad_gate.astype(jnp.bfloat16), "fsdp", scatter_dimension=0, tiled=True
        ).astype(jnp.float32),
        lax.psum_scatter(
            grad_up.astype(jnp.bfloat16), "fsdp", scatter_dimension=0, tiled=True
        ).astype(jnp.float32),
        lax.psum_scatter(
            grad_down.astype(jnp.bfloat16), "fsdp", scatter_dimension=0, tiled=True
        ).astype(jnp.float32),
        lax.psum_scatter(
            grad_attn_gain.astype(jnp.bfloat16), "fsdp", scatter_dimension=0, tiled=True
        ).astype(jnp.float32),
        lax.psum_scatter(
            grad_ffn_gain.astype(jnp.bfloat16), "fsdp", scatter_dimension=0, tiled=True
        ).astype(jnp.float32),
    )
    shares = (
        lax.psum(shares[0].astype(jnp.bfloat16), "ctx").astype(jnp.float32),
        lax.psum(shares[1].astype(jnp.bfloat16), "ctx").astype(jnp.float32),
        lax.psum(shares[2].astype(jnp.bfloat16), "ctx").astype(jnp.float32),
        lax.psum(shares[3].astype(jnp.bfloat16), "ctx").astype(jnp.float32),
        lax.psum(shares[4].astype(jnp.bfloat16), "ctx").astype(jnp.float32),
        lax.psum(shares[5].astype(jnp.bfloat16), "ctx").astype(jnp.float32),
        lax.psum(shares[6].astype(jnp.bfloat16), "ctx").astype(jnp.float32),
        lax.psum(shares[7].astype(jnp.bfloat16), "ctx").astype(jnp.float32),
        lax.psum(shares[8].astype(jnp.bfloat16), "ctx").astype(jnp.float32),
    )
    return (
        output,
        input_grad,
        shares[0],
        shares[1],
        shares[2],
        shares[3],
        shares[4],
        shares[5],
        shares[6],
        shares[7],
        shares[8],
    )


LANES = 128
CORE, ALONG_X, ALONG_Y = 1, 2, 4
RELATIVE = (0, 2, 4, 6, 1, 3, 5, 7)
MIB = 2**20
COST = 10**6


def lane_dot(left, right):
    return lax.dot_general(left, right, (((1,), (1,)), ((), ())), preferred_element_type=jnp.float32)


def plain_dot(left, right):
    return lax.dot_general(left, right, (((1,), (0,)), ((), ())), preferred_element_type=jnp.float32)


def row_dot(left, right):
    return lax.dot_general(left, right, (((0,), (0,)), ((), ())), preferred_element_type=jnp.float32)


def rows_at(index, size):
    return pl.ds(pl.multiple_of(index * size, size), size)


def wide(value):
    return value.astype(jnp.float32)


def narrow(value):
    return value.astype(jnp.bfloat16)


def lanes_of(rows):
    return lax.broadcasted_iota(jnp.int32, (rows, LANES), 1)


def shape(dims, kind=jnp.bfloat16):
    return jax.ShapeDtypeStruct(dims, kind)


def after(value, *others):
    return lax.optimization_barrier((value, *others))[0]


class Steps:

    def __init__(self, ticket):
        self.ticket = ticket
        self.pending = []

    def wait(self, *values):
        self.pending.extend(values)

    def run(
        self,
        body,
        outs,
        small,
        arrays,
        far=(),
        pinned=(),
        far_outs=(),
        scratch=(),
        limit=20,
        micros=2,
    ):
        near = pl.BlockSpec(memory_space=pltpu.VMEM)
        scalars = pl.BlockSpec(memory_space=pltpu.SMEM)
        away = pl.BlockSpec(memory_space=pl.ANY)
        stored = pl.BlockSpec(memory_space=pltpu.HBM)
        single = not isinstance(outs, tuple)
        out_shapes = ((outs,) if single else outs) + tuple(far_outs)
        out_specs = [near] * (len(out_shapes) - len(far_outs)) + [stored] * len(far_outs)
        ticket = after(self.ticket, *self.pending) if self.pending else self.ticket
        results = pl.pallas_call(
            lambda _, *refs: body(*refs),
            out_shape=out_shapes,
            in_specs=[scalars] * (1 + len(small))
            + [near] * len(arrays)
            + [away] * len(far)
            + [stored] * len(pinned),
            out_specs=out_specs,
            scratch_shapes=list(scratch),
            compiler_params=pltpu.CompilerParams(vmem_limit_bytes=limit * MIB),
            cost_estimate=pl.CostEstimate(
                flops=micros * COST, bytes_accessed=0, transcendentals=0
            ),
        )(ticket, *small, *arrays, *far, *pinned)
        self.pending = [results[-1]]
        return results[0] if single and not far_outs else results


def window_of(weight, start):
    base = jnp.minimum(start // LANES * LANES, weight.shape[1] - 2 * LANES)
    return weight.at[:, pl.ds(pl.multiple_of(base, LANES), 2 * LANES)], start - base


def drawn(window_ref, shift):
    size = 2 * LANES
    return pltpu.roll(wide(window_ref[...]), (size - shift) % size, 1)


def join_fields(one, two, three, four):
    lane = lanes_of(one.shape[0])
    two = pltpu.roll(two, 96, 1)
    three = pltpu.roll(three, 64, 1)
    four = pltpu.roll(four, 32, 1)
    return jnp.concatenate(
        [
            jnp.where(lane < 96, one, two),
            jnp.where(lane < 64, two, three),
            jnp.where(lane < 32, three, four),
        ],
        axis=1,
    )


def part_fields(block):
    lane = lanes_of(block.shape[0])
    one, two, three = (block[:, start : start + LANES] for start in (0, LANES, 2 * LANES))
    fields = (
        one,
        jnp.where(lane < 32, pltpu.roll(one, 32, 1), pltpu.roll(two, 32, 1)),
        jnp.where(lane < 64, pltpu.roll(two, 64, 1), pltpu.roll(three, 64, 1)),
        pltpu.roll(three, 96, 1),
    )
    return [jnp.where(lane < DH, field, 0.0) for field in fields]


def pack_kernel(
    mine_ref,
    gain_ref,
    query_in,
    key_in,
    value_in,
    out_in,
    first_ref,
    query_ref,
    key_ref,
    value_ref,
    out_ref,
    done,
):
    mine = mine_ref[0]
    shard = query_ref.shape[0]
    four = 4 * DH
    slab = out_ref.shape[0]
    slabs = out_ref.shape[1] // four
    query_window, query_shift = window_of(query_in, mine * 2 * DH)
    key_window, shift = window_of(key_in, mine * DH)
    value_window, _ = window_of(value_in, mine * DH)
    copies = [
        fetch(source, target, done.at[index])
        for index, (source, target) in enumerate(
            (
                (query_window, query_ref),
                (key_window, key_ref),
                (value_window, value_ref),
                (out_in.at[rows_at(mine, slab), :], out_ref),
            )
        )
    ]
    for copy in copies:
        copy.wait()
    query = drawn(query_ref, query_shift)
    key = pltpu.roll(drawn(key_ref, shift)[:, :LANES], 64, 1)
    value = pltpu.roll(drawn(value_ref, shift)[:, :LANES], 32, 1)
    lane = lanes_of(shard)
    first_ref[:shard, :LANES] = narrow(query[:, :LANES])
    first_ref[:shard, LANES : 2 * LANES] = narrow(jnp.where(lane < 64, query[:, LANES:], key))
    first_ref[:shard, 2 * LANES :] = narrow(jnp.where(lane < 32, key, value))
    for index in range(slabs):
        here = shard + index * slab
        first_ref[here : here + slab, :] = out_ref[:, index * four : (index + 1) * four]
    first_ref[shard + slabs * slab :, :] = gain_ref[...]


def strip_kernel(mine_ref, gate_ref, up_ref, down_ref, all_ref):
    quarters = gate_ref.shape[1] // (8 * LANES)
    start = 2 * quarters * LANES
    for index in range(quarters):
        place = rows_at(index * 8 + mine_ref[0], LANES)
        here = index * LANES
        all_ref[:, here : here + LANES] = gate_ref[:, place]
        here += quarters * LANES
        all_ref[:, here : here + LANES] = up_ref[:, place]
    rows = down_ref.shape[0] // 8
    cut = all_ref.shape[1] - start
    for index in range(all_ref.shape[0] // rows):
        all_ref[index * rows : (index + 1) * rows, start:] = down_ref[
            rows_at(mine_ref[0], rows), index * cut : (index + 1) * cut
        ]


def fold(block):
    rows = block.shape[0]
    tail = block[:, LANES:]
    lower = jnp.where(lanes_of(rows // 2) < 64, tail[: rows // 2], pltpu.roll(tail[rows // 2 :], 64, 1))
    return jnp.concatenate([block[:, :LANES], lower], axis=0)


def unfold(block):
    rows = block.shape[0] // 3 * 2
    half = rows // 2
    tail = block[rows:]
    keep = lanes_of(half) < 64
    tail = jnp.concatenate(
        [jnp.where(keep, tail, 0.0), jnp.where(keep, pltpu.roll(tail, 64, 1), 0.0)], axis=0
    )
    return jnp.concatenate([block[:rows], tail], axis=1)


def branch_kernel(owner_ref, folded_ref, stream_ref, gain_ref, *refs):
    pieces, refs = refs[:8], refs[8:]
    one_ref, normed_ref, inverse_ref, heads_ref, full_out, full_ref, piece_ref, done = refs
    copies = [fetch(piece, piece_ref.at[i], done.at[i]) for i, piece in enumerate(pieces)]
    width = full_ref.shape[1]
    slab = width // 32
    size = 2 * DH
    four = pieces[0].shape[1]
    gap = jnp.zeros((folded_ref.shape[1] // 3 * 2, LANES), jnp.float32)
    for index in range(0, folded_ref.shape[0], 2):
        one = unfold(wide(folded_ref[index]))
        two = unfold(wide(folded_ref[index + 1]))
        both = jnp.concatenate([one, gap], axis=1) + pltpu.roll(
            jnp.concatenate([two, gap], axis=1), size, 1
        )
        heads_ref[:, index * size : (index + 2) * size] = narrow(both)
    for index, copy in enumerate(copies):
        copy.wait()
        for quarter in range(4):
            row = pl.multiple_of(quarter * 8 * slab + owner_ref[index] * slab, 16)
            for part in range(width // four):
                start = (quarter * (width // four) + part) * slab
                full_ref[pl.ds(row, slab), part * four : (part + 1) * four] = piece_ref[
                    index, start : start + slab, :
                ]
    copy = fetch(full_ref, full_out, done.at[0])
    total = wide(stream_ref[...]) + plain_dot(heads_ref[...], full_ref[...])
    one_ref[...] = total
    inverse = lax.rsqrt(jnp.mean(total * total, axis=1, keepdims=True) + epsilon)
    normed_ref[...] = narrow(total * inverse * gain_ref[8:9])
    inverse_ref[...] = jnp.broadcast_to(inverse, inverse_ref.shape)
    copy.wait()


def strips_kernel(count, carry, *refs):
    before, refs = refs[: int(carry)], refs[int(carry) :]
    normed_in, grad_in, refs = refs[:count], refs[count : 2 * count], refs[2 * count :]
    strips_in, refs = refs[0], refs[1:]
    grad_out, stream_refs, refs = refs[0], refs[1 : 1 + count], refs[1 + count :]
    sum_ref, tail_ref, both_out, *refs = refs
    down_grad, gate_up_ref, down_ref, normed_ref, grad_ref, both_ref, done, out_done, weight_done = refs
    part = down_ref.shape[0]
    rows = normed_in[0].shape[0]
    size = 2 * rows
    columns = gate_up_ref.shape[1]
    strip = down_ref.shape[0] // 4
    shard = strips_in.shape[0] // 4
    cut = strips_in.shape[1] - columns
    copies = []

    def fetch_rows(index):
        here = pl.ds(index * rows, rows)
        copies.append(
            (
                fetch(normed_in[index], normed_ref.at[here, :], done.at[index]),
                fetch(grad_in[index], grad_ref.at[here, :], done.at[count + index]),
            )
        )

    fetch_rows(0)
    fetch_rows(1)
    gate_up_copy = fetch(strips_in.at[:, pl.ds(0, columns)], gate_up_ref, weight_done.at[0])
    downs = []
    for quarter in range(4):
        for index in range(shard // strip):
            downs.append(
                fetch(
                    strips_in.at[
                        pl.ds(quarter * shard + index * strip, strip), pl.ds(columns, cut)
                    ],
                    down_ref.at[pl.ds(quarter * strip, strip), pl.ds(index * cut, cut)],
                    weight_done.at[1 + quarter * (shard // strip) + index],
                )
            )
    for index in range(2, count):
        fetch_rows(index)
    outs = []
    gate_up_copy.wait()
    for step in range(count // 2):
        for index in (2 * step, 2 * step + 1):
            copies[index][0].wait()
        here = slice(step * size, (step + 1) * size)
        normed = normed_ref[here, :]
        gate = plain_dot(normed, gate_up_ref[:, :part])
        up = plain_dot(normed, gate_up_ref[:, part:])
        sigma = jax.nn.sigmoid(gate)
        turned = gate * sigma
        hidden = narrow(turned * up)
        if step == 0:
            for copy in downs:
                copy.wait()
        for index in (2 * step, 2 * step + 1):
            copies[index][1].wait()
        grad = grad_ref[here, :]
        d_hidden = lane_dot(grad, down_ref[...])
        d_gate = narrow(d_hidden * up * sigma * (1.0 + gate * (1.0 - sigma)))
        d_up = narrow(d_hidden * turned)
        both_ref[here, :part] = d_gate
        both_ref[here, part:] = d_up
        there = pl.ds(step * size, size)
        outs.append(fetch(both_ref.at[there, :], both_out.at[there, :], out_done.at[step]))
        d_normed = narrow(
            lane_dot(d_gate, gate_up_ref[:, :part]) + lane_dot(d_up, gate_up_ref[:, part:])
        )
        sums = narrow(plain_dot(hidden, down_ref[...]))
        for index in range(2):
            block = 2 * step + index
            stream_refs[block][...] = d_normed[index * rows : (index + 1) * rows]
            if block < count - 1:
                sum_ref[block * rows : (block + 1) * rows, :] = sums[
                    index * rows : (index + 1) * rows
                ]
            else:
                tail_ref[...] = sums[index * rows : (index + 1) * rows]
        product = row_dot(hidden, grad)
        if step == 0:
            down_grad[...] = product + before[0][...] if carry else product
        elif step < count // 2 - 1:
            down_grad[...] += product
        else:
            grad_out[...] = (down_grad[...] + product).astype(grad_out.dtype)
    for copy in outs:
        copy.wait()


def strip_grad_kernel(count, *refs):
    gain_ref, refs = refs[0], refs[1:]
    normed_in, (own_in, twin_in, strips_in), refs = refs[:count], refs[count : count + 3], refs[count + 3 :]
    out_ref, row_ref, normed_ref, both_ref, weight_ref, done = refs
    size = 2 * LANES
    rows = normed_in[0].shape[0]
    half = own_in.shape[0]
    copies = [
        fetch(piece, normed_ref.at[pl.ds(index * rows, rows), :], done.at[index])
        for index, piece in enumerate(normed_in)
    ]
    copies.append(fetch(own_in, both_ref.at[pl.ds(0, half), :], done.at[count]))
    copies.append(fetch(twin_in, both_ref.at[pl.ds(half, half), :], done.at[count + 1]))
    columns = weight_ref.shape[1]
    copies.append(fetch(strips_in.at[:, pl.ds(0, columns)], weight_ref, done.at[count + 2]))
    for copy in copies:
        copy.wait()
    ones = jnp.ones((8, out_ref.shape[1]), jnp.bfloat16)

    def one(index, _):
        columns = rows_at(index, size)
        total = row_dot(normed_ref[:, columns], both_ref[...])
        out_ref[columns, :] = narrow(total)
        share = narrow(total * wide(weight_ref[columns, :]))
        row_ref[:, columns] = lane_dot(ones, share) / gain_ref[8:, columns]
        return 0

    lax.fori_loop(0, out_ref.shape[0] // size, one, 0)


def add_twin_kernel(core_ref, *refs):
    (*refs, send_ref, keep_ref, self_ref) = refs
    rows = keep_ref.shape[0]
    count = len(refs) // 2
    core = core_ref[0]

    def total(index):
        if count == 4:
            return wide(refs[index][...]) + wide(refs[4 + index][...])
        here = slice(index * rows, (index + 1) * rows)
        if count == 1:
            return wide(refs[0][here, :]) + wide(refs[1][here, :])
        before = slice((index - 1) * rows, index * rows)
        own = refs[1][before, :] if index else refs[0][...]
        twin = refs[2][here, :] if index < 3 else refs[3][...]
        return wide(own) + wide(twin)

    self_ref[...] = total(0)
    send_ref[:rows, :] = narrow(total(3))
    along_x = total(1)
    along_y = total(2)

    @pl.when(core == 0)
    def _():
        send_ref[rows:, :] = narrow(along_y)
        keep_ref[...] = along_x

    @pl.when(core == 1)
    def _():
        send_ref[rows:, :] = narrow(along_x)
        keep_ref[...] = along_y


def add_late_kernel(keep_in, got_in, late_ref, keep_ref, got_ref, done):
    rows = keep_ref.shape[0]
    copies = (
        fetch(keep_in, keep_ref, done.at[0]),
        fetch(got_in.at[pl.ds(0, rows), :], got_ref, done.at[1]),
    )
    for copy in copies:
        copy.wait()
    late_ref[...] = narrow(keep_ref[...] + wide(got_ref[...]))


def summed(self_ref, got_ref, late_ref):
    rows = self_ref.shape[0]
    return self_ref[...] + wide(got_ref[rows:, :]) + wide(late_ref[...])


def norm_down(d_normed, stream, inverse, gain):
    scaled = d_normed * gain
    cubed = inverse * inverse * inverse
    return inverse * scaled - stream * cubed * jnp.mean(scaled * stream, axis=1, keepdims=True)


def branch_back_kernel(
    self_ref,
    got_ref,
    late_ref,
    grad_ref,
    one_ref,
    inverse_ref,
    gain_ref,
    full_ref,
    stream_out,
    heads_out,
):
    d_normed = summed(self_ref, got_ref, late_ref)
    d_stream = wide(grad_ref[...]) + norm_down(
        d_normed, one_ref[...], inverse_ref[:, :1], gain_ref[8:9]
    )
    stream_out[...] = d_stream
    d_branch = narrow(d_stream)
    rows = d_branch.shape[0]
    size = 2 * DH
    gap = jnp.zeros((rows, 2 * LANES - size), jnp.float32)
    keep = lanes_of(rows) < size - LANES
    tall = heads_out.shape[1] // 2
    for index in range(heads_out.shape[0]):
        heads = lane_dot(d_branch, full_ref[index * size : (index + 1) * size, :])
        heads_out[index, :tall, :] = narrow(fold(jnp.concatenate([heads, gap], axis=1)))
        start = index * size // LANES * LANES
        columns = wide(d_branch[:, start : start + 2 * LANES])
        if index % 2:
            columns = pltpu.roll(columns, 2 * LANES - 64, 1)
        columns = jnp.concatenate(
            [columns[:, :LANES], jnp.where(keep, columns[:, LANES:], 0.0)], axis=1
        )
        heads_out[index, tall:, :] = narrow(fold(columns))


def stream_grad_kernel(start, fields_ref, weight_ref, out_ref):
    rows = out_ref.shape[0]
    size = rows // 2
    for step in range(2):
        here = slice(step * size, (step + 1) * size)
        there = slice(start + step * size, start + (step + 1) * size)
        out_ref[here, :] = narrow(lane_dot(fields_ref[there, :], weight_ref[...]))


def place_strips_kernel(owner_ref, *refs):
    pieces, (gate_out, up_out, low_ref, wide_ref, done, out_done) = refs[:-6], refs[-6:]
    copies = [fetch(piece, low_ref.at[i], done.at[i]) for i, piece in enumerate(pieces)]
    quarters = low_ref.shape[2] // (2 * LANES)
    outs = []
    for index, copy in enumerate(copies):
        copy.wait()
        wide_ref[index] = wide(low_ref[index])
        for part in range(2 * quarters):
            there = rows_at(part % quarters * 8 + owner_ref[index], LANES)
            target = gate_out if part < quarters else up_out
            outs.append(
                fetch(
                    wide_ref.at[index, :, pl.ds(part * LANES, LANES)],
                    target.at[:, there],
                    out_done.at[index, part],
                )
            )
    for copy in outs:
        copy.wait()


def place_down_kernel(owner_ref, *refs):
    pieces, (down_out, low_ref, wide_ref, done) = refs[:-4], refs[-4:]
    copies = [fetch(piece, low_ref.at[i], done.at[0, i]) for i, piece in enumerate(pieces)]
    outs = []
    for index, copy in enumerate(copies):
        copy.wait()
        wide_ref[index] = wide(low_ref[index])
        there = rows_at(owner_ref[index], wide_ref.shape[1])
        outs.append(fetch(wide_ref.at[index], down_out.at[there, :], done.at[1, index]))
    for copy in outs:
        copy.wait()


def place_last(copies, low_ref, refs, outs, gain_ref, out_done):
    query_ref, key_ref, value_ref, out_ref = refs
    shard = query_ref.shape[0]
    half = shard // 2
    end = shard + half
    for copy in copies:
        copy.wait()
    full = lanes_of(shard) < 64
    keep = lanes_of(half) < 64
    gains = jnp.zeros(gain_ref.shape, jnp.float32)
    targets = []
    for quad in range(2):
        keys, values = [], []
        for pair in (2 * quad, 2 * quad + 1):
            columns = slice(pair * 4 * DH, (pair + 1) * 4 * DH)
            tiles = []
            for index in (2 * pair, 2 * pair + 1):
                block = wide(low_ref[index, :shard, :])
                one, two, key, value = part_fields(block)
                keys.append(key)
                values.append(value)
                tiles.append((block[:, :LANES], block[:, LANES : 2 * LANES]))
                gains = gains + wide(low_ref[index, end : end + 16, :])
            (one, two), (three, four) = tiles
            three, four = pltpu.roll(three, 64, 1), pltpu.roll(four, 64, 1)
            query_ref[:, columns] = jnp.concatenate(
                [one, jnp.where(full, two, three), jnp.where(full, three, four)], axis=1
            )
            for part in range(2):
                tiles = []
                for index in (2 * pair, 2 * pair + 1):
                    block = wide(low_ref[index, shard:end, :])
                    one, two, three = (
                        block[:, start : start + LANES] for start in (0, LANES, 2 * LANES)
                    )
                    if part:
                        two, three = pltpu.roll(two, 64, 1), pltpu.roll(three, 64, 1)
                        one, two = jnp.where(keep, two, three), three
                    tiles.append((one, two))
                (one, two), (three, four) = tiles
                three, four = pltpu.roll(three, 64, 1), pltpu.roll(four, 64, 1)
                out_ref[part * half : (part + 1) * half, columns] = jnp.concatenate(
                    [one, jnp.where(keep, two, three), jnp.where(keep, three, four)], axis=1
                )
        columns = slice(quad * 4 * DH, (quad + 1) * 4 * DH)
        key_ref[:, columns] = join_fields(*keys)
        value_ref[:, columns] = join_fields(*values)
        wide_columns = pl.ds(quad * 8 * DH, 8 * DH)
        some_columns = pl.ds(quad * 4 * DH, 4 * DH)
        for index, (ref, out, here) in enumerate(
            (
                (query_ref, outs[0], wide_columns),
                (key_ref, outs[1], some_columns),
                (value_ref, outs[2], some_columns),
                (out_ref, outs[3], wide_columns),
            )
        ):
            targets.append(fetch(ref.at[:, here], out.at[:, here], out_done.at[4 * quad + index]))
    gain_ref[...] = gains
    return targets


def output_kernel(self_ref, got_ref, late_ref, one_ref, out_ref):
    out_ref[...] = narrow(one_ref[...] + summed(self_ref, got_ref, late_ref))


def finish_kernel(
    owner_ref,
    self_ref,
    got_ref,
    late_ref,
    stream_ref,
    back_ref,
    norm_ref,
    *refs,
):
    last_pieces, gain_ref, refs = refs[:8], refs[8], refs[9:]
    (input_out, *last_outs), refs = refs[:5], refs[5:]
    input_ref, last_low, *refs = refs
    last_refs, (done, out_done, last_done) = refs[:4], refs[4:]
    lasts = [
        fetch(piece, last_low.at[owner_ref[index]], done.at[index])
        for index, piece in enumerate(last_pieces)
    ]
    d_normed = summed(self_ref, got_ref, late_ref)
    stream = wide(stream_ref[...])
    inverse = lax.rsqrt(jnp.mean(stream * stream, axis=1, keepdims=True) + epsilon)
    input_ref[...] = back_ref[...] + norm_down(d_normed, stream, inverse, norm_ref[:1])
    outs = [fetch(input_ref, input_out, out_done.at[0])]
    outs += place_last(lasts, last_low, last_refs, last_outs, gain_ref, last_done)
    for copy in outs:
        copy.wait()


def swapped(field):
    half = DH // 2
    lane = lanes_of(field.shape[0])
    return jnp.where(lane < half, pltpu.roll(field, LANES - half, 1), pltpu.roll(field, half, 1))


def rows_of(weights, field):
    return lax.dot_general(
        weights,
        field,
        (((1,), (1,)), ((), ())),
        precision=lax.Precision.HIGHEST,
        preferred_element_type=jnp.float32,
    )


def fetch(source, target, done):
    copy = pltpu.make_async_copy(source, target, done)
    copy.start()
    return copy


def attend_kernel(
    span,
    near_ref,
    slot_ref,
    cos_ref,
    sin_ref,
    *refs,
):
    (*piece_refs, first_ref), refs = refs[:9], refs[9:]
    (low_ref, gain_ref, level_ref), refs = refs[:3], refs[3:]
    (normed_out, weight_out, query_out, key_out, value_out, mixed_out), refs = refs[:6], refs[6:]
    stream_ref, weight_ref, gains_ref, raw_ref, query_ref, key_ref, value_ref, mixed_ref = refs[:8]
    score_ref, top_ref, sum_ref, in_done, out_done = refs[8:]
    spans = near_ref.shape[0]
    block = 2 * span
    pair = 2 * block
    turns = spans // 2
    quarters, packed, four = first_ref.shape
    shard = weight_ref.shape[0] // quarters
    factor = LOG2E / math.sqrt(DH)

    gain_copies = [
        fetch(
            first_ref.at[quarter, pl.ds(packed - 32, 32), :],
            gains_ref.at[pl.ds(quarter * 32, 32), :],
            in_done.at[turns + quarter],
        )
        for quarter in range(quarters)
    ]
    weight_copies = [
        fetch(
            first_ref.at[quarter, pl.ds(0, shard), :],
            weight_ref.at[pl.ds(quarter * shard, shard), :],
            in_done.at[turns + quarters + quarter],
        )
        for quarter in range(quarters)
    ]
    copies = [
        fetch(piece, stream_ref.at[pl.ds(index * block, block), :], in_done.at[index])
        for index, piece in enumerate(piece_refs)
    ]
    for copy in gain_copies:
        copy.wait()
    for quarter in range(quarters):
        rows = wide(gains_ref[quarter * 32 : quarter * 32 + 16, :])
        here = slice(quarter * shard, (quarter + 1) * shard)
        gain_ref[:8, here] = jnp.broadcast_to(rows[:1, :shard], (8, shard))
        gain_ref[8:, here] = jnp.broadcast_to(rows[1:2, :shard], (8, shard))
    for copy in weight_copies:
        copy.wait()
    out_copies = [fetch(weight_ref, weight_out, out_done.at[0])]
    gain = gain_ref[:1, :]

    def norm(start):
        here = pl.ds(start, span)
        stream = wide(stream_ref[here, :])
        inverse = lax.rsqrt(jnp.mean(stream * stream, axis=1, keepdims=True) + epsilon)
        stream_ref[here, :] = narrow(stream * inverse * gain)

    for step in range(turns // 2):
        copies[2 * step].wait()
        copies[2 * step + 1].wait()
        here = pl.ds(step * pair, pair)
        for part in range(4):
            norm(step * pair + part * span)
        raw_ref[here, :] = plain_dot(stream_ref[here, :], weight_ref[...])
        out_copies.append(
            fetch(stream_ref.at[here, :], normed_out.at[here, :], out_done.at[1 + step])
        )

    lane = lanes_of(span)

    def place(index, _):
        raw = raw_ref[rows_at(near_ref[index], span), :]
        cosine = cos_ref[rows_at(index, span), :]
        sine = sin_ref[rows_at(index, span), :]
        one, two, three, four = part_fields(raw)

        def turned(field):
            return narrow(field * cosine + swapped(field) * sine)

        first = (index // 2) * 4 + index % 2
        query_ref[rows_at(first, span), :] = turned(one)
        query_ref[rows_at(first + 2, span), :] = turned(two)
        key_ref[rows_at(index, span), :] = turned(three)
        value_ref[rows_at(index, span), :] = narrow(jnp.where(lane == DH, 1.0, four))
        return 0

    lax.fori_loop(0, spans, place, 0, unroll=2)
    next_done = 1 + turns // 2
    for source, target in ((query_ref, query_out), (key_ref, key_out), (value_ref, value_out)):
        out_copies.append(fetch(source, target, out_done.at[next_done]))
        next_done += 1

    wide_lane = lanes_of(pair)
    picked = (lanes_of(8) == 0).astype(jnp.float32)

    def store(index, both, rest):
        slot = slot_ref[index]
        low_ref[slot // 2, rows_at(slot % 2, span), :] = narrow(both)
        tail = narrow(rest)
        turned = narrow(pltpu.roll(rest, 64, 1))

        @pl.when(slot % 2 == 0)
        def _():
            low_ref[slot // 2, 2 * span :, :64] = tail[:, :64]

        @pl.when(slot % 2 == 1)
        def _():
            low_ref[slot // 2, 2 * span :, 64:] = turned[:, 64:]

    def widest(top, scores):
        for start in range(0, block, LANES):
            top = jnp.maximum(top, scores[:, start : start + LANES])
        return top

    def score(turn, step):
        scores = lane_dot(query_ref[rows_at(turn, pair), :], key_ref[rows_at(step, block), :])
        score_ref[turn % 2, :, rows_at(step, block)] = scores
        top_ref[...] = widest(top_ref[...], scores)

    def edge(turn):
        row = lax.broadcasted_iota(jnp.int32, (pair, block), 0) % block
        column = lax.broadcasted_iota(jnp.int32, (pair, block), 1)
        scores = lane_dot(query_ref[rows_at(turn, pair), :], key_ref[rows_at(turn, block), :])
        scores = jnp.where(column <= row, scores, masked_score)
        score_ref[turn % 2, :, rows_at(turn, block)] = scores
        top = jnp.max(widest(top_ref[...], scores), axis=1, keepdims=True) * factor
        return jnp.broadcast_to(top, (pair, LANES))

    def weigh(turn, step, top):
        scores = score_ref[turn % 2, :, rows_at(step, block)]
        weights = jnp.exp2(scores * factor - top[:, :1])
        sum_ref[...] += plain_dot(narrow(weights), value_ref[rows_at(step, block), :])

    def finish(turn, top):
        total = sum_ref[:, DH : DH + 1]
        mixed = jnp.where(wide_lane < DH, sum_ref[...] / total, 0.0)
        mixed_ref[rows_at(turn, pair), :] = mixed
        level = top + jnp.log2(total)
        level_ref[rows_at(turn, 8), :] = rows_of(picked, level)
        fetch(
            mixed_ref.at[rows_at(turn, pair), :],
            mixed_out.at[rows_at(turn, pair), :],
            out_done.at[next_done + turn],
        )
        one, two = mixed[:block], pltpu.roll(mixed[block:], DH, 1)
        first = jnp.where(wide_lane[:block] < DH, one, two)
        store(2 * turn, first[:span], two[:span])
        store(2 * turn + 1, first[span:], two[span:])

    def clear():
        sum_ref[...] = jnp.zeros_like(sum_ref)
        top_ref[...] = jnp.full(top_ref.shape, masked_score, jnp.float32)

    def one_turn(turn, top):
        clear()

        def both(step, _):
            weigh(turn, step, top)
            score(turn + 1, step)
            return 0

        lax.fori_loop(0, turn + 1, both, 0)
        finish(turn, top)
        return edge(turn + 1)

    clear()
    top = lax.fori_loop(0, turns - 1, one_turn, edge(0))
    clear()

    def only(step, _):
        weigh(turns - 1, step, top)
        return 0

    lax.fori_loop(0, turns, only, 0)
    finish(turns - 1, top)
    for copy in out_copies:
        copy.wait()
    for turn in range(turns):
        here = pl.ds(turn * pair, pair)
        pltpu.make_async_copy(
            mixed_ref.at[here, :], mixed_out.at[here, :], out_done.at[next_done + turn]
        ).wait()


def attend(steps, near, slot, cosine, sine, first, pieces, span):
    tokens = cosine.shape[0]
    turns = tokens // (2 * span)
    quarters, _, four = first.shape
    block, width = pieces[0].shape
    f32 = jnp.float32
    near_out = (
        shape((turns, 3 * span, LANES)),
        shape((16, width), f32),
        shape((8 * turns, 4 * span), f32),
    )
    far_out = (
        shape((tokens, width)),
        shape((width, four)),
        shape((2 * tokens, LANES)),
        shape((tokens, LANES)),
        shape((tokens, LANES)),
        shape((2 * tokens, LANES), f32),
    )
    state = pltpu.VMEM((4 * span, LANES), f32)
    return steps.run(
        functools.partial(attend_kernel, span),
        near_out,
        (near, slot),
        (cosine, sine),
        far=(*pieces,),
        pinned=(first,),
        far_outs=far_out,
        scratch=(
            pltpu.VMEM((tokens, width), jnp.bfloat16),
            pltpu.VMEM((width, four), jnp.bfloat16),
            pltpu.VMEM((32 * quarters, four), jnp.bfloat16),
            pltpu.VMEM((tokens, four), f32),
            pltpu.VMEM((2 * tokens, LANES), jnp.bfloat16),
            pltpu.VMEM((tokens, LANES), jnp.bfloat16),
            pltpu.VMEM((tokens, LANES), jnp.bfloat16),
            pltpu.VMEM((2 * tokens, LANES), f32),
            pltpu.VMEM((2, 4 * span, tokens), f32),
            state,
            state,
            pltpu.SemaphoreType.DMA((turns + 2 * quarters,)),
            pltpu.SemaphoreType.DMA((4 + turns // 2 + turns,)),
        ),
        limit=60,
        micros=33,
    )


def weight_grads(
    owner_ref, fields_ref, weight_ref, gain_ref, row_ref, branch_ref, heads, copies, last_ref, normed_ref, heads_ref, sum_ref
):
    quarters = last_ref.shape[0]
    four = weight_ref.shape[1]
    shard = weight_ref.shape[0] // quarters
    half = shard // 2
    size = 2 * DH
    tall = branch_ref.shape[1] // 2
    for index, copy in enumerate(heads):
        columns = narrow(unfold(wide(branch_ref[owner_ref[index], tall:, :])))
        copy.wait()
        rows = columns.shape[0]
        sum_ref[index * rows : (index + 1) * rows, :] = columns
    ones = jnp.ones((8, four), jnp.bfloat16)
    gap = jnp.zeros((half, LANES), jnp.float32)
    for quarter in range(quarters):
        here = slice(quarter * shard, (quarter + 1) * shard)
        copies[quarter].wait()
        total = jnp.transpose(row_dot(fields_ref[...], normed_ref[:, here]))
        last_ref[quarter, :shard, :] = narrow(total)
        share = narrow(total * wide(weight_ref[here, :]))
        attn = lane_dot(ones, share) / gain_ref[:8, here]
        rows = jnp.concatenate([attn, row_ref[:, here]], axis=0)
        out_grad = jnp.transpose(row_dot(sum_ref[...], heads_ref[:, here]))
        one, two = out_grad[:half], out_grad[half:]
        both = jnp.concatenate([one, gap], axis=1) + pltpu.roll(
            jnp.concatenate([two, gap], axis=1), size, 1
        )
        last_ref[quarter, shard : shard + half, :] = narrow(both)
        end = shard + half
        last_ref[quarter, end : end + 16, :] = narrow(rows)
        last_ref[quarter, end + 16 :, :] = jnp.zeros_like(last_ref[quarter, end + 16 :, :])


def attend_back_kernel(
    span,
    near_ref,
    slot_ref,
    owner_ref,
    grad_ref,
    total_ref,
    weight_ref,
    gain_ref,
    row_ref,
    *refs,
):
    (*heads_in, normed_in, cos_in, sin_in, query_in, key_in, value_in, mixed_in), refs = refs[:15], refs[15:]
    out_ref, last_ref, cos_ref, sin_ref, query_ref, key_ref, value_ref, mixed_ref, *refs = refs
    head_ref, delta_ref, query_sum, key_sum, value_sum, normed_ref, heads_ref, sum_ref, done = refs
    spans = near_ref.shape[0]
    block = 2 * span
    pair = 2 * block
    turns = spans // 2
    factor = LOG2E / math.sqrt(DH)
    scale = 1.0 / math.sqrt(DH)
    lane = lax.broadcasted_iota(jnp.int32, (span, LANES), 1)
    copies = [
        fetch(source, target, done.at[index])
        for index, (source, target) in enumerate(
            (
                (mixed_in, mixed_ref),
                (key_in, key_ref),
                (query_in, query_ref),
                (value_in, value_ref),
                (cos_in, cos_ref),
                (sin_in, sin_ref),
            )
        )
    ]

    quarters = last_ref.shape[0]
    shard = normed_ref.shape[1] // quarters
    heads = [
        fetch(piece, heads_ref.at[pl.ds(index * block, block), :], done.at[6 + index])
        for index, piece in enumerate(heads_in)
    ]
    normed = [
        fetch(
            normed_in.at[:, pl.ds(quarter * shard, shard)],
            normed_ref.at[:, pl.ds(quarter * shard, shard)],
            done.at[6 + len(heads) + quarter],
        )
        for quarter in range(quarters)
    ]

    def split(index, _):
        slot = slot_ref[index]
        grad = wide(grad_ref[slot // 2, rows_at(slot % 2, span), :])
        tail = wide(grad_ref[slot // 2, 2 * span : 3 * span, :])
        first = (index // 2) * 4 + index % 2
        one = jnp.where(lane < DH, grad, 0.0)
        tail = pltpu.roll(tail, 32 + 64 * (slot % 2), 1)
        two = jnp.where(lane < 32, pltpu.roll(grad, 32, 1), tail)
        two = jnp.where(lane < DH, two, 0.0)
        head_ref[rows_at(first, span), :] = narrow(one)
        head_ref[rows_at(first + 2, span), :] = narrow(two)
        return 0

    lax.fori_loop(0, spans, split, 0, unroll=4)
    copies[0].wait()

    def prepare(turn, _):
        here = rows_at(turn, pair)
        product = wide(head_ref[here, :]) * mixed_ref[here, :]
        delta_ref[rows_at(turn, 8), :] = rows_of(jnp.ones((8, LANES), jnp.float32), product)
        query_sum[rows_at(turn, LANES), :] = jnp.zeros((LANES, pair), jnp.float32)
        return 0

    lax.fori_loop(0, turns, prepare, 0, unroll=2)
    for copy in copies[1:]:
        copy.wait()

    def turned_back(field, index):
        cosine = cos_ref[rows_at(index, span), :]
        sine = sin_ref[rows_at(index, span), :]
        field = field * scale
        return wide(narrow(field * cosine - swapped(field) * sine))

    def one_block(turn, _):
        key = key_ref[rows_at(turn, block), :]
        value = value_ref[rows_at(turn, block), :]
        key_across = narrow(jnp.transpose(wide(key)))

        def one_step(step, diagonal):
            here = rows_at(step, pair)
            query = query_ref[here, :]
            head = head_ref[here, :]
            level = total_ref[rows_at(step, 8), :][:1]
            delta = delta_ref[rows_at(step, 8), :][:1]
            probs = jnp.exp2(lane_dot(key, query) * factor - level)
            if diagonal:
                row = lax.broadcasted_iota(jnp.int32, (block, pair), 0)
                column = lax.broadcasted_iota(jnp.int32, (block, pair), 1) % block
                probs = jnp.where(row <= column, probs, 0.0)
            d_scores = narrow(probs * (lane_dot(value, head) - delta))
            query_sum[rows_at(step, LANES), :] += plain_dot(key_across, d_scores)
            return plain_dot(d_scores, query), plain_dot(narrow(probs), head)

        key_part, value_part = one_step(turn, True)
        key_sum[...] = key_part
        value_sum[...] = value_part

        def two_steps(index, _):
            step = turn + 1 + 2 * index
            key_one, value_one = one_step(step, False)
            key_two, value_two = one_step(step + 1, False)
            key_sum[...] += key_one + key_two
            value_sum[...] += value_one + value_two
            return 0

        left = turns - 1 - turn
        lax.fori_loop(0, left // 2, two_steps, 0)

        @pl.when(left % 2 == 1)
        def _():
            key_one, value_one = one_step(turns - 1, False)
            key_sum[...] += key_one
            value_sum[...] += value_one

        for part in range(2):
            index = 2 * turn + part
            here = rows_at(near_ref[index], span)
            rows = slice(part * span, (part + 1) * span)
            across = query_sum[rows_at(turn, LANES), :]
            first = part * span
            one = turned_back(jnp.transpose(across[:, first : first + span]), index)
            first += block
            two = turned_back(jnp.transpose(across[:, first : first + span]), index)
            three = turned_back(key_sum[rows, :], index)
            out_ref[here, :] = narrow(join_fields(one, two, three, value_sum[rows, :]))
        return 0

    lax.fori_loop(0, turns, one_block, 0)
    weight_grads(
        owner_ref, out_ref, weight_ref, gain_ref, row_ref, grad_ref, heads, normed, last_ref, normed_ref, heads_ref, sum_ref
    )


def attend_back(
    steps, near, slot, owners, grad, total, weights, cosine, sine, query, key, value, mixed, heads, normed, packed, span
):
    tokens, width = normed.shape
    f32 = jnp.float32
    rows = pltpu.VMEM((2 * span, LANES), f32)
    shard = 4 * DH
    return steps.run(
        functools.partial(attend_back_kernel, span),
        (shape((tokens, 4 * DH)), shape((width // shard, packed, 4 * DH))),
        (near, slot, owners),
        (grad, total, *weights),
        far=heads,
        pinned=(normed, cosine, sine, query, key, value, mixed),
        scratch=(
            pltpu.VMEM(cosine.shape, f32),
            pltpu.VMEM(cosine.shape, f32),
            pltpu.VMEM(query.shape, jnp.bfloat16),
            pltpu.VMEM(key.shape, jnp.bfloat16),
            pltpu.VMEM(value.shape, jnp.bfloat16),
            pltpu.VMEM(mixed.shape, f32),
            pltpu.VMEM((2 * tokens, LANES), jnp.bfloat16),
            pltpu.VMEM(total.shape, f32),
            pltpu.VMEM((LANES * (tokens // (2 * span)), 4 * span), f32),
            rows,
            rows,
            pltpu.VMEM((tokens, width), jnp.bfloat16),
            pltpu.VMEM((tokens, width), jnp.bfloat16),
            pltpu.VMEM((tokens, 2 * LANES), jnp.bfloat16),
            pltpu.SemaphoreType.DMA((6 + len(heads) + width // shard,)),
        ),
        limit=60,
        micros=38,
    )


def turn_tables(tokens):
    half = DH // 2
    freqs = jnp.exp(-math.log(rope_base) * 2.0 * jnp.arange(half, dtype=jnp.float32) / DH)
    angle = jnp.arange(tokens, dtype=jnp.int32).astype(jnp.float32)[:, None] * freqs[None, :]
    gap = jnp.zeros((tokens, LANES - DH), jnp.float32)
    cosine, sine = jnp.cos(angle), jnp.sin(angle)
    return (
        jnp.concatenate([cosine, cosine, gap], axis=1),
        jnp.concatenate([-sine, sine, gap], axis=1),
    )


def swap(block, bits):
    routes = [(i, i ^ bits) for i in range(lax.axis_size("ctx"))]
    return lax.ppermute(block, "ctx", routes)


def swap_split(block, even, odd):
    routes = [(i, i ^ (odd if i & CORE else even)) for i in range(lax.axis_size("ctx"))]
    return lax.ppermute(block, "ctx", routes)


def gather_spans(block, core, between=None):
    from_x = swap(block, ALONG_X)
    from_y = swap(block, ALONG_Y)
    twin = swap(block, CORE)
    first = between(from_x, from_y) if between else from_x
    corner = swap_split(jnp.where(core[0] == 0, first, from_y), ALONG_Y, ALONG_X)
    return [block, from_x, from_y, corner] + [
        twin,
        swap(first, CORE),
        swap(from_y, CORE),
        swap(corner, CORE),
    ]


def gather_direct(block):
    blocks = [block] + [swap(block, way) for way in (ALONG_X, ALONG_Y, ALONG_X | ALONG_Y)]
    return blocks + [swap(part, CORE) for part in blocks]


def open_scatter(steps, own, twin, core, limit=20):
    rows, width = sum(part.shape[0] for part in own) // 4, own[0].shape[1]
    some = shape((rows, width), jnp.float32)
    return steps.run(
        add_twin_kernel,
        (shape((2 * rows, width)), some, some),
        (core,),
        (*own, *twin),
        limit=limit,
    )


def turn_scatter(steps, keep, got):
    late = steps.run(
        add_late_kernel,
        shape(keep.shape),
        (),
        (),
        far=(keep, got),
        scratch=(
            pltpu.VMEM(keep.shape, jnp.float32),
            pltpu.VMEM(keep.shape, jnp.bfloat16),
            pltpu.SemaphoreType.DMA((2,)),
        ),
        limit=60,
    )
    return swap_split(late, ALONG_X, ALONG_Y)


def plane_layer(
    activations,
    span_order,
    w_query,
    w_key,
    w_value,
    w_out,
    w_gate,
    w_up,
    w_down,
    attn_gain,
    ffn_gain,
    cotangent,
):
    f32 = jnp.float32
    cycles = lax.axis_size("ctx")
    quarters = lax.axis_size("fsdp")
    mine = lax.axis_index("ctx")
    span = activations.shape[2]
    width = activations.shape[3]
    tokens = 2 * span
    length = cycles * tokens
    half = length // 2
    shard = w_query.shape[0]
    four = 4 * DH
    hidden_size = quarters * w_down.shape[0]
    strip = hidden_size // (quarters * cycles)
    part = hidden_size // cycles
    slab = w_out.shape[0] // cycles
    slabs = width // four
    packed = shard + slabs * slab + 32
    owners = mine ^ jnp.array(RELATIVE, jnp.int32)
    away = mine ^ jnp.arange(cycles, dtype=jnp.int32)
    seat = (away & 1) * 4 + (away >> 2) * 2 + ((away >> 1) & 1)
    slot_of = jnp.argsort(span_order).astype(jnp.int32)
    near_slot = 2 * seat[slot_of // 2] + slot_of % 2
    here = mine.reshape(1).astype(jnp.int32)
    core = here & CORE
    stream = activations.reshape(tokens, width)
    grad_rows = cotangent.reshape(tokens, width)

    steps = Steps(core)
    low = jnp.bfloat16

    gains = jnp.pad(jnp.stack([attn_gain, ffn_gain]), ((0, 30), (0, four - shard)))
    window = pltpu.VMEM((shard, 2 * LANES), low)
    first = steps.run(
        pack_kernel,
        shape((packed, four)),
        (here,),
        (gains,),
        pinned=(w_query, w_key, w_value, w_out),
        scratch=(
            window,
            window,
            window,
            pltpu.VMEM((slab, width), low),
            pltpu.SemaphoreType.DMA((4,)),
        ),
        limit=60,
    )
    first = lax.all_gather(first, "fsdp", axis=0)
    own_strips = steps.run(
        strip_kernel,
        shape((shard, 2 * part + width * strip // shard)),
        (here,),
        (w_gate, w_up, w_down),
        limit=28,
    )
    all_strips = lax.all_gather(own_strips, "fsdp", axis=0, tiled=True)
    cosine, sine = turn_tables(length)
    streams = gather_spans(
        stream, core, lambda one, two: after(one, two, own_strips, cosine, sine, near_slot, slot_of)
    )
    out_part = first[:, shard : shard + slabs * slab].reshape(quarters * slabs * slab, four)
    folded, gains, level, normed1, w_fields, query, key, value, attended = attend(
        steps, near_slot, slot_of, cosine, sine, first, streams, span
    )
    grads = gather_spans(
        after(grad_rows, streams[3]), core, lambda one, two: after(one, two, folded)
    )
    outs = gather_direct(out_part)
    steps.wait(*outs, grads[3])
    folded = lax.all_to_all(after(folded, *grads[1:3], *outs[1:4]), "ctx", 0, 0)
    one_tile = shape((tokens, LANES), f32)
    stream_one, normed2, inverse, heads_low, full_out = steps.run(
        branch_kernel,
        (shape((tokens, width), f32), shape((tokens, width)), one_tile, shape((tokens, width))),
        (owners,),
        (folded, stream, gains),
        far=outs,
        far_outs=(shape((width, width)),),
        scratch=(
            pltpu.VMEM((width, width), low),
            pltpu.VMEM((cycles, *outs[0].shape), low),
            pltpu.SemaphoreType.DMA((cycles,)),
        ),
        limit=60,
        micros=6,
    )
    normed2 = gather_spans(normed2, core)
    def strips(pieces, grad_pieces, *before):
        results = steps.run(
            functools.partial(strips_kernel, len(pieces), bool(before)),
            (
                shape((part, width), low if before else f32),
                *(shape((tokens, width)),) * 4,
                shape((3 * tokens, width)),
                shape((tokens, width)),
            ),
            (),
            before,
            far=(*pieces, *grad_pieces),
            pinned=(all_strips,),
            far_outs=(shape((half, 2 * part)),),
            scratch=(
                pltpu.VMEM((part, width), f32),
                pltpu.VMEM((width, 2 * part), low),
                pltpu.VMEM((part, width), low),
                pltpu.VMEM((half, width), low),
                pltpu.VMEM((half, width), low),
                pltpu.VMEM((half, 2 * part), low),
                pltpu.SemaphoreType.DMA((2 * len(pieces),)),
                pltpu.SemaphoreType.DMA((len(pieces) // 2,)),
                pltpu.SemaphoreType.DMA((1 + quarters * (shard // strip),)),
            ),
                limit=60,
            micros=20,
        )
        return results[0], results[1:5], results[5], results[6], results[7]

    early, later = (4, 5, 6, 0), (1, 2, 3, 7)
    down_early, streams_early, sums_twin, sum_self, both_early = strips(
        [normed2[i] for i in early], [grads[i] for i in early]
    )
    heads = gather_spans(
        after(heads_low, normed2[1], normed2[2]), core, lambda one, two: after(one, two, down_early)
    )
    steps.wait(heads[1], heads[2])
    twins = [swap(block, CORE) for block in streams_early[:3]]
    normed2[7] = swap(after(normed2[3], down_early), CORE)
    down_sum, streams_later, sums_own, sum_corner, both_later = strips(
        [normed2[i] for i in later], [grads[i] for i in later], down_early
    )
    twins.append(swap(streams_later[3], CORE))
    grad_down = lax.psum_scatter(
        after(down_sum, heads[3]), "fsdp", scatter_dimension=0, tiled=True
    )
    sums_twin = swap(after(sums_twin, down_sum), CORE)
    sum_corner = swap(sum_corner, CORE)
    send, keep, total = open_scatter(
        steps, (streams_early[3], *streams_later[:3]), twins, core, 60
    )
    got = swap_split(send, ALONG_Y, ALONG_X)
    steps.wait(heads[3])
    grad_both, grad_ffn = steps.run(
        functools.partial(strip_grad_kernel, cycles),
        (shape((width, 2 * part)), shape((8, width), f32)),
        (),
        (gains,),
        far=[normed2[i] for i in early + later],
        pinned=(both_early, both_later, all_strips),
        scratch=(
            pltpu.VMEM((length, width), low),
            pltpu.VMEM((length, 2 * part), low),
            pltpu.VMEM((width, 2 * part), low),
            pltpu.SemaphoreType.DMA((cycles + 3,)),
        ),
        limit=60,
        micros=12,
    )
    grad_both = lax.psum_scatter(after(grad_both, got), "fsdp", scatter_dimension=0, tiled=True)
    late_got = turn_scatter(steps, keep, got)
    ffn_send, ffn_keep, ffn_total = open_scatter(
        steps, (sum_self, sums_own), (sums_twin, sum_corner), core
    )
    d_stream_one, d_heads = steps.run(
        branch_back_kernel,
        (
            shape((tokens, width), f32),
            shape((cycles, 6 * span, LANES)),
        ),
        (),
        (total, got, late_got, grad_rows, stream_one, inverse, gains, full_out),
        limit=28,
        micros=4,
    )
    d_heads = lax.all_to_all(d_heads, "ctx", 0, 0)
    ffn_got = swap_split(after(ffn_send, d_heads), ALONG_Y, ALONG_X)
    grad_downs = gather_direct(after(grad_down, d_heads))
    d_fields, last = attend_back(
        steps,
        near_slot,
        slot_of,
        owners,
        d_heads,
        level,
        (w_fields, gains, grad_ffn),
        cosine,
        sine,
        query,
        key,
        value,
        attended,
        heads,
        normed1,
        packed,
        span,
    )
    last = after(last, ffn_got, *grad_downs[1:4])
    last = lax.psum_scatter(last, "fsdp", scatter_dimension=0, tiled=False)
    steps.wait(ffn_got, *grad_downs[1:4])

    def stream_grad(start):
        return steps.run(
            functools.partial(stream_grad_kernel, start),
            shape((half, width)),
            (),
            (d_fields, w_fields),
            micros=2,
        )

    d_normed1_twin = swap(stream_grad(half), CORE)
    d_normed1_own = stream_grad(0)
    send, keep, total = open_scatter(steps, (d_normed1_own,), (d_normed1_twin,), core)
    both_pieces = gather_spans(
        after(grad_both, d_fields), core, lambda one, two: after(one, two, send)
    )
    got = swap_split(send, ALONG_Y, ALONG_X)
    ffn_late_got = turn_scatter(steps, ffn_keep, ffn_got)
    steps.wait(both_pieces[1], both_pieces[2])
    grad_down = steps.run(
        place_down_kernel,
        (),
        (owners,),
        (),
        far=grad_downs,
        far_outs=(shape((hidden_size // quarters, width), f32),),
        scratch=(
            pltpu.VMEM((cycles, strip, width), low),
            pltpu.VMEM((cycles, strip, width), f32),
            pltpu.SemaphoreType.DMA((2, cycles)),
        ),
        limit=60,
        micros=1000,
    )[0]
    wide_strip = shape((shard, hidden_size), f32)
    grad_gate, grad_up = steps.run(
        place_strips_kernel,
        (),
        (owners,),
        (),
        far=both_pieces,
        far_outs=(wide_strip, wide_strip),
        scratch=(
            pltpu.VMEM((cycles, shard, 2 * part), low),
            pltpu.VMEM((cycles, shard, 2 * part), f32),
            pltpu.SemaphoreType.DMA((cycles,)),
            pltpu.SemaphoreType.DMA((cycles, 2 * quarters)),
        ),
        limit=60,
    )
    output = steps.run(
        output_kernel,
        shape((tokens, width)),
        (),
        (ffn_total, ffn_got, ffn_late_got, stream_one),
    )
    late_got = turn_scatter(steps, keep, got)
    last = gather_direct(after(last, grad_down))
    narrow_grad = shape((shard, width // 2), f32)
    wide_grad = shape((shard, width), f32)
    grad_gains, input_grad, *weight_grads = steps.run(
        finish_kernel,
        (shape((16, four), f32),),
        (owners,),
        (
            total,
            got,
            late_got,
            stream,
            d_stream_one,
            gains,
        ),
        far=last,
        far_outs=(
            shape((tokens, width), f32),
            wide_grad,
            narrow_grad,
            narrow_grad,
            wide_grad,
        ),
        scratch=(
            pltpu.VMEM((tokens, width), f32),
            pltpu.VMEM((cycles, packed, four), low),
            pltpu.VMEM((shard, width), f32),
            pltpu.VMEM((shard, width // 2), f32),
            pltpu.VMEM((shard, width // 2), f32),
            pltpu.VMEM((shard, width), f32),
            pltpu.SemaphoreType.DMA((cycles,)),
            pltpu.SemaphoreType.DMA((1,)),
            pltpu.SemaphoreType.DMA((8,)),
        ),
        limit=60,
    )
    grad_query, grad_key, grad_value, grad_out = weight_grads
    return (
        output.reshape(activations.shape),
        input_grad.reshape(activations.shape),
        grad_query,
        grad_key,
        grad_value,
        grad_out,
        grad_gate,
        grad_up,
        grad_down,
        grad_gains[0],
        grad_gains[8],
    )


def solution(mesh):
    in_specs = (
        P("fsdp", "ctx", None, None),
        P(),
        P("fsdp", None),
        P("fsdp", None),
        P("fsdp", None),
        P("fsdp", None),
        P("fsdp", None),
        P("fsdp", None),
        P("fsdp", None),
        P("fsdp"),
        P("fsdp"),
        P("fsdp", "ctx", None, None),
    )
    out_specs = (
        P("fsdp", "ctx", None, None),
        P("fsdp", "ctx", None, None),
        P("fsdp", None),
        P("fsdp", None),
        P("fsdp", None),
        P("fsdp", None),
        P("fsdp", None),
        P("fsdp", None),
        P("fsdp", None),
        P("fsdp"),
        P("fsdp"),
    )
    cycles = mesh.shape["ctx"]

    def per_device(*arrays):
        heads = arrays[3].shape[1] // DH
        if cycles == len(RELATIVE) == heads and arrays[2].shape == (4 * DH, 2 * heads * DH):
            return plane_layer(*arrays)
        return ring_layer(*arrays)

    return jax.shard_map(
        per_device, mesh=mesh, in_specs=in_specs, out_specs=out_specs, check_vma=False
    )
```
